32 devices in a mesh: seq: 8 (over z, x), dp: 4 (over y, core).
Axes of the slice: x: 2, y: 2, z: 4, core: 2. Of those that a mesh axis runs over, the one named last changes fastest.
Arguments:
- tokens: bfloat16 [4, 1024, 2048], P('dp', 'seq'), may hold values from -6 to 6
- cotangent: bfloat16 [4, 1024, 2048], P('dp', 'seq'), may hold values from -6 to 6
- qkv_weight: float32 [2048, 6144], P(('seq', 'dp')), may hold values from -0.125 to 0.125
- out_weight: float32 [2048, 2048], P(('seq', 'dp')), may hold values from -3 to 3
- gate_up_weight: float32 [2048, 16384], P(('seq', 'dp')), may hold values from -0.125 to 0.125
- down_weight: float32 [2048, 8192], P(('seq', 'dp')), may hold values from -0.0625 to 0.0625
- gains: float32 [2, 2048], P(None, ('seq', 'dp')), may hold values from 0.5 to 1.5
- qkv_first: float32 [2048, 6144], P(('seq', 'dp')), may hold values from -48 to 48
- out_first: float32 [2048, 2048], P(('seq', 'dp')), may hold values from -8 to 8
- gate_up_first: float32 [2048, 16384], P(('seq', 'dp')), may hold values from -12 to 12
- down_first: float32 [2048, 8192], P(('seq', 'dp')), may hold values from -24 to 24
- gains_first: float32 [2, 2048], P(None, ('seq', 'dp')), may hold values from -64 to 64
- qkv_second: float32 [2048, 6144], P(('seq', 'dp')), may hold values from 6.144 to 24.576
- out_second: float32 [2048, 2048], P(('seq', 'dp')), may hold values from 0.14 to 0.56
- gate_up_second: float32 [2048, 16384], P(('seq', 'dp')), may hold values from 0.36864 to 1.47456
- down_second: float32 [2048, 8192], P(('seq', 'dp')), may hold values from 1.47456 to 5.89824
- gains_second: float32 [2, 2048], P(None, ('seq', 'dp')), may hold values from 8.192 to 32.768
Outputs:
- block_out: bfloat16 [4, 1024, 2048], P('dp', 'seq')
- input_grad: float32 [4, 1024, 2048], P('dp', 'seq')
- new_qkv_weight: float32 [2048, 6144], P(('seq', 'dp'))
- new_out_weight: float32 [2048, 2048], P(('seq', 'dp'))
- new_gate_up_weight: float32 [2048, 16384], P(('seq', 'dp'))
- new_down_weight: float32 [2048, 8192], P(('seq', 'dp'))
- new_gains: float32 [2, 2048], P(None, ('seq', 'dp'))
- new_qkv_first: float32 [2048, 6144], P(('seq', 'dp'))
- new_out_first: float32 [2048, 2048], P(('seq', 'dp'))
- new_gate_up_first: float32 [2048, 16384], P(('seq', 'dp'))
- new_down_first: float32 [2048, 8192], P(('seq', 'dp'))
- new_gains_first: float32 [2, 2048], P(None, ('seq', 'dp'))
- new_qkv_second: float32 [2048, 6144], P(('seq', 'dp'))
- new_out_second: float32 [2048, 2048], P(('seq', 'dp'))
- new_gate_up_second: float32 [2048, 16384], P(('seq', 'dp'))
- new_down_second: float32 [2048, 8192], P(('seq', 'dp'))
- new_gains_second: float32 [2, 2048], P(None, ('seq', 'dp'))
The draws below stay inside these ranges and needn't reach their ends.
All inputs are finite; a program needn't handle non-finite values.
Results may differ from the reference program's by a relative error of at most 0.014.
The reference program's roundings to bfloat16 on the way count: a program that leaves them out, or rounds other values in their place, can miss the bound.
Values may be sent and summed in bfloat16 or wider, within the bound.
A program may use at most 832 MiB of HBM per device.

```python
import math
import jax
import jax.numpy as jnp
from jax import lax

D = 2048
HEADS = 32
HEAD_DIM = 64
FF = 8192
BLOCK = 512
STEP = 10
LENGTH = 1024
SEQS = 4
TOKENS = 4096


def block_scale(own_key, shape, pieces, least, largest):
    level, own = 1.0, jax.random.fold_in(own_key, 6)
    for dim, shards_of in pieces:
        draws = jnp.exp(jax.random.uniform(jax.random.fold_in(own, dim), (shards_of,), jnp.float32, least / len(pieces), largest / len(pieces)))
        level = level * jnp.repeat(draws, shape[dim] // shards_of).reshape([-1 if axis == dim else 1 for axis in range(len(shape))])
    return level


def gaussian(stream_key, dims, width, most, pieces=(), kind=jnp.bfloat16):
    gain = block_scale(stream_key, dims, pieces, -0.22, 0.18) if pieces else 1.0
    drawn = jax.random.normal(stream_key, dims, jnp.float32) * width * gain
    return jnp.minimum(jnp.maximum(drawn, -most), most).astype(kind)


def setup_inputs(seed: int = 0) -> dict:
    streams_of = jax.random.split(jax.random.key(seed), 18)
    tokens = gaussian(streams_of[0], (SEQS, LENGTH, D), 1.0, 6.0, ((0, 4), (1, 8)))
    cotangent = gaussian(streams_of[1], (SEQS, LENGTH, D), 1.0, 6.0, ((0, 4), (1, 8)))
    qkv_weight = gaussian(streams_of[2], (D, 3 * D), D ** -0.5, 0.125, ((0, 32),), jnp.float32)
    out_weight = gaussian(streams_of[3], (D, D), (max(D // 512, 1)) ** -0.5, 3.0, ((0, 32),), jnp.float32)
    gate_up_weight = gaussian(streams_of[4], (D, 2 * FF), D ** -0.5, 0.125, ((0, 32),), jnp.float32)
    down_weight = gaussian(streams_of[5], (D, FF), FF ** -0.5, 0.0625, ((0, 32),), jnp.float32)
    gains = jnp.clip(1.0 + 0.1 * jax.random.normal(streams_of[6], (2, D), jnp.float32), 0.5, 1.5)
    qkv_first = gaussian(streams_of[7], (D, 3 * D), (0.13 * TOKENS ** 0.5), 48.0, ((0, 32),), jnp.float32)
    out_first = gaussian(streams_of[8], (D, D), (0.65 * SEQS ** 0.5), 8.0, ((0, 32),), jnp.float32)
    gate_up_first = gaussian(streams_of[9], (D, 2 * FF), (0.033 * TOKENS ** 0.5), 12.0, ((0, 32),), jnp.float32)
    down_first = gaussian(streams_of[10], (D, FF), (0.066 * TOKENS ** 0.5), 24.0, ((0, 32),), jnp.float32)
    gains_first = gaussian(streams_of[11], (2, D), (0.16 * TOKENS ** 0.5), 64.0, ((1, 32),), jnp.float32)
    qkv_second = jnp.clip(jnp.exp(math.log(24.576) - 1.3862944 * jax.random.uniform(streams_of[12], (D, 3 * D), jnp.float32) ** block_scale(streams_of[12], (D, 3 * D), ((0, 32),), -0.2, 0.2)), 6.144, 24.576)
    out_second = jnp.clip(jnp.exp(math.log(0.56) - 1.3862944 * jax.random.uniform(streams_of[13], (D, D), jnp.float32) ** block_scale(streams_of[13], (D, D), ((0, 32),), -0.2, 0.2)), 0.14, 0.56)
    gate_up_second = jnp.clip(jnp.exp(math.log(1.47456) - 1.3862944 * jax.random.uniform(streams_of[14], (D, 2 * FF), jnp.float32) ** block_scale(streams_of[14], (D, 2 * FF), ((0, 32),), -0.2, 0.2)), 0.36864, 1.47456)
    down_second = jnp.clip(jnp.exp(math.log(5.89824) - 1.3862944 * jax.random.uniform(streams_of[15], (D, FF), jnp.float32) ** block_scale(streams_of[15], (D, FF), ((0, 32),), -0.2, 0.2)), 1.47456, 5.89824)
    gains_second = jnp.clip(jnp.exp(math.log(32.768) - 1.3862944 * jax.random.uniform(streams_of[16], (2, D), jnp.float32) ** block_scale(streams_of[16], (2, D), ((1, 32),), -0.2, 0.2)), 8.192, 32.768)
    return {"tokens": tokens, "cotangent": cotangent, "qkv_weight": qkv_weight, "out_weight": out_weight, "gate_up_weight": gate_up_weight, "down_weight": down_weight, "gains": gains, "qkv_first": qkv_first, "out_first": out_first, "gate_up_first": gate_up_first, "down_first": down_first, "gains_first": gains_first, "qkv_second": qkv_second, "out_second": out_second, "gate_up_second": gate_up_second, "down_second": down_second, "gains_second": gains_second}


NORM_EPS = 1e-05
ROPE_BASE = 130000.0
BETA_ONE = 0.9
BETA_TWO = 0.999
ADAM_EPS = 1e-08
WEIGHT_DECAY = 0.1
MASKED = -1e+30
HIGHEST = lax.Precision.HIGHEST

@jax.custom_vjp
def low(v):
    return lax.optimization_barrier(v.astype(jnp.bfloat16)).astype(jnp.float32)

@jax.custom_vjp
def low_back(v):
    return v

def low_keep(v):
    return (low(v), None)

def low_pass(kept, grad):
    return (grad,)

def back_keep(v):
    return (v, None)

def back_low(kept, grad):
    return (low(grad),)
low.defvjp(low_keep, low_pass)
low_back.defvjp(back_keep, back_low)

def matmul(left, right):
    return jnp.dot(left, right, precision=HIGHEST, preferred_element_type=jnp.float32)

def rms_norm(values, gain_row):
    inverse = lax.rsqrt(lax.optimization_barrier(jnp.mean(values * values, axis=-1, keepdims=True)) + NORM_EPS)
    return values * inverse * gain_row

def rope_tables(length):
    half_dim = HEAD_DIM // 2
    exponent = jnp.arange(half_dim, dtype=jnp.float32) * (2.0 / HEAD_DIM)
    frequency = ROPE_BASE ** (-exponent)
    angles = jnp.arange(length, dtype=jnp.float32)[:, None] * frequency[None, :]
    return (jnp.cos(angles)[:, None, :], jnp.sin(angles)[:, None, :])

def rotate(tensor, cosines, sines):
    half_dim = HEAD_DIM // 2
    lower_half = tensor[..., :half_dim]
    upper_half = tensor[..., half_dim:]
    return jnp.concatenate([lower_half * cosines - upper_half * sines, upper_half * cosines + lower_half * sines], axis=-1)

def attention(queries, keys_all, values_all):
    block_count = LENGTH // BLOCK
    columns = jnp.arange(LENGTH, dtype=jnp.int32)

    def one_block(pair):
        query_rows, row_start = pair
        products = jnp.einsum('qhd,khd->hqk', query_rows, keys_all, precision=HIGHEST)
        products = low_back(products)
        row_ids = row_start + jnp.arange(BLOCK, dtype=jnp.int32)
        scores = jnp.where(columns[None, None, :] <= row_ids[None, :, None], products * HEAD_DIM ** (-0.5), MASKED)
        row_max = lax.optimization_barrier(jnp.max(scores, axis=-1, keepdims=True))
        expo_vals = jnp.exp(scores - row_max)
        attend_weights = low(expo_vals / lax.optimization_barrier(jnp.sum(expo_vals, axis=-1, keepdims=True)))
        return jnp.einsum('hqk,khd->qhd', attend_weights, values_all, precision=HIGHEST)
    blocks = queries.reshape(block_count, BLOCK, HEADS, HEAD_DIM)
    starts = jnp.arange(block_count, dtype=jnp.int32) * BLOCK
    results = lax.map(jax.checkpoint(one_block), (blocks, starts))
    return results.reshape(LENGTH, HEADS, HEAD_DIM)

def layer(hidden_in, qkv_weight, out_weight, gate_up_weight, down_weight, gains):
    cosines, sines = rope_tables(LENGTH)
    normed_one = low(rms_norm(hidden_in, low(gains[0])))
    projected = low_back(matmul(normed_one, low(qkv_weight)))
    shaped = projected.reshape(LENGTH, 3, HEADS, HEAD_DIM)
    queries = low(rotate(shaped[:, 0], cosines, sines))
    keys_all = low(rotate(shaped[:, 1], cosines, sines))
    values_all = low(shaped[:, 2])
    attended = low(low_back(attention(queries, keys_all, values_all).reshape(LENGTH, D)))
    residual = hidden_in + low_back(matmul(attended, low(out_weight)))
    normed_two = low(rms_norm(residual, low(gains[1])))
    gate_up = low_back(matmul(normed_two, low(gate_up_weight)))
    gate_vals = gate_up[:, :FF]
    up_vals = gate_up[:, FF:]
    activated = low(gate_vals * jax.nn.sigmoid(gate_vals) * up_vals)
    return residual + jnp.dot(activated, low(down_weight).T, precision=HIGHEST, preferred_element_type=jnp.float32)

def forward(hidden_all, qkv_weight, out_weight, gate_up_weight, down_weight, gains):

    def per_sequence(hidden_in):
        return layer(hidden_in, qkv_weight, out_weight, gate_up_weight, down_weight, gains)
    return lax.map(per_sequence, hidden_all)

def adam_step(weight, gradient, first, second, rate, decay):
    new_first = BETA_ONE * first + (1.0 - BETA_ONE) * gradient
    new_second = BETA_TWO * second + (1.0 - BETA_TWO) * gradient * gradient
    first_hat = new_first / (1.0 - BETA_ONE ** STEP)
    second_hat = new_second / (1.0 - BETA_TWO ** STEP)
    new_weight = weight - rate * (first_hat / (jnp.sqrt(second_hat) + ADAM_EPS) + decay * weight)
    return (new_weight, new_first, new_second)

def reference(tokens, cotangent, qkv_weight, out_weight, gate_up_weight, down_weight, gains, qkv_first, out_first, gate_up_first, down_first, gains_first, qkv_second, out_second, gate_up_second, down_second, gains_second):
    hidden_all = tokens.astype(jnp.float32)
    result, pull_back = jax.vjp(forward, hidden_all, qkv_weight, out_weight, gate_up_weight, down_weight, gains)
    gradients = pull_back(cotangent.astype(jnp.float32))
    wide_rate = 2.5 * D ** (-0.5)
    out_rate = 2.5 * max(D // 512, 1) ** (-0.5)
    down_rate = 2.5 * FF ** (-0.5)
    qkv_new = adam_step(qkv_weight, gradients[1], qkv_first, qkv_second, wide_rate, WEIGHT_DECAY)
    out_new = adam_step(out_weight, gradients[2], out_first, out_second, out_rate, WEIGHT_DECAY)
    gate_up_new = adam_step(gate_up_weight, gradients[3], gate_up_first, gate_up_second, wide_rate, WEIGHT_DECAY)
    down_new = adam_step(down_weight, gradients[4], down_first, down_second, down_rate, WEIGHT_DECAY)
    gains_new = adam_step(gains, gradients[5], gains_first, gains_second, 0.5, 0.0)
    return (result.astype(jnp.bfloat16), gradients[0], qkv_new[0], out_new[0], gate_up_new[0], down_new[0], gains_new[0], qkv_new[1], out_new[1], gate_up_new[1], down_new[1], gains_new[1], qkv_new[2], out_new[2], gate_up_new[2], down_new[2], gains_new[2])
```

```python
import jax
import jax.numpy as jnp
from jax import lax
from jax.sharding import Mesh
from jax.sharding import PartitionSpec as P

D = 2048
HEADS = 32
HEAD_DIM = 64
FF = 8192
BLOCK = 512
STEP = 10


NORM_EPS = 1e-05
ROPE_BASE = 130000.0
BETA_ONE = 0.9
BETA_TWO = 0.999
ADAM_EPS = 1e-08
WEIGHT_DECAY = 0.1
MASKED = -1e30


def rms_parts(values):
    inverse = lax.rsqrt(jnp.mean(values * values, axis=-1, keepdims=True) + NORM_EPS)
    return (values * inverse, inverse)


def rope_tables(positions):
    half_dim = HEAD_DIM // 2
    exponent = jnp.arange(half_dim, dtype=jnp.float32) * (2.0 / HEAD_DIM)
    frequency = ROPE_BASE ** (-exponent)
    angles = positions.astype(jnp.float32)[:, None] * frequency[None, :]
    return (jnp.cos(angles)[:, None, :], jnp.sin(angles)[:, None, :])


def rotate(tensor, cosines, sines):
    half_dim = HEAD_DIM // 2
    lower_half = tensor[..., :half_dim]
    upper_half = tensor[..., half_dim:]
    return jnp.concatenate(
        [lower_half * cosines - upper_half * sines, upper_half * cosines + lower_half * sines],
        axis=-1,
    )


def unrotate(tensor, cosines, sines):
    half_dim = HEAD_DIM // 2
    lower_half = tensor[..., :half_dim]
    upper_half = tensor[..., half_dim:]
    return jnp.concatenate(
        [lower_half * cosines + upper_half * sines, upper_half * cosines - lower_half * sines],
        axis=-1,
    )


def block_scores(query_rows, key_heads, key_id, block_id):
    key_rows = lax.dynamic_slice_in_dim(key_heads, key_id * BLOCK, BLOCK, 0)
    products = jnp.einsum(
        "qhd,khd->hqk", query_rows, key_rows, preferred_element_type=jnp.float32
    ) * HEAD_DIM ** (-0.5)
    local_ids = jnp.arange(BLOCK, dtype=jnp.int32)
    allowed = (key_id < block_id) | (local_ids[None, :] <= local_ids[:, None])
    return jnp.where(allowed[None], products, MASKED)


def row_normalizer(query_rows, key_heads, block_id):
    row_shape = (query_rows.shape[1], BLOCK, 1)

    def absorb(key_id, state):
        running_max, running_total = state
        scores = block_scores(query_rows, key_heads, key_id, block_id)
        new_max = jnp.maximum(running_max, jnp.max(scores, axis=-1, keepdims=True))
        running_total = running_total * jnp.exp(running_max - new_max) + jnp.sum(
            jnp.exp(scores - new_max), axis=-1, keepdims=True
        )
        return (new_max, running_total)

    start_state = (jnp.full(row_shape, MASKED, jnp.float32), jnp.zeros(row_shape, jnp.float32))
    final_max, final_total = lax.fori_loop(0, block_id + 1, absorb, start_state)
    return final_max + jnp.log(final_total)


def attend_forward(query_heads, key_heads, value_heads):
    seq_len, heads_here, head_dim = query_heads.shape

    def one_block(block_id, carry):
        out_all, lse_all = carry
        row_start = block_id * BLOCK
        query_rows = lax.dynamic_slice_in_dim(query_heads, row_start, BLOCK, 0)
        row_lse = row_normalizer(query_rows, key_heads, block_id)

        def weigh_values(key_id, running):
            scores = block_scores(query_rows, key_heads, key_id, block_id)
            weights_low = jnp.exp(scores - row_lse).astype(jnp.bfloat16)
            value_rows = lax.dynamic_slice_in_dim(value_heads, key_id * BLOCK, BLOCK, 0)
            return running + jnp.einsum(
                "hqk,khd->qhd", weights_low, value_rows, preferred_element_type=jnp.float32
            )

        attended = lax.fori_loop(
            0, block_id + 1, weigh_values, jnp.zeros((BLOCK, heads_here, head_dim), jnp.float32)
        )
        out_all = lax.dynamic_update_slice_in_dim(
            out_all, attended.astype(jnp.bfloat16), row_start, 0
        )
        lse_all = lax.dynamic_update_slice_in_dim(lse_all, row_lse, row_start, 1)
        return (out_all, lse_all)

    start_carry = (
        jnp.zeros((seq_len, heads_here, head_dim), jnp.bfloat16),
        jnp.zeros((heads_here, seq_len, 1), jnp.float32),
    )
    return lax.fori_loop(0, seq_len // BLOCK, one_block, start_carry)


def attend_backward(query_heads, key_heads, value_heads, grad_heads, lse_all):
    seq_len, heads_here, head_dim = query_heads.shape
    score_scale = HEAD_DIM ** (-0.5)

    def one_block(block_id, carry):
        grad_q_all, grad_k_all, grad_v_all = carry
        row_start = block_id * BLOCK
        query_rows = lax.dynamic_slice_in_dim(query_heads, row_start, BLOCK, 0)
        grad_rows = lax.dynamic_slice_in_dim(grad_heads, row_start, BLOCK, 0)
        row_lse = lax.dynamic_slice_in_dim(lse_all, row_start, BLOCK, 1)

        def probs_and_grads(key_id):
            scores = block_scores(query_rows, key_heads, key_id, block_id)
            probs = jnp.exp(scores - row_lse)
            value_rows = lax.dynamic_slice_in_dim(value_heads, key_id * BLOCK, BLOCK, 0)
            grad_probs = jnp.einsum(
                "qhd,khd->hqk", grad_rows, value_rows, preferred_element_type=jnp.float32
            )
            return (probs, grad_probs)

        def add_delta(key_id, running):
            probs, grad_probs = probs_and_grads(key_id)
            return running + jnp.sum(probs * grad_probs, axis=-1, keepdims=True)

        row_delta = lax.fori_loop(
            0, block_id + 1, add_delta, jnp.zeros((heads_here, BLOCK, 1), jnp.float32)
        )

        def spread(key_id, inner):
            grad_q_rows, grad_k_acc, grad_v_acc = inner
            probs, grad_probs = probs_and_grads(key_id)
            key_start = key_id * BLOCK
            key_rows = lax.dynamic_slice_in_dim(key_heads, key_start, BLOCK, 0)
            grad_scores = (probs * (grad_probs - row_delta) * score_scale).astype(jnp.bfloat16)
            grad_q_rows = grad_q_rows + jnp.einsum(
                "hqk,khd->qhd", grad_scores, key_rows, preferred_element_type=jnp.float32
            )
            grad_k_part = jnp.einsum(
                "hqk,qhd->khd", grad_scores, query_rows, preferred_element_type=jnp.float32
            )
            grad_v_part = jnp.einsum(
                "hqk,qhd->khd",
                probs.astype(jnp.bfloat16),
                grad_rows,
                preferred_element_type=jnp.float32,
            )
            grad_k_acc = lax.dynamic_update_slice_in_dim(
                grad_k_acc,
                lax.dynamic_slice_in_dim(grad_k_acc, key_start, BLOCK, 0) + grad_k_part,
                key_start,
                0,
            )
            grad_v_acc = lax.dynamic_update_slice_in_dim(
                grad_v_acc,
                lax.dynamic_slice_in_dim(grad_v_acc, key_start, BLOCK, 0) + grad_v_part,
                key_start,
                0,
            )
            return (grad_q_rows, grad_k_acc, grad_v_acc)

        start_inner = (
            jnp.zeros((BLOCK, heads_here, head_dim), jnp.float32),
            grad_k_all,
            grad_v_all,
        )
        grad_q_rows, grad_k_all, grad_v_all = lax.fori_loop(0, block_id + 1, spread, start_inner)
        grad_q_all = lax.dynamic_update_slice_in_dim(grad_q_all, grad_q_rows, row_start, 0)
        return (grad_q_all, grad_k_all, grad_v_all)

    zeros_all = jnp.zeros((seq_len, heads_here, head_dim), jnp.float32)
    return lax.fori_loop(0, seq_len // BLOCK, one_block, (zeros_all, zeros_all, zeros_all))


def adam_step(weight, gradient, first, second, rate, decay):
    new_first = BETA_ONE * first + (1.0 - BETA_ONE) * gradient
    new_second = BETA_TWO * second + (1.0 - BETA_TWO) * gradient * gradient
    first_hat = new_first / (1.0 - BETA_ONE**STEP)
    second_hat = new_second / (1.0 - BETA_TWO**STEP)
    new_weight = weight - rate * (first_hat / (jnp.sqrt(second_hat) + ADAM_EPS) + decay * weight)
    return (new_weight, new_first, new_second)


def shards(
    tokens,
    cotangent,
    qkv_weight,
    out_weight,
    gate_up_weight,
    down_weight,
    gains,
    qkv_first,
    out_first,
    gate_up_first,
    down_first,
    gains_first,
    qkv_second,
    out_second,
    gate_up_second,
    down_second,
    gains_second,
):
    seq_count = lax.axis_size("seq")
    tok_rows = tokens.shape[1]
    width = tokens.shape[2]
    seq_len = tok_rows * seq_count
    heads_here = HEADS // seq_count
    width_here = heads_here * HEAD_DIM
    contract_last = (((1,), (1,)), ((), ()))
    contract_first = (((0,), (0,)), ((), ()))
    qkv_full, proj_full, gain_full = (
        lax.all_gather(qkv_weight.astype(jnp.bfloat16), ("seq", "dp"), axis=0, tiled=True),
        lax.all_gather(out_weight.astype(jnp.bfloat16), ("seq", "dp"), axis=0, tiled=True),
        lax.all_gather(gains.astype(jnp.bfloat16), ("seq", "dp"), axis=1, tiled=True),
    )
    up_full, down_full = (
        lax.all_gather(gate_up_weight.astype(jnp.bfloat16), ("seq", "dp"), axis=0, tiled=True),
        lax.all_gather(down_weight.astype(jnp.bfloat16), ("seq", "dp"), axis=0, tiled=True),
    )
    hidden_in = tokens[0].astype(jnp.float32)
    unit_one, inverse_one = rms_parts(hidden_in)
    normed_one = (unit_one * gain_full[0].astype(jnp.float32)).astype(jnp.bfloat16)
    projected = jnp.einsum(
        "te,ecd->ctd",
        normed_one,
        qkv_full.reshape(width, 3, width),
        preferred_element_type=jnp.float32,
    )
    positions = lax.axis_index("seq") * tok_rows + jnp.arange(tok_rows, dtype=jnp.int32)
    cos_local, sin_local = rope_tables(positions)
    turned = rotate(projected[:2].reshape(2, tok_rows, HEADS, HEAD_DIM), cos_local, sin_local)
    packed = jnp.concatenate([turned.reshape(2, tok_rows, width), projected[2:]], axis=0).astype(
        jnp.bfloat16
    )
    by_heads = lax.all_to_all(packed, "seq", split_axis=2, concat_axis=1, tiled=True)
    query_heads = by_heads[0].reshape(seq_len, heads_here, HEAD_DIM)
    key_heads = by_heads[1].reshape(seq_len, heads_here, HEAD_DIM)
    value_heads = by_heads[2].reshape(seq_len, heads_here, HEAD_DIM)
    out_heads, lse_all = attend_forward(query_heads, key_heads, value_heads)
    attended = lax.all_to_all(
        out_heads.reshape(seq_len, width_here), "seq", split_axis=0, concat_axis=1, tiled=True
    )
    residual = hidden_in + jnp.dot(attended, proj_full, preferred_element_type=jnp.float32)
    unit_two, inverse_two = rms_parts(residual)
    normed_two = (unit_two * gain_full[1].astype(jnp.float32)).astype(jnp.bfloat16)
    gate_up = jnp.dot(normed_two, up_full, preferred_element_type=jnp.float32)
    gate_vals = gate_up[:, :FF]
    up_vals = gate_up[:, FF:]
    sigmoid_gate = jax.nn.sigmoid(gate_vals)
    activated = (gate_vals * sigmoid_gate * up_vals).astype(jnp.bfloat16)
    mlp_out = lax.dot_general(
        activated, down_full, contract_last, preferred_element_type=jnp.float32
    )
    block_out = (residual + mlp_out).astype(jnp.bfloat16)[None]
    back_up, back_down, back_gain = (
        lax.all_gather(gate_up_weight.astype(jnp.bfloat16), ("seq", "dp"), axis=0, tiled=True),
        lax.all_gather(down_weight.astype(jnp.bfloat16), ("seq", "dp"), axis=0, tiled=True),
        lax.all_gather(gains.astype(jnp.bfloat16), ("seq", "dp"), axis=1, tiled=True),
    )
    grad_out = cotangent[0]
    grad_act = jnp.dot(grad_out, back_down, preferred_element_type=jnp.float32)
    grad_gate = grad_act * up_vals * sigmoid_gate * (1.0 + gate_vals * (1.0 - sigmoid_gate))
    grad_up = grad_act * gate_vals * sigmoid_gate
    grad_gate_up = jnp.concatenate([grad_gate, grad_up], axis=1).astype(jnp.bfloat16)
    grad_normed_two = lax.dot_general(
        grad_gate_up, back_up, contract_last, preferred_element_type=jnp.float32
    )
    gain_two_grad = jnp.sum(grad_normed_two * unit_two, axis=0)
    grad_unit_two = grad_normed_two * back_gain[1].astype(jnp.float32)
    grad_residual = grad_out.astype(jnp.float32) + inverse_two * (
        grad_unit_two - unit_two * jnp.mean(grad_unit_two * unit_two, axis=-1, keepdims=True)
    )
    gate_up_rows = lax.dot_general(
        normed_two, grad_gate_up, contract_first, preferred_element_type=jnp.float32
    )
    down_rows = lax.dot_general(
        grad_out, activated, contract_first, preferred_element_type=jnp.float32
    )
    mlp_grad = lax.psum_scatter(
        jnp.concatenate([gate_up_rows, down_rows], axis=1),
        ("seq", "dp"),
        scatter_dimension=0,
        tiled=True,
    )
    back_qkv, back_proj = (
        lax.all_gather(qkv_weight.astype(jnp.bfloat16), ("seq", "dp"), axis=0, tiled=True),
        lax.all_gather(out_weight.astype(jnp.bfloat16), ("seq", "dp"), axis=0, tiled=True),
    )
    grad_branch = grad_residual.astype(jnp.bfloat16)
    proj_grad = lax.dot_general(
        attended, grad_branch, contract_first, preferred_element_type=jnp.float32
    )
    grad_attended = lax.dot_general(
        grad_branch, back_proj, contract_last, preferred_element_type=jnp.float32
    ).astype(jnp.bfloat16)
    grad_heads = lax.all_to_all(
        grad_attended, "seq", split_axis=1, concat_axis=0, tiled=True
    ).reshape(seq_len, heads_here, HEAD_DIM)
    grad_q_all, grad_k_all, grad_v_all = attend_backward(
        query_heads, key_heads, value_heads, grad_heads, lse_all
    )
    cos_whole, sin_whole = rope_tables(jnp.arange(seq_len, dtype=jnp.int32))
    grad_pack = jnp.stack(
        [
            unrotate(grad_q_all, cos_whole, sin_whole).reshape(seq_len, width_here),
            unrotate(grad_k_all, cos_whole, sin_whole).reshape(seq_len, width_here),
            grad_v_all.reshape(seq_len, width_here),
        ],
        axis=0,
    ).astype(jnp.bfloat16)
    grad_projected = lax.all_to_all(grad_pack, "seq", split_axis=1, concat_axis=2, tiled=True)
    qkv_cube = back_qkv.reshape(width, 3, width)
    grad_normed_one = jnp.einsum(
        "ctd,ecd->te", grad_projected, qkv_cube, preferred_element_type=jnp.float32
    )
    qkv_grad = jnp.einsum(
        "te,ctd->ecd", normed_one, grad_projected, preferred_element_type=jnp.float32
    ).reshape(width, 3 * width)
    gain_one_grad = jnp.sum(grad_normed_one * unit_one, axis=0)
    grad_unit_one = grad_normed_one * back_gain[0].astype(jnp.float32)
    input_grad = grad_residual + inverse_one * (
        grad_unit_one - unit_one * jnp.mean(grad_unit_one * unit_one, axis=-1, keepdims=True)
    )
    gains_grad = jnp.stack([gain_one_grad, gain_two_grad], axis=0)
    qkv_sum, proj_sum, gains_sum = (
        lax.psum_scatter(qkv_grad, ("seq", "dp"), scatter_dimension=0, tiled=True),
        lax.psum_scatter(proj_grad, ("seq", "dp"), scatter_dimension=0, tiled=True),
        lax.psum_scatter(gains_grad, ("seq", "dp"), scatter_dimension=1, tiled=True),
    )
    wide_rate = 2.5 * D ** (-0.5)
    out_rate = 2.5 * max(D // 512, 1) ** (-0.5)
    down_rate = 2.5 * FF ** (-0.5)
    qkv_new = adam_step(qkv_weight, qkv_sum, qkv_first, qkv_second, wide_rate, WEIGHT_DECAY)
    out_new = adam_step(out_weight, proj_sum, out_first, out_second, out_rate, WEIGHT_DECAY)
    gate_up_new = adam_step(
        gate_up_weight,
        mlp_grad[:, : 2 * FF],
        gate_up_first,
        gate_up_second,
        wide_rate,
        WEIGHT_DECAY,
    )
    down_new = adam_step(
        down_weight, mlp_grad[:, 2 * FF :], down_first, down_second, down_rate, WEIGHT_DECAY
    )
    gains_new = adam_step(gains, gains_sum, gains_first, gains_second, 0.5, 0.0)
    return (
        block_out,
        input_grad[None],
        qkv_new[0],
        out_new[0],
        gate_up_new[0],
        down_new[0],
        gains_new[0],
        qkv_new[1],
        out_new[1],
        gate_up_new[1],
        down_new[1],
        gains_new[1],
        qkv_new[2],
        out_new[2],
        gate_up_new[2],
        down_new[2],
        gains_new[2],
    )


GRID = ("z", "x", "y", "c")
RING = ("z", "c")
PLANE = ("x", "y")
CONTRACT_LAST = (((1,), (1,)), ((), ()))
CONTRACT_FIRST = (((0,), (0,)), ((), ()))
SWAP = [(0, 0), (1, 2), (2, 1), (3, 3)]


def swap_blocks(block):
    return lax.ppermute(block, ("x", "c"), SWAP)


def gather_tokens(block):
    return lax.all_gather(block, RING, axis=0, tiled=True)


def scatter_tokens(partial):
    return lax.psum_scatter(
        partial.astype(jnp.bfloat16), RING, scatter_dimension=0, tiled=True
    ).astype(jnp.float32)


def gather_columns(blocks):
    mixed = lax.all_to_all(blocks, RING, split_axis=0, concat_axis=0, tiled=True)
    groups, rows, columns = mixed.shape
    cores = lax.axis_size("c")
    depth = groups // cores
    full = lax.all_gather(mixed.reshape(depth, 1, cores * rows, columns), PLANE, axis=1, tiled=True)
    return full.reshape(-1, columns)


def scatter_columns(partial):
    depth, plane = lax.axis_size("z"), lax.axis_size(PLANE)
    cores = lax.axis_size("c")
    columns = partial.shape[1]
    summed = lax.psum_scatter(
        partial.astype(jnp.bfloat16).reshape(depth, plane, -1, columns),
        PLANE,
        scatter_dimension=1,
        tiled=True,
    )
    return lax.all_to_all(
        summed.reshape(depth * cores, -1, columns), RING, split_axis=0, concat_axis=0, tiled=True
    )


def split_qkv(weight, grid):
    rows = weight.shape[0]
    depth, wide, high, cores = grid
    cube = weight.reshape(rows, 3, depth, wide * high, cores, HEAD_DIM)
    return cube.transpose(2, 4, 0, 1, 3, 5).reshape(depth * cores, rows, -1)


def join_qkv(blocks, grid):
    depth, wide, high, cores = grid
    rows = blocks.shape[1]
    cube = blocks.reshape(depth, cores, rows, 3, wide * high, HEAD_DIM)
    return cube.transpose(2, 3, 0, 4, 1, 5).reshape(rows, -1)


def split_wide(weight, parts, groups):
    rows = weight.shape[0]
    return (
        weight.reshape(rows, parts, groups, -1).transpose(2, 0, 1, 3).reshape(groups, rows, -1)
    )


def join_wide(blocks, parts):
    groups, rows = blocks.shape[:2]
    return blocks.reshape(groups, rows, parts, -1).transpose(1, 2, 0, 3).reshape(rows, -1)


def grid_shards(
    tokens,
    cotangent,
    qkv_weight,
    out_weight,
    gate_up_weight,
    down_weight,
    gains,
    qkv_first,
    out_first,
    gate_up_first,
    down_first,
    gains_first,
    qkv_second,
    out_second,
    gate_up_second,
    down_second,
    gains_second,
):
    grid = tuple(lax.axis_size(name) for name in GRID)
    groups = grid[0] * grid[3]
    heads_here = HEADS // groups
    width_here = heads_here * HEAD_DIM
    width = tokens.shape[2]
    low = jnp.bfloat16
    own_tokens = swap_blocks(tokens[0])
    all_tokens = gather_tokens(own_tokens)
    seq_len = all_tokens.shape[0]
    qkv_full = gather_columns(split_qkv(qkv_weight.astype(low), grid))
    gain_full = lax.all_gather(gains.astype(low), GRID, axis=1, tiled=True)
    out_full = lax.all_gather(out_weight.astype(low), PLANE, axis=0, tiled=True)
    gate_up_full = gather_columns(split_wide(gate_up_weight.astype(low), 2, groups))
    down_full = gather_columns(split_wide(down_weight.astype(low), 1, groups))
    own_grad = swap_blocks(cotangent[0])
    grad_out = gather_tokens(own_grad)

    hidden_all = all_tokens.astype(jnp.float32)
    unit_all, _ = rms_parts(hidden_all)
    normed_one = (unit_all * gain_full[0].astype(jnp.float32)).astype(low)
    hidden_in = own_tokens.astype(jnp.float32)
    unit_one, inverse_one = rms_parts(hidden_in)
    projected = jnp.dot(normed_one, qkv_full, preferred_element_type=jnp.float32)
    cosines, sines = rope_tables(jnp.arange(seq_len, dtype=jnp.int32))
    by_heads = projected.reshape(seq_len, 3, heads_here, HEAD_DIM)
    query_heads = rotate(by_heads[:, 0], cosines, sines).astype(low)
    key_heads = rotate(by_heads[:, 1], cosines, sines).astype(low)
    value_heads = by_heads[:, 2].astype(low)
    out_heads, lse_all = attend_forward(query_heads, key_heads, value_heads)
    attended = out_heads.reshape(seq_len, width_here)
    residual = hidden_in + scatter_tokens(
        jnp.dot(attended, out_full, preferred_element_type=jnp.float32)
    )
    unit_two, inverse_two = rms_parts(residual)
    normed_two = gather_tokens((unit_two * gain_full[1].astype(jnp.float32)).astype(low))
    gate_up = jnp.dot(normed_two, gate_up_full, preferred_element_type=jnp.float32)
    ff_here = gate_up.shape[1] // 2
    gate_vals = gate_up[:, :ff_here]
    up_vals = gate_up[:, ff_here:]
    sigmoid_gate = jax.nn.sigmoid(gate_vals)
    activated = (gate_vals * sigmoid_gate * up_vals).astype(low)
    mlp_out = scatter_tokens(
        lax.dot_general(activated, down_full, CONTRACT_LAST, preferred_element_type=jnp.float32)
    )
    block_out = swap_blocks((residual + mlp_out).astype(low))[None]

    grad_act = jnp.dot(grad_out, down_full, preferred_element_type=jnp.float32)
    grad_gate = grad_act * up_vals * sigmoid_gate * (1.0 + gate_vals * (1.0 - sigmoid_gate))
    grad_up = grad_act * gate_vals * sigmoid_gate
    grad_gate_up = jnp.concatenate([grad_gate, grad_up], axis=1).astype(low)
    grad_normed_two = scatter_tokens(
        lax.dot_general(
            grad_gate_up, gate_up_full, CONTRACT_LAST, preferred_element_type=jnp.float32
        )
    )
    gate_up_sum = scatter_columns(
        lax.dot_general(
            normed_two, grad_gate_up, CONTRACT_FIRST, preferred_element_type=jnp.float32
        )
    )
    down_sum = scatter_columns(
        lax.dot_general(grad_out, activated, CONTRACT_FIRST, preferred_element_type=jnp.float32)
    )
    gain_two_grad = jnp.sum(grad_normed_two * unit_two, axis=0)
    grad_unit_two = grad_normed_two * gain_full[1].astype(jnp.float32)
    grad_residual = own_grad.astype(jnp.float32) + inverse_two * (
        grad_unit_two - unit_two * jnp.mean(grad_unit_two * unit_two, axis=-1, keepdims=True)
    )
    grad_branch = gather_tokens(grad_residual.astype(low))
    out_sum = lax.psum_scatter(
        lax.dot_general(
            attended, grad_branch, CONTRACT_FIRST, preferred_element_type=jnp.float32
        ).astype(low),
        PLANE,
        scatter_dimension=0,
        tiled=True,
    )
    grad_heads = (
        lax.dot_general(grad_branch, out_full, CONTRACT_LAST, preferred_element_type=jnp.float32)
        .astype(low)
        .reshape(seq_len, heads_here, HEAD_DIM)
    )
    grad_q_all, grad_k_all, grad_v_all = attend_backward(
        query_heads, key_heads, value_heads, grad_heads, lse_all
    )
    grad_projected = (
        jnp.stack(
            [
                unrotate(grad_q_all, cosines, sines),
                unrotate(grad_k_all, cosines, sines),
                grad_v_all,
            ],
            axis=1,
        )
        .reshape(seq_len, 3 * width_here)
        .astype(low)
    )
    grad_normed_one = scatter_tokens(
        lax.dot_general(
            grad_projected, qkv_full, CONTRACT_LAST, preferred_element_type=jnp.float32
        )
    )
    qkv_sum = scatter_columns(
        lax.dot_general(
            normed_one, grad_projected, CONTRACT_FIRST, preferred_element_type=jnp.float32
        )
    )
    gain_one_grad = jnp.sum(grad_normed_one * unit_one, axis=0)
    grad_unit_one = grad_normed_one * gain_full[0].astype(jnp.float32)
    input_grad = swap_blocks(
        grad_residual
        + inverse_one
        * (grad_unit_one - unit_one * jnp.mean(grad_unit_one * unit_one, axis=-1, keepdims=True))
    )
    gains_sum = lax.psum_scatter(
        jnp.stack([gain_one_grad, gain_two_grad], axis=0), GRID, scatter_dimension=1, tiled=True
    )
    wide_rate = 2.5 * D ** (-0.5)
    out_rate = 2.5 * max(D // 512, 1) ** (-0.5)
    down_rate = 2.5 * FF ** (-0.5)
    wide = jnp.float32
    qkv_new = adam_step(
        qkv_weight,
        join_qkv(qkv_sum, grid).astype(wide),
        qkv_first,
        qkv_second,
        wide_rate,
        WEIGHT_DECAY,
    )
    out_new = adam_step(
        out_weight, out_sum.astype(wide), out_first, out_second, out_rate, WEIGHT_DECAY
    )
    gate_up_new = adam_step(
        gate_up_weight,
        join_wide(gate_up_sum, 2).astype(wide),
        gate_up_first,
        gate_up_second,
        wide_rate,
        WEIGHT_DECAY,
    )
    down_new = adam_step(
        down_weight,
        join_wide(down_sum, 1).astype(wide),
        down_first,
        down_second,
        down_rate,
        WEIGHT_DECAY,
    )
    gains_new = adam_step(gains, gains_sum, gains_first, gains_second, 0.5, 0.0)
    return (
        block_out,
        input_grad[None],
        qkv_new[0],
        out_new[0],
        gate_up_new[0],
        down_new[0],
        gains_new[0],
        qkv_new[1],
        out_new[1],
        gate_up_new[1],
        down_new[1],
        gains_new[1],
        qkv_new[2],
        out_new[2],
        gate_up_new[2],
        down_new[2],
        gains_new[2],
    )


def mapped(body, mesh, token_spec, row_spec, gain_spec):
    one_set = (row_spec, row_spec, row_spec, row_spec, gain_spec)
    return jax.shard_map(
        body,
        mesh=mesh,
        in_specs=(token_spec, token_spec) + one_set * 3,
        out_specs=(token_spec, token_spec) + one_set * 3,
        check_vma=False,
    )


def solution(mesh):
    if mesh.shape["seq"] == 8 and mesh.shape["dp"] == 4:
        grid_mesh = Mesh(mesh.devices.reshape(4, 2, 2, 2), GRID)
        return mapped(
            grid_shards,
            grid_mesh,
            P(("y", "c"), ("z", "x"), None),
            P(GRID, None),
            P(None, GRID),
        )
    return mapped(
        shards, mesh, P("dp", "seq", None), P(("seq", "dp"), None), P(None, ("seq", "dp"))
    )
```

```python
import jax
import jax.numpy as jnp
from jax import lax
from jax.experimental import pallas as pl
from jax.experimental.pallas import tpu as pltpu
from jax.sharding import Mesh
from jax.sharding import PartitionSpec as P

D = 2048
HEADS = 32
HEAD_DIM = 64
FF = 8192
BLOCK = 512
STEP = 10


NORM_EPS = 1e-05
ROPE_BASE = 130000.0
BETA_ONE = 0.9
BETA_TWO = 0.999
ADAM_EPS = 1e-08
WEIGHT_DECAY = 0.1
MASKED = -1e30


def rms_parts(values):
    inverse = lax.rsqrt(jnp.mean(values * values, axis=-1, keepdims=True) + NORM_EPS)
    return (values * inverse, inverse)


def rope_tables(positions):
    half_dim = HEAD_DIM // 2
    exponent = jnp.arange(half_dim, dtype=jnp.float32) * (2.0 / HEAD_DIM)
    frequency = ROPE_BASE ** (-exponent)
    angles = positions.astype(jnp.float32)[:, None] * frequency[None, :]
    return (jnp.cos(angles)[:, None, :], jnp.sin(angles)[:, None, :])


def rotate(tensor, cosines, sines):
    half_dim = HEAD_DIM // 2
    lower_half = tensor[..., :half_dim]
    upper_half = tensor[..., half_dim:]
    return jnp.concatenate(
        [lower_half * cosines - upper_half * sines, upper_half * cosines + lower_half * sines],
        axis=-1,
    )


def unrotate(tensor, cosines, sines):
    half_dim = HEAD_DIM // 2
    lower_half = tensor[..., :half_dim]
    upper_half = tensor[..., half_dim:]
    return jnp.concatenate(
        [lower_half * cosines + upper_half * sines, upper_half * cosines - lower_half * sines],
        axis=-1,
    )


def block_scores(query_rows, key_heads, key_id, block_id):
    key_rows = lax.dynamic_slice_in_dim(key_heads, key_id * BLOCK, BLOCK, 0)
    products = jnp.einsum(
        "qhd,khd->hqk", query_rows, key_rows, preferred_element_type=jnp.float32
    ) * HEAD_DIM ** (-0.5)
    local_ids = jnp.arange(BLOCK, dtype=jnp.int32)
    allowed = (key_id < block_id) | (local_ids[None, :] <= local_ids[:, None])
    return jnp.where(allowed[None], products, MASKED)


def row_normalizer(query_rows, key_heads, block_id):
    row_shape = (query_rows.shape[1], BLOCK, 1)

    def absorb(key_id, state):
        running_max, running_total = state
        scores = block_scores(query_rows, key_heads, key_id, block_id)
        new_max = jnp.maximum(running_max, jnp.max(scores, axis=-1, keepdims=True))
        running_total = running_total * jnp.exp(running_max - new_max) + jnp.sum(
            jnp.exp(scores - new_max), axis=-1, keepdims=True
        )
        return (new_max, running_total)

    start_state = (jnp.full(row_shape, MASKED, jnp.float32), jnp.zeros(row_shape, jnp.float32))
    final_max, final_total = lax.fori_loop(0, block_id + 1, absorb, start_state)
    return final_max + jnp.log(final_total)


def attend_forward(query_heads, key_heads, value_heads):
    seq_len, heads_here, head_dim = query_heads.shape

    def one_block(block_id, carry):
        out_all, lse_all = carry
        row_start = block_id * BLOCK
        query_rows = lax.dynamic_slice_in_dim(query_heads, row_start, BLOCK, 0)
        row_lse = row_normalizer(query_rows, key_heads, block_id)

        def weigh_values(key_id, running):
            scores = block_scores(query_rows, key_heads, key_id, block_id)
            weights_low = jnp.exp(scores - row_lse).astype(jnp.bfloat16)
            value_rows = lax.dynamic_slice_in_dim(value_heads, key_id * BLOCK, BLOCK, 0)
            return running + jnp.einsum(
                "hqk,khd->qhd", weights_low, value_rows, preferred_element_type=jnp.float32
            )

        attended = lax.fori_loop(
            0, block_id + 1, weigh_values, jnp.zeros((BLOCK, heads_here, head_dim), jnp.float32)
        )
        out_all = lax.dynamic_update_slice_in_dim(
            out_all, attended.astype(jnp.bfloat16), row_start, 0
        )
        lse_all = lax.dynamic_update_slice_in_dim(lse_all, row_lse, row_start, 1)
        return (out_all, lse_all)

    start_carry = (
        jnp.zeros((seq_len, heads_here, head_dim), jnp.bfloat16),
        jnp.zeros((heads_here, seq_len, 1), jnp.float32),
    )
    return lax.fori_loop(0, seq_len // BLOCK, one_block, start_carry)


def attend_backward(query_heads, key_heads, value_heads, grad_heads, lse_all):
    seq_len, heads_here, head_dim = query_heads.shape
    score_scale = HEAD_DIM ** (-0.5)

    def one_block(block_id, carry):
        grad_q_all, grad_k_all, grad_v_all = carry
        row_start = block_id * BLOCK
        query_rows = lax.dynamic_slice_in_dim(query_heads, row_start, BLOCK, 0)
        grad_rows = lax.dynamic_slice_in_dim(grad_heads, row_start, BLOCK, 0)
        row_lse = lax.dynamic_slice_in_dim(lse_all, row_start, BLOCK, 1)

        def probs_and_grads(key_id):
            scores = block_scores(query_rows, key_heads, key_id, block_id)
            probs = jnp.exp(scores - row_lse)
            value_rows = lax.dynamic_slice_in_dim(value_heads, key_id * BLOCK, BLOCK, 0)
            grad_probs = jnp.einsum(
                "qhd,khd->hqk", grad_rows, value_rows, preferred_element_type=jnp.float32
            )
            return (probs, grad_probs)

        def add_delta(key_id, running):
            probs, grad_probs = probs_and_grads(key_id)
            return running + jnp.sum(probs * grad_probs, axis=-1, keepdims=True)

        row_delta = lax.fori_loop(
            0, block_id + 1, add_delta, jnp.zeros((heads_here, BLOCK, 1), jnp.float32)
        )

        def spread(key_id, inner):
            grad_q_rows, grad_k_acc, grad_v_acc = inner
            probs, grad_probs = probs_and_grads(key_id)
            key_start = key_id * BLOCK
            key_rows = lax.dynamic_slice_in_dim(key_heads, key_start, BLOCK, 0)
            grad_scores = (probs * (grad_probs - row_delta) * score_scale).astype(jnp.bfloat16)
            grad_q_rows = grad_q_rows + jnp.einsum(
                "hqk,khd->qhd", grad_scores, key_rows, preferred_element_type=jnp.float32
            )
            grad_k_part = jnp.einsum(
                "hqk,qhd->khd", grad_scores, query_rows, preferred_element_type=jnp.float32
            )
            grad_v_part = jnp.einsum(
                "hqk,qhd->khd",
                probs.astype(jnp.bfloat16),
                grad_rows,
                preferred_element_type=jnp.float32,
            )
            grad_k_acc = lax.dynamic_update_slice_in_dim(
                grad_k_acc,
                lax.dynamic_slice_in_dim(grad_k_acc, key_start, BLOCK, 0) + grad_k_part,
                key_start,
                0,
            )
            grad_v_acc = lax.dynamic_update_slice_in_dim(
                grad_v_acc,
                lax.dynamic_slice_in_dim(grad_v_acc, key_start, BLOCK, 0) + grad_v_part,
                key_start,
                0,
            )
            return (grad_q_rows, grad_k_acc, grad_v_acc)

        start_inner = (
            jnp.zeros((BLOCK, heads_here, head_dim), jnp.float32),
            grad_k_all,
            grad_v_all,
        )
        grad_q_rows, grad_k_all, grad_v_all = lax.fori_loop(0, block_id + 1, spread, start_inner)
        grad_q_all = lax.dynamic_update_slice_in_dim(grad_q_all, grad_q_rows, row_start, 0)
        return (grad_q_all, grad_k_all, grad_v_all)

    zeros_all = jnp.zeros((seq_len, heads_here, head_dim), jnp.float32)
    return lax.fori_loop(0, seq_len // BLOCK, one_block, (zeros_all, zeros_all, zeros_all))


def adam_step(weight, gradient, first, second, rate, decay):
    new_first = BETA_ONE * first + (1.0 - BETA_ONE) * gradient
    new_second = BETA_TWO * second + (1.0 - BETA_TWO) * gradient * gradient
    first_hat = new_first / (1.0 - BETA_ONE**STEP)
    second_hat = new_second / (1.0 - BETA_TWO**STEP)
    new_weight = weight - rate * (first_hat / (jnp.sqrt(second_hat) + ADAM_EPS) + decay * weight)
    return (new_weight, new_first, new_second)


def shards(
    tokens,
    cotangent,
    qkv_weight,
    out_weight,
    gate_up_weight,
    down_weight,
    gains,
    qkv_first,
    out_first,
    gate_up_first,
    down_first,
    gains_first,
    qkv_second,
    out_second,
    gate_up_second,
    down_second,
    gains_second,
):
    seq_count = lax.axis_size("seq")
    tok_rows = tokens.shape[1]
    width = tokens.shape[2]
    seq_len = tok_rows * seq_count
    heads_here = HEADS // seq_count
    width_here = heads_here * HEAD_DIM
    contract_last = (((1,), (1,)), ((), ()))
    contract_first = (((0,), (0,)), ((), ()))
    qkv_full, proj_full, gain_full = (
        lax.all_gather(qkv_weight.astype(jnp.bfloat16), ("seq", "dp"), axis=0, tiled=True),
        lax.all_gather(out_weight.astype(jnp.bfloat16), ("seq", "dp"), axis=0, tiled=True),
        lax.all_gather(gains.astype(jnp.bfloat16), ("seq", "dp"), axis=1, tiled=True),
    )
    up_full, down_full = (
        lax.all_gather(gate_up_weight.astype(jnp.bfloat16), ("seq", "dp"), axis=0, tiled=True),
        lax.all_gather(down_weight.astype(jnp.bfloat16), ("seq", "dp"), axis=0, tiled=True),
    )
    hidden_in = tokens[0].astype(jnp.float32)
    unit_one, inverse_one = rms_parts(hidden_in)
    normed_one = (unit_one * gain_full[0].astype(jnp.float32)).astype(jnp.bfloat16)
    projected = jnp.einsum(
        "te,ecd->ctd",
        normed_one,
        qkv_full.reshape(width, 3, width),
        preferred_element_type=jnp.float32,
    )
    positions = lax.axis_index("seq") * tok_rows + jnp.arange(tok_rows, dtype=jnp.int32)
    cos_local, sin_local = rope_tables(positions)
    turned = rotate(projected[:2].reshape(2, tok_rows, HEADS, HEAD_DIM), cos_local, sin_local)
    packed = jnp.concatenate([turned.reshape(2, tok_rows, width), projected[2:]], axis=0).astype(
        jnp.bfloat16
    )
    by_heads = lax.all_to_all(packed, "seq", split_axis=2, concat_axis=1, tiled=True)
    query_heads = by_heads[0].reshape(seq_len, heads_here, HEAD_DIM)
    key_heads = by_heads[1].reshape(seq_len, heads_here, HEAD_DIM)
    value_heads = by_heads[2].reshape(seq_len, heads_here, HEAD_DIM)
    out_heads, lse_all = attend_forward(query_heads, key_heads, value_heads)
    attended = lax.all_to_all(
        out_heads.reshape(seq_len, width_here), "seq", split_axis=0, concat_axis=1, tiled=True
    )
    residual = hidden_in + jnp.dot(attended, proj_full, preferred_element_type=jnp.float32)
    unit_two, inverse_two = rms_parts(residual)
    normed_two = (unit_two * gain_full[1].astype(jnp.float32)).astype(jnp.bfloat16)
    gate_up = jnp.dot(normed_two, up_full, preferred_element_type=jnp.float32)
    gate_vals = gate_up[:, :FF]
    up_vals = gate_up[:, FF:]
    sigmoid_gate = jax.nn.sigmoid(gate_vals)
    activated = (gate_vals * sigmoid_gate * up_vals).astype(jnp.bfloat16)
    mlp_out = lax.dot_general(
        activated, down_full, contract_last, preferred_element_type=jnp.float32
    )
    block_out = (residual + mlp_out).astype(jnp.bfloat16)[None]
    back_up, back_down, back_gain = (
        lax.all_gather(gate_up_weight.astype(jnp.bfloat16), ("seq", "dp"), axis=0, tiled=True),
        lax.all_gather(down_weight.astype(jnp.bfloat16), ("seq", "dp"), axis=0, tiled=True),
        lax.all_gather(gains.astype(jnp.bfloat16), ("seq", "dp"), axis=1, tiled=True),
    )
    grad_out = cotangent[0]
    grad_act = jnp.dot(grad_out, back_down, preferred_element_type=jnp.float32)
    grad_gate = grad_act * up_vals * sigmoid_gate * (1.0 + gate_vals * (1.0 - sigmoid_gate))
    grad_up = grad_act * gate_vals * sigmoid_gate
    grad_gate_up = jnp.concatenate([grad_gate, grad_up], axis=1).astype(jnp.bfloat16)
    grad_normed_two = lax.dot_general(
        grad_gate_up, back_up, contract_last, preferred_element_type=jnp.float32
    )
    gain_two_grad = jnp.sum(grad_normed_two * unit_two, axis=0)
    grad_unit_two = grad_normed_two * back_gain[1].astype(jnp.float32)
    grad_residual = grad_out.astype(jnp.float32) + inverse_two * (
        grad_unit_two - unit_two * jnp.mean(grad_unit_two * unit_two, axis=-1, keepdims=True)
    )
    gate_up_rows = lax.dot_general(
        normed_two, grad_gate_up, contract_first, preferred_element_type=jnp.float32
    )
    down_rows = lax.dot_general(
        grad_out, activated, contract_first, preferred_element_type=jnp.float32
    )
    mlp_grad = lax.psum_scatter(
        jnp.concatenate([gate_up_rows, down_rows], axis=1),
        ("seq", "dp"),
        scatter_dimension=0,
        tiled=True,
    )
    back_qkv, back_proj = (
        lax.all_gather(qkv_weight.astype(jnp.bfloat16), ("seq", "dp"), axis=0, tiled=True),
        lax.all_gather(out_weight.astype(jnp.bfloat16), ("seq", "dp"), axis=0, tiled=True),
    )
    grad_branch = grad_residual.astype(jnp.bfloat16)
    proj_grad = lax.dot_general(
        attended, grad_branch, contract_first, preferred_element_type=jnp.float32
    )
    grad_attended = lax.dot_general(
        grad_branch, back_proj, contract_last, preferred_element_type=jnp.float32
    ).astype(jnp.bfloat16)
    grad_heads = lax.all_to_all(
        grad_attended, "seq", split_axis=1, concat_axis=0, tiled=True
    ).reshape(seq_len, heads_here, HEAD_DIM)
    grad_q_all, grad_k_all, grad_v_all = attend_backward(
        query_heads, key_heads, value_heads, grad_heads, lse_all
    )
    cos_whole, sin_whole = rope_tables(jnp.arange(seq_len, dtype=jnp.int32))
    grad_pack = jnp.stack(
        [
            unrotate(grad_q_all, cos_whole, sin_whole).reshape(seq_len, width_here),
            unrotate(grad_k_all, cos_whole, sin_whole).reshape(seq_len, width_here),
            grad_v_all.reshape(seq_len, width_here),
        ],
        axis=0,
    ).astype(jnp.bfloat16)
    grad_projected = lax.all_to_all(grad_pack, "seq", split_axis=1, concat_axis=2, tiled=True)
    qkv_cube = back_qkv.reshape(width, 3, width)
    grad_normed_one = jnp.einsum(
        "ctd,ecd->te", grad_projected, qkv_cube, preferred_element_type=jnp.float32
    )
    qkv_grad = jnp.einsum(
        "te,ctd->ecd", normed_one, grad_projected, preferred_element_type=jnp.float32
    ).reshape(width, 3 * width)
    gain_one_grad = jnp.sum(grad_normed_one * unit_one, axis=0)
    grad_unit_one = grad_normed_one * back_gain[0].astype(jnp.float32)
    input_grad = grad_residual + inverse_one * (
        grad_unit_one - unit_one * jnp.mean(grad_unit_one * unit_one, axis=-1, keepdims=True)
    )
    gains_grad = jnp.stack([gain_one_grad, gain_two_grad], axis=0)
    qkv_sum, proj_sum, gains_sum = (
        lax.psum_scatter(qkv_grad, ("seq", "dp"), scatter_dimension=0, tiled=True),
        lax.psum_scatter(proj_grad, ("seq", "dp"), scatter_dimension=0, tiled=True),
        lax.psum_scatter(gains_grad, ("seq", "dp"), scatter_dimension=1, tiled=True),
    )
    wide_rate = 2.5 * D ** (-0.5)
    out_rate = 2.5 * max(D // 512, 1) ** (-0.5)
    down_rate = 2.5 * FF ** (-0.5)
    qkv_new = adam_step(qkv_weight, qkv_sum, qkv_first, qkv_second, wide_rate, WEIGHT_DECAY)
    out_new = adam_step(out_weight, proj_sum, out_first, out_second, out_rate, WEIGHT_DECAY)
    gate_up_new = adam_step(
        gate_up_weight,
        mlp_grad[:, : 2 * FF],
        gate_up_first,
        gate_up_second,
        wide_rate,
        WEIGHT_DECAY,
    )
    down_new = adam_step(
        down_weight, mlp_grad[:, 2 * FF :], down_first, down_second, down_rate, WEIGHT_DECAY
    )
    gains_new = adam_step(gains, gains_sum, gains_first, gains_second, 0.5, 0.0)
    return (
        block_out,
        input_grad[None],
        qkv_new[0],
        out_new[0],
        gate_up_new[0],
        down_new[0],
        gains_new[0],
        qkv_new[1],
        out_new[1],
        gate_up_new[1],
        down_new[1],
        gains_new[1],
        qkv_new[2],
        out_new[2],
        gate_up_new[2],
        down_new[2],
        gains_new[2],
    )


GRID = ("z", "x", "y", "c")
RING = ("z", "c")
PLANE = ("x", "y")
CONTRACT_LAST = (((1,), (1,)), ((), ()))
CONTRACT_FIRST = (((0,), (0,)), ((), ()))
SWAP = [(0, 0), (1, 2), (2, 1), (3, 3)]


def swap_blocks(block):
    return lax.ppermute(block, ("x", "c"), SWAP)


def gather_tokens(block):
    return lax.all_gather(block, RING, axis=0, tiled=True)


def scatter_tokens(partial):
    return lax.psum_scatter(
        partial.astype(jnp.bfloat16), RING, scatter_dimension=0, tiled=True
    ).astype(jnp.float32)


def gather_columns(blocks):
    mixed = lax.all_to_all(blocks, RING, split_axis=0, concat_axis=0, tiled=True)
    groups, rows, columns = mixed.shape
    cores = lax.axis_size("c")
    depth = groups // cores
    full = lax.all_gather(mixed.reshape(depth, 1, cores * rows, columns), PLANE, axis=1, tiled=True)
    return full.reshape(-1, columns)


def scatter_columns(partial):
    depth, plane = lax.axis_size("z"), lax.axis_size(PLANE)
    cores = lax.axis_size("c")
    columns = partial.shape[1]
    summed = lax.psum_scatter(
        partial.astype(jnp.bfloat16).reshape(depth, plane, -1, columns),
        PLANE,
        scatter_dimension=1,
        tiled=True,
    )
    return lax.all_to_all(
        summed.reshape(depth * cores, -1, columns), RING, split_axis=0, concat_axis=0, tiled=True
    )


def split_qkv(weight, grid):
    rows = weight.shape[0]
    depth, wide, high, cores = grid
    cube = weight.reshape(rows, 3, depth, wide * high, cores, HEAD_DIM)
    return cube.transpose(2, 4, 0, 1, 3, 5).reshape(depth * cores, rows, -1)


def join_qkv(blocks, grid):
    depth, wide, high, cores = grid
    rows = blocks.shape[1]
    cube = blocks.reshape(depth, cores, rows, 3, wide * high, HEAD_DIM)
    return cube.transpose(2, 3, 0, 4, 1, 5).reshape(rows, -1)


def split_wide(weight, parts, groups):
    rows = weight.shape[0]
    return (
        weight.reshape(rows, parts, groups, -1).transpose(2, 0, 1, 3).reshape(groups, rows, -1)
    )


def join_wide(blocks, parts):
    groups, rows = blocks.shape[:2]
    return blocks.reshape(groups, rows, parts, -1).transpose(1, 2, 0, 3).reshape(rows, -1)


def remote(source, target, send, receive, **place):
    return pltpu.make_async_remote_copy(
        src_ref=source,
        dst_ref=target,
        send_sem=send,
        recv_sem=receive,
        device_id=place,
        device_id_type=pl.DeviceIdType.MESH,
    )


class Place:
    def __init__(self):
        self.z, self.x, self.y, self.c = (lax.axis_index(name) for name in GRID)
        self.slot = 2 * self.z + self.c

    def block(self, slot, x, y):
        return (((slot // 2) * 2 + x) * 2 + y) * 2 + lax.rem(slot, 2)

    def meet(self, plane):
        barrier = pltpu.get_barrier_semaphore()
        others = [
            {"z": slot // 2, "c": lax.rem(slot, 2)}
            for slot in (lax.rem(self.slot + step, 8) for step in range(1, 8))
        ]
        if plane:
            others += [{"x": 1 - self.x}, {"y": 1 - self.y}, {"x": 1 - self.x, "c": 1 - self.c}]
        for other in others:
            pl.semaphore_signal(
                barrier, inc=1, device_id=other, device_id_type=pl.DeviceIdType.MESH
            )
        pl.semaphore_wait(barrier, len(others))


class LineGather:
    def __init__(self, place, buffer, got, up, down, across):
        self.place, self.buffer = place, buffer
        self.got, self.sems = got, (up, down, across)

    def copy(self, slot, way):
        p, block = self.place, self.buffer.at[slot]
        if way == 0:
            where = {"z": jnp.minimum(p.z + 1, 3)}
        elif way == 1:
            where = {"z": jnp.maximum(p.z - 1, 0)}
        else:
            where = {"c": 1 - p.c}
        return remote(block, block, self.sems[way].at[slot], self.got.at[slot], **where)

    def _pass_on(self, slot, way):
        p = self.place
        if way == 0:
            pl.when(p.z < 3)(lambda: self.copy(slot, 0).start())
        elif way == 1:
            pl.when(p.z > 0)(lambda: self.copy(slot, 1).start())

    def start(self):
        slot = self.place.slot
        self._pass_on(slot, 0)
        self._pass_on(slot, 1)
        self.copy(slot, 2).start()

    def step(self, distance):
        p = self.place

        @pl.when(p.z + distance <= 3)
        def _():
            slot = p.slot + 2 * distance
            self.copy(slot, 2).wait_recv()
            self._pass_on(slot, 1)
            self.copy(slot, 2).start()

        @pl.when(p.z >= distance)
        def _():
            slot = p.slot - 2 * distance
            self.copy(slot, 2).wait_recv()
            self._pass_on(slot, 0)
            self.copy(slot, 2).start()

    def finish(self):
        p = self.place
        for z in range(4):
            self.copy(2 * z + 1 - p.c, 2).wait_recv()

    def drain(self):
        p = self.place
        for z in range(4):
            slot = 2 * z + p.c
            self.copy(slot, 2).wait_send()
            pl.when((z <= p.z) & (p.z < 3))(lambda: self.copy(slot, 0).wait_send())
            pl.when((z >= p.z) & (p.z > 0))(lambda: self.copy(slot, 1).wait_send())


class Relayout:
    def __init__(self, place, source, target, sems):
        self.place, self.source, self.target = place, source, target
        self.sems = sems

    def sem(self, kind, slot):
        return self.sems.at[kind, slot]

    def line(self, step):
        p = self.place
        slot = lax.rem(p.slot + step, 8)
        spot = self.target.at[p.block(p.slot, p.x, p.y)]
        if step == 0:
            return pltpu.make_async_copy(self.source.at[slot], spot, self.sem(1, p.slot))
        return remote(
            self.source.at[slot],
            spot,
            self.sem(0, slot),
            self.sem(1, p.slot),
            z=slot // 2,
            c=lax.rem(slot, 2),
        )

    def plane(self, slot, x, y, way, send, receive):
        p = self.place
        spot = self.target.at[p.block(slot, x, y)]
        where = {"x": 1 - p.x} if way == 0 else {"y": 1 - p.y}
        return remote(spot, spot, self.sem(send, slot), self.sem(receive, slot), **where)

    def from_own(self, slot, way):
        p = self.place
        return self.plane(slot, p.x, p.y, way, 2 + 2 * way, 3 + 2 * way)

    def corner(self, slot, way):
        p = self.place
        x, y = (p.x, 1 - p.y) if way == 0 else (1 - p.x, p.y)
        return self.plane(slot, x, y, way, 6, 7)

    def start(self):
        for step in range(8):
            self.line(step).start()

    def spread(self, step):
        p = self.place
        slot = lax.rem(p.slot + 8 - step, 8)
        if step == 0:
            self.line(0).wait()
        else:
            self.from_own_wait(slot)
        for way in range(2):
            self.from_own(slot, way).start()

    def from_own_wait(self, slot):
        p = self.place
        spot = self.target.at[p.block(slot, p.x, p.y)]
        remote(spot, spot, self.sem(0, slot), self.sem(1, slot), z=p.z).wait_recv()

    def corners(self, z):
        self.from_own(2 * z, 0).wait_recv()
        self.corner(2 * z, 1).start()
        self.from_own(2 * z + 1, 1).wait_recv()
        self.corner(2 * z + 1, 0).start()

    def finish(self):
        for z in range(4):
            self.from_own(2 * z, 1).wait_recv()
            self.from_own(2 * z + 1, 0).wait_recv()
            self.corner(2 * z, 1).wait_recv()
            self.corner(2 * z + 1, 0).wait_recv()

    def drain(self):
        for step in range(1, 8):
            self.line(step).wait_send()
        for z in range(4):
            self.corner(2 * z, 1).wait_send()
            self.corner(2 * z + 1, 0).wait_send()
        for slot in range(8):
            for way in range(2):
                self.from_own(slot, way).wait_send()


def fetch_kernel(
    tok, cot, wq, wg, wd, wo, all_tok, all_cot, full_q, full_g, full_d, full_o, *sems
):
    swap_sems, tok_sems, cot_sems, q_sems, g_sems, d_sems, o_sems = sems
    p = Place()
    p.meet(True)
    weights = [
        Relayout(p, source, target, sem)
        for source, target, sem in (
            (wq, full_q, q_sems),
            (wg, full_g, g_sems),
            (wd, full_d, d_sems),
        )
    ]
    gathers = [
        LineGather(p, buffer, *(sem.at[kind] for kind in range(4)))
        for buffer, sem in ((all_tok, tok_sems), (all_cot, cot_sems))
    ]

    def swap(i):
        source, target = ((tok, all_tok), (cot, all_cot))[i]
        spot = target.at[2 * p.z + 1 - p.c]
        away = remote(source, spot, swap_sems.at[i, 0], swap_sems.at[i, 1], x=1 - p.x, c=1 - p.c)
        here = pltpu.make_async_copy(source, target.at[p.slot], swap_sems.at[i, 2])
        return away, here

    def swap_start(i):
        away, here = swap(i)
        pl.when(p.x != p.c)(lambda: away.start())
        pl.when(p.x == p.c)(lambda: here.start())

    def swap_wait(i):
        away, here = swap(i)
        pl.when(p.x != p.c)(lambda: away.wait_recv())
        pl.when(p.x == p.c)(lambda: here.wait())

    def out_copy(kind):
        mine, beside, above = 2 * p.x + p.y, 2 * (1 - p.x) + p.y, 2 * p.x + 1 - p.y
        half = wo.shape[0] // 2
        send, got = o_sems.at[0, kind], o_sems.at[1, kind]
        if kind == 0:
            return remote(wo, full_o.at[mine], send, got, x=1 - p.x)
        if kind == 1:
            return remote(wo, full_o.at[mine], send, got, y=1 - p.y)
        if kind == 2:
            spot = full_o.at[beside, pl.ds(0, half)]
            return remote(spot, spot, send, got, y=1 - p.y)
        spot = full_o.at[above, pl.ds(half, half)]
        return remote(spot, spot, send, got, x=1 - p.x)

    own_out = pltpu.make_async_copy(wo, full_o.at[2 * p.x + p.y], o_sems.at[0, 4])

    swap_start(0)
    weights[0].start()
    own_out.start()
    out_copy(0).start()
    out_copy(1).start()
    swap_start(1)
    swap_wait(0)
    gathers[0].start()
    for step in range(8):
        weights[0].spread(step)
    out_copy(0).wait_recv()
    out_copy(2).start()
    out_copy(1).wait_recv()
    out_copy(3).start()
    gathers[0].step(1)
    gathers[0].step(2)
    weights[1].start()
    for z in range(4):
        weights[0].corners(z)
    gathers[0].step(3)
    for step in range(8):
        weights[1].spread(step)
    weights[2].start()
    for z in range(4):
        weights[1].corners(z)
    swap_wait(1)
    gathers[1].start()
    for step in range(8):
        weights[2].spread(step)
    for distance in range(1, 4):
        gathers[1].step(distance)
    for z in range(4):
        weights[2].corners(z)
    out_copy(2).wait_recv()
    out_copy(3).wait_recv()
    own_out.wait()
    for kind in range(4):
        out_copy(kind).wait_send()
    for i in range(2):
        away, _ = swap(i)
        pl.when(p.x != p.c)(lambda: away.wait_send())
    for part in gathers + weights:
        part.finish()
        part.drain()


def fetch_all(tokens, cotangent, qkv_blocks, gate_up_blocks, down_blocks, out_rows):
    low = jnp.bfloat16
    rows, width = tokens.shape
    shapes = [(8, rows, width)] * 2
    shapes += [
        (4 * b.shape[0],) + b.shape[1:] for b in (qkv_blocks, gate_up_blocks, down_blocks)
    ]
    shapes += [(4,) + out_rows.shape]
    anywhere = pl.BlockSpec(memory_space=pl.ANY)
    dma = pltpu.SemaphoreType.DMA
    return pl.pallas_call(
        fetch_kernel,
        out_shape=[jax.ShapeDtypeStruct(shape, low) for shape in shapes],
        in_specs=[anywhere] * 6,
        out_specs=[anywhere] * 6,
        scratch_shapes=[dma((2, 3)), dma((4, 8)), dma((4, 8))] + [dma((8, 8))] * 3 + [dma((2, 5))],
        compiler_params=pltpu.CompilerParams(collective_id=1, has_side_effects=True),
        name="fetch_all",
    )(tokens, cotangent, qkv_blocks, gate_up_blocks, down_blocks, out_rows)


def grid_shards(
    tokens,
    cotangent,
    qkv_weight,
    out_weight,
    gate_up_weight,
    down_weight,
    gains,
    qkv_first,
    out_first,
    gate_up_first,
    down_first,
    gains_first,
    qkv_second,
    out_second,
    gate_up_second,
    down_second,
    gains_second,
):
    grid = tuple(lax.axis_size(name) for name in GRID)
    groups = grid[0] * grid[3]
    heads_here = HEADS // groups
    width_here = heads_here * HEAD_DIM
    width = tokens.shape[2]
    low = jnp.bfloat16
    qkv_blocks = split_qkv(qkv_weight.astype(low), grid)
    gain_columns = jnp.pad(gains.astype(low).T, ((0, 0), (0, 126)))
    qkv_blocks = jnp.concatenate(
        [qkv_blocks, jnp.broadcast_to(gain_columns[None], (groups,) + gain_columns.shape)], axis=2
    )
    all_tokens, grad_out, qkv_full, gate_up_full, down_full, out_full = fetch_all(
        tokens[0],
        cotangent[0],
        qkv_blocks,
        split_wide(gate_up_weight.astype(low), 2, groups),
        split_wide(down_weight.astype(low), 1, groups),
        out_weight.astype(low),
    )
    own_slot = lax.axis_index(RING)
    own_tokens = lax.dynamic_index_in_dim(all_tokens, own_slot, 0, keepdims=False)
    own_grad = lax.dynamic_index_in_dim(grad_out, own_slot, 0, keepdims=False)
    all_tokens, grad_out = all_tokens.reshape(-1, width), grad_out.reshape(-1, width)
    qkv_full = qkv_full.reshape(width, -1)
    gain_full = qkv_full[:, 3 * width_here : 3 * width_here + 2].T
    qkv_full = qkv_full[:, : 3 * width_here]
    gate_up_full = gate_up_full.reshape(width, -1)
    down_full = down_full.reshape(width, -1)
    out_full = out_full.reshape(-1, width)
    seq_len = all_tokens.shape[0]

    hidden_all = all_tokens.astype(jnp.float32)
    unit_all, _ = rms_parts(hidden_all)
    normed_one = (unit_all * gain_full[0].astype(jnp.float32)).astype(low)
    hidden_in = own_tokens.astype(jnp.float32)
    unit_one, inverse_one = rms_parts(hidden_in)
    projected = jnp.dot(normed_one, qkv_full, preferred_element_type=jnp.float32)
    cosines, sines = rope_tables(jnp.arange(seq_len, dtype=jnp.int32))
    by_heads = projected.reshape(seq_len, 3, heads_here, HEAD_DIM)
    query_heads = rotate(by_heads[:, 0], cosines, sines).astype(low)
    key_heads = rotate(by_heads[:, 1], cosines, sines).astype(low)
    value_heads = by_heads[:, 2].astype(low)
    out_heads, lse_all = attend_forward(query_heads, key_heads, value_heads)
    attended = out_heads.reshape(seq_len, width_here)
    residual = hidden_in + scatter_tokens(
        jnp.dot(attended, out_full, preferred_element_type=jnp.float32)
    )
    unit_two, inverse_two = rms_parts(residual)
    normed_two = gather_tokens((unit_two * gain_full[1].astype(jnp.float32)).astype(low))
    gate_up = jnp.dot(normed_two, gate_up_full, preferred_element_type=jnp.float32)
    ff_here = gate_up.shape[1] // 2
    gate_vals = gate_up[:, :ff_here]
    up_vals = gate_up[:, ff_here:]
    sigmoid_gate = jax.nn.sigmoid(gate_vals)
    activated = (gate_vals * sigmoid_gate * up_vals).astype(low)
    mlp_out = scatter_tokens(
        lax.dot_general(activated, down_full, CONTRACT_LAST, preferred_element_type=jnp.float32)
    )
    block_out = swap_blocks((residual + mlp_out).astype(low))[None]

    grad_act = jnp.dot(grad_out, down_full, preferred_element_type=jnp.float32)
    grad_gate = grad_act * up_vals * sigmoid_gate * (1.0 + gate_vals * (1.0 - sigmoid_gate))
    grad_up = grad_act * gate_vals * sigmoid_gate
    grad_gate_up = jnp.concatenate([grad_gate, grad_up], axis=1).astype(low)
    grad_normed_two = scatter_tokens(
        lax.dot_general(
            grad_gate_up, gate_up_full, CONTRACT_LAST, preferred_element_type=jnp.float32
        )
    )
    gate_up_sum = scatter_columns(
        lax.dot_general(
            normed_two, grad_gate_up, CONTRACT_FIRST, preferred_element_type=jnp.float32
        )
    )
    down_sum = scatter_columns(
        lax.dot_general(grad_out, activated, CONTRACT_FIRST, preferred_element_type=jnp.float32)
    )
    grad_unit_two = grad_normed_two * gain_full[1].astype(jnp.float32)
    grad_residual = own_grad.astype(jnp.float32) + inverse_two * (
        grad_unit_two - unit_two * jnp.mean(grad_unit_two * unit_two, axis=-1, keepdims=True)
    )
    grad_branch = gather_tokens(grad_residual.astype(low))
    out_sum = lax.psum_scatter(
        lax.dot_general(
            attended, grad_branch, CONTRACT_FIRST, preferred_element_type=jnp.float32
        ).astype(low),
        PLANE,
        scatter_dimension=0,
        tiled=True,
    )
    grad_heads = (
        lax.dot_general(grad_branch, out_full, CONTRACT_LAST, preferred_element_type=jnp.float32)
        .astype(low)
        .reshape(seq_len, heads_here, HEAD_DIM)
    )
    grad_q_all, grad_k_all, grad_v_all = attend_backward(
        query_heads, key_heads, value_heads, grad_heads, lse_all
    )
    grad_projected = (
        jnp.stack(
            [
                unrotate(grad_q_all, cosines, sines),
                unrotate(grad_k_all, cosines, sines),
                grad_v_all,
            ],
            axis=1,
        )
        .reshape(seq_len, 3 * width_here)
        .astype(low)
    )
    grad_normed_one = scatter_tokens(
        lax.dot_general(
            grad_projected, qkv_full, CONTRACT_LAST, preferred_element_type=jnp.float32
        )
    )
    qkv_sum = scatter_columns(
        lax.dot_general(
            normed_one, grad_projected, CONTRACT_FIRST, preferred_element_type=jnp.float32
        )
    )
    grad_unit_one = grad_normed_one * gain_full[0].astype(jnp.float32)
    input_grad = swap_blocks(
        grad_residual
        + inverse_one
        * (grad_unit_one - unit_one * jnp.mean(grad_unit_one * unit_one, axis=-1, keepdims=True))
    )
    qkv_sum = join_qkv(qkv_sum, grid).astype(jnp.float32)
    gate_up_sum = join_wide(gate_up_sum, 2).astype(jnp.float32)
    down_sum = join_wide(down_sum, 1).astype(jnp.float32)
    gains_sum = jnp.stack(
        [
            jnp.sum(weight.astype(low).astype(jnp.float32) * total, axis=1)
            for weight, total in ((qkv_weight, qkv_sum), (gate_up_weight, gate_up_sum))
        ],
        axis=0,
    ) / gains.astype(low).astype(jnp.float32)
    wide_rate = 2.5 * D ** (-0.5)
    out_rate = 2.5 * max(D // 512, 1) ** (-0.5)
    down_rate = 2.5 * FF ** (-0.5)
    wide = jnp.float32
    qkv_new = adam_step(
        qkv_weight,
        qkv_sum,
        qkv_first,
        qkv_second,
        wide_rate,
        WEIGHT_DECAY,
    )
    out_new = adam_step(
        out_weight, out_sum.astype(wide), out_first, out_second, out_rate, WEIGHT_DECAY
    )
    gate_up_new = adam_step(
        gate_up_weight,
        gate_up_sum,
        gate_up_first,
        gate_up_second,
        wide_rate,
        WEIGHT_DECAY,
    )
    down_new = adam_step(
        down_weight,
        down_sum,
        down_first,
        down_second,
        down_rate,
        WEIGHT_DECAY,
    )
    gains_new = adam_step(gains, gains_sum, gains_first, gains_second, 0.5, 0.0)
    return (
        block_out,
        input_grad[None],
        qkv_new[0],
        out_new[0],
        gate_up_new[0],
        down_new[0],
        gains_new[0],
        qkv_new[1],
        out_new[1],
        gate_up_new[1],
        down_new[1],
        gains_new[1],
        qkv_new[2],
        out_new[2],
        gate_up_new[2],
        down_new[2],
        gains_new[2],
    )


def mapped(body, mesh, token_spec, row_spec, gain_spec):
    one_set = (row_spec, row_spec, row_spec, row_spec, gain_spec)
    return jax.shard_map(
        body,
        mesh=mesh,
        in_specs=(token_spec, token_spec) + one_set * 3,
        out_specs=(token_spec, token_spec) + one_set * 3,
        check_vma=False,
    )


def solution(mesh):
    if mesh.shape["seq"] == 8 and mesh.shape["dp"] == 4:
        grid_mesh = Mesh(mesh.devices.reshape(4, 2, 2, 2), GRID)
        return mapped(
            grid_shards,
            grid_mesh,
            P(("y", "c"), ("z", "x"), None),
            P(GRID, None),
            P(None, GRID),
        )
    return mapped(
        shards, mesh, P("dp", "seq", None), P(("seq", "dp"), None), P(None, ("seq", "dp"))
    )
```

```python
import jax
import jax.numpy as jnp
from jax import lax
from jax.experimental import pallas as pl
from jax.experimental.pallas import tpu as pltpu
from jax.sharding import Mesh
from jax.sharding import PartitionSpec as P

D = 2048
HEADS = 32
HEAD_DIM = 64
FF = 8192
BLOCK = 512
STEP = 10


NORM_EPS = 1e-05
ROPE_BASE = 130000.0
BETA_ONE = 0.9
BETA_TWO = 0.999
ADAM_EPS = 1e-08
WEIGHT_DECAY = 0.1
MASKED = -1e30


def rms_parts(values):
    inverse = lax.rsqrt(jnp.mean(values * values, axis=-1, keepdims=True) + NORM_EPS)
    return (values * inverse, inverse)


def rope_tables(positions):
    half_dim = HEAD_DIM // 2
    exponent = jnp.arange(half_dim, dtype=jnp.float32) * (2.0 / HEAD_DIM)
    frequency = ROPE_BASE ** (-exponent)
    angles = positions.astype(jnp.float32)[:, None] * frequency[None, :]
    return (jnp.cos(angles)[:, None, :], jnp.sin(angles)[:, None, :])


def rotate(tensor, cosines, sines):
    half_dim = HEAD_DIM // 2
    lower_half = tensor[..., :half_dim]
    upper_half = tensor[..., half_dim:]
    return jnp.concatenate(
        [lower_half * cosines - upper_half * sines, upper_half * cosines + lower_half * sines],
        axis=-1,
    )


def unrotate(tensor, cosines, sines):
    half_dim = HEAD_DIM // 2
    lower_half = tensor[..., :half_dim]
    upper_half = tensor[..., half_dim:]
    return jnp.concatenate(
        [lower_half * cosines + upper_half * sines, upper_half * cosines - lower_half * sines],
        axis=-1,
    )


def block_scores(query_rows, key_heads, key_id, block_id):
    key_rows = lax.dynamic_slice_in_dim(key_heads, key_id * BLOCK, BLOCK, 0)
    products = jnp.einsum(
        "qhd,khd->hqk", query_rows, key_rows, preferred_element_type=jnp.float32
    ) * HEAD_DIM ** (-0.5)
    local_ids = jnp.arange(BLOCK, dtype=jnp.int32)
    allowed = (key_id < block_id) | (local_ids[None, :] <= local_ids[:, None])
    return jnp.where(allowed[None], products, MASKED)


def row_normalizer(query_rows, key_heads, block_id):
    row_shape = (query_rows.shape[1], BLOCK, 1)

    def absorb(key_id, state):
        running_max, running_total = state
        scores = block_scores(query_rows, key_heads, key_id, block_id)
        new_max = jnp.maximum(running_max, jnp.max(scores, axis=-1, keepdims=True))
        running_total = running_total * jnp.exp(running_max - new_max) + jnp.sum(
            jnp.exp(scores - new_max), axis=-1, keepdims=True
        )
        return (new_max, running_total)

    start_state = (jnp.full(row_shape, MASKED, jnp.float32), jnp.zeros(row_shape, jnp.float32))
    final_max, final_total = lax.fori_loop(0, block_id + 1, absorb, start_state)
    return final_max + jnp.log(final_total)


def attend_forward(query_heads, key_heads, value_heads):
    seq_len, heads_here, head_dim = query_heads.shape

    def one_block(block_id, carry):
        out_all, lse_all = carry
        row_start = block_id * BLOCK
        query_rows = lax.dynamic_slice_in_dim(query_heads, row_start, BLOCK, 0)
        row_lse = row_normalizer(query_rows, key_heads, block_id)

        def weigh_values(key_id, running):
            scores = block_scores(query_rows, key_heads, key_id, block_id)
            weights_low = jnp.exp(scores - row_lse).astype(jnp.bfloat16)
            value_rows = lax.dynamic_slice_in_dim(value_heads, key_id * BLOCK, BLOCK, 0)
            return running + jnp.einsum(
                "hqk,khd->qhd", weights_low, value_rows, preferred_element_type=jnp.float32
            )

        attended = lax.fori_loop(
            0, block_id + 1, weigh_values, jnp.zeros((BLOCK, heads_here, head_dim), jnp.float32)
        )
        out_all = lax.dynamic_update_slice_in_dim(
            out_all, attended.astype(jnp.bfloat16), row_start, 0
        )
        lse_all = lax.dynamic_update_slice_in_dim(lse_all, row_lse, row_start, 1)
        return (out_all, lse_all)

    start_carry = (
        jnp.zeros((seq_len, heads_here, head_dim), jnp.bfloat16),
        jnp.zeros((heads_here, seq_len, 1), jnp.float32),
    )
    return lax.fori_loop(0, seq_len // BLOCK, one_block, start_carry)


def attend_backward(query_heads, key_heads, value_heads, grad_heads, lse_all):
    seq_len, heads_here, head_dim = query_heads.shape
    score_scale = HEAD_DIM ** (-0.5)

    def one_block(block_id, carry):
        grad_q_all, grad_k_all, grad_v_all = carry
        row_start = block_id * BLOCK
        query_rows = lax.dynamic_slice_in_dim(query_heads, row_start, BLOCK, 0)
        grad_rows = lax.dynamic_slice_in_dim(grad_heads, row_start, BLOCK, 0)
        row_lse = lax.dynamic_slice_in_dim(lse_all, row_start, BLOCK, 1)

        def probs_and_grads(key_id):
            scores = block_scores(query_rows, key_heads, key_id, block_id)
            probs = jnp.exp(scores - row_lse)
            value_rows = lax.dynamic_slice_in_dim(value_heads, key_id * BLOCK, BLOCK, 0)
            grad_probs = jnp.einsum(
                "qhd,khd->hqk", grad_rows, value_rows, preferred_element_type=jnp.float32
            )
            return (probs, grad_probs)

        def add_delta(key_id, running):
            probs, grad_probs = probs_and_grads(key_id)
            return running + jnp.sum(probs * grad_probs, axis=-1, keepdims=True)

        row_delta = lax.fori_loop(
            0, block_id + 1, add_delta, jnp.zeros((heads_here, BLOCK, 1), jnp.float32)
        )

        def spread(key_id, inner):
            grad_q_rows, grad_k_acc, grad_v_acc = inner
            probs, grad_probs = probs_and_grads(key_id)
            key_start = key_id * BLOCK
            key_rows = lax.dynamic_slice_in_dim(key_heads, key_start, BLOCK, 0)
            grad_scores = (probs * (grad_probs - row_delta) * score_scale).astype(jnp.bfloat16)
            grad_q_rows = grad_q_rows + jnp.einsum(
                "hqk,khd->qhd", grad_scores, key_rows, preferred_element_type=jnp.float32
            )
            grad_k_part = jnp.einsum(
                "hqk,qhd->khd", grad_scores, query_rows, preferred_element_type=jnp.float32
            )
            grad_v_part = jnp.einsum(
                "hqk,qhd->khd",
                probs.astype(jnp.bfloat16),
                grad_rows,
                preferred_element_type=jnp.float32,
            )
            grad_k_acc = lax.dynamic_update_slice_in_dim(
                grad_k_acc,
                lax.dynamic_slice_in_dim(grad_k_acc, key_start, BLOCK, 0) + grad_k_part,
                key_start,
                0,
            )
            grad_v_acc = lax.dynamic_update_slice_in_dim(
                grad_v_acc,
                lax.dynamic_slice_in_dim(grad_v_acc, key_start, BLOCK, 0) + grad_v_part,
                key_start,
                0,
            )
            return (grad_q_rows, grad_k_acc, grad_v_acc)

        start_inner = (
            jnp.zeros((BLOCK, heads_here, head_dim), jnp.float32),
            grad_k_all,
            grad_v_all,
        )
        grad_q_rows, grad_k_all, grad_v_all = lax.fori_loop(0, block_id + 1, spread, start_inner)
        grad_q_all = lax.dynamic_update_slice_in_dim(grad_q_all, grad_q_rows, row_start, 0)
        return (grad_q_all, grad_k_all, grad_v_all)

    zeros_all = jnp.zeros((seq_len, heads_here, head_dim), jnp.float32)
    return lax.fori_loop(0, seq_len // BLOCK, one_block, (zeros_all, zeros_all, zeros_all))


def adam_step(weight, gradient, first, second, rate, decay):
    new_first = BETA_ONE * first + (1.0 - BETA_ONE) * gradient
    new_second = BETA_TWO * second + (1.0 - BETA_TWO) * gradient * gradient
    first_hat = new_first / (1.0 - BETA_ONE**STEP)
    second_hat = new_second / (1.0 - BETA_TWO**STEP)
    new_weight = weight - rate * (first_hat / (jnp.sqrt(second_hat) + ADAM_EPS) + decay * weight)
    return (new_weight, new_first, new_second)


def shards(
    tokens,
    cotangent,
    qkv_weight,
    out_weight,
    gate_up_weight,
    down_weight,
    gains,
    qkv_first,
    out_first,
    gate_up_first,
    down_first,
    gains_first,
    qkv_second,
    out_second,
    gate_up_second,
    down_second,
    gains_second,
):
    seq_count = lax.axis_size("seq")
    tok_rows = tokens.shape[1]
    width = tokens.shape[2]
    seq_len = tok_rows * seq_count
    heads_here = HEADS // seq_count
    width_here = heads_here * HEAD_DIM
    contract_last = (((1,), (1,)), ((), ()))
    contract_first = (((0,), (0,)), ((), ()))
    qkv_full, proj_full, gain_full = (
        lax.all_gather(qkv_weight.astype(jnp.bfloat16), ("seq", "dp"), axis=0, tiled=True),
        lax.all_gather(out_weight.astype(jnp.bfloat16), ("seq", "dp"), axis=0, tiled=True),
        lax.all_gather(gains.astype(jnp.bfloat16), ("seq", "dp"), axis=1, tiled=True),
    )
    up_full, down_full = (
        lax.all_gather(gate_up_weight.astype(jnp.bfloat16), ("seq", "dp"), axis=0, tiled=True),
        lax.all_gather(down_weight.astype(jnp.bfloat16), ("seq", "dp"), axis=0, tiled=True),
    )
    hidden_in = tokens[0].astype(jnp.float32)
    unit_one, inverse_one = rms_parts(hidden_in)
    normed_one = (unit_one * gain_full[0].astype(jnp.float32)).astype(jnp.bfloat16)
    projected = jnp.einsum(
        "te,ecd->ctd",
        normed_one,
        qkv_full.reshape(width, 3, width),
        preferred_element_type=jnp.float32,
    )
    positions = lax.axis_index("seq") * tok_rows + jnp.arange(tok_rows, dtype=jnp.int32)
    cos_local, sin_local = rope_tables(positions)
    turned = rotate(projected[:2].reshape(2, tok_rows, HEADS, HEAD_DIM), cos_local, sin_local)
    packed = jnp.concatenate([turned.reshape(2, tok_rows, width), projected[2:]], axis=0).astype(
        jnp.bfloat16
    )
    by_heads = lax.all_to_all(packed, "seq", split_axis=2, concat_axis=1, tiled=True)
    query_heads = by_heads[0].reshape(seq_len, heads_here, HEAD_DIM)
    key_heads = by_heads[1].reshape(seq_len, heads_here, HEAD_DIM)
    value_heads = by_heads[2].reshape(seq_len, heads_here, HEAD_DIM)
    out_heads, lse_all = attend_forward(query_heads, key_heads, value_heads)
    attended = lax.all_to_all(
        out_heads.reshape(seq_len, width_here), "seq", split_axis=0, concat_axis=1, tiled=True
    )
    residual = hidden_in + jnp.dot(attended, proj_full, preferred_element_type=jnp.float32)
    unit_two, inverse_two = rms_parts(residual)
    normed_two = (unit_two * gain_full[1].astype(jnp.float32)).astype(jnp.bfloat16)
    gate_up = jnp.dot(normed_two, up_full, preferred_element_type=jnp.float32)
    gate_vals = gate_up[:, :FF]
    up_vals = gate_up[:, FF:]
    sigmoid_gate = jax.nn.sigmoid(gate_vals)
    activated = (gate_vals * sigmoid_gate * up_vals).astype(jnp.bfloat16)
    mlp_out = lax.dot_general(
        activated, down_full, contract_last, preferred_element_type=jnp.float32
    )
    block_out = (residual + mlp_out).astype(jnp.bfloat16)[None]
    back_up, back_down, back_gain = (
        lax.all_gather(gate_up_weight.astype(jnp.bfloat16), ("seq", "dp"), axis=0, tiled=True),
        lax.all_gather(down_weight.astype(jnp.bfloat16), ("seq", "dp"), axis=0, tiled=True),
        lax.all_gather(gains.astype(jnp.bfloat16), ("seq", "dp"), axis=1, tiled=True),
    )
    grad_out = cotangent[0]
    grad_act = jnp.dot(grad_out, back_down, preferred_element_type=jnp.float32)
    grad_gate = grad_act * up_vals * sigmoid_gate * (1.0 + gate_vals * (1.0 - sigmoid_gate))
    grad_up = grad_act * gate_vals * sigmoid_gate
    grad_gate_up = jnp.concatenate([grad_gate, grad_up], axis=1).astype(jnp.bfloat16)
    grad_normed_two = lax.dot_general(
        grad_gate_up, back_up, contract_last, preferred_element_type=jnp.float32
    )
    gain_two_grad = jnp.sum(grad_normed_two * unit_two, axis=0)
    grad_unit_two = grad_normed_two * back_gain[1].astype(jnp.float32)
    grad_residual = grad_out.astype(jnp.float32) + inverse_two * (
        grad_unit_two - unit_two * jnp.mean(grad_unit_two * unit_two, axis=-1, keepdims=True)
    )
    gate_up_rows = lax.dot_general(
        normed_two, grad_gate_up, contract_first, preferred_element_type=jnp.float32
    )
    down_rows = lax.dot_general(
        grad_out, activated, contract_first, preferred_element_type=jnp.float32
    )
    mlp_grad = lax.psum_scatter(
        jnp.concatenate([gate_up_rows, down_rows], axis=1),
        ("seq", "dp"),
        scatter_dimension=0,
        tiled=True,
    )
    back_qkv, back_proj = (
        lax.all_gather(qkv_weight.astype(jnp.bfloat16), ("seq", "dp"), axis=0, tiled=True),
        lax.all_gather(out_weight.astype(jnp.bfloat16), ("seq", "dp"), axis=0, tiled=True),
    )
    grad_branch = grad_residual.astype(jnp.bfloat16)
    proj_grad = lax.dot_general(
        attended, grad_branch, contract_first, preferred_element_type=jnp.float32
    )
    grad_attended = lax.dot_general(
        grad_branch, back_proj, contract_last, preferred_element_type=jnp.float32
    ).astype(jnp.bfloat16)
    grad_heads = lax.all_to_all(
        grad_attended, "seq", split_axis=1, concat_axis=0, tiled=True
    ).reshape(seq_len, heads_here, HEAD_DIM)
    grad_q_all, grad_k_all, grad_v_all = attend_backward(
        query_heads, key_heads, value_heads, grad_heads, lse_all
    )
    cos_whole, sin_whole = rope_tables(jnp.arange(seq_len, dtype=jnp.int32))
    grad_pack = jnp.stack(
        [
            unrotate(grad_q_all, cos_whole, sin_whole).reshape(seq_len, width_here),
            unrotate(grad_k_all, cos_whole, sin_whole).reshape(seq_len, width_here),
            grad_v_all.reshape(seq_len, width_here),
        ],
        axis=0,
    ).astype(jnp.bfloat16)
    grad_projected = lax.all_to_all(grad_pack, "seq", split_axis=1, concat_axis=2, tiled=True)
    qkv_cube = back_qkv.reshape(width, 3, width)
    grad_normed_one = jnp.einsum(
        "ctd,ecd->te", grad_projected, qkv_cube, preferred_element_type=jnp.float32
    )
    qkv_grad = jnp.einsum(
        "te,ctd->ecd", normed_one, grad_projected, preferred_element_type=jnp.float32
    ).reshape(width, 3 * width)
    gain_one_grad = jnp.sum(grad_normed_one * unit_one, axis=0)
    grad_unit_one = grad_normed_one * back_gain[0].astype(jnp.float32)
    input_grad = grad_residual + inverse_one * (
        grad_unit_one - unit_one * jnp.mean(grad_unit_one * unit_one, axis=-1, keepdims=True)
    )
    gains_grad = jnp.stack([gain_one_grad, gain_two_grad], axis=0)
    qkv_sum, proj_sum, gains_sum = (
        lax.psum_scatter(qkv_grad, ("seq", "dp"), scatter_dimension=0, tiled=True),
        lax.psum_scatter(proj_grad, ("seq", "dp"), scatter_dimension=0, tiled=True),
        lax.psum_scatter(gains_grad, ("seq", "dp"), scatter_dimension=1, tiled=True),
    )
    wide_rate = 2.5 * D ** (-0.5)
    out_rate = 2.5 * max(D // 512, 1) ** (-0.5)
    down_rate = 2.5 * FF ** (-0.5)
    qkv_new = adam_step(qkv_weight, qkv_sum, qkv_first, qkv_second, wide_rate, WEIGHT_DECAY)
    out_new = adam_step(out_weight, proj_sum, out_first, out_second, out_rate, WEIGHT_DECAY)
    gate_up_new = adam_step(
        gate_up_weight,
        mlp_grad[:, : 2 * FF],
        gate_up_first,
        gate_up_second,
        wide_rate,
        WEIGHT_DECAY,
    )
    down_new = adam_step(
        down_weight, mlp_grad[:, 2 * FF :], down_first, down_second, down_rate, WEIGHT_DECAY
    )
    gains_new = adam_step(gains, gains_sum, gains_first, gains_second, 0.5, 0.0)
    return (
        block_out,
        input_grad[None],
        qkv_new[0],
        out_new[0],
        gate_up_new[0],
        down_new[0],
        gains_new[0],
        qkv_new[1],
        out_new[1],
        gate_up_new[1],
        down_new[1],
        gains_new[1],
        qkv_new[2],
        out_new[2],
        gate_up_new[2],
        down_new[2],
        gains_new[2],
    )


GRID = ("z", "x", "y", "c")
RING = ("z", "c")
PLANE = ("x", "y")
LOW = jnp.bfloat16
WIDE = jnp.float32
CONTRACT_LAST = (((1,), (1,)), ((), ()))
CONTRACT_FIRST = (((0,), (0,)), ((), ()))
DMA = pltpu.SemaphoreType.DMA
ANYWHERE = pl.BlockSpec(memory_space=pl.ANY)
IN_VMEM = pl.BlockSpec(memory_space=pltpu.VMEM)


def remote(source, target, send, receive, **place):
    return pltpu.make_async_remote_copy(
        src_ref=source,
        dst_ref=target,
        send_sem=send,
        recv_sem=receive,
        device_id=place,
        device_id_type=pl.DeviceIdType.MESH,
    )


def lanes(start, size):
    return pl.ds(pl.multiple_of(start, 128), size)


class Place:
    def __init__(self):
        self.z, self.x, self.y, self.c = (lax.axis_index(name) for name in GRID)
        self.slot = 2 * self.z + self.c
        self.block_here = self.block(self.slot, self.x, self.y)

    def block(self, slot, x, y):
        return (((slot // 2) * 2 + x) * 2 + y) * 2 + lax.rem(slot, 2)

    def meet(self, plane):
        barrier = pltpu.get_barrier_semaphore()
        others = [
            {"z": slot // 2, "c": lax.rem(slot, 2)}
            for slot in (lax.rem(self.slot + step, 8) for step in range(1, 8))
        ]
        if plane:
            others += [{"x": 1 - self.x}, {"y": 1 - self.y}, {"x": 1 - self.x, "c": 1 - self.c}]
        for other in others:
            pl.semaphore_signal(
                barrier, inc=1, device_id=other, device_id_type=pl.DeviceIdType.MESH
            )
        pl.semaphore_wait(barrier, len(others))


class Swap:
    def __init__(self, place, source, spot_there, spot_here, sems):
        p = self.place = place
        self.away = lambda: remote(
            source, spot_there, sems.at[0], sems.at[1], x=1 - p.x, c=1 - p.c
        )
        self.here = lambda: pltpu.make_async_copy(source, spot_here, sems.at[2])

    def start(self):
        p = self.place
        pl.when(p.x != p.c)(lambda: self.away().start())
        pl.when(p.x == p.c)(lambda: self.here().start())

    def wait(self):
        p = self.place
        pl.when(p.x != p.c)(lambda: self.away().wait_recv())
        pl.when(p.x == p.c)(lambda: self.here().wait())

    def drain(self):
        p = self.place
        pl.when(p.x != p.c)(lambda: self.away().wait_send())


class LineGather:
    SEMS = (4, 8)

    def __init__(self, place, buffer, sems, mine=None):
        self.place, self.buffer, self.sems = place, buffer, sems
        self.mine = mine

    def copy(self, slot, way, own=False):
        p, block = self.place, self.buffer.at[slot]
        if way == 0:
            where = {"z": jnp.minimum(p.z + 1, 3)}
        elif way == 1:
            where = {"z": jnp.maximum(p.z - 1, 0)}
        else:
            where = {"c": 1 - p.c}
        source = self.mine if own and self.mine is not None else block
        return remote(source, block, self.sems.at[way, slot], self.sems.at[3, slot], **where)

    def _pass_on(self, slot, way, own=False):
        p = self.place
        if way == 0:
            pl.when(p.z < 3)(lambda: self.copy(slot, 0, own).start())
        elif way == 1:
            pl.when(p.z > 0)(lambda: self.copy(slot, 1, own).start())

    def start(self):
        slot = self.place.slot
        self._pass_on(slot, 0, True)
        self._pass_on(slot, 1, True)
        self.copy(slot, 2, True).start()
        if self.mine is not None:
            self.keep().start()

    def keep(self):
        slot = self.place.slot
        return pltpu.make_async_copy(self.mine, self.buffer.at[slot], self.sems.at[3, slot])

    def step(self, distance):
        p = self.place

        @pl.when(p.z + distance <= 3)
        def _():
            slot = p.slot + 2 * distance
            self.copy(slot, 2).wait_recv()
            self._pass_on(slot, 1)
            self.copy(slot, 2).start()

        @pl.when(p.z >= distance)
        def _():
            slot = p.slot - 2 * distance
            self.copy(slot, 2).wait_recv()
            self._pass_on(slot, 0)
            self.copy(slot, 2).start()

    def finish(self):
        p = self.place
        if self.mine is not None:
            self.keep().wait()
        for z in range(4):
            self.copy(2 * z + 1 - p.c, 2).wait_recv()

    def drain(self):
        p = self.place
        for z in range(4):
            slot = 2 * z + p.c
            self.copy(slot, 2).wait_send()
            pl.when((z <= p.z) & (p.z < 3))(lambda: self.copy(slot, 0).wait_send())
            pl.when((z >= p.z) & (p.z > 0))(lambda: self.copy(slot, 1).wait_send())


def add_blocks(target, sources):
    def some(step, carry):
        rows = pl.ds(pl.multiple_of(step * 16, 16), 16)
        total = sources[0][rows, :].astype(WIDE)
        for source in sources[1:]:
            total = total + source[rows, :].astype(WIDE)
        target[rows, :] = total.astype(target.dtype)
        return carry

    lax.fori_loop(0, target.shape[0] // 16, some, 0)


class LineScatter:
    SEMS = (6, 4)

    @staticmethod
    def scratch(rows, width):
        return [pltpu.VMEM((4, rows, width), LOW) for _ in range(5)] + [DMA(LineScatter.SEMS)]

    def __init__(self, place, partial, across, below, above, stage_up, stage_down, sems):
        self.place, self.partial, self.sems = place, partial, sems
        self.across, self.below, self.above = across, below, above
        self.stages = (stage_up, stage_down)

    def cross(self, z):
        p = self.place
        return remote(
            self.partial.at[2 * z + 1 - p.c],
            self.across.at[z],
            self.sems.at[0, z],
            self.sems.at[1, z],
            c=1 - p.c,
        )

    def hop(self, z, way):
        p = self.place
        target = (self.below, self.above)[way]
        there = jnp.minimum(p.z + 1, 3) if way == 0 else jnp.maximum(p.z - 1, 0)
        return remote(
            self.stages[way].at[z],
            target.at[z],
            self.sems.at[2 + 2 * way, z],
            self.sems.at[3 + 2 * way, z],
            z=there,
        )

    def start(self):
        p = self.place
        for z in range(4):
            self.cross(z).start()

        @pl.when(p.z == 0)
        def _():
            self.below[...] = jnp.zeros_like(self.below)

        @pl.when(p.z == 3)
        def _():
            self.above[...] = jnp.zeros_like(self.above)

    def step(self, index):
        p = self.place
        if index == 0:
            for z in range(4):
                self.cross(z).wait_recv()
        for way, z in ((0, 3 - index), (1, index)):
            sending = p.z < z if way == 0 else p.z > z
            receiving = p.z > 0 if way == 0 else p.z < 3
            passing = (self.below, self.above)[way]

            @pl.when(sending)
            def _():
                pl.when(receiving)(lambda: self.hop(z, way).wait_recv())
                add_blocks(
                    self.stages[way].at[z],
                    [self.partial.at[2 * z + p.c], self.across.at[z], passing.at[z]],
                )
                self.hop(z, way).start()

    def arrive(self):
        p = self.place
        pl.when(p.z > 0)(lambda: self.hop(p.z, 0).wait_recv())
        pl.when(p.z < 3)(lambda: self.hop(p.z, 1).wait_recv())

        @pl.when(p.z == 0)
        def _():
            self.below[0] = jnp.zeros_like(self.below[0])

        @pl.when(p.z == 3)
        def _():
            self.above[3] = jnp.zeros_like(self.above[3])

    def total(self, rows):
        p = self.place
        parts = (
            self.partial[p.slot, rows, :],
            self.across[p.z, rows, :],
            self.below[p.z, rows, :],
            self.above[p.z, rows, :],
        )
        return sum(part.astype(WIDE) for part in parts)

    def drain(self):
        p = self.place
        for z in range(4):
            self.cross(z).wait_send()
            pl.when(p.z < z)(lambda: self.hop(z, 0).wait_send())
            pl.when(p.z > z)(lambda: self.hop(z, 1).wait_send())


class Relayout:
    SEMS = (8, 8)

    def __init__(self, place, parts, target, sems):
        self.place, self.parts, self.target, self.sems = place, parts, target, sems

    def sem(self, kind, slot):
        return self.sems.at[kind, slot]

    def line(self, step):
        p = self.place
        slot = lax.rem(p.slot + step, 8)
        copies = []
        for source, first, size, there in self.parts:
            same_for_all = source.shape[1] == size
            columns = lanes(first if same_for_all else first + size * slot, size)
            piece = source.at[:, columns]
            spot = self.target.at[p.block_here, :, pl.ds(there, size)]
            if step == 0:
                copies.append(pltpu.make_async_copy(piece, spot, self.sem(1, p.slot)))
            else:
                copies.append(
                    remote(
                        piece,
                        spot,
                        self.sem(0, slot),
                        self.sem(1, p.slot),
                        z=slot // 2,
                        c=lax.rem(slot, 2),
                    )
                )
        return copies

    def whole(self, slot):
        p = self.place
        spot = self.target.at[p.block(slot, p.x, p.y)]
        return remote(spot, spot, self.sem(0, slot), self.sem(1, slot), c=1 - p.c)

    def plane(self, slot, x, y, way, send, receive):
        p = self.place
        spot = self.target.at[p.block(slot, x, y)]
        where = {"x": 1 - p.x} if way == 0 else {"y": 1 - p.y}
        return remote(spot, spot, self.sem(send, slot), self.sem(receive, slot), **where)

    def from_own(self, slot, way):
        p = self.place
        return self.plane(slot, p.x, p.y, way, 2 + 2 * way, 3 + 2 * way)

    def corner(self, slot, way):
        p = self.place
        x, y = (p.x, 1 - p.y) if way == 0 else (1 - p.x, p.y)
        return self.plane(slot, x, y, way, 6, 7)

    def start(self):
        for step in range(8):
            for copy in self.line(step):
                copy.start()

    def spread(self, step):
        p = self.place
        slot = lax.rem(p.slot + 8 - step, 8)
        if step == 0:
            spot = self.target.at[p.block_here]
            pltpu.make_async_copy(spot, spot, self.sem(1, p.slot)).wait()
        else:
            self.whole(slot).wait_recv()
        for way in range(2):
            self.from_own(slot, way).start()

    def corners(self, z):
        self.from_own(2 * z, 0).wait_recv()
        self.corner(2 * z, 1).start()
        self.from_own(2 * z + 1, 1).wait_recv()
        self.corner(2 * z + 1, 0).start()

    def finish(self):
        for z in range(4):
            self.from_own(2 * z, 1).wait_recv()
            self.from_own(2 * z + 1, 0).wait_recv()
            self.corner(2 * z, 1).wait_recv()
            self.corner(2 * z + 1, 0).wait_recv()

    def drain(self):
        for step in range(1, 8):
            self.whole(lax.rem(self.place.slot + step, 8)).wait_send()
        for z in range(4):
            self.corner(2 * z, 1).wait_send()
            self.corner(2 * z + 1, 0).wait_send()
        for slot in range(8):
            for way in range(2):
                self.from_own(slot, way).wait_send()


class PlaneScatter:
    @staticmethod
    def scratch(units, rows, width):
        shape = (rows, width)
        return [
            pltpu.VMEM((2, 2, units) + shape, LOW),
            pltpu.VMEM((2, 2, units) + shape, LOW),
            pltpu.VMEM((2, units) + shape, LOW),
            pltpu.VMEM((2, units) + shape, LOW),
            DMA((5, 2, 2, units)),
        ]

    def __init__(self, place, part, units, sums, held, got, stage, last, sems):
        self.place, self.part, self.units, self.sums = place, part, units, sums
        self.held, self.got, self.stage, self.last = held, got, stage, last
        self.sems = sems

    def pair(self, near):
        p = self.place
        x, y = (p.x, p.y) if near else (1 - p.x, 1 - p.y)
        return ((p.x, y), (x, p.y))

    def load(self, half, near, unit):
        x, y = self.pair(near)[half]
        return pltpu.make_async_copy(
            self.part(half, unit, x, y),
            self.held.at[half, near, unit],
            self.sems.at[0, half, near, unit],
        )

    def first(self, half, near, unit):
        p = self.place
        x, y = self.pair(near)[half]
        x, y = (1 - x, y) if half == 0 else (x, 1 - y)
        where = {"x": 1 - p.x} if half == 0 else {"y": 1 - p.y}
        return remote(
            self.part(half, unit, x, y),
            self.got.at[half, near, unit],
            self.sems.at[1, half, near, unit],
            self.sems.at[2, half, near, unit],
            **where,
        )

    def second(self, half, unit):
        p = self.place
        where = {"y": 1 - p.y} if half == 0 else {"x": 1 - p.x}
        return remote(
            self.stage.at[half, unit],
            self.last.at[half, unit],
            self.sems.at[3, half, 0, unit],
            self.sems.at[4, half, 0, unit],
            **where,
        )

    def each(self, call):
        lax.fori_loop(0, self.units, lambda unit, carry: (call(unit), carry)[1], 0)

    def start(self):
        for near in range(2):

            def begin(unit):
                for half in range(2):
                    self.first(half, near, unit).start()
                    self.load(half, near, unit).start()

            self.each(begin)

    def middle(self, unit):
        for half in range(2):
            self.load(half, 0, unit).wait()
            self.first(half, 0, unit).wait_recv()
            add_blocks(
                self.stage.at[half, unit], [self.held.at[half, 0, unit], self.got.at[half, 0, unit]]
            )
            self.second(half, unit).start()

    def final(self, unit):
        for half in range(2):
            self.load(half, 1, unit).wait()
            self.first(half, 1, unit).wait_recv()
            self.second(half, unit).wait_recv()
            add_blocks(
                self.sums(half, unit),
                [
                    self.held.at[half, 1, unit],
                    self.got.at[half, 1, unit],
                    self.last.at[half, unit],
                ],
            )

    def drain(self):
        def end(unit):
            for half in range(2):
                for near in range(2):
                    self.first(half, near, unit).wait_send()
                self.second(half, unit).wait_send()

        self.each(end)


class LineReturn:
    SEMS = (2, 8)

    def __init__(self, place, sums, parts, target, sems):
        self.place, self.sums, self.parts = place, sums, parts
        self.target, self.sems = target, sems

    def copies(self, z, c, local):
        p = self.place
        made = []
        for here, size, first in self.parts:
            piece = self.sums.at[z, c, :, pl.ds(here, size)]
            spot = self.target.at[:, lanes(first + size * p.slot, size)]
            if local:
                made.append(pltpu.make_async_copy(piece, spot, self.sems.at[1, p.slot]))
            else:
                made.append(
                    remote(
                        piece, spot, self.sems.at[0, 2 * z + c], self.sems.at[1, p.slot], z=z, c=c
                    )
                )
        return made

    def send(self, z):
        p = self.place
        for c in range(2):
            mine = (z == p.z) & (c == p.c)

            @pl.when(mine)
            def _():
                for copy in self.copies(z, c, True):
                    copy.start()

            @pl.when(jnp.logical_not(mine))
            def _():
                for copy in self.copies(z, c, False):
                    copy.start()

    def finish(self):
        p = self.place
        spot = self.sums.at[0, 0]
        pltpu.make_async_copy(spot, spot, self.sems.at[1, p.slot]).wait()
        for step in range(1, 8):
            slot = lax.rem(p.slot + step, 8)
            whole = remote(
                spot, spot, self.sems.at[0, slot], self.sems.at[1, slot], c=1 - p.c
            )
            whole.wait_recv()
            whole.wait_send()


def fetch_kernel(
    tok, cot, wq, gain, wg, wd, wo, all_tok, all_cot, full_q, full_g, full_d, full_o, *sems
):
    tok_swap, cot_swap, out_swap, tok_sems, cot_sems, q_sems, g_sems, d_sems, o_sems = sems
    p = Place()
    p.meet(True)
    step_q, step_g, step_d = wq.shape[1] // 24, wg.shape[1] // 16, wd.shape[1] // 8
    q_parts = [(wq, i * 8 * step_q, step_q, i * step_q) for i in range(3)]
    q_parts.append((gain, 0, gain.shape[1], 3 * step_q))
    weights = [
        Relayout(p, q_parts, full_q, q_sems),
        Relayout(p, [(wg, i * 8 * step_g, step_g, i * step_g) for i in range(2)], full_g, g_sems),
        Relayout(p, [(wd, 0, step_d, 0)], full_d, d_sems),
    ]
    gathers = [LineGather(p, all_tok, tok_sems), LineGather(p, all_cot, cot_sems)]
    away = 2 * p.z + 1 - p.c
    swaps = [
        Swap(p, tok, all_tok.at[away], all_tok.at[p.slot], tok_swap),
        Swap(p, cot, all_cot.at[away], all_cot.at[p.slot], cot_swap),
        Swap(p, wo, full_o.at[2 * p.y + 1 - p.x], full_o.at[2 * p.y + p.x], out_swap),
    ]
    half = wo.shape[0] // 2

    def out_copy(kind):
        mine, beside, above = 2 * p.y + p.x, 2 * p.y + 1 - p.x, 2 * (1 - p.y) + p.x
        send, got = o_sems.at[0, kind], o_sems.at[1, kind]
        if kind < 2:
            where = {"x": 1 - p.x} if kind == 0 else {"y": 1 - p.y}
            return remote(full_o.at[mine], full_o.at[mine], send, got, **where)
        spot = full_o.at[beside if kind == 2 else above, pl.ds((kind - 2) * half, half)]
        where = {"y": 1 - p.y} if kind == 2 else {"x": 1 - p.x}
        return remote(spot, spot, send, got, **where)

    swaps[0].start()
    weights[0].start()
    swaps[2].start()
    swaps[1].start()
    swaps[0].wait()
    gathers[0].start()
    for step in range(8):
        weights[0].spread(step)
    gathers[0].step(1)
    gathers[0].step(2)
    weights[1].start()
    for z in range(4):
        weights[0].corners(z)
    gathers[0].step(3)
    swaps[2].wait()
    out_copy(0).start()
    out_copy(1).start()
    for step in range(8):
        weights[1].spread(step)
    weights[2].start()
    out_copy(0).wait_recv()
    out_copy(2).start()
    out_copy(1).wait_recv()
    out_copy(3).start()
    for z in range(4):
        weights[1].corners(z)
    swaps[1].wait()
    gathers[1].start()
    for step in range(8):
        weights[2].spread(step)
    for distance in range(1, 4):
        gathers[1].step(distance)
    for z in range(4):
        weights[2].corners(z)
    out_copy(2).wait_recv()
    out_copy(3).wait_recv()
    for kind in range(4):
        out_copy(kind).wait_send()
    for part in swaps:
        part.drain()
    for part in gathers + weights:
        part.finish()
        part.drain()


def kernel_call(kernel, name, number, inputs, in_specs, outputs, out_specs, scratch):
    return pl.pallas_call(
        kernel,
        out_shape=[jax.ShapeDtypeStruct(shape, dtype) for shape, dtype in outputs],
        in_specs=in_specs,
        out_specs=out_specs,
        scratch_shapes=scratch,
        compiler_params=pltpu.CompilerParams(
            collective_id=number, has_side_effects=True, vmem_limit_bytes=56 * 2**20
        ),
        name=name,
    )(*inputs)


def fetch_all(tokens, cotangent, qkv, gain_columns, gate_up, down, out_rows):
    rows, width = tokens.shape
    own = qkv.shape[0]
    shapes = [(8, rows, width)] * 2
    shapes += [(32, own, qkv.shape[1] // 8 + gain_columns.shape[1])]
    shapes += [(32, own, gate_up.shape[1] // 8), (32, own, down.shape[1] // 8)]
    shapes += [(4,) + out_rows.shape]
    return kernel_call(
        fetch_kernel,
        "fetch_all",
        1,
        (tokens, cotangent, qkv, gain_columns, gate_up, down, out_rows),
        [ANYWHERE] * 7,
        [(shape, LOW) for shape in shapes],
        [ANYWHERE] * 6,
        [DMA((3,))] * 3 + [DMA(LineGather.SEMS)] * 2 + [DMA(Relayout.SEMS)] * 3 + [DMA((2, 4))],
    )


CHUNK = 16


def by_rows(count, call):
    def some(step, carry):
        call(pl.ds(pl.multiple_of(step * CHUNK, CHUNK), CHUNK))
        return carry

    lax.fori_loop(0, count // CHUNK, some, 0)


def normed_back(grad_normed, unit, inverse, gain):
    grad_unit = grad_normed * gain
    return inverse * (grad_unit - unit * jnp.mean(grad_unit * unit, axis=-1, keepdims=True))


def branch_kernel(partial, hidden, gain, residual, normed, mine, *scratch):
    p = Place()
    p.meet(False)
    line = LineScatter(p, partial, *scratch[:6])
    gather = LineGather(p, normed, scratch[6], mine)
    line.start()
    for index in range(3):
        line.step(index)
    line.arrive()

    def local(rows):
        total = hidden[rows, :].astype(WIDE) + line.total(rows)
        residual[rows, :] = total
        unit, _ = rms_parts(total)
        mine[rows, :] = (unit * gain[...]).astype(LOW)

    by_rows(hidden.shape[0], local)
    gather.start()
    for distance in range(1, 4):
        gather.step(distance)
    gather.finish()
    line.drain()
    gather.drain()


def branch_sum(partial, hidden, gain):
    _, rows, width = partial.shape
    return kernel_call(
        branch_kernel,
        "branch_sum",
        2,
        (partial, hidden, gain),
        [IN_VMEM] * 3,
        [((rows, width), WIDE), ((8, rows, width), LOW)],
        [IN_VMEM, ANYWHERE],
        [pltpu.VMEM((rows, width), LOW)]
        + LineScatter.scratch(rows, width)
        + [DMA(LineGather.SEMS)],
    )


def weight_part(place, ref):
    return lambda half, unit, x, y: ref.at[place.block(2 * unit + half, x, y)]


def middle_kernel(
    partial, residual, grad_out, gain, wide_grad, grad_residual, branch, wide_sum, mine, *scratch
):
    p = Place()
    p.meet(True)
    line = LineScatter(p, partial, *scratch[:6])
    gather = LineGather(p, branch, scratch[6], mine)
    units = wide_grad.shape[0] // 8
    plane = PlaneScatter(
        p, weight_part(p, wide_grad), units, lambda h, u: wide_sum.at[u, h], *scratch[7:]
    )
    line.start()
    plane.start()
    line.step(0)
    plane.middle(0)
    plane.middle(1)
    line.step(1)
    plane.middle(2)
    plane.middle(3)
    line.step(2)
    line.arrive()

    def local(rows):
        unit, inverse = rms_parts(residual[rows, :])
        total = grad_out[rows, :].astype(WIDE) + normed_back(
            line.total(rows), unit, inverse, gain[...]
        )
        grad_residual[rows, :] = total
        mine[rows, :] = total.astype(LOW)

    by_rows(residual.shape[0], local)
    gather.start()
    for distance in range(1, 4):
        gather.step(distance)
    plane.each(plane.final)
    gather.finish()
    line.drain()
    gather.drain()
    plane.drain()


def middle_sum(partial, residual, grad_out, gain, wide_grad):
    _, rows, width = partial.shape
    units, own, columns = wide_grad.shape[0] // 8, wide_grad.shape[1], wide_grad.shape[2]
    return kernel_call(
        middle_kernel,
        "middle_sum",
        3,
        (partial, residual, grad_out, gain, wide_grad),
        [IN_VMEM] * 4 + [ANYWHERE],
        [
            ((rows, width), WIDE),
            ((8, rows, width), LOW),
            ((units, 2, own, columns), LOW),
        ],
        [IN_VMEM, ANYWHERE, IN_VMEM],
        [pltpu.VMEM((rows, width), LOW)]
        + LineScatter.scratch(rows, width)
        + [DMA(LineGather.SEMS)]
        + PlaneScatter.scratch(units, own, columns),
    )


def last_kernel(
    partial,
    tokens,
    grad_residual,
    gain,
    block,
    wide_sum,
    q_grad,
    d_grad,
    o_grad,
    input_grad,
    block_out,
    q_out,
    g_out,
    d_out,
    o_out,
    mine,
    q_sum,
    d_sum,
    o_sum,
    *scratch,
):
    p = Place()
    p.meet(True)
    line = LineScatter(p, partial, *scratch[:6])
    rest = scratch[6:]
    units = q_grad.shape[0] // 8
    half = o_grad.shape[1] // 2
    planes = [
        PlaneScatter(
            p, weight_part(p, q_grad), units, lambda h, u: q_sum.at[u, h], *rest[:5]
        ),
        PlaneScatter(
            p, weight_part(p, d_grad), units, lambda h, u: d_sum.at[u, h], *rest[5:10]
        ),
        PlaneScatter(
            p,
            lambda h, u, x, y: o_grad.at[2 * y + x, pl.ds(h * half, half)],
            1,
            lambda h, u: o_sum.at[pl.ds(h * half, half)],
            *rest[10:15],
        ),
    ]
    q_sems, g_sems, d_sems, out_swap, in_swap, block_swap = rest[15:]
    step_q, step_g, step_d = q_grad.shape[2] // 3, wide_sum.shape[3] // 2, d_grad.shape[2]
    returns = [
        LineReturn(p, q_sum, [(i * step_q, step_q, i * 8 * step_q) for i in range(3)], q_out, q_sems),
        LineReturn(
            p, wide_sum, [(i * step_g, step_g, i * 8 * step_g) for i in range(2)], g_out, g_sems
        ),
        LineReturn(p, d_sum, [(0, step_d, 0)], d_out, d_sems),
    ]
    swaps = [
        Swap(p, mine, input_grad, input_grad, in_swap),
        Swap(p, block, block_out, block_out, block_swap),
        Swap(p, o_sum, o_out, o_out, out_swap),
    ]
    line.start()
    for plane in planes:
        plane.start()
    for z in range(4):
        returns[1].send(z)
    swaps[1].start()
    line.step(0)
    planes[0].each(planes[0].middle)
    line.step(1)
    planes[1].each(planes[1].middle)
    planes[2].each(planes[2].middle)
    line.step(2)
    line.arrive()

    def local(rows):
        unit, inverse = rms_parts(tokens[rows, :].astype(WIDE))
        mine[rows, :] = grad_residual[rows, :] + normed_back(
            line.total(rows), unit, inverse, gain[...]
        )

    by_rows(tokens.shape[0], local)
    swaps[0].start()
    for z in range(4):
        planes[0].final(z)
        returns[0].send(z)
    for z in range(4):
        planes[1].final(z)
        returns[2].send(z)
    planes[2].final(0)
    swaps[2].start()
    for part in returns:
        part.finish()
    for part in swaps:
        part.wait()
        part.drain()
    line.drain()
    for part in planes:
        part.drain()


def last_sum(partial, tokens, grad_residual, gain, block, wide_sum, q_grad, d_grad, o_grad):
    _, rows, width = partial.shape
    units, own = q_grad.shape[0] // 8, q_grad.shape[1]
    sizes = [grad.shape[2] for grad in (q_grad, d_grad)]
    vmem = lambda shape, dtype=LOW: pltpu.VMEM(shape, dtype)
    return kernel_call(
        last_kernel,
        "last_sum",
        4,
        (partial, tokens, grad_residual, gain, block, wide_sum, q_grad, d_grad, o_grad),
        [IN_VMEM] * 4 + [ANYWHERE] * 5,
        [
            ((rows, width), WIDE),
            ((rows, width), LOW),
            ((own, 8 * sizes[0]), LOW),
            ((own, 8 * wide_sum.shape[3]), LOW),
            ((own, 8 * sizes[1]), LOW),
            ((own, width), LOW),
        ],
        [ANYWHERE] * 6,
        [vmem((rows, width), WIDE)]
        + [vmem((units, 2, own, size)) for size in sizes]
        + [vmem((own, width))]
        + LineScatter.scratch(rows, width)
        + PlaneScatter.scratch(units, own, sizes[0])
        + PlaneScatter.scratch(units, own, sizes[1])
        + PlaneScatter.scratch(1, own // 2, width)
        + [DMA(LineReturn.SEMS)] * 3
        + [DMA((3,))] * 3,
    )


def grid_shards(
    tokens,
    cotangent,
    qkv_weight,
    out_weight,
    gate_up_weight,
    down_weight,
    gains,
    qkv_first,
    out_first,
    gate_up_first,
    down_first,
    gains_first,
    qkv_second,
    out_second,
    gate_up_second,
    down_second,
    gains_second,
):
    rows, width = tokens.shape[1:]
    heads_here = HEADS // 8
    width_here = heads_here * HEAD_DIM
    gain_columns = jnp.pad(gains.astype(LOW).T, ((0, 0), (0, 126)))
    all_tokens, grad_out, qkv_full, gate_up_full, down_full, out_full = fetch_all(
        tokens[0],
        cotangent[0],
        qkv_weight.astype(LOW),
        gain_columns,
        gate_up_weight.astype(LOW),
        down_weight.astype(LOW),
        out_weight.astype(LOW),
    )
    own_slot = lax.axis_index(RING)
    own_tokens = lax.dynamic_index_in_dim(all_tokens, own_slot, 0, keepdims=False)
    own_grad = lax.dynamic_index_in_dim(grad_out, own_slot, 0, keepdims=False)
    all_tokens, grad_out = all_tokens.reshape(-1, width), grad_out.reshape(-1, width)
    qkv_full = qkv_full.reshape(width, -1)
    gain_full = qkv_full[:, 3 * width_here : 3 * width_here + 2].T.astype(WIDE)
    qkv_full = qkv_full[:, : 3 * width_here]
    gate_up_full = gate_up_full.reshape(width, -1)
    down_full = down_full.reshape(width, -1)
    out_full = out_full.reshape(-1, width)
    seq_len = all_tokens.shape[0]

    unit_all, _ = rms_parts(all_tokens.astype(WIDE))
    normed_one = (unit_all * gain_full[0]).astype(LOW)
    projected = jnp.dot(normed_one, qkv_full, preferred_element_type=WIDE)
    cosines, sines = rope_tables(jnp.arange(seq_len, dtype=jnp.int32))
    by_heads = projected.reshape(seq_len, 3, heads_here, HEAD_DIM)
    query_heads = rotate(by_heads[:, 0], cosines, sines).astype(LOW)
    key_heads = rotate(by_heads[:, 1], cosines, sines).astype(LOW)
    value_heads = by_heads[:, 2].astype(LOW)
    out_heads, lse_all = attend_forward(query_heads, key_heads, value_heads)
    attended = out_heads.reshape(seq_len, width_here)
    branch = jnp.dot(attended, out_full, preferred_element_type=WIDE).astype(LOW)
    residual, normed_two = branch_sum(branch.reshape(8, rows, width), own_tokens, gain_full[1:])
    normed_two = normed_two.reshape(seq_len, width)
    gate_up = jnp.dot(normed_two, gate_up_full, preferred_element_type=WIDE)
    ff_here = gate_up.shape[1] // 2
    gate_vals = gate_up[:, :ff_here]
    up_vals = gate_up[:, ff_here:]
    sigmoid_gate = jax.nn.sigmoid(gate_vals)
    activated = (gate_vals * sigmoid_gate * up_vals).astype(LOW)
    mlp_out = lax.psum_scatter(
        lax.dot_general(activated, down_full, CONTRACT_LAST, preferred_element_type=WIDE).astype(
            LOW
        ),
        RING,
        scatter_dimension=0,
        tiled=True,
    ).astype(WIDE)
    block_own = (residual + mlp_out).astype(LOW)

    grad_act = jnp.dot(grad_out, down_full, preferred_element_type=WIDE)
    grad_gate = grad_act * up_vals * sigmoid_gate * (1.0 + gate_vals * (1.0 - sigmoid_gate))
    grad_up = grad_act * gate_vals * sigmoid_gate
    grad_gate_up = jnp.concatenate([grad_gate, grad_up], axis=1).astype(LOW)
    grad_normed_two = lax.dot_general(
        grad_gate_up, gate_up_full, CONTRACT_LAST, preferred_element_type=WIDE
    ).astype(LOW)
    gate_up_part = lax.dot_general(
        normed_two, grad_gate_up, CONTRACT_FIRST, preferred_element_type=WIDE
    ).astype(LOW)
    down_part = lax.dot_general(
        grad_out, activated, CONTRACT_FIRST, preferred_element_type=WIDE
    ).astype(LOW)
    own_rows = qkv_weight.shape[0]
    grad_residual, grad_branch, gate_up_half = middle_sum(
        grad_normed_two.reshape(8, rows, width),
        residual,
        own_grad,
        gain_full[1:],
        gate_up_part.reshape(32, own_rows, -1),
    )
    grad_branch = grad_branch.reshape(seq_len, width)
    out_part = lax.dot_general(
        attended, grad_branch, CONTRACT_FIRST, preferred_element_type=WIDE
    ).astype(LOW)
    grad_heads = (
        lax.dot_general(grad_branch, out_full, CONTRACT_LAST, preferred_element_type=WIDE)
        .astype(LOW)
        .reshape(seq_len, heads_here, HEAD_DIM)
    )
    grad_q_all, grad_k_all, grad_v_all = attend_backward(
        query_heads, key_heads, value_heads, grad_heads, lse_all
    )
    grad_projected = (
        jnp.stack(
            [
                unrotate(grad_q_all, cosines, sines),
                unrotate(grad_k_all, cosines, sines),
                grad_v_all,
            ],
            axis=1,
        )
        .reshape(seq_len, 3 * width_here)
        .astype(LOW)
    )
    grad_normed_one = lax.dot_general(
        grad_projected, qkv_full, CONTRACT_LAST, preferred_element_type=WIDE
    ).astype(LOW)
    qkv_part = lax.dot_general(
        normed_one, grad_projected, CONTRACT_FIRST, preferred_element_type=WIDE
    ).astype(LOW)
    input_grad, block_out, qkv_sum, gate_up_sum, down_sum, out_sum = last_sum(
        grad_normed_one.reshape(8, rows, width),
        own_tokens,
        grad_residual,
        gain_full[:1],
        block_own,
        gate_up_half,
        qkv_part.reshape(32, own_rows, -1),
        down_part.reshape(32, own_rows, -1),
        out_part.reshape(4, own_rows, -1),
    )
    qkv_sum, gate_up_sum, down_sum, out_sum = (
        total.astype(WIDE) for total in (qkv_sum, gate_up_sum, down_sum, out_sum)
    )
    gains_sum = jnp.stack(
        [
            jnp.sum(weight.astype(LOW).astype(WIDE) * total, axis=1)
            for weight, total in ((qkv_weight, qkv_sum), (gate_up_weight, gate_up_sum))
        ],
        axis=0,
    ) / gains.astype(LOW).astype(WIDE)
    wide_rate = 2.5 * D ** (-0.5)
    out_rate = 2.5 * max(D // 512, 1) ** (-0.5)
    down_rate = 2.5 * FF ** (-0.5)
    qkv_new = adam_step(qkv_weight, qkv_sum, qkv_first, qkv_second, wide_rate, WEIGHT_DECAY)
    out_new = adam_step(out_weight, out_sum, out_first, out_second, out_rate, WEIGHT_DECAY)
    gate_up_new = adam_step(
        gate_up_weight, gate_up_sum, gate_up_first, gate_up_second, wide_rate, WEIGHT_DECAY
    )
    down_new = adam_step(
        down_weight, down_sum, down_first, down_second, down_rate, WEIGHT_DECAY
    )
    gains_new = adam_step(gains, gains_sum, gains_first, gains_second, 0.5, 0.0)
    return (
        block_out[None],
        input_grad[None],
        qkv_new[0],
        out_new[0],
        gate_up_new[0],
        down_new[0],
        gains_new[0],
        qkv_new[1],
        out_new[1],
        gate_up_new[1],
        down_new[1],
        gains_new[1],
        qkv_new[2],
        out_new[2],
        gate_up_new[2],
        down_new[2],
        gains_new[2],
    )


def mapped(body, mesh, token_spec, row_spec, gain_spec):
    one_set = (row_spec, row_spec, row_spec, row_spec, gain_spec)
    return jax.shard_map(
        body,
        mesh=mesh,
        in_specs=(token_spec, token_spec) + one_set * 3,
        out_specs=(token_spec, token_spec) + one_set * 3,
        check_vma=False,
    )


def solution(mesh):
    if mesh.shape["seq"] == 8 and mesh.shape["dp"] == 4:
        grid_mesh = Mesh(mesh.devices.reshape(4, 2, 2, 2), GRID)
        return mapped(
            grid_shards,
            grid_mesh,
            P(("y", "c"), ("z", "x"), None),
            P(GRID, None),
            P(None, GRID),
        )
    return mapped(
        shards, mesh, P("dp", "seq", None), P(("seq", "dp"), None), P(None, ("seq", "dp"))
    )
```

```python
import jax
import jax.numpy as jnp
from jax import lax
from jax.experimental import pallas as pl
from jax.experimental.pallas import tpu as pltpu
from jax.sharding import Mesh
from jax.sharding import PartitionSpec as P

D = 2048
HEADS = 32
HEAD_DIM = 64
FF = 8192
BLOCK = 512
STEP = 10


NORM_EPS = 1e-05
ROPE_BASE = 130000.0
BETA_ONE = 0.9
BETA_TWO = 0.999
ADAM_EPS = 1e-08
WEIGHT_DECAY = 0.1
MASKED = -1e30


def rms_parts(values):
    inverse = lax.rsqrt(jnp.mean(values * values, axis=-1, keepdims=True) + NORM_EPS)
    return (values * inverse, inverse)


def rope_tables(positions):
    half_dim = HEAD_DIM // 2
    exponent = jnp.arange(half_dim, dtype=jnp.float32) * (2.0 / HEAD_DIM)
    frequency = ROPE_BASE ** (-exponent)
    angles = positions.astype(jnp.float32)[:, None] * frequency[None, :]
    return (jnp.cos(angles)[:, None, :], jnp.sin(angles)[:, None, :])


def rotate(tensor, cosines, sines):
    half_dim = HEAD_DIM // 2
    lower_half = tensor[..., :half_dim]
    upper_half = tensor[..., half_dim:]
    return jnp.concatenate(
        [lower_half * cosines - upper_half * sines, upper_half * cosines + lower_half * sines],
        axis=-1,
    )


def unrotate(tensor, cosines, sines):
    half_dim = HEAD_DIM // 2
    lower_half = tensor[..., :half_dim]
    upper_half = tensor[..., half_dim:]
    return jnp.concatenate(
        [lower_half * cosines + upper_half * sines, upper_half * cosines - lower_half * sines],
        axis=-1,
    )


def block_scores(query_rows, key_heads, key_id, block_id):
    key_rows = lax.dynamic_slice_in_dim(key_heads, key_id * BLOCK, BLOCK, 0)
    products = jnp.einsum(
        "qhd,khd->hqk", query_rows, key_rows, preferred_element_type=jnp.float32
    ) * HEAD_DIM ** (-0.5)
    local_ids = jnp.arange(BLOCK, dtype=jnp.int32)
    allowed = (key_id < block_id) | (local_ids[None, :] <= local_ids[:, None])
    return jnp.where(allowed[None], products, MASKED)


def row_normalizer(query_rows, key_heads, block_id):
    row_shape = (query_rows.shape[1], BLOCK, 1)

    def absorb(key_id, state):
        running_max, running_total = state
        scores = block_scores(query_rows, key_heads, key_id, block_id)
        new_max = jnp.maximum(running_max, jnp.max(scores, axis=-1, keepdims=True))
        running_total = running_total * jnp.exp(running_max - new_max) + jnp.sum(
            jnp.exp(scores - new_max), axis=-1, keepdims=True
        )
        return (new_max, running_total)

    start_state = (jnp.full(row_shape, MASKED, jnp.float32), jnp.zeros(row_shape, jnp.float32))
    final_max, final_total = lax.fori_loop(0, block_id + 1, absorb, start_state)
    return final_max + jnp.log(final_total)


def attend_forward(query_heads, key_heads, value_heads):
    seq_len, heads_here, head_dim = query_heads.shape

    def one_block(block_id, carry):
        out_all, lse_all = carry
        row_start = block_id * BLOCK
        query_rows = lax.dynamic_slice_in_dim(query_heads, row_start, BLOCK, 0)
        row_lse = row_normalizer(query_rows, key_heads, block_id)

        def weigh_values(key_id, running):
            scores = block_scores(query_rows, key_heads, key_id, block_id)
            weights_low = jnp.exp(scores - row_lse).astype(jnp.bfloat16)
            value_rows = lax.dynamic_slice_in_dim(value_heads, key_id * BLOCK, BLOCK, 0)
            return running + jnp.einsum(
                "hqk,khd->qhd", weights_low, value_rows, preferred_element_type=jnp.float32
            )

        attended = lax.fori_loop(
            0, block_id + 1, weigh_values, jnp.zeros((BLOCK, heads_here, head_dim), jnp.float32)
        )
        out_all = lax.dynamic_update_slice_in_dim(
            out_all, attended.astype(jnp.bfloat16), row_start, 0
        )
        lse_all = lax.dynamic_update_slice_in_dim(lse_all, row_lse, row_start, 1)
        return (out_all, lse_all)

    start_carry = (
        jnp.zeros((seq_len, heads_here, head_dim), jnp.bfloat16),
        jnp.zeros((heads_here, seq_len, 1), jnp.float32),
    )
    return lax.fori_loop(0, seq_len // BLOCK, one_block, start_carry)


def attend_backward(query_heads, key_heads, value_heads, grad_heads, lse_all):
    seq_len, heads_here, head_dim = query_heads.shape
    score_scale = HEAD_DIM ** (-0.5)

    def one_block(block_id, carry):
        grad_q_all, grad_k_all, grad_v_all = carry
        row_start = block_id * BLOCK
        query_rows = lax.dynamic_slice_in_dim(query_heads, row_start, BLOCK, 0)
        grad_rows = lax.dynamic_slice_in_dim(grad_heads, row_start, BLOCK, 0)
        row_lse = lax.dynamic_slice_in_dim(lse_all, row_start, BLOCK, 1)

        def probs_and_grads(key_id):
            scores = block_scores(query_rows, key_heads, key_id, block_id)
            probs = jnp.exp(scores - row_lse)
            value_rows = lax.dynamic_slice_in_dim(value_heads, key_id * BLOCK, BLOCK, 0)
            grad_probs = jnp.einsum(
                "qhd,khd->hqk", grad_rows, value_rows, preferred_element_type=jnp.float32
            )
            return (probs, grad_probs)

        def add_delta(key_id, running):
            probs, grad_probs = probs_and_grads(key_id)
            return running + jnp.sum(probs * grad_probs, axis=-1, keepdims=True)

        row_delta = lax.fori_loop(
            0, block_id + 1, add_delta, jnp.zeros((heads_here, BLOCK, 1), jnp.float32)
        )

        def spread(key_id, inner):
            grad_q_rows, grad_k_acc, grad_v_acc = inner
            probs, grad_probs = probs_and_grads(key_id)
            key_start = key_id * BLOCK
            key_rows = lax.dynamic_slice_in_dim(key_heads, key_start, BLOCK, 0)
            grad_scores = (probs * (grad_probs - row_delta) * score_scale).astype(jnp.bfloat16)
            grad_q_rows = grad_q_rows + jnp.einsum(
                "hqk,khd->qhd", grad_scores, key_rows, preferred_element_type=jnp.float32
            )
            grad_k_part = jnp.einsum(
                "hqk,qhd->khd", grad_scores, query_rows, preferred_element_type=jnp.float32
            )
            grad_v_part = jnp.einsum(
                "hqk,qhd->khd",
                probs.astype(jnp.bfloat16),
                grad_rows,
                preferred_element_type=jnp.float32,
            )
            grad_k_acc = lax.dynamic_update_slice_in_dim(
                grad_k_acc,
                lax.dynamic_slice_in_dim(grad_k_acc, key_start, BLOCK, 0) + grad_k_part,
                key_start,
                0,
            )
            grad_v_acc = lax.dynamic_update_slice_in_dim(
                grad_v_acc,
                lax.dynamic_slice_in_dim(grad_v_acc, key_start, BLOCK, 0) + grad_v_part,
                key_start,
                0,
            )
            return (grad_q_rows, grad_k_acc, grad_v_acc)

        start_inner = (
            jnp.zeros((BLOCK, heads_here, head_dim), jnp.float32),
            grad_k_all,
            grad_v_all,
        )
        grad_q_rows, grad_k_all, grad_v_all = lax.fori_loop(0, block_id + 1, spread, start_inner)
        grad_q_all = lax.dynamic_update_slice_in_dim(grad_q_all, grad_q_rows, row_start, 0)
        return (grad_q_all, grad_k_all, grad_v_all)

    zeros_all = jnp.zeros((seq_len, heads_here, head_dim), jnp.float32)
    return lax.fori_loop(0, seq_len // BLOCK, one_block, (zeros_all, zeros_all, zeros_all))


def adam_step(weight, gradient, first, second, rate, decay):
    new_first = BETA_ONE * first + (1.0 - BETA_ONE) * gradient
    new_second = BETA_TWO * second + (1.0 - BETA_TWO) * gradient * gradient
    first_hat = new_first / (1.0 - BETA_ONE**STEP)
    second_hat = new_second / (1.0 - BETA_TWO**STEP)
    new_weight = weight - rate * (first_hat / (jnp.sqrt(second_hat) + ADAM_EPS) + decay * weight)
    return (new_weight, new_first, new_second)


def shards(
    tokens,
    cotangent,
    qkv_weight,
    out_weight,
    gate_up_weight,
    down_weight,
    gains,
    qkv_first,
    out_first,
    gate_up_first,
    down_first,
    gains_first,
    qkv_second,
    out_second,
    gate_up_second,
    down_second,
    gains_second,
):
    seq_count = lax.axis_size("seq")
    tok_rows = tokens.shape[1]
    width = tokens.shape[2]
    seq_len = tok_rows * seq_count
    heads_here = HEADS // seq_count
    width_here = heads_here * HEAD_DIM
    contract_last = (((1,), (1,)), ((), ()))
    contract_first = (((0,), (0,)), ((), ()))
    qkv_full, proj_full, gain_full = (
        lax.all_gather(qkv_weight.astype(jnp.bfloat16), ("seq", "dp"), axis=0, tiled=True),
        lax.all_gather(out_weight.astype(jnp.bfloat16), ("seq", "dp"), axis=0, tiled=True),
        lax.all_gather(gains.astype(jnp.bfloat16), ("seq", "dp"), axis=1, tiled=True),
    )
    up_full, down_full = (
        lax.all_gather(gate_up_weight.astype(jnp.bfloat16), ("seq", "dp"), axis=0, tiled=True),
        lax.all_gather(down_weight.astype(jnp.bfloat16), ("seq", "dp"), axis=0, tiled=True),
    )
    hidden_in = tokens[0].astype(jnp.float32)
    unit_one, inverse_one = rms_parts(hidden_in)
    normed_one = (unit_one * gain_full[0].astype(jnp.float32)).astype(jnp.bfloat16)
    projected = jnp.einsum(
        "te,ecd->ctd",
        normed_one,
        qkv_full.reshape(width, 3, width),
        preferred_element_type=jnp.float32,
    )
    positions = lax.axis_index("seq") * tok_rows + jnp.arange(tok_rows, dtype=jnp.int32)
    cos_local, sin_local = rope_tables(positions)
    turned = rotate(projected[:2].reshape(2, tok_rows, HEADS, HEAD_DIM), cos_local, sin_local)
    packed = jnp.concatenate([turned.reshape(2, tok_rows, width), projected[2:]], axis=0).astype(
        jnp.bfloat16
    )
    by_heads = lax.all_to_all(packed, "seq", split_axis=2, concat_axis=1, tiled=True)
    query_heads = by_heads[0].reshape(seq_len, heads_here, HEAD_DIM)
    key_heads = by_heads[1].reshape(seq_len, heads_here, HEAD_DIM)
    value_heads = by_heads[2].reshape(seq_len, heads_here, HEAD_DIM)
    out_heads, lse_all = attend_forward(query_heads, key_heads, value_heads)
    attended = lax.all_to_all(
        out_heads.reshape(seq_len, width_here), "seq", split_axis=0, concat_axis=1, tiled=True
    )
    residual = hidden_in + jnp.dot(attended, proj_full, preferred_element_type=jnp.float32)
    unit_two, inverse_two = rms_parts(residual)
    normed_two = (unit_two * gain_full[1].astype(jnp.float32)).astype(jnp.bfloat16)
    gate_up = jnp.dot(normed_two, up_full, preferred_element_type=jnp.float32)
    gate_vals = gate_up[:, :FF]
    up_vals = gate_up[:, FF:]
    sigmoid_gate = jax.nn.sigmoid(gate_vals)
    activated = (gate_vals * sigmoid_gate * up_vals).astype(jnp.bfloat16)
    mlp_out = lax.dot_general(
        activated, down_full, contract_last, preferred_element_type=jnp.float32
    )
    block_out = (residual + mlp_out).astype(jnp.bfloat16)[None]
    back_up, back_down, back_gain = (
        lax.all_gather(gate_up_weight.astype(jnp.bfloat16), ("seq", "dp"), axis=0, tiled=True),
        lax.all_gather(down_weight.astype(jnp.bfloat16), ("seq", "dp"), axis=0, tiled=True),
        lax.all_gather(gains.astype(jnp.bfloat16), ("seq", "dp"), axis=1, tiled=True),
    )
    grad_out = cotangent[0]
    grad_act = jnp.dot(grad_out, back_down, preferred_element_type=jnp.float32)
    grad_gate = grad_act * up_vals * sigmoid_gate * (1.0 + gate_vals * (1.0 - sigmoid_gate))
    grad_up = grad_act * gate_vals * sigmoid_gate
    grad_gate_up = jnp.concatenate([grad_gate, grad_up], axis=1).astype(jnp.bfloat16)
    grad_normed_two = lax.dot_general(
        grad_gate_up, back_up, contract_last, preferred_element_type=jnp.float32
    )
    gain_two_grad = jnp.sum(grad_normed_two * unit_two, axis=0)
    grad_unit_two = grad_normed_two * back_gain[1].astype(jnp.float32)
    grad_residual = grad_out.astype(jnp.float32) + inverse_two * (
        grad_unit_two - unit_two * jnp.mean(grad_unit_two * unit_two, axis=-1, keepdims=True)
    )
    gate_up_rows = lax.dot_general(
        normed_two, grad_gate_up, contract_first, preferred_element_type=jnp.float32
    )
    down_rows = lax.dot_general(
        grad_out, activated, contract_first, preferred_element_type=jnp.float32
    )
    mlp_grad = lax.psum_scatter(
        jnp.concatenate([gate_up_rows, down_rows], axis=1),
        ("seq", "dp"),
        scatter_dimension=0,
        tiled=True,
    )
    back_qkv, back_proj = (
        lax.all_gather(qkv_weight.astype(jnp.bfloat16), ("seq", "dp"), axis=0, tiled=True),
        lax.all_gather(out_weight.astype(jnp.bfloat16), ("seq", "dp"), axis=0, tiled=True),
    )
    grad_branch = grad_residual.astype(jnp.bfloat16)
    proj_grad = lax.dot_general(
        attended, grad_branch, contract_first, preferred_element_type=jnp.float32
    )
    grad_attended = lax.dot_general(
        grad_branch, back_proj, contract_last, preferred_element_type=jnp.float32
    ).astype(jnp.bfloat16)
    grad_heads = lax.all_to_all(
        grad_attended, "seq", split_axis=1, concat_axis=0, tiled=True
    ).reshape(seq_len, heads_here, HEAD_DIM)
    grad_q_all, grad_k_all, grad_v_all = attend_backward(
        query_heads, key_heads, value_heads, grad_heads, lse_all
    )
    cos_whole, sin_whole = rope_tables(jnp.arange(seq_len, dtype=jnp.int32))
    grad_pack = jnp.stack(
        [
            unrotate(grad_q_all, cos_whole, sin_whole).reshape(seq_len, width_here),
            unrotate(grad_k_all, cos_whole, sin_whole).reshape(seq_len, width_here),
            grad_v_all.reshape(seq_len, width_here),
        ],
        axis=0,
    ).astype(jnp.bfloat16)
    grad_projected = lax.all_to_all(grad_pack, "seq", split_axis=1, concat_axis=2, tiled=True)
    qkv_cube = back_qkv.reshape(width, 3, width)
    grad_normed_one = jnp.einsum(
        "ctd,ecd->te", grad_projected, qkv_cube, preferred_element_type=jnp.float32
    )
    qkv_grad = jnp.einsum(
        "te,ctd->ecd", normed_one, grad_projected, preferred_element_type=jnp.float32
    ).reshape(width, 3 * width)
    gain_one_grad = jnp.sum(grad_normed_one * unit_one, axis=0)
    grad_unit_one = grad_normed_one * back_gain[0].astype(jnp.float32)
    input_grad = grad_residual + inverse_one * (
        grad_unit_one - unit_one * jnp.mean(grad_unit_one * unit_one, axis=-1, keepdims=True)
    )
    gains_grad = jnp.stack([gain_one_grad, gain_two_grad], axis=0)
    qkv_sum, proj_sum, gains_sum = (
        lax.psum_scatter(qkv_grad, ("seq", "dp"), scatter_dimension=0, tiled=True),
        lax.psum_scatter(proj_grad, ("seq", "dp"), scatter_dimension=0, tiled=True),
        lax.psum_scatter(gains_grad, ("seq", "dp"), scatter_dimension=1, tiled=True),
    )
    wide_rate = 2.5 * D ** (-0.5)
    out_rate = 2.5 * max(D // 512, 1) ** (-0.5)
    down_rate = 2.5 * FF ** (-0.5)
    qkv_new = adam_step(qkv_weight, qkv_sum, qkv_first, qkv_second, wide_rate, WEIGHT_DECAY)
    out_new = adam_step(out_weight, proj_sum, out_first, out_second, out_rate, WEIGHT_DECAY)
    gate_up_new = adam_step(
        gate_up_weight,
        mlp_grad[:, : 2 * FF],
        gate_up_first,
        gate_up_second,
        wide_rate,
        WEIGHT_DECAY,
    )
    down_new = adam_step(
        down_weight, mlp_grad[:, 2 * FF :], down_first, down_second, down_rate, WEIGHT_DECAY
    )
    gains_new = adam_step(gains, gains_sum, gains_first, gains_second, 0.5, 0.0)
    return (
        block_out,
        input_grad[None],
        qkv_new[0],
        out_new[0],
        gate_up_new[0],
        down_new[0],
        gains_new[0],
        qkv_new[1],
        out_new[1],
        gate_up_new[1],
        down_new[1],
        gains_new[1],
        qkv_new[2],
        out_new[2],
        gate_up_new[2],
        down_new[2],
        gains_new[2],
    )


GRID = ("z", "x", "y", "c")
RING = ("z", "c")
PLANE = ("x", "y")
LOW = jnp.bfloat16
WIDE = jnp.float32
CONTRACT_LAST = (((1,), (1,)), ((), ()))
CONTRACT_FIRST = (((0,), (0,)), ((), ()))
DMA = pltpu.SemaphoreType.DMA
ANYWHERE = pl.BlockSpec(memory_space=pl.ANY)
IN_VMEM = pl.BlockSpec(memory_space=pltpu.VMEM)


def remote(source, target, send, receive, **place):
    return pltpu.make_async_remote_copy(
        src_ref=source,
        dst_ref=target,
        send_sem=send,
        recv_sem=receive,
        device_id=place,
        device_id_type=pl.DeviceIdType.MESH,
    )


def lanes(start, size):
    return pl.ds(pl.multiple_of(start, 128), size)


class Place:
    def __init__(self):
        self.z, self.x, self.y, self.c = (lax.axis_index(name) for name in GRID)
        self.slot = 2 * self.z + self.c
        self.block_here = self.block(self.slot, self.x, self.y)

    def block(self, slot, x, y):
        return (((slot // 2) * 2 + x) * 2 + y) * 2 + lax.rem(slot, 2)

    def meet(self, plane):
        barrier = pltpu.get_barrier_semaphore()
        others = [
            {"z": slot // 2, "c": lax.rem(slot, 2)}
            for slot in (lax.rem(self.slot + step, 8) for step in range(1, 8))
        ]
        if plane:
            others += [{"x": 1 - self.x}, {"y": 1 - self.y}, {"x": 1 - self.x, "c": 1 - self.c}]
        for other in others:
            pl.semaphore_signal(
                barrier, inc=1, device_id=other, device_id_type=pl.DeviceIdType.MESH
            )
        pl.semaphore_wait(barrier, len(others))


class Swap:
    def __init__(self, place, source, spot_there, spot_here, sems):
        p = self.place = place
        self.away = lambda: remote(
            source, spot_there, sems.at[0], sems.at[1], x=1 - p.x, c=1 - p.c
        )
        self.here = lambda: pltpu.make_async_copy(source, spot_here, sems.at[2])

    def start(self):
        p = self.place
        pl.when(p.x != p.c)(lambda: self.away().start())
        pl.when(p.x == p.c)(lambda: self.here().start())

    def wait(self):
        p = self.place
        pl.when(p.x != p.c)(lambda: self.away().wait_recv())
        pl.when(p.x == p.c)(lambda: self.here().wait())

    def drain(self):
        p = self.place
        pl.when(p.x != p.c)(lambda: self.away().wait_send())


class LineGather:
    SEMS = (4, 8)

    def __init__(self, place, buffer, sems, mine=None, rows=None):
        self.place, self.sems, self.mine = place, sems, mine
        self.spot = (lambda slot: buffer.at[slot]) if rows is None else (lambda slot: buffer.at[slot, rows])

    def copy(self, slot, way, own=False):
        p, block = self.place, self.spot(slot)
        if way == 0:
            where = {"z": jnp.minimum(p.z + 1, 3)}
        elif way == 1:
            where = {"z": jnp.maximum(p.z - 1, 0)}
        else:
            where = {"c": 1 - p.c}
        source = self.mine if own and self.mine is not None else block
        return remote(source, block, self.sems.at[way, slot], self.sems.at[3, slot], **where)

    def _pass_on(self, slot, way, own=False):
        p = self.place
        if way == 0:
            pl.when(p.z < 3)(lambda: self.copy(slot, 0, own).start())
        elif way == 1:
            pl.when(p.z > 0)(lambda: self.copy(slot, 1, own).start())

    def start(self):
        slot = self.place.slot
        self._pass_on(slot, 0, True)
        self._pass_on(slot, 1, True)
        self.copy(slot, 2, True).start()
        if self.mine is not None:
            self.keep().start()

    def keep(self):
        slot = self.place.slot
        return pltpu.make_async_copy(self.mine, self.spot(slot), self.sems.at[3, slot])

    def step(self, distance):
        p = self.place

        @pl.when(p.z + distance <= 3)
        def _():
            slot = p.slot + 2 * distance
            self.copy(slot, 2).wait_recv()
            self._pass_on(slot, 1)
            self.copy(slot, 2).start()

        @pl.when(p.z >= distance)
        def _():
            slot = p.slot - 2 * distance
            self.copy(slot, 2).wait_recv()
            self._pass_on(slot, 0)
            self.copy(slot, 2).start()

    def finish(self):
        p = self.place
        if self.mine is not None:
            self.keep().wait()
        for z in range(4):
            self.copy(2 * z + 1 - p.c, 2).wait_recv()

    def drain(self):
        p = self.place
        for z in range(4):
            slot = 2 * z + p.c
            self.copy(slot, 2).wait_send()
            pl.when((z <= p.z) & (p.z < 3))(lambda: self.copy(slot, 0).wait_send())
            pl.when((z >= p.z) & (p.z > 0))(lambda: self.copy(slot, 1).wait_send())


def add_blocks(target, sources):
    def some(step, carry):
        rows = pl.ds(pl.multiple_of(step * 16, 16), 16)
        total = sources[0][rows, :].astype(WIDE)
        for source in sources[1:]:
            total = total + source[rows, :].astype(WIDE)
        target[rows, :] = total.astype(target.dtype)
        return carry

    lax.fori_loop(0, target.shape[0] // 16, some, 0)


class LineScatter:
    SEMS = (6, 4)

    @staticmethod
    def buffers(rows, width):
        return [pltpu.VMEM((4, rows, width), LOW) for _ in range(5)]

    def __init__(self, place, partial, across, below, above, stage_up, stage_down, sems, rows):
        self.place, self.partial, self.sems, self.rows = place, partial, sems, rows
        self.across, self.below, self.above = across, below, above
        self.stages = (stage_up, stage_down)

    def cross(self, z):
        p = self.place
        return remote(
            self.partial.at[2 * z + 1 - p.c, self.rows],
            self.across.at[z, self.rows],
            self.sems.at[0, z],
            self.sems.at[1, z],
            c=1 - p.c,
        )

    def hop(self, z, way):
        p = self.place
        target = (self.below, self.above)[way]
        there = jnp.minimum(p.z + 1, 3) if way == 0 else jnp.maximum(p.z - 1, 0)
        return remote(
            self.stages[way].at[z, self.rows],
            target.at[z, self.rows],
            self.sems.at[2 + 2 * way, z],
            self.sems.at[3 + 2 * way, z],
            z=there,
        )

    def start(self):
        for z in range(4):
            self.cross(z).start()

    def head(self):
        p = self.place
        for z in range(4):
            self.cross(z).wait_recv()
        for way, end in ((0, 0), (1, 3)):

            @pl.when(p.z == end)
            def _():
                for index in range(3):
                    z = 3 - index if way == 0 else index
                    add_blocks(
                        self.stages[way].at[z, self.rows],
                        [self.partial.at[2 * z + p.c, self.rows], self.across.at[z, self.rows]],
                    )
                    self.hop(z, way).start()

    def step(self, index):
        p = self.place
        for way, z in ((0, 3 - index), (1, index)):
            inside = (p.z < z) & (p.z > 0) if way == 0 else (p.z > z) & (p.z < 3)
            passing = (self.below, self.above)[way]

            @pl.when(inside)
            def _():
                self.hop(z, way).wait_recv()
                add_blocks(
                    self.stages[way].at[z, self.rows],
                    [
                        self.partial.at[2 * z + p.c, self.rows],
                        self.across.at[z, self.rows],
                        passing.at[z, self.rows],
                    ],
                )
                self.hop(z, way).start()

    def arrive(self):
        p = self.place
        pl.when(p.z > 0)(lambda: self.hop(p.z, 0).wait_recv())
        pl.when(p.z < 3)(lambda: self.hop(p.z, 1).wait_recv())

        @pl.when(p.z == 0)
        def _():
            spot = self.below.at[0, self.rows]
            spot[...] = jnp.zeros(spot.shape, LOW)

        @pl.when(p.z == 3)
        def _():
            spot = self.above.at[3, self.rows]
            spot[...] = jnp.zeros(spot.shape, LOW)

    def total(self, rows):
        p = self.place
        parts = (
            self.partial[p.slot, rows, :],
            self.across[p.z, rows, :],
            self.below[p.z, rows, :],
            self.above[p.z, rows, :],
        )
        return sum(part.astype(WIDE) for part in parts)

    def drain(self):
        p = self.place
        for z in range(4):
            self.cross(z).wait_send()
            pl.when(p.z < z)(lambda: self.hop(z, 0).wait_send())
            pl.when(p.z > z)(lambda: self.hop(z, 1).wait_send())


class Relayout:
    SEMS = (8, 8)

    def __init__(self, place, parts, target, sems):
        self.place, self.parts, self.target, self.sems = place, parts, target, sems

    def sem(self, kind, slot):
        return self.sems.at[kind, slot]

    def line(self, step):
        p = self.place
        slot = lax.rem(p.slot + step, 8)
        copies = []
        for source, first, size, there in self.parts:
            same_for_all = source.shape[1] == size
            columns = lanes(first if same_for_all else first + size * slot, size)
            piece = source.at[:, columns]
            spot = self.target.at[p.block_here, :, pl.ds(there, size)]
            if step == 0:
                copies.append(pltpu.make_async_copy(piece, spot, self.sem(1, p.slot)))
            else:
                copies.append(
                    remote(
                        piece,
                        spot,
                        self.sem(0, slot),
                        self.sem(1, p.slot),
                        z=slot // 2,
                        c=lax.rem(slot, 2),
                    )
                )
        return copies

    def whole(self, slot):
        p = self.place
        spot = self.target.at[p.block(slot, p.x, p.y)]
        return remote(spot, spot, self.sem(0, slot), self.sem(1, slot), c=1 - p.c)

    def plane(self, slot, x, y, way, send, receive):
        p = self.place
        spot = self.target.at[p.block(slot, x, y)]
        where = {"x": 1 - p.x} if way == 0 else {"y": 1 - p.y}
        return remote(spot, spot, self.sem(send, slot), self.sem(receive, slot), **where)

    def from_own(self, slot, way):
        p = self.place
        return self.plane(slot, p.x, p.y, way, 2 + 2 * way, 3 + 2 * way)

    def corner(self, slot, way):
        p = self.place
        x, y = (p.x, 1 - p.y) if way == 0 else (1 - p.x, p.y)
        return self.plane(slot, x, y, way, 6, 7)

    def start(self):
        for step in range(8):
            for copy in self.line(step):
                copy.start()

    def spread(self, step):
        p = self.place
        slot = lax.rem(p.slot + 8 - step, 8)
        if isinstance(step, int) and step == 0:
            spot = self.target.at[p.block_here]
            pltpu.make_async_copy(spot, spot, self.sem(1, p.slot)).wait()
        else:
            self.whole(slot).wait_recv()
        for way in range(2):
            self.from_own(slot, way).start()

    def corners(self, z):
        self.from_own(2 * z, 0).wait_recv()
        self.corner(2 * z, 1).start()
        self.from_own(2 * z + 1, 1).wait_recv()
        self.corner(2 * z + 1, 0).start()

    def finish(self):
        for z in range(4):
            self.from_own(2 * z, 1).wait_recv()
            self.from_own(2 * z + 1, 0).wait_recv()
            self.corner(2 * z, 1).wait_recv()
            self.corner(2 * z + 1, 0).wait_recv()

    def drain(self):
        for step in range(1, 8):
            self.whole(lax.rem(self.place.slot + step, 8)).wait_send()
        for z in range(4):
            self.corner(2 * z, 1).wait_send()
            self.corner(2 * z + 1, 0).wait_send()
        for slot in range(8):
            for way in range(2):
                self.from_own(slot, way).wait_send()


class PlaneScatter:
    @staticmethod
    def scratch(units, rows, width):
        shape = (rows, width)
        return [
            pltpu.VMEM((2, 2, units) + shape, LOW),
            pltpu.VMEM((2, 2, units) + shape, LOW),
            pltpu.VMEM((2, units) + shape, LOW),
            pltpu.VMEM((2, units) + shape, LOW),
            DMA((5, 2, 2, units)),
        ]

    def __init__(self, place, part, units, sums, held, got, stage, last, sems):
        self.place, self.part, self.units, self.sums = place, part, units, sums
        self.held, self.got, self.stage, self.last = held, got, stage, last
        self.sems = sems

    def pair(self, near):
        p = self.place
        x, y = (p.x, p.y) if near else (1 - p.x, 1 - p.y)
        return ((p.x, y), (x, p.y))

    def load(self, half, near, unit):
        x, y = self.pair(near)[half]
        return pltpu.make_async_copy(
            self.part(half, unit, x, y),
            self.held.at[half, near, unit],
            self.sems.at[0, half, near, unit],
        )

    def first(self, half, near, unit):
        p = self.place
        x, y = self.pair(near)[half]
        x, y = (1 - x, y) if half == 0 else (x, 1 - y)
        where = {"x": 1 - p.x} if half == 0 else {"y": 1 - p.y}
        return remote(
            self.part(half, unit, x, y),
            self.got.at[half, near, unit],
            self.sems.at[1, half, near, unit],
            self.sems.at[2, half, near, unit],
            **where,
        )

    def second(self, half, unit):
        p = self.place
        where = {"y": 1 - p.y} if half == 0 else {"x": 1 - p.x}
        return remote(
            self.stage.at[half, unit],
            self.last.at[half, unit],
            self.sems.at[3, half, 0, unit],
            self.sems.at[4, half, 0, unit],
            **where,
        )

    def each(self, call):
        lax.fori_loop(0, self.units, lambda unit, carry: (call(unit), carry)[1], 0)

    def start(self):
        for near in range(2):

            def begin(unit):
                for half in range(2):
                    self.first(half, near, unit).start()
                    self.load(half, near, unit).start()

            self.each(begin)

    def middle(self, unit):
        for half in range(2):
            self.load(half, 0, unit).wait()
            self.first(half, 0, unit).wait_recv()
            add_blocks(
                self.stage.at[half, unit], [self.held.at[half, 0, unit], self.got.at[half, 0, unit]]
            )
            self.second(half, unit).start()

    def final(self, unit):
        for half in range(2):
            self.load(half, 1, unit).wait()
            self.first(half, 1, unit).wait_recv()
            self.second(half, unit).wait_recv()
            add_blocks(
                self.sums(half, unit),
                [
                    self.held.at[half, 1, unit],
                    self.got.at[half, 1, unit],
                    self.last.at[half, unit],
                ],
            )

    def drain(self):
        def end(unit):
            for half in range(2):
                for near in range(2):
                    self.first(half, near, unit).wait_send()
                self.second(half, unit).wait_send()

        self.each(end)


class LineReturn:
    SEMS = (2, 8)

    def __init__(self, place, sums, parts, target, sems):
        self.place, self.sums, self.parts = place, sums, parts
        self.target, self.sems = target, sems

    def copies(self, z, c, local):
        p = self.place
        made = []
        for here, size, first in self.parts:
            piece = self.sums.at[z, c, :, pl.ds(here, size)]
            spot = self.target.at[:, lanes(first + size * p.slot, size)]
            if local:
                made.append(pltpu.make_async_copy(piece, spot, self.sems.at[1, p.slot]))
            else:
                made.append(
                    remote(
                        piece, spot, self.sems.at[0, 2 * z + c], self.sems.at[1, p.slot], z=z, c=c
                    )
                )
        return made

    def send(self, z):
        p = self.place
        for c in range(2):
            mine = (z == p.z) & (c == p.c)

            @pl.when(mine)
            def _():
                for copy in self.copies(z, c, True):
                    copy.start()

            @pl.when(jnp.logical_not(mine))
            def _():
                for copy in self.copies(z, c, False):
                    copy.start()

    def finish(self):
        p = self.place
        spot = self.sums.at[0, 0]
        pltpu.make_async_copy(spot, spot, self.sems.at[1, p.slot]).wait()
        for step in range(1, 8):
            slot = lax.rem(p.slot + step, 8)
            whole = remote(
                spot, spot, self.sems.at[0, slot], self.sems.at[1, slot], c=1 - p.c
            )
            whole.wait_recv()
            whole.wait_send()


def kernel_call(kernel, name, number, inputs, in_specs, outputs, out_specs, scratch):
    return pl.pallas_call(
        kernel,
        out_shape=[jax.ShapeDtypeStruct(shape, dtype) for shape, dtype in outputs],
        in_specs=in_specs,
        out_specs=out_specs,
        scratch_shapes=scratch,
        compiler_params=pltpu.CompilerParams(
            collective_id=number, has_side_effects=True, vmem_limit_bytes=56 * 2**20
        ),
        name=name,
    )(*inputs)


CHUNK = 16


def by_rows(count, call):
    def some(step, carry):
        call(pl.ds(pl.multiple_of(step * CHUNK, CHUNK), CHUNK))
        return carry

    lax.fori_loop(0, count // CHUNK, some, 0)


def normed_back(grad_normed, unit, inverse, gain):
    grad_unit = grad_normed * gain
    return inverse * (grad_unit - unit * jnp.mean(grad_unit * unit, axis=-1, keepdims=True))


def turn(values, cosines, sines):
    lane = lax.broadcasted_iota(jnp.int32, values.shape, 1)
    half_dim = HEAD_DIM // 2
    width = values.shape[1]
    partner = jnp.where(
        lax.rem(lane, HEAD_DIM) < half_dim,
        pltpu.roll(values, width - half_dim, 1),
        pltpu.roll(values, half_dim, 1),
    )
    return values * cosines + partner * sines


def head_mask(head):
    lane = lax.broadcasted_iota(jnp.int32, (1, 128), 1)
    return (lane // HEAD_DIM == lax.rem(head, 2)).astype(WIDE).astype(LOW)


def scaled_probs(queries, keys, first_row):
    scores = lax.dot_general(queries, keys, CONTRACT_LAST, preferred_element_type=WIDE)
    scores = scores * HEAD_DIM ** (-0.5)
    row = lax.broadcasted_iota(jnp.int32, scores.shape, 0) + first_row
    column = lax.broadcasted_iota(jnp.int32, scores.shape, 1)
    scores = jnp.where(column <= row, scores, MASKED)
    expo = jnp.exp(scores - jnp.max(scores, axis=1, keepdims=True))
    return expo * (1.0 / jnp.sum(expo, axis=1, keepdims=True))


QUERY_ROWS = 256


def attend_head(head, qkv, total):
    pair = lanes(head // 2 * 128, 128)
    mask = head_mask(head)
    for block in range(qkv.shape[1] // QUERY_ROWS):
        rows = pl.ds(block * QUERY_ROWS, QUERY_ROWS)
        keys = pl.ds(0, (block + 1) * QUERY_ROWS)
        probs = scaled_probs(qkv[0, rows, pair] * mask, qkv[1, keys, pair], block * QUERY_ROWS)
        total[rows, pair] += jnp.dot(
            probs.astype(LOW), qkv[2, keys, pair] * mask, preferred_element_type=WIDE
        )


def forward_kernel(
    tok,
    cot,
    wq,
    gain,
    wg,
    wd,
    wo,
    cosines,
    sines,
    all_cot,
    normed_two,
    full_g,
    full_d,
    out_q,
    out_o,
    out_normed,
    out_qkv,
    out_attended,
    out_residual,
    out_gains,
    out_tok,
    all_tok,
    full_q,
    full_o,
    normed_one,
    qkv,
    heads,
    attended,
    residual,
    gain_rows,
    mine,
    partial,
    *scratch,
):
    buffers, sems = scratch[:5], scratch[5:]
    tok_swap, cot_swap, out_swap, tok_sems, cot_sems, q_sems, g_sems, d_sems = sems[:8]
    o_sems, sum_a, sum_b, gather_a, gather_b, keep_sems = sems[8:]
    p = Place()
    p.meet(True)
    rows_own = tok.shape[0]
    seq_len = 8 * rows_own
    step_q, step_g, step_d = wq.shape[1] // 24, wg.shape[1] // 16, wd.shape[1] // 8
    q_parts = [(wq, i * 8 * step_q, step_q, i * step_q) for i in range(3)]
    q_parts.append((gain, 0, gain.shape[1], 3 * step_q))
    move_q = Relayout(p, q_parts, full_q, q_sems)
    move_g = Relayout(
        p, [(wg, i * 8 * step_g, step_g, i * step_g) for i in range(2)], full_g, g_sems
    )
    move_d = Relayout(p, [(wd, 0, step_d, 0)], full_d, d_sems)
    tokens, cotangents = LineGather(p, all_tok, tok_sems), LineGather(p, all_cot, cot_sems)
    away = 2 * p.z + 1 - p.c
    swap_tok = Swap(p, tok, all_tok.at[away], all_tok.at[p.slot], tok_swap)
    swap_cot = Swap(p, cot, all_cot.at[away], all_cot.at[p.slot], cot_swap)
    swap_out = Swap(p, wo, full_o.at[2 * p.y + 1 - p.x], full_o.at[2 * p.y + p.x], out_swap)
    half = wo.shape[0] // 2

    def out_copy(kind):
        own, beside, above = 2 * p.y + p.x, 2 * p.y + 1 - p.x, 2 * (1 - p.y) + p.x
        send, got = o_sems.at[0, kind], o_sems.at[1, kind]
        if kind < 2:
            where = {"x": 1 - p.x} if kind == 0 else {"y": 1 - p.y}
            return remote(full_o.at[own], full_o.at[own], send, got, **where)
        spot = full_o.at[beside if kind == 2 else above, pl.ds((kind - 2) * half, half)]
        where = {"y": 1 - p.y} if kind == 2 else {"x": 1 - p.x}
        return remote(spot, spot, send, got, **where)

    kept = []

    def keep(source, target):
        copy = pltpu.make_async_copy(source, target, keep_sems.at[len(kept)])
        copy.start()
        kept.append(copy)

    swap_tok.start()
    move_q.start()
    swap_out.start()
    swap_tok.wait()
    tokens.start()
    swap_cot.start()
    for step in range(8):
        move_q.spread(step)
    tokens.step(1)
    swap_out.wait()
    out_copy(0).start()
    out_copy(1).start()
    tokens.step(2)
    move_g.start()
    for z in range(4):
        move_q.corners(z)
    tokens.step(3)
    out_copy(0).wait_recv()
    out_copy(2).start()
    out_copy(1).wait_recv()
    out_copy(3).start()
    move_q.finish()
    columns = full_q.shape[2]
    gain_block = full_q[:, :, pl.ds(3 * step_q, columns - 3 * step_q)].reshape(-1, 128)
    pick = lax.broadcasted_iota(jnp.int32, (8, 128), 0) == lax.broadcasted_iota(
        jnp.int32, (8, 128), 1
    )
    gain_rows[...] = lax.dot_general(
        pick.astype(WIDE).astype(LOW), gain_block, CONTRACT_LAST, preferred_element_type=WIDE
    )
    keep(full_q, out_q)
    keep(gain_rows, out_gains)
    tokens.finish()
    keep(all_tok.at[p.slot], out_tok)

    def norm_slot(slot, carry):
        def some(rows):
            unit, _ = rms_parts(all_tok[slot, rows, :].astype(WIDE))
            there = pl.ds(pl.multiple_of(slot * rows_own + rows.start, CHUNK), CHUNK)
            normed_one[there, :] = (unit * gain_rows[pl.ds(0, 1), :]).astype(LOW)

        by_rows(rows_own, some)
        return carry

    lax.fori_loop(0, 8, norm_slot, 0)
    keep(normed_one, out_normed)
    move_g.spread(0)

    def project(part, carry):
        rows = pl.ds(pl.multiple_of(part * 512, 512), 512)
        for kind in range(3):
            weight = full_q[:, :, pl.ds(kind * step_q, step_q)].reshape(-1, step_q)
            made = jnp.dot(normed_one[rows, :], weight, preferred_element_type=WIDE)
            if kind < 2:
                made = turn(
                    made,
                    jnp.concatenate([cosines[rows, :]] * 2, axis=1),
                    jnp.concatenate([sines[rows, :]] * 2, axis=1),
                )
            qkv[kind, rows, :] = made.astype(LOW)
        return carry

    lax.fori_loop(0, seq_len // 512, project, 0)
    keep(qkv, out_qkv)
    heads[...] = jnp.zeros_like(heads)

    def one_head(head, carry):
        attend_head(head, qkv, heads)
        return carry

    lax.fori_loop(0, 4, one_head, 0)
    attended[...] = heads[...].astype(LOW)
    keep(attended, out_attended)
    out_copy(2).wait_recv()
    out_copy(3).wait_recv()
    keep(full_o, out_o)
    out_weight = lambda: full_o[...].reshape(-1, full_o.shape[2])

    def project_out(part, carry):
        rows = pl.ds(pl.multiple_of(part * 256, 256), 256)
        made = jnp.dot(attended[rows, :], out_weight(), preferred_element_type=WIDE)
        partial[pl.ds(2 * part, 2)] = made.astype(LOW).reshape(2, rows_own, -1)
        return carry

    lax.fori_loop(0, seq_len // 256, project_out, 0)

    part_rows = [pl.ds(0, rows_own // 2), pl.ds(rows_own // 2, rows_own // 2)]
    sums = [
        LineScatter(p, partial, *buffers, sem, rows) for sem, rows in zip((sum_a, sum_b), part_rows)
    ]
    gathers = [
        LineGather(p, normed_two, sem, mine.at[rows], rows)
        for sem, rows in zip((gather_a, gather_b), part_rows)
    ]

    def local(part):
        def some(rows):
            there = pl.ds(pl.multiple_of(part * (rows_own // 2) + rows.start, CHUNK), CHUNK)
            total = all_tok[p.slot, there, :].astype(WIDE) + sums[part].total(there)
            residual[there, :] = total
            unit, _ = rms_parts(total)
            mine[there, :] = (unit * gain_rows[pl.ds(1, 1), :]).astype(LOW)

        by_rows(rows_own // 2, some)

    for part in sums:
        part.start()
    for part in sums:
        part.head()
    move_d.start()
    for index in range(3):
        sums[0].step(index)
    for step in range(1, 4):
        move_g.spread(step)
    sums[0].arrive()
    local(0)
    gathers[0].start()
    swap_cot.wait()
    cotangents.start()
    for index in range(3):
        sums[1].step(index)
        gathers[0].step(index + 1)
    for step in range(4, 8):
        move_g.spread(step)
    sums[1].arrive()
    local(1)
    gathers[1].start()
    keep(residual, out_residual)
    for z in range(4):
        move_g.corners(z)
    for step in range(4):
        move_d.spread(step)
    for distance in range(1, 4):
        gathers[1].step(distance)
        cotangents.step(distance)
    for step in range(4, 8):
        move_d.spread(step)
    for z in range(4):
        move_d.corners(z)
    for kind in range(4):
        out_copy(kind).wait_send()
    for part in (swap_tok, swap_cot, swap_out):
        part.drain()
    for part in gathers + [cotangents, move_g, move_d]:
        part.finish()
    for part in gathers + sums + [tokens, cotangents, move_q, move_g, move_d]:
        part.drain()
    for copy in kept:
        copy.wait()


def forward(tokens, cotangent, qkv, gain_columns, gate_up, down, out_rows, cosines, sines):
    rows, width = tokens.shape
    own = qkv.shape[0]
    here = qkv.shape[1] // 24
    q_shape = (32, own, 3 * here + gain_columns.shape[1])
    vmem = lambda shape, dtype=LOW: pltpu.VMEM(shape, dtype)
    outputs = [
        ((8, rows, width), LOW),
        ((8, rows, width), LOW),
        ((32, own, gate_up.shape[1] // 8), LOW),
        ((32, own, down.shape[1] // 8), LOW),
        (q_shape, LOW),
        ((4, own, width), LOW),
        ((8 * rows, width), LOW),
        ((3, 8 * rows, here), LOW),
        ((8 * rows, here), LOW),
        ((rows, width), WIDE),
        ((8, width), WIDE),
        ((rows, width), LOW),
    ]
    return kernel_call(
        forward_kernel,
        "forward",
        1,
        (tokens, cotangent, qkv, gain_columns, gate_up, down, out_rows, cosines, sines),
        [ANYWHERE] * 7 + [IN_VMEM] * 2,
        outputs,
        [ANYWHERE] * len(outputs),
        [
            vmem((8, rows, width)),
            vmem(q_shape),
            vmem((4, own, width)),
            vmem((8 * rows, width)),
            vmem((3, 8 * rows, here)),
            vmem((8 * rows, here), WIDE),
            vmem((8 * rows, here)),
            vmem((rows, width), WIDE),
            vmem((8, width), WIDE),
            vmem((rows, width)),
            vmem((8, rows, width)),
        ]
        + LineScatter.buffers(rows, width)
        + [DMA((3,))] * 3
        + [DMA(LineGather.SEMS)] * 2
        + [DMA(Relayout.SEMS)] * 3
        + [DMA((2, 4))]
        + [DMA(LineScatter.SEMS)] * 2
        + [DMA(LineGather.SEMS)] * 2
        + [DMA((8,))],
    )


def weight_part(place, ref):
    return lambda half, unit, x, y: ref.at[place.block(2 * unit + half, x, y)]


def middle_kernel(
    partial, residual, grad_out, gain, wide_grad, grad_residual, branch, wide_sum, mine, *scratch
):
    p = Place()
    p.meet(True)
    line = LineScatter(p, partial, *scratch[:6], pl.ds(0, partial.shape[1]))
    gather = LineGather(p, branch, scratch[6], mine)
    units = wide_grad.shape[0] // 8
    plane = PlaneScatter(
        p, weight_part(p, wide_grad), units, lambda h, u: wide_sum.at[u, h], *scratch[7:]
    )
    line.start()
    plane.start()
    line.head()
    line.step(0)
    plane.middle(0)
    plane.middle(1)
    line.step(1)
    plane.middle(2)
    plane.middle(3)
    line.step(2)
    line.arrive()

    def local(rows):
        unit, inverse = rms_parts(residual[rows, :])
        total = grad_out[rows, :].astype(WIDE) + normed_back(
            line.total(rows), unit, inverse, gain[...]
        )
        grad_residual[rows, :] = total
        mine[rows, :] = total.astype(LOW)

    by_rows(residual.shape[0], local)
    gather.start()
    for distance in range(1, 4):
        gather.step(distance)
    plane.each(plane.final)
    gather.finish()
    line.drain()
    gather.drain()
    plane.drain()


def middle_sum(partial, residual, grad_out, gain, wide_grad):
    _, rows, width = partial.shape
    units, own, columns = wide_grad.shape[0] // 8, wide_grad.shape[1], wide_grad.shape[2]
    return kernel_call(
        middle_kernel,
        "middle_sum",
        3,
        (partial, residual, grad_out, gain, wide_grad),
        [IN_VMEM] * 4 + [ANYWHERE],
        [
            ((rows, width), WIDE),
            ((8, rows, width), LOW),
            ((units, 2, own, columns), LOW),
        ],
        [IN_VMEM, ANYWHERE, IN_VMEM],
        [pltpu.VMEM((rows, width), LOW)]
        + LineScatter.buffers(rows, width)
        + [DMA(LineScatter.SEMS)]
        + [DMA(LineGather.SEMS)]
        + PlaneScatter.scratch(units, own, columns),
    )


def last_kernel(
    partial,
    tokens,
    grad_residual,
    gain,
    block,
    wide_sum,
    q_grad,
    d_grad,
    o_grad,
    input_grad,
    block_out,
    q_out,
    g_out,
    d_out,
    o_out,
    mine,
    q_sum,
    d_sum,
    o_sum,
    *scratch,
):
    p = Place()
    p.meet(True)
    line = LineScatter(p, partial, *scratch[:6], pl.ds(0, partial.shape[1]))
    rest = scratch[6:]
    units = q_grad.shape[0] // 8
    half = o_grad.shape[1] // 2
    planes = [
        PlaneScatter(
            p, weight_part(p, q_grad), units, lambda h, u: q_sum.at[u, h], *rest[:5]
        ),
        PlaneScatter(
            p, weight_part(p, d_grad), units, lambda h, u: d_sum.at[u, h], *rest[5:10]
        ),
        PlaneScatter(
            p,
            lambda h, u, x, y: o_grad.at[2 * y + x, pl.ds(h * half, half)],
            1,
            lambda h, u: o_sum.at[pl.ds(h * half, half)],
            *rest[10:15],
        ),
    ]
    q_sems, g_sems, d_sems, out_swap, in_swap, block_swap = rest[15:]
    step_q, step_g, step_d = q_grad.shape[2] // 3, wide_sum.shape[3] // 2, d_grad.shape[2]
    returns = [
        LineReturn(p, q_sum, [(i * step_q, step_q, i * 8 * step_q) for i in range(3)], q_out, q_sems),
        LineReturn(
            p, wide_sum, [(i * step_g, step_g, i * 8 * step_g) for i in range(2)], g_out, g_sems
        ),
        LineReturn(p, d_sum, [(0, step_d, 0)], d_out, d_sems),
    ]
    swaps = [
        Swap(p, mine, input_grad, input_grad, in_swap),
        Swap(p, block, block_out, block_out, block_swap),
        Swap(p, o_sum, o_out, o_out, out_swap),
    ]
    line.start()
    for plane in planes:
        plane.start()
    for z in range(4):
        returns[1].send(z)
    swaps[1].start()
    line.head()
    line.step(0)
    planes[0].each(planes[0].middle)
    line.step(1)
    planes[1].each(planes[1].middle)
    planes[2].each(planes[2].middle)
    line.step(2)
    line.arrive()

    def local(rows):
        unit, inverse = rms_parts(tokens[rows, :].astype(WIDE))
        mine[rows, :] = grad_residual[rows, :] + normed_back(
            line.total(rows), unit, inverse, gain[...]
        )

    by_rows(tokens.shape[0], local)
    swaps[0].start()
    for z in range(4):
        planes[0].final(z)
        returns[0].send(z)
    for z in range(4):
        planes[1].final(z)
        returns[2].send(z)
    planes[2].final(0)
    swaps[2].start()
    for part in returns:
        part.finish()
    for part in swaps:
        part.wait()
        part.drain()
    line.drain()
    for part in planes:
        part.drain()


def last_sum(partial, tokens, grad_residual, gain, block, wide_sum, q_grad, d_grad, o_grad):
    _, rows, width = partial.shape
    units, own = q_grad.shape[0] // 8, q_grad.shape[1]
    sizes = [grad.shape[2] for grad in (q_grad, d_grad)]
    vmem = lambda shape, dtype=LOW: pltpu.VMEM(shape, dtype)
    return kernel_call(
        last_kernel,
        "last_sum",
        4,
        (partial, tokens, grad_residual, gain, block, wide_sum, q_grad, d_grad, o_grad),
        [IN_VMEM] * 4 + [ANYWHERE] * 5,
        [
            ((rows, width), WIDE),
            ((rows, width), LOW),
            ((own, 8 * sizes[0]), LOW),
            ((own, 8 * wide_sum.shape[3]), LOW),
            ((own, 8 * sizes[1]), LOW),
            ((own, width), LOW),
        ],
        [ANYWHERE] * 6,
        [vmem((rows, width), WIDE)]
        + [vmem((units, 2, own, size)) for size in sizes]
        + [vmem((own, width))]
        + LineScatter.buffers(rows, width)
        + [DMA(LineScatter.SEMS)]
        + PlaneScatter.scratch(units, own, sizes[0])
        + PlaneScatter.scratch(units, own, sizes[1])
        + PlaneScatter.scratch(1, own // 2, width)
        + [DMA(LineReturn.SEMS)] * 3
        + [DMA((3,))] * 3,
    )


def grid_shards(
    tokens,
    cotangent,
    qkv_weight,
    out_weight,
    gate_up_weight,
    down_weight,
    gains,
    qkv_first,
    out_first,
    gate_up_first,
    down_first,
    gains_first,
    qkv_second,
    out_second,
    gate_up_second,
    down_second,
    gains_second,
):
    rows, width = tokens.shape[1:]
    heads_here = HEADS // 8
    width_here = heads_here * HEAD_DIM
    seq_len = 8 * rows
    gain_columns = jnp.pad(gains.astype(LOW).T, ((0, 0), (0, 126)))
    cosines, sines = rope_tables(jnp.arange(seq_len, dtype=jnp.int32))
    (
        grad_out,
        normed_two,
        gate_up_full,
        down_full,
        qkv_full,
        out_full,
        normed_one,
        qkv_heads,
        attended,
        residual,
        gain_full,
        own_tokens,
    ) = forward(
        tokens[0],
        cotangent[0],
        qkv_weight.astype(LOW),
        gain_columns,
        gate_up_weight.astype(LOW),
        down_weight.astype(LOW),
        out_weight.astype(LOW),
        jnp.tile(cosines[:, 0], (1, 4)),
        jnp.tile(jnp.concatenate([-sines[:, 0], sines[:, 0]], axis=1), (1, 2)),
    )
    own_grad = lax.dynamic_index_in_dim(grad_out, lax.axis_index(RING), 0, keepdims=False)
    grad_out, normed_two = grad_out.reshape(-1, width), normed_two.reshape(-1, width)
    qkv_full = qkv_full.reshape(width, -1)[:, : 3 * width_here]
    gate_up_full = gate_up_full.reshape(width, -1)
    down_full = down_full.reshape(width, -1)
    out_full = out_full.reshape(-1, width)
    query_heads, key_heads, value_heads = (
        part.reshape(seq_len, heads_here, HEAD_DIM) for part in qkv_heads
    )
    lse_all = jnp.zeros((heads_here, seq_len, 1), WIDE)
    for block in range(seq_len // BLOCK):
        lse_rows = row_normalizer(query_heads[block * BLOCK : (block + 1) * BLOCK], key_heads, block)
        lse_all = lse_all.at[:, block * BLOCK : (block + 1) * BLOCK].set(lse_rows)
    gate_up = jnp.dot(normed_two, gate_up_full, preferred_element_type=WIDE)
    ff_here = gate_up.shape[1] // 2
    gate_vals = gate_up[:, :ff_here]
    up_vals = gate_up[:, ff_here:]
    sigmoid_gate = jax.nn.sigmoid(gate_vals)
    activated = (gate_vals * sigmoid_gate * up_vals).astype(LOW)
    mlp_out = lax.psum_scatter(
        lax.dot_general(activated, down_full, CONTRACT_LAST, preferred_element_type=WIDE).astype(
            LOW
        ),
        RING,
        scatter_dimension=0,
        tiled=True,
    ).astype(WIDE)
    block_own = (residual + mlp_out).astype(LOW)

    grad_act = jnp.dot(grad_out, down_full, preferred_element_type=WIDE)
    grad_gate = grad_act * up_vals * sigmoid_gate * (1.0 + gate_vals * (1.0 - sigmoid_gate))
    grad_up = grad_act * gate_vals * sigmoid_gate
    grad_gate_up = jnp.concatenate([grad_gate, grad_up], axis=1).astype(LOW)
    grad_normed_two = lax.dot_general(
        grad_gate_up, gate_up_full, CONTRACT_LAST, preferred_element_type=WIDE
    ).astype(LOW)
    gate_up_part = lax.dot_general(
        normed_two, grad_gate_up, CONTRACT_FIRST, preferred_element_type=WIDE
    ).astype(LOW)
    down_part = lax.dot_general(
        grad_out, activated, CONTRACT_FIRST, preferred_element_type=WIDE
    ).astype(LOW)
    own_rows = qkv_weight.shape[0]
    grad_residual, grad_branch, gate_up_half = middle_sum(
        grad_normed_two.reshape(8, rows, width),
        residual,
        own_grad,
        gain_full[1:2],
        gate_up_part.reshape(32, own_rows, -1),
    )
    grad_branch = grad_branch.reshape(seq_len, width)
    out_part = lax.dot_general(
        attended, grad_branch, CONTRACT_FIRST, preferred_element_type=WIDE
    ).astype(LOW)
    grad_heads = (
        lax.dot_general(grad_branch, out_full, CONTRACT_LAST, preferred_element_type=WIDE)
        .astype(LOW)
        .reshape(seq_len, heads_here, HEAD_DIM)
    )
    grad_q_all, grad_k_all, grad_v_all = attend_backward(
        query_heads, key_heads, value_heads, grad_heads, lse_all
    )
    grad_projected = (
        jnp.stack(
            [
                unrotate(grad_q_all, cosines, sines),
                unrotate(grad_k_all, cosines, sines),
                grad_v_all,
            ],
            axis=1,
        )
        .reshape(seq_len, 3 * width_here)
        .astype(LOW)
    )
    grad_normed_one = lax.dot_general(
        grad_projected, qkv_full, CONTRACT_LAST, preferred_element_type=WIDE
    ).astype(LOW)
    qkv_part = lax.dot_general(
        normed_one, grad_projected, CONTRACT_FIRST, preferred_element_type=WIDE
    ).astype(LOW)
    input_grad, block_out, qkv_sum, gate_up_sum, down_sum, out_sum = last_sum(
        grad_normed_one.reshape(8, rows, width),
        own_tokens,
        grad_residual,
        gain_full[:1],
        block_own,
        gate_up_half,
        qkv_part.reshape(32, own_rows, -1),
        down_part.reshape(32, own_rows, -1),
        out_part.reshape(4, own_rows, -1),
    )
    qkv_sum, gate_up_sum, down_sum, out_sum = (
        total.astype(WIDE) for total in (qkv_sum, gate_up_sum, down_sum, out_sum)
    )
    gains_sum = jnp.stack(
        [
            jnp.sum(weight.astype(LOW).astype(WIDE) * total, axis=1)
            for weight, total in ((qkv_weight, qkv_sum), (gate_up_weight, gate_up_sum))
        ],
        axis=0,
    ) / gains.astype(LOW).astype(WIDE)
    wide_rate = 2.5 * D ** (-0.5)
    out_rate = 2.5 * max(D // 512, 1) ** (-0.5)
    down_rate = 2.5 * FF ** (-0.5)
    qkv_new = adam_step(qkv_weight, qkv_sum, qkv_first, qkv_second, wide_rate, WEIGHT_DECAY)
    out_new = adam_step(out_weight, out_sum, out_first, out_second, out_rate, WEIGHT_DECAY)
    gate_up_new = adam_step(
        gate_up_weight, gate_up_sum, gate_up_first, gate_up_second, wide_rate, WEIGHT_DECAY
    )
    down_new = adam_step(
        down_weight, down_sum, down_first, down_second, down_rate, WEIGHT_DECAY
    )
    gains_new = adam_step(gains, gains_sum, gains_first, gains_second, 0.5, 0.0)
    return (
        block_out[None],
        input_grad[None],
        qkv_new[0],
        out_new[0],
        gate_up_new[0],
        down_new[0],
        gains_new[0],
        qkv_new[1],
        out_new[1],
        gate_up_new[1],
        down_new[1],
        gains_new[1],
        qkv_new[2],
        out_new[2],
        gate_up_new[2],
        down_new[2],
        gains_new[2],
    )


def mapped(body, mesh, token_spec, row_spec, gain_spec):
    one_set = (row_spec, row_spec, row_spec, row_spec, gain_spec)
    return jax.shard_map(
        body,
        mesh=mesh,
        in_specs=(token_spec, token_spec) + one_set * 3,
        out_specs=(token_spec, token_spec) + one_set * 3,
        check_vma=False,
    )


def solution(mesh):
    if mesh.shape["seq"] == 8 and mesh.shape["dp"] == 4:
        grid_mesh = Mesh(mesh.devices.reshape(4, 2, 2, 2), GRID)
        return mapped(
            grid_shards,
            grid_mesh,
            P(("y", "c"), ("z", "x"), None),
            P(GRID, None),
            P(None, GRID),
        )
    return mapped(
        shards, mesh, P("dp", "seq", None), P(("seq", "dp"), None), P(None, ("seq", "dp"))
    )
```

```python
import jax
import jax.numpy as jnp
from jax import lax
from jax.experimental import pallas as pl
from jax.experimental.pallas import tpu as pltpu
from jax.sharding import Mesh
from jax.sharding import PartitionSpec as P

D = 2048
HEADS = 32
HEAD_DIM = 64
FF = 8192
BLOCK = 512
STEP = 10


NORM_EPS = 1e-05
ROPE_BASE = 130000.0
BETA_ONE = 0.9
BETA_TWO = 0.999
ADAM_EPS = 1e-08
WEIGHT_DECAY = 0.1
MASKED = -1e30


def rms_parts(values):
    inverse = lax.rsqrt(jnp.mean(values * values, axis=-1, keepdims=True) + NORM_EPS)
    return (values * inverse, inverse)


def rope_tables(positions):
    half_dim = HEAD_DIM // 2
    exponent = jnp.arange(half_dim, dtype=jnp.float32) * (2.0 / HEAD_DIM)
    frequency = ROPE_BASE ** (-exponent)
    angles = positions.astype(jnp.float32)[:, None] * frequency[None, :]
    return (jnp.cos(angles)[:, None, :], jnp.sin(angles)[:, None, :])


def rotate(tensor, cosines, sines):
    half_dim = HEAD_DIM // 2
    lower_half = tensor[..., :half_dim]
    upper_half = tensor[..., half_dim:]
    return jnp.concatenate(
        [lower_half * cosines - upper_half * sines, upper_half * cosines + lower_half * sines],
        axis=-1,
    )


def unrotate(tensor, cosines, sines):
    half_dim = HEAD_DIM // 2
    lower_half = tensor[..., :half_dim]
    upper_half = tensor[..., half_dim:]
    return jnp.concatenate(
        [lower_half * cosines + upper_half * sines, upper_half * cosines - lower_half * sines],
        axis=-1,
    )


def block_scores(query_rows, key_heads, key_id, block_id):
    key_rows = lax.dynamic_slice_in_dim(key_heads, key_id * BLOCK, BLOCK, 0)
    products = jnp.einsum(
        "qhd,khd->hqk", query_rows, key_rows, preferred_element_type=jnp.float32
    ) * HEAD_DIM ** (-0.5)
    local_ids = jnp.arange(BLOCK, dtype=jnp.int32)
    allowed = (key_id < block_id) | (local_ids[None, :] <= local_ids[:, None])
    return jnp.where(allowed[None], products, MASKED)


def row_normalizer(query_rows, key_heads, block_id):
    row_shape = (query_rows.shape[1], BLOCK, 1)

    def absorb(key_id, state):
        running_max, running_total = state
        scores = block_scores(query_rows, key_heads, key_id, block_id)
        new_max = jnp.maximum(running_max, jnp.max(scores, axis=-1, keepdims=True))
        running_total = running_total * jnp.exp(running_max - new_max) + jnp.sum(
            jnp.exp(scores - new_max), axis=-1, keepdims=True
        )
        return (new_max, running_total)

    start_state = (jnp.full(row_shape, MASKED, jnp.float32), jnp.zeros(row_shape, jnp.float32))
    final_max, final_total = lax.fori_loop(0, block_id + 1, absorb, start_state)
    return final_max + jnp.log(final_total)


def attend_forward(query_heads, key_heads, value_heads):
    seq_len, heads_here, head_dim = query_heads.shape

    def one_block(block_id, carry):
        out_all, lse_all = carry
        row_start = block_id * BLOCK
        query_rows = lax.dynamic_slice_in_dim(query_heads, row_start, BLOCK, 0)
        row_lse = row_normalizer(query_rows, key_heads, block_id)

        def weigh_values(key_id, running):
            scores = block_scores(query_rows, key_heads, key_id, block_id)
            weights_low = jnp.exp(scores - row_lse).astype(jnp.bfloat16)
            value_rows = lax.dynamic_slice_in_dim(value_heads, key_id * BLOCK, BLOCK, 0)
            return running + jnp.einsum(
                "hqk,khd->qhd", weights_low, value_rows, preferred_element_type=jnp.float32
            )

        attended = lax.fori_loop(
            0, block_id + 1, weigh_values, jnp.zeros((BLOCK, heads_here, head_dim), jnp.float32)
        )
        out_all = lax.dynamic_update_slice_in_dim(
            out_all, attended.astype(jnp.bfloat16), row_start, 0
        )
        lse_all = lax.dynamic_update_slice_in_dim(lse_all, row_lse, row_start, 1)
        return (out_all, lse_all)

    start_carry = (
        jnp.zeros((seq_len, heads_here, head_dim), jnp.bfloat16),
        jnp.zeros((heads_here, seq_len, 1), jnp.float32),
    )
    return lax.fori_loop(0, seq_len // BLOCK, one_block, start_carry)


def attend_backward(query_heads, key_heads, value_heads, grad_heads, lse_all):
    seq_len, heads_here, head_dim = query_heads.shape
    score_scale = HEAD_DIM ** (-0.5)

    def one_block(block_id, carry):
        grad_q_all, grad_k_all, grad_v_all = carry
        row_start = block_id * BLOCK
        query_rows = lax.dynamic_slice_in_dim(query_heads, row_start, BLOCK, 0)
        grad_rows = lax.dynamic_slice_in_dim(grad_heads, row_start, BLOCK, 0)
        row_lse = lax.dynamic_slice_in_dim(lse_all, row_start, BLOCK, 1)

        def probs_and_grads(key_id):
            scores = block_scores(query_rows, key_heads, key_id, block_id)
            probs = jnp.exp(scores - row_lse)
            value_rows = lax.dynamic_slice_in_dim(value_heads, key_id * BLOCK, BLOCK, 0)
            grad_probs = jnp.einsum(
                "qhd,khd->hqk", grad_rows, value_rows, preferred_element_type=jnp.float32
            )
            return (probs, grad_probs)

        def add_delta(key_id, running):
            probs, grad_probs = probs_and_grads(key_id)
            return running + jnp.sum(probs * grad_probs, axis=-1, keepdims=True)

        row_delta = lax.fori_loop(
            0, block_id + 1, add_delta, jnp.zeros((heads_here, BLOCK, 1), jnp.float32)
        )

        def spread(key_id, inner):
            grad_q_rows, grad_k_acc, grad_v_acc = inner
            probs, grad_probs = probs_and_grads(key_id)
            key_start = key_id * BLOCK
            key_rows = lax.dynamic_slice_in_dim(key_heads, key_start, BLOCK, 0)
            grad_scores = (probs * (grad_probs - row_delta) * score_scale).astype(jnp.bfloat16)
            grad_q_rows = grad_q_rows + jnp.einsum(
                "hqk,khd->qhd", grad_scores, key_rows, preferred_element_type=jnp.float32
            )
            grad_k_part = jnp.einsum(
                "hqk,qhd->khd", grad_scores, query_rows, preferred_element_type=jnp.float32
            )
            grad_v_part = jnp.einsum(
                "hqk,qhd->khd",
                probs.astype(jnp.bfloat16),
                grad_rows,
                preferred_element_type=jnp.float32,
            )
            grad_k_acc = lax.dynamic_update_slice_in_dim(
                grad_k_acc,
                lax.dynamic_slice_in_dim(grad_k_acc, key_start, BLOCK, 0) + grad_k_part,
                key_start,
                0,
            )
            grad_v_acc = lax.dynamic_update_slice_in_dim(
                grad_v_acc,
                lax.dynamic_slice_in_dim(grad_v_acc, key_start, BLOCK, 0) + grad_v_part,
                key_start,
                0,
            )
            return (grad_q_rows, grad_k_acc, grad_v_acc)

        start_inner = (
            jnp.zeros((BLOCK, heads_here, head_dim), jnp.float32),
            grad_k_all,
            grad_v_all,
        )
        grad_q_rows, grad_k_all, grad_v_all = lax.fori_loop(0, block_id + 1, spread, start_inner)
        grad_q_all = lax.dynamic_update_slice_in_dim(grad_q_all, grad_q_rows, row_start, 0)
        return (grad_q_all, grad_k_all, grad_v_all)

    zeros_all = jnp.zeros((seq_len, heads_here, head_dim), jnp.float32)
    return lax.fori_loop(0, seq_len // BLOCK, one_block, (zeros_all, zeros_all, zeros_all))


def adam_step(weight, gradient, first, second, rate, decay):
    new_first = BETA_ONE * first + (1.0 - BETA_ONE) * gradient
    new_second = BETA_TWO * second + (1.0 - BETA_TWO) * gradient * gradient
    first_hat = new_first / (1.0 - BETA_ONE**STEP)
    second_hat = new_second / (1.0 - BETA_TWO**STEP)
    new_weight = weight - rate * (first_hat / (jnp.sqrt(second_hat) + ADAM_EPS) + decay * weight)
    return (new_weight, new_first, new_second)


def shards(
    tokens,
    cotangent,
    qkv_weight,
    out_weight,
    gate_up_weight,
    down_weight,
    gains,
    qkv_first,
    out_first,
    gate_up_first,
    down_first,
    gains_first,
    qkv_second,
    out_second,
    gate_up_second,
    down_second,
    gains_second,
):
    seq_count = lax.axis_size("seq")
    tok_rows = tokens.shape[1]
    width = tokens.shape[2]
    seq_len = tok_rows * seq_count
    heads_here = HEADS // seq_count
    width_here = heads_here * HEAD_DIM
    contract_last = (((1,), (1,)), ((), ()))
    contract_first = (((0,), (0,)), ((), ()))
    qkv_full, proj_full, gain_full = (
        lax.all_gather(qkv_weight.astype(jnp.bfloat16), ("seq", "dp"), axis=0, tiled=True),
        lax.all_gather(out_weight.astype(jnp.bfloat16), ("seq", "dp"), axis=0, tiled=True),
        lax.all_gather(gains.astype(jnp.bfloat16), ("seq", "dp"), axis=1, tiled=True),
    )
    up_full, down_full = (
        lax.all_gather(gate_up_weight.astype(jnp.bfloat16), ("seq", "dp"), axis=0, tiled=True),
        lax.all_gather(down_weight.astype(jnp.bfloat16), ("seq", "dp"), axis=0, tiled=True),
    )
    hidden_in = tokens[0].astype(jnp.float32)
    unit_one, inverse_one = rms_parts(hidden_in)
    normed_one = (unit_one * gain_full[0].astype(jnp.float32)).astype(jnp.bfloat16)
    projected = jnp.einsum(
        "te,ecd->ctd",
        normed_one,
        qkv_full.reshape(width, 3, width),
        preferred_element_type=jnp.float32,
    )
    positions = lax.axis_index("seq") * tok_rows + jnp.arange(tok_rows, dtype=jnp.int32)
    cos_local, sin_local = rope_tables(positions)
    turned = rotate(projected[:2].reshape(2, tok_rows, HEADS, HEAD_DIM), cos_local, sin_local)
    packed = jnp.concatenate([turned.reshape(2, tok_rows, width), projected[2:]], axis=0).astype(
        jnp.bfloat16
    )
    by_heads = lax.all_to_all(packed, "seq", split_axis=2, concat_axis=1, tiled=True)
    query_heads = by_heads[0].reshape(seq_len, heads_here, HEAD_DIM)
    key_heads = by_heads[1].reshape(seq_len, heads_here, HEAD_DIM)
    value_heads = by_heads[2].reshape(seq_len, heads_here, HEAD_DIM)
    out_heads, lse_all = attend_forward(query_heads, key_heads, value_heads)
    attended = lax.all_to_all(
        out_heads.reshape(seq_len, width_here), "seq", split_axis=0, concat_axis=1, tiled=True
    )
    residual = hidden_in + jnp.dot(attended, proj_full, preferred_element_type=jnp.float32)
    unit_two, inverse_two = rms_parts(residual)
    normed_two = (unit_two * gain_full[1].astype(jnp.float32)).astype(jnp.bfloat16)
    gate_up = jnp.dot(normed_two, up_full, preferred_element_type=jnp.float32)
    gate_vals = gate_up[:, :FF]
    up_vals = gate_up[:, FF:]
    sigmoid_gate = jax.nn.sigmoid(gate_vals)
    activated = (gate_vals * sigmoid_gate * up_vals).astype(jnp.bfloat16)
    mlp_out = lax.dot_general(
        activated, down_full, contract_last, preferred_element_type=jnp.float32
    )
    block_out = (residual + mlp_out).astype(jnp.bfloat16)[None]
    back_up, back_down, back_gain = (
        lax.all_gather(gate_up_weight.astype(jnp.bfloat16), ("seq", "dp"), axis=0, tiled=True),
        lax.all_gather(down_weight.astype(jnp.bfloat16), ("seq", "dp"), axis=0, tiled=True),
        lax.all_gather(gains.astype(jnp.bfloat16), ("seq", "dp"), axis=1, tiled=True),
    )
    grad_out = cotangent[0]
    grad_act = jnp.dot(grad_out, back_down, preferred_element_type=jnp.float32)
    grad_gate = grad_act * up_vals * sigmoid_gate * (1.0 + gate_vals * (1.0 - sigmoid_gate))
    grad_up = grad_act * gate_vals * sigmoid_gate
    grad_gate_up = jnp.concatenate([grad_gate, grad_up], axis=1).astype(jnp.bfloat16)
    grad_normed_two = lax.dot_general(
        grad_gate_up, back_up, contract_last, preferred_element_type=jnp.float32
    )
    gain_two_grad = jnp.sum(grad_normed_two * unit_two, axis=0)
    grad_unit_two = grad_normed_two * back_gain[1].astype(jnp.float32)
    grad_residual = grad_out.astype(jnp.float32) + inverse_two * (
        grad_unit_two - unit_two * jnp.mean(grad_unit_two * unit_two, axis=-1, keepdims=True)
    )
    gate_up_rows = lax.dot_general(
        normed_two, grad_gate_up, contract_first, preferred_element_type=jnp.float32
    )
    down_rows = lax.dot_general(
        grad_out, activated, contract_first, preferred_element_type=jnp.float32
    )
    mlp_grad = lax.psum_scatter(
        jnp.concatenate([gate_up_rows, down_rows], axis=1),
        ("seq", "dp"),
        scatter_dimension=0,
        tiled=True,
    )
    back_qkv, back_proj = (
        lax.all_gather(qkv_weight.astype(jnp.bfloat16), ("seq", "dp"), axis=0, tiled=True),
        lax.all_gather(out_weight.astype(jnp.bfloat16), ("seq", "dp"), axis=0, tiled=True),
    )
    grad_branch = grad_residual.astype(jnp.bfloat16)
    proj_grad = lax.dot_general(
        attended, grad_branch, contract_first, preferred_element_type=jnp.float32
    )
    grad_attended = lax.dot_general(
        grad_branch, back_proj, contract_last, preferred_element_type=jnp.float32
    ).astype(jnp.bfloat16)
    grad_heads = lax.all_to_all(
        grad_attended, "seq", split_axis=1, concat_axis=0, tiled=True
    ).reshape(seq_len, heads_here, HEAD_DIM)
    grad_q_all, grad_k_all, grad_v_all = attend_backward(
        query_heads, key_heads, value_heads, grad_heads, lse_all
    )
    cos_whole, sin_whole = rope_tables(jnp.arange(seq_len, dtype=jnp.int32))
    grad_pack = jnp.stack(
        [
            unrotate(grad_q_all, cos_whole, sin_whole).reshape(seq_len, width_here),
            unrotate(grad_k_all, cos_whole, sin_whole).reshape(seq_len, width_here),
            grad_v_all.reshape(seq_len, width_here),
        ],
        axis=0,
    ).astype(jnp.bfloat16)
    grad_projected = lax.all_to_all(grad_pack, "seq", split_axis=1, concat_axis=2, tiled=True)
    qkv_cube = back_qkv.reshape(width, 3, width)
    grad_normed_one = jnp.einsum(
        "ctd,ecd->te", grad_projected, qkv_cube, preferred_element_type=jnp.float32
    )
    qkv_grad = jnp.einsum(
        "te,ctd->ecd", normed_one, grad_projected, preferred_element_type=jnp.float32
    ).reshape(width, 3 * width)
    gain_one_grad = jnp.sum(grad_normed_one * unit_one, axis=0)
    grad_unit_one = grad_normed_one * back_gain[0].astype(jnp.float32)
    input_grad = grad_residual + inverse_one * (
        grad_unit_one - unit_one * jnp.mean(grad_unit_one * unit_one, axis=-1, keepdims=True)
    )
    gains_grad = jnp.stack([gain_one_grad, gain_two_grad], axis=0)
    qkv_sum, proj_sum, gains_sum = (
        lax.psum_scatter(qkv_grad, ("seq", "dp"), scatter_dimension=0, tiled=True),
        lax.psum_scatter(proj_grad, ("seq", "dp"), scatter_dimension=0, tiled=True),
        lax.psum_scatter(gains_grad, ("seq", "dp"), scatter_dimension=1, tiled=True),
    )
    wide_rate = 2.5 * D ** (-0.5)
    out_rate = 2.5 * max(D // 512, 1) ** (-0.5)
    down_rate = 2.5 * FF ** (-0.5)
    qkv_new = adam_step(qkv_weight, qkv_sum, qkv_first, qkv_second, wide_rate, WEIGHT_DECAY)
    out_new = adam_step(out_weight, proj_sum, out_first, out_second, out_rate, WEIGHT_DECAY)
    gate_up_new = adam_step(
        gate_up_weight,
        mlp_grad[:, : 2 * FF],
        gate_up_first,
        gate_up_second,
        wide_rate,
        WEIGHT_DECAY,
    )
    down_new = adam_step(
        down_weight, mlp_grad[:, 2 * FF :], down_first, down_second, down_rate, WEIGHT_DECAY
    )
    gains_new = adam_step(gains, gains_sum, gains_first, gains_second, 0.5, 0.0)
    return (
        block_out,
        input_grad[None],
        qkv_new[0],
        out_new[0],
        gate_up_new[0],
        down_new[0],
        gains_new[0],
        qkv_new[1],
        out_new[1],
        gate_up_new[1],
        down_new[1],
        gains_new[1],
        qkv_new[2],
        out_new[2],
        gate_up_new[2],
        down_new[2],
        gains_new[2],
    )


GRID = ("z", "x", "y", "c")
RING = ("z", "c")
PLANE = ("x", "y")
LOW = jnp.bfloat16
WIDE = jnp.float32
CONTRACT_LAST = (((1,), (1,)), ((), ()))
CONTRACT_FIRST = (((0,), (0,)), ((), ()))
DMA = pltpu.SemaphoreType.DMA
ANYWHERE = pl.BlockSpec(memory_space=pl.ANY)
IN_VMEM = pl.BlockSpec(memory_space=pltpu.VMEM)


def remote(source, target, send, receive, **place):
    return pltpu.make_async_remote_copy(
        src_ref=source,
        dst_ref=target,
        send_sem=send,
        recv_sem=receive,
        device_id=place,
        device_id_type=pl.DeviceIdType.MESH,
    )


def lanes(start, size):
    return pl.ds(pl.multiple_of(start, 128), size)


class Place:
    def __init__(self):
        self.z, self.x, self.y, self.c = (lax.axis_index(name) for name in GRID)
        self.slot = 2 * self.z + self.c
        self.block_here = self.block(self.slot, self.x, self.y)

    def block(self, slot, x, y):
        return (((slot // 2) * 2 + x) * 2 + y) * 2 + lax.rem(slot, 2)

    def meet(self, plane):
        barrier = pltpu.get_barrier_semaphore()
        others = [
            {"z": slot // 2, "c": lax.rem(slot, 2)}
            for slot in (lax.rem(self.slot + step, 8) for step in range(1, 8))
        ]
        if plane:
            others += [{"x": 1 - self.x}, {"y": 1 - self.y}, {"x": 1 - self.x, "c": 1 - self.c}]
        for other in others:
            pl.semaphore_signal(
                barrier, inc=1, device_id=other, device_id_type=pl.DeviceIdType.MESH
            )
        pl.semaphore_wait(barrier, len(others))


class Swap:
    def __init__(self, place, source, spot_there, spot_here, sems):
        p = self.place = place
        self.away = lambda: remote(
            source, spot_there, sems.at[0], sems.at[1], x=1 - p.x, c=1 - p.c
        )
        self.here = lambda: pltpu.make_async_copy(source, spot_here, sems.at[2])

    def start(self):
        p = self.place
        pl.when(p.x != p.c)(lambda: self.away().start())
        pl.when(p.x == p.c)(lambda: self.here().start())

    def wait(self):
        p = self.place
        pl.when(p.x != p.c)(lambda: self.away().wait_recv())
        pl.when(p.x == p.c)(lambda: self.here().wait())

    def drain(self):
        p = self.place
        pl.when(p.x != p.c)(lambda: self.away().wait_send())


class LineGather:
    SEMS = (4, 8)

    def __init__(self, place, buffer, sems, mine=None, rows=None):
        self.place, self.sems, self.mine = place, sems, mine
        self.spot = (lambda slot: buffer.at[slot]) if rows is None else (lambda slot: buffer.at[slot, rows])

    def copy(self, slot, way, own=False):
        p, block = self.place, self.spot(slot)
        if way == 0:
            where = {"z": jnp.minimum(p.z + 1, 3)}
        elif way == 1:
            where = {"z": jnp.maximum(p.z - 1, 0)}
        else:
            where = {"c": 1 - p.c}
        source = self.mine if own and self.mine is not None else block
        return remote(source, block, self.sems.at[way, slot], self.sems.at[3, slot], **where)

    def _pass_on(self, slot, way, own=False):
        p = self.place
        if way == 0:
            pl.when(p.z < 3)(lambda: self.copy(slot, 0, own).start())
        elif way == 1:
            pl.when(p.z > 0)(lambda: self.copy(slot, 1, own).start())

    def start(self):
        slot = self.place.slot
        self._pass_on(slot, 0, True)
        self._pass_on(slot, 1, True)
        self.copy(slot, 2, True).start()
        if self.mine is not None:
            self.keep().start()

    def keep(self):
        slot = self.place.slot
        return pltpu.make_async_copy(self.mine, self.spot(slot), self.sems.at[3, slot])

    def step(self, distance):
        p = self.place

        @pl.when(p.z + distance <= 3)
        def _():
            slot = p.slot + 2 * distance
            self.copy(slot, 2).wait_recv()
            self._pass_on(slot, 1)
            self.copy(slot, 2).start()

        @pl.when(p.z >= distance)
        def _():
            slot = p.slot - 2 * distance
            self.copy(slot, 2).wait_recv()
            self._pass_on(slot, 0)
            self.copy(slot, 2).start()

    def finish(self):
        p = self.place
        if self.mine is not None:
            self.keep().wait()
        for z in range(4):
            self.copy(2 * z + 1 - p.c, 2).wait_recv()

    def drain(self):
        p = self.place
        for z in range(4):
            slot = 2 * z + p.c
            self.copy(slot, 2).wait_send()
            pl.when((z <= p.z) & (p.z < 3))(lambda: self.copy(slot, 0).wait_send())
            pl.when((z >= p.z) & (p.z > 0))(lambda: self.copy(slot, 1).wait_send())


def add_blocks(target, sources):
    def some(step, carry):
        rows = pl.ds(pl.multiple_of(step * 16, 16), 16)
        total = sources[0][rows, :].astype(WIDE)
        for source in sources[1:]:
            total = total + source[rows, :].astype(WIDE)
        target[rows, :] = total.astype(target.dtype)
        return carry

    lax.fori_loop(0, target.shape[0] // 16, some, 0)


class LineScatter:
    SEMS = (6, 4)

    @staticmethod
    def buffers(rows, width):
        return [pltpu.VMEM((4, rows, width), LOW) for _ in range(4)]

    def __init__(self, place, partial, across, below, above, stage, sems, rows):
        self.place, self.partial, self.sems, self.rows = place, partial, sems, rows
        self.across, self.below, self.above = across, below, above
        self.stage = stage

    def cross(self, z):
        p = self.place
        return remote(
            self.partial.at[2 * z + 1 - p.c, self.rows],
            self.across.at[z, self.rows],
            self.sems.at[0, z],
            self.sems.at[1, z],
            c=1 - p.c,
        )

    def hop(self, z, way):
        p = self.place
        target = (self.below, self.above)[way]
        there = jnp.minimum(p.z + 1, 3) if way == 0 else jnp.maximum(p.z - 1, 0)
        return remote(
            self.stage.at[z, self.rows],
            target.at[z, self.rows],
            self.sems.at[2 + 2 * way, z],
            self.sems.at[3 + 2 * way, z],
            z=there,
        )

    def start(self):
        for z in range(4):
            self.cross(z).start()

    def head(self):
        p = self.place
        for z in range(4):
            self.cross(z).wait_recv()
        for way, end in ((0, 0), (1, 3)):

            @pl.when(p.z == end)
            def _():
                for index in range(3):
                    z = 3 - index if way == 0 else index
                    add_blocks(
                        self.stage.at[z, self.rows],
                        [self.partial.at[2 * z + p.c, self.rows], self.across.at[z, self.rows]],
                    )
                    self.hop(z, way).start()

    def step(self, index):
        p = self.place
        for way, z in ((0, 3 - index), (1, index)):
            inside = (p.z < z) & (p.z > 0) if way == 0 else (p.z > z) & (p.z < 3)
            passing = (self.below, self.above)[way]

            @pl.when(inside)
            def _():
                self.hop(z, way).wait_recv()
                add_blocks(
                    self.stage.at[z, self.rows],
                    [
                        self.partial.at[2 * z + p.c, self.rows],
                        self.across.at[z, self.rows],
                        passing.at[z, self.rows],
                    ],
                )
                self.hop(z, way).start()

    def arrive(self):
        p = self.place
        pl.when(p.z > 0)(lambda: self.hop(p.z, 0).wait_recv())
        pl.when(p.z < 3)(lambda: self.hop(p.z, 1).wait_recv())

        @pl.when(p.z == 0)
        def _():
            spot = self.below.at[0, self.rows]
            spot[...] = jnp.zeros(spot.shape, LOW)

        @pl.when(p.z == 3)
        def _():
            spot = self.above.at[3, self.rows]
            spot[...] = jnp.zeros(spot.shape, LOW)

    def total(self, rows):
        p = self.place
        parts = (
            self.partial[p.slot, rows, :],
            self.across[p.z, rows, :],
            self.below[p.z, rows, :],
            self.above[p.z, rows, :],
        )
        return sum(part.astype(WIDE) for part in parts)

    def drain(self):
        p = self.place
        for z in range(4):
            self.cross(z).wait_send()
            pl.when(p.z < z)(lambda: self.hop(z, 0).wait_send())
            pl.when(p.z > z)(lambda: self.hop(z, 1).wait_send())


class Relayout:
    SEMS = (8, 8)

    def __init__(self, place, parts, target, sems):
        self.place, self.parts, self.target, self.sems = place, parts, target, sems

    def sem(self, kind, slot):
        return self.sems.at[kind, slot]

    def line(self, step):
        p = self.place
        slot = lax.rem(p.slot + step, 8)
        copies = []
        for source, first, size, there in self.parts:
            same_for_all = source.shape[1] == size
            columns = lanes(first if same_for_all else first + size * slot, size)
            piece = source.at[:, columns]
            spot = self.target.at[p.block_here, :, pl.ds(there, size)]
            if step == 0:
                copies.append(pltpu.make_async_copy(piece, spot, self.sem(1, p.slot)))
            else:
                copies.append(
                    remote(
                        piece,
                        spot,
                        self.sem(0, slot),
                        self.sem(1, p.slot),
                        z=slot // 2,
                        c=lax.rem(slot, 2),
                    )
                )
        return copies

    def whole(self, slot):
        p = self.place
        spot = self.target.at[p.block(slot, p.x, p.y)]
        return remote(spot, spot, self.sem(0, slot), self.sem(1, slot), c=1 - p.c)

    def plane(self, slot, x, y, way, send, receive):
        p = self.place
        spot = self.target.at[p.block(slot, x, y)]
        where = {"x": 1 - p.x} if way == 0 else {"y": 1 - p.y}
        return remote(spot, spot, self.sem(send, slot), self.sem(receive, slot), **where)

    def from_own(self, slot, way):
        p = self.place
        return self.plane(slot, p.x, p.y, way, 2 + 2 * way, 3 + 2 * way)

    def corner(self, slot, way):
        p = self.place
        x, y = (p.x, 1 - p.y) if way == 0 else (1 - p.x, p.y)
        return self.plane(slot, x, y, way, 6, 7)

    def start(self):
        for step in range(8):
            for copy in self.line(step):
                copy.start()

    def spread(self, step):
        p = self.place
        slot = lax.rem(p.slot + 8 - step, 8)
        if isinstance(step, int) and step == 0:
            spot = self.target.at[p.block_here]
            pltpu.make_async_copy(spot, spot, self.sem(1, p.slot)).wait()
        else:
            self.whole(slot).wait_recv()
        for way in range(2):
            self.from_own(slot, way).start()

    def corners(self, z):
        self.from_own(2 * z, 0).wait_recv()
        self.corner(2 * z, 1).start()
        self.from_own(2 * z + 1, 1).wait_recv()
        self.corner(2 * z + 1, 0).start()

    def finish(self):
        for z in range(4):
            self.from_own(2 * z, 1).wait_recv()
            self.from_own(2 * z + 1, 0).wait_recv()
            self.corner(2 * z, 1).wait_recv()
            self.corner(2 * z + 1, 0).wait_recv()

    def drain(self):
        for step in range(1, 8):
            self.whole(lax.rem(self.place.slot + step, 8)).wait_send()
        for z in range(4):
            self.corner(2 * z, 1).wait_send()
            self.corner(2 * z + 1, 0).wait_send()
        for slot in range(8):
            for way in range(2):
                self.from_own(slot, way).wait_send()


class PlaneScatter:
    @staticmethod
    def scratch(units, rows, width):
        shape = (rows, width)
        return [
            pltpu.VMEM((2, 2, units) + shape, LOW),
            pltpu.VMEM((2, 2, units) + shape, LOW),
            pltpu.VMEM((2, units) + shape, LOW),
            DMA((5, 2, 2, units)),
        ]

    def __init__(self, place, part, units, held, got, last, sems):
        self.place, self.part, self.units = place, part, units
        self.held, self.got, self.last, self.sems = held, got, last, sems

    def pair(self, near):
        p = self.place
        x, y = (p.x, p.y) if near else (1 - p.x, 1 - p.y)
        return ((p.x, y), (x, p.y))

    def load(self, half, near, unit):
        x, y = self.pair(near)[half]
        return pltpu.make_async_copy(
            self.part(half, unit, x, y),
            self.held.at[half, near, unit],
            self.sems.at[0, half, near, unit],
        )

    def first(self, half, near, unit):
        p = self.place
        x, y = self.pair(near)[half]
        x, y = (1 - x, y) if half == 0 else (x, 1 - y)
        where = {"x": 1 - p.x} if half == 0 else {"y": 1 - p.y}
        return remote(
            self.part(half, unit, x, y),
            self.got.at[half, near, unit],
            self.sems.at[1, half, near, unit],
            self.sems.at[2, half, near, unit],
            **where,
        )

    def second(self, half, unit):
        p = self.place
        where = {"y": 1 - p.y} if half == 0 else {"x": 1 - p.x}
        return remote(
            self.held.at[half, 0, unit],
            self.last.at[half, unit],
            self.sems.at[3, half, 0, unit],
            self.sems.at[4, half, 0, unit],
            **where,
        )

    def each(self, call):
        lax.fori_loop(0, self.units, lambda unit, carry: (call(unit), carry)[1], 0)

    def start(self):
        for near in range(2):

            def begin(unit):
                for half in range(2):
                    self.first(half, near, unit).start()
                    self.load(half, near, unit).start()

            self.each(begin)

    def middle(self, unit):
        for half in range(2):
            self.load(half, 0, unit).wait()
            self.first(half, 0, unit).wait_recv()
            spot = self.held.at[half, 0, unit]
            add_blocks(spot, [spot, self.got.at[half, 0, unit]])
            self.second(half, unit).start()

    def final(self, unit):
        for half in range(2):
            self.load(half, 1, unit).wait()
            self.first(half, 1, unit).wait_recv()
            self.second(half, unit).wait_recv()
            spot = self.held.at[half, 1, unit]
            add_blocks(spot, [spot, self.got.at[half, 1, unit], self.last.at[half, unit]])

    def drain(self):
        def end(unit):
            for half in range(2):
                for near in range(2):
                    self.first(half, near, unit).wait_send()
                self.second(half, unit).wait_send()

        self.each(end)


class LineReturn:
    SEMS = (2, 8)

    def __init__(self, place, plane, parts, target, sems):
        self.place, self.sums, self.parts = place, plane.held, parts
        self.target, self.sems = target, sems

    def copies(self, z, c, local):
        p = self.place
        made = []
        for here, size, first in self.parts:
            piece = self.sums.at[c, 1, z, :, pl.ds(here, size)]
            spot = self.target.at[:, lanes(first + size * p.slot, size)]
            if local:
                made.append(pltpu.make_async_copy(piece, spot, self.sems.at[1, p.slot]))
            else:
                made.append(
                    remote(
                        piece, spot, self.sems.at[0, 2 * z + c], self.sems.at[1, p.slot], z=z, c=c
                    )
                )
        return made

    def send(self, z):
        p = self.place
        for c in range(2):
            mine = (z == p.z) & (c == p.c)

            @pl.when(mine)
            def _():
                for copy in self.copies(z, c, True):
                    copy.start()

            @pl.when(jnp.logical_not(mine))
            def _():
                for copy in self.copies(z, c, False):
                    copy.start()

    def finish(self):
        p = self.place
        spot = self.sums.at[0, 1, 0]
        pltpu.make_async_copy(spot, spot, self.sems.at[1, p.slot]).wait()
        for step in range(1, 8):
            slot = lax.rem(p.slot + step, 8)
            whole = remote(
                spot, spot, self.sems.at[0, slot], self.sems.at[1, slot], c=1 - p.c
            )
            whole.wait_recv()
            whole.wait_send()


def kernel_call(kernel, name, number, inputs, in_specs, outputs, out_specs, scratch):
    return pl.pallas_call(
        kernel,
        out_shape=[jax.ShapeDtypeStruct(shape, dtype) for shape, dtype in outputs],
        in_specs=in_specs,
        out_specs=out_specs,
        scratch_shapes=scratch,
        compiler_params=pltpu.CompilerParams(
            collective_id=number, has_side_effects=True, vmem_limit_bytes=60 * 2**20
        ),
        name=name,
    )(*inputs)


CHUNK = 16


def by_rows(count, call):
    def some(step, carry):
        call(pl.ds(pl.multiple_of(step * CHUNK, CHUNK), CHUNK))
        return carry

    lax.fori_loop(0, count // CHUNK, some, 0)


def normed_back(grad_normed, unit, inverse, gain):
    grad_unit = grad_normed * gain
    return inverse * (grad_unit - unit * jnp.mean(grad_unit * unit, axis=-1, keepdims=True))


def turn(values, cosines, sines):
    lane = lax.broadcasted_iota(jnp.int32, values.shape, 1)
    half_dim = HEAD_DIM // 2
    width = values.shape[1]
    partner = jnp.where(
        lax.rem(lane, HEAD_DIM) < half_dim,
        pltpu.roll(values, width - half_dim, 1),
        pltpu.roll(values, half_dim, 1),
    )
    return values * cosines + partner * sines


def head_mask(head):
    lane = lax.broadcasted_iota(jnp.int32, (1, 128), 1)
    return (lane // HEAD_DIM == lax.rem(head, 2)).astype(WIDE).astype(LOW)


def scaled_probs(queries, keys, first_row):
    scores = lax.dot_general(queries, keys, CONTRACT_LAST, preferred_element_type=WIDE)
    scores = scores * HEAD_DIM ** (-0.5)
    row = lax.broadcasted_iota(jnp.int32, scores.shape, 0) + first_row
    column = lax.broadcasted_iota(jnp.int32, scores.shape, 1)
    scores = jnp.where(column <= row, scores, MASKED)
    expo = jnp.exp(scores - jnp.max(scores, axis=1, keepdims=True))
    return expo * (1.0 / jnp.sum(expo, axis=1, keepdims=True))


QUERY_ROWS = 256


def attend_head(head, qkv, total):
    pair = lanes(head // 2 * 128, 128)
    mask = head_mask(head)
    for block in range(qkv.shape[1] // QUERY_ROWS):
        rows = pl.ds(block * QUERY_ROWS, QUERY_ROWS)
        keys = pl.ds(0, (block + 1) * QUERY_ROWS)
        probs = scaled_probs(qkv[0, rows, pair] * mask, qkv[1, keys, pair], block * QUERY_ROWS)
        total[rows, pair] += jnp.dot(
            probs.astype(LOW), qkv[2, keys, pair] * mask, preferred_element_type=WIDE
        )


def forward_kernel(
    tok,
    cot,
    wq,
    gain,
    wg,
    wd,
    wo,
    cosines,
    sines,
    all_cot,
    normed_two,
    full_g,
    full_d,
    out_q,
    out_o,
    out_normed,
    out_qkv,
    out_attended,
    out_residual,
    out_gains,
    out_tok,
    all_tok,
    full_q,
    full_o,
    normed_one,
    qkv,
    heads,
    attended,
    residual,
    gain_rows,
    mine,
    partial,
    *scratch,
):
    buffers, sems = scratch[:4], scratch[4:]
    tok_swap, cot_swap, out_swap, tok_sems, cot_sems, q_sems, g_sems, d_sems = sems[:8]
    o_sems, sum_a, sum_b, gather_a, gather_b, keep_sems = sems[8:]
    p = Place()
    p.meet(True)
    rows_own = tok.shape[0]
    seq_len = 8 * rows_own
    step_q, step_g, step_d = wq.shape[1] // 24, wg.shape[1] // 16, wd.shape[1] // 8
    q_parts = [(wq, i * 8 * step_q, step_q, i * step_q) for i in range(3)]
    q_parts.append((gain, 0, gain.shape[1], 3 * step_q))
    move_q = Relayout(p, q_parts, full_q, q_sems)
    move_g = Relayout(
        p, [(wg, i * 8 * step_g, step_g, i * step_g) for i in range(2)], full_g, g_sems
    )
    move_d = Relayout(p, [(wd, 0, step_d, 0)], full_d, d_sems)
    tokens, cotangents = LineGather(p, all_tok, tok_sems), LineGather(p, all_cot, cot_sems)
    away = 2 * p.z + 1 - p.c
    swap_tok = Swap(p, tok, all_tok.at[away], all_tok.at[p.slot], tok_swap)
    swap_cot = Swap(p, cot, all_cot.at[away], all_cot.at[p.slot], cot_swap)
    swap_out = Swap(p, wo, full_o.at[2 * p.y + 1 - p.x], full_o.at[2 * p.y + p.x], out_swap)
    half = wo.shape[0] // 2

    def out_copy(kind):
        own, beside, above = 2 * p.y + p.x, 2 * p.y + 1 - p.x, 2 * (1 - p.y) + p.x
        send, got = o_sems.at[0, kind], o_sems.at[1, kind]
        if kind < 2:
            where = {"x": 1 - p.x} if kind == 0 else {"y": 1 - p.y}
            return remote(full_o.at[own], full_o.at[own], send, got, **where)
        spot = full_o.at[beside if kind == 2 else above, pl.ds((kind - 2) * half, half)]
        where = {"y": 1 - p.y} if kind == 2 else {"x": 1 - p.x}
        return remote(spot, spot, send, got, **where)

    kept = []

    def keep(source, target):
        copy = pltpu.make_async_copy(source, target, keep_sems.at[len(kept)])
        copy.start()
        kept.append(copy)

    swap_tok.start()
    move_q.start()
    swap_out.start()
    swap_tok.wait()
    tokens.start()
    swap_cot.start()
    for step in range(8):
        move_q.spread(step)
    tokens.step(1)
    swap_out.wait()
    out_copy(0).start()
    out_copy(1).start()
    tokens.step(2)
    move_g.start()
    for z in range(4):
        move_q.corners(z)
    tokens.step(3)
    out_copy(0).wait_recv()
    out_copy(2).start()
    out_copy(1).wait_recv()
    out_copy(3).start()
    move_q.finish()
    columns = full_q.shape[2]
    gain_block = full_q[:, :, pl.ds(3 * step_q, columns - 3 * step_q)].reshape(-1, 128)
    pick = lax.broadcasted_iota(jnp.int32, (8, 128), 0) == lax.broadcasted_iota(
        jnp.int32, (8, 128), 1
    )
    gain_rows[...] = lax.dot_general(
        pick.astype(WIDE).astype(LOW), gain_block, CONTRACT_LAST, preferred_element_type=WIDE
    )
    keep(full_q, out_q)
    keep(gain_rows, out_gains)
    tokens.finish()
    keep(all_tok.at[p.slot], out_tok)

    def norm_slot(slot, carry):
        def some(rows):
            unit, _ = rms_parts(all_tok[slot, rows, :].astype(WIDE))
            there = pl.ds(pl.multiple_of(slot * rows_own + rows.start, CHUNK), CHUNK)
            normed_one[there, :] = (unit * gain_rows[pl.ds(0, 1), :]).astype(LOW)

        by_rows(rows_own, some)
        return carry

    lax.fori_loop(0, 8, norm_slot, 0)
    keep(normed_one, out_normed)
    move_g.spread(0)

    def project(part, carry):
        rows = pl.ds(pl.multiple_of(part * 512, 512), 512)
        for kind in range(3):
            weight = full_q[:, :, pl.ds(kind * step_q, step_q)].reshape(-1, step_q)
            made = jnp.dot(normed_one[rows, :], weight, preferred_element_type=WIDE)
            if kind < 2:
                made = turn(
                    made,
                    jnp.concatenate([cosines[rows, :]] * 2, axis=1),
                    jnp.concatenate([sines[rows, :]] * 2, axis=1),
                )
            qkv[kind, rows, :] = made.astype(LOW)
        return carry

    lax.fori_loop(0, seq_len // 512, project, 0)
    keep(qkv, out_qkv)
    heads[...] = jnp.zeros_like(heads)

    def one_head(head, carry):
        attend_head(head, qkv, heads)
        return carry

    lax.fori_loop(0, 4, one_head, 0)
    attended[...] = heads[...].astype(LOW)
    keep(attended, out_attended)
    out_copy(2).wait_recv()
    out_copy(3).wait_recv()
    keep(full_o, out_o)
    out_weight = lambda: full_o[...].reshape(-1, full_o.shape[2])

    def project_out(part, carry):
        rows = pl.ds(pl.multiple_of(part * 256, 256), 256)
        made = jnp.dot(attended[rows, :], out_weight(), preferred_element_type=WIDE)
        partial[pl.ds(2 * part, 2)] = made.astype(LOW).reshape(2, rows_own, -1)
        return carry

    lax.fori_loop(0, seq_len // 256, project_out, 0)

    part_rows = [pl.ds(0, rows_own // 2), pl.ds(rows_own // 2, rows_own // 2)]
    sums = [
        LineScatter(p, partial, *buffers, sem, rows) for sem, rows in zip((sum_a, sum_b), part_rows)
    ]
    gathers = [
        LineGather(p, normed_two, sem, mine.at[rows], rows)
        for sem, rows in zip((gather_a, gather_b), part_rows)
    ]

    def local(part):
        def some(rows):
            there = pl.ds(pl.multiple_of(part * (rows_own // 2) + rows.start, CHUNK), CHUNK)
            total = all_tok[p.slot, there, :].astype(WIDE) + sums[part].total(there)
            residual[there, :] = total
            unit, _ = rms_parts(total)
            mine[there, :] = (unit * gain_rows[pl.ds(1, 1), :]).astype(LOW)

        by_rows(rows_own // 2, some)

    for part in sums:
        part.start()
    for part in sums:
        part.head()
    move_d.start()
    for index in range(3):
        sums[0].step(index)
    for step in range(1, 4):
        move_g.spread(step)
    sums[0].arrive()
    local(0)
    gathers[0].start()
    swap_cot.wait()
    cotangents.start()
    for index in range(3):
        sums[1].step(index)
        gathers[0].step(index + 1)
    for step in range(4, 8):
        move_g.spread(step)
    sums[1].arrive()
    local(1)
    gathers[1].start()
    keep(residual, out_residual)
    for z in range(4):
        move_g.corners(z)
    for step in range(4):
        move_d.spread(step)
    for distance in range(1, 4):
        gathers[1].step(distance)
        cotangents.step(distance)
    for step in range(4, 8):
        move_d.spread(step)
    for z in range(4):
        move_d.corners(z)
    for kind in range(4):
        out_copy(kind).wait_send()
    for part in (swap_tok, swap_cot, swap_out):
        part.drain()
    for part in gathers + [cotangents, move_g, move_d]:
        part.finish()
    for part in gathers + sums + [tokens, cotangents, move_q, move_g, move_d]:
        part.drain()
    for copy in kept:
        copy.wait()


def forward(tokens, cotangent, qkv, gain_columns, gate_up, down, out_rows, cosines, sines):
    rows, width = tokens.shape
    own = qkv.shape[0]
    here = qkv.shape[1] // 24
    q_shape = (32, own, 3 * here + gain_columns.shape[1])
    vmem = lambda shape, dtype=LOW: pltpu.VMEM(shape, dtype)
    outputs = [
        ((8, rows, width), LOW),
        ((8, rows, width), LOW),
        ((32, own, gate_up.shape[1] // 8), LOW),
        ((32, own, down.shape[1] // 8), LOW),
        (q_shape, LOW),
        ((4, own, width), LOW),
        ((8 * rows, width), LOW),
        ((3, 8 * rows, here), LOW),
        ((8 * rows, here), LOW),
        ((rows, width), WIDE),
        ((8, width), WIDE),
        ((rows, width), LOW),
    ]
    return kernel_call(
        forward_kernel,
        "forward",
        1,
        (tokens, cotangent, qkv, gain_columns, gate_up, down, out_rows, cosines, sines),
        [ANYWHERE] * 7 + [IN_VMEM] * 2,
        outputs,
        [ANYWHERE] * len(outputs),
        [
            vmem((8, rows, width)),
            vmem(q_shape),
            vmem((4, own, width)),
            vmem((8 * rows, width)),
            vmem((3, 8 * rows, here)),
            vmem((8 * rows, here), WIDE),
            vmem((8 * rows, here)),
            vmem((rows, width), WIDE),
            vmem((8, width), WIDE),
            vmem((rows, width)),
            vmem((8, rows, width)),
        ]
        + LineScatter.buffers(rows, width)
        + [DMA((3,))] * 3
        + [DMA(LineGather.SEMS)] * 2
        + [DMA(Relayout.SEMS)] * 3
        + [DMA((2, 4))]
        + [DMA(LineScatter.SEMS)] * 2
        + [DMA(LineGather.SEMS)] * 2
        + [DMA((8,))],
    )


def weight_part(place, ref):
    return lambda half, unit, x, y: ref.at[place.block(2 * unit + half, x, y)]


def attend_back(head, qkv, grad_heads, grads):
    pair = lanes(head // 2 * 128, 128)
    mask = head_mask(head)
    for block in range(qkv.shape[1] // QUERY_ROWS):
        rows = pl.ds(block * QUERY_ROWS, QUERY_ROWS)
        keys = pl.ds(0, (block + 1) * QUERY_ROWS)
        queries, grad_rows = qkv[0, rows, pair] * mask, grad_heads[rows, pair] * mask
        key_rows = qkv[1, keys, pair]
        probs = scaled_probs(queries, key_rows, block * QUERY_ROWS)
        grad_probs = lax.dot_general(
            grad_rows, qkv[2, keys, pair], CONTRACT_LAST, preferred_element_type=WIDE
        )
        delta = jnp.sum(probs * grad_probs, axis=1, keepdims=True)
        grad_scores = (probs * (grad_probs - delta) * HEAD_DIM ** (-0.5)).astype(LOW)
        grads[0, rows, pair] += jnp.dot(grad_scores, key_rows * mask, preferred_element_type=WIDE)
        grads[1, keys, pair] += lax.dot_general(
            grad_scores, queries, CONTRACT_FIRST, preferred_element_type=WIDE
        )
        grads[2, keys, pair] += lax.dot_general(
            probs.astype(LOW), grad_rows, CONTRACT_FIRST, preferred_element_type=WIDE
        )


def backward_kernel(
    part_two,
    part_out,
    residual,
    cot,
    gain_rows,
    own_tok,
    full_q,
    full_o,
    qkv,
    attended,
    normed_one,
    cosines,
    sines,
    g_part,
    d_part,
    input_grad,
    block_out,
    q_out,
    g_out,
    d_out,
    o_out,
    work,
    branch,
    own_cot,
    mine,
    grad_residual,
    grad_heads,
    grads,
    grad_projected,
    q_part,
    o_part,
    o_sum,
    *scratch,
):
    buffers, rest = scratch[:4], scratch[4:]
    p = Place()
    rows_own, width = residual.shape
    seq_len = 8 * rows_own
    own = g_part.shape[1]
    units = g_part.shape[0] // 8
    half = own // 2
    step_q, step_g, step_d = q_part.shape[2] // 3, g_part.shape[2] // 2, d_part.shape[2]
    plane_g = PlaneScatter(p, weight_part(p, g_part), units, *rest[:4])
    plane_d = PlaneScatter(p, weight_part(p, d_part), units, *rest[4:8])
    plane_q = PlaneScatter(p, weight_part(p, q_part), units, *rest[8:12])
    plane_o = PlaneScatter(
        p, lambda h, u, x, y: o_part.at[2 * y + x, pl.ds(h * half, half)], 1, *rest[12:16]
    )
    rest = rest[16:]
    sum_sems, gather_sems, return_sems, swap_sems, load_sems, free = (
        rest[:5],
        rest[5:7],
        rest[7:10],
        rest[10:14],
        rest[14],
        rest[15],
    )
    part_rows = [pl.ds(0, rows_own // 2), pl.ds(rows_own // 2, rows_own // 2)]
    sum_two = [
        LineScatter(p, work, *buffers, sem, rows) for sem, rows in zip(sum_sems[:2], part_rows)
    ]
    sum_out = LineScatter(p, work, *buffers, sum_sems[2], pl.ds(0, rows_own))
    sum_one = [
        LineScatter(p, branch, *buffers, sem, rows) for sem, rows in zip(sum_sems[3:], part_rows)
    ]
    gathers = [
        LineGather(p, branch, sem, mine.at[rows], rows)
        for sem, rows in zip(gather_sems, part_rows)
    ]
    return_q = LineReturn(
        p, plane_q, [(i * step_q, step_q, i * 8 * step_q) for i in range(3)], q_out, return_sems[0]
    )
    return_g = LineReturn(
        p, plane_g, [(i * step_g, step_g, i * 8 * step_g) for i in range(2)], g_out, return_sems[1]
    )
    return_d = LineReturn(p, plane_d, [(0, step_d, 0)], d_out, return_sems[2])
    swap_in = [
        Swap(p, grad_residual.at[rows], input_grad.at[rows], input_grad.at[rows], sem)
        for sem, rows in zip(swap_sems[:2], part_rows)
    ]
    swap_block = Swap(p, mine, block_out, block_out, swap_sems[2])
    swap_out = Swap(p, o_sum, o_out, o_out, swap_sems[3])

    def load(source, target, index):
        return pltpu.make_async_copy(source, target, load_sems.at[index])

    def there(part, rows):
        return pl.ds(pl.multiple_of(part * (rows_own // 2) + rows.start, CHUNK), CHUNK)

    load(part_two, work, 0).start()
    load(cot.at[p.slot], own_cot, 1).start()
    p.meet(True)
    plane_g.start()
    load(part_two, work, 0).wait()
    for part in sum_two:
        part.start()
    for part in sum_two:
        part.head()
    load(cot.at[p.slot], own_cot, 1).wait()

    def local_two(part):
        def some(rows):
            spot = there(part, rows)
            unit, inverse = rms_parts(residual[spot, :])
            total = own_cot[spot, :].astype(WIDE) + normed_back(
                sum_two[part].total(spot), unit, inverse, gain_rows[pl.ds(1, 1), :]
            )
            grad_residual[spot, :] = total
            mine[spot, :] = total.astype(LOW)

        by_rows(rows_own // 2, some)

    for index in range(3):
        sum_two[0].step(index)
    sum_two[0].arrive()
    local_two(0)
    gathers[0].start()
    plane_g.middle(0)
    for index in range(3):
        sum_two[1].step(index)
        gathers[0].step(index + 1)
    sum_two[1].arrive()
    local_two(1)
    gathers[1].start()
    for part in sum_two:
        part.drain()
    load(part_out, work, 0).start()
    for unit in range(1, units):
        plane_g.middle(unit)
    for distance in range(1, 4):
        gathers[1].step(distance)
    for part in gathers:
        part.finish()
    plane_d.start()
    load(part_out, work, 0).wait()
    sum_out.start()

    def back_out(part, carry):
        rows = pl.ds(pl.multiple_of(part * 256, 256), 256)
        made = lax.dot_general(
            branch[pl.ds(2 * part, 2)].reshape(256, width),
            full_o[...].reshape(-1, width),
            CONTRACT_LAST,
            preferred_element_type=WIDE,
        )
        grad_heads[rows, :] = made.astype(LOW)
        return carry

    lax.fori_loop(0, seq_len // 256, back_out, 0)

    def out_grad(part, carry):
        columns = lanes(part * 512, 512)
        made = lax.dot_general(
            attended[...],
            branch[:, :, columns].reshape(seq_len, 512),
            CONTRACT_FIRST,
            preferred_element_type=WIDE,
        )
        o_part[:, :, columns] = made.astype(LOW).reshape(4, own, 512)
        return carry

    lax.fori_loop(0, width // 512, out_grad, 0)
    plane_o.start()
    sum_out.head()
    for part in gathers:
        part.drain()
    grads[...] = jnp.zeros_like(grads)

    def one_head(head, carry):
        attend_back(head, qkv, grad_heads, grads)
        plane_g.final(head)
        return_g.send(head)
        return carry

    lax.fori_loop(0, 4, one_head, 0)
    for index in range(3):
        sum_out.step(index)
    for unit in range(units):
        plane_d.middle(unit)
    plane_o.middle(0)

    def back_turn(part, carry):
        rows = pl.ds(pl.multiple_of(part * 256, 256), 256)
        for kind in range(3):
            made = grads[kind, rows, :]
            if kind < 2:
                made = turn(
                    made,
                    jnp.concatenate([cosines[rows, :]] * 2, axis=1),
                    jnp.concatenate([-sines[rows, :]] * 2, axis=1),
                )
            grad_projected[rows, pl.ds(kind * step_q, step_q)] = made.astype(LOW)
        return carry

    lax.fori_loop(0, seq_len // 256, back_turn, 0)

    def back_qkv(part, carry):
        weight = full_q[pl.ds(part * 8, 8), :, pl.ds(0, 3 * step_q)].reshape(8 * own, 3 * step_q)
        for block in range(seq_len // 512):
            made = lax.dot_general(
                grad_projected[pl.ds(block * 512, 512), :],
                weight,
                CONTRACT_LAST,
                preferred_element_type=WIDE,
            )
            branch[pl.ds(block * 4, 4), :, lanes(part * 8 * own, 8 * own)] = made.astype(
                LOW
            ).reshape(4, rows_own, 8 * own)
        return carry

    lax.fori_loop(0, 4, back_qkv, 0)
    sum_out.arrive()

    def local_out(rows):
        mine[rows, :] = (residual[rows, :] + sum_out.total(rows)).astype(LOW)

    by_rows(rows_own, local_out)
    swap_block.start()
    sum_out.drain()
    load(normed_one, work, 0).start()
    signal = lambda index, **place: pl.semaphore_signal(
        free.at[index], inc=1, device_id=place, device_id_type=pl.DeviceIdType.MESH
    )
    signal(0, c=1 - p.c)
    pl.when(p.z < 3)(lambda: signal(1, z=p.z + 1))
    pl.when(p.z > 0)(lambda: signal(2, z=p.z - 1))
    pl.semaphore_wait(free.at[0], 1)
    pl.when(p.z > 0)(lambda: pl.semaphore_wait(free.at[1], 1))
    pl.when(p.z < 3)(lambda: pl.semaphore_wait(free.at[2], 1))
    for part in sum_one:
        part.start()
    load(normed_one, work, 0).wait()
    for part in sum_one:
        part.head()

    def qkv_grad(part, carry):
        made = lax.dot_general(
            work[:, :, lanes(part * 8 * own, 8 * own)].reshape(seq_len, 8 * own),
            grad_projected[...],
            CONTRACT_FIRST,
            preferred_element_type=WIDE,
        )
        q_part[pl.ds(part * 8, 8)] = made.astype(LOW).reshape(8, own, 3 * step_q)
        return carry

    lax.fori_loop(0, 4, qkv_grad, 0)
    plane_q.start()

    def local_one(part):
        def some(rows):
            spot = there(part, rows)
            unit, inverse = rms_parts(own_tok[spot, :].astype(WIDE))
            grad_residual[spot, :] = grad_residual[spot, :] + normed_back(
                sum_one[part].total(spot), unit, inverse, gain_rows[pl.ds(0, 1), :]
            )

        by_rows(rows_own // 2, some)

    for index in range(3):
        sum_one[0].step(index)
    sum_one[0].arrive()
    local_one(0)
    swap_in[0].start()
    for unit in range(units):
        plane_d.final(unit)
        return_d.send(unit)
    for index in range(3):
        sum_one[1].step(index)
    for unit in range(units):
        plane_q.middle(unit)
    plane_o.final(0)
    for h in range(2):
        o_sum[pl.ds(h * half, half), :] = plane_o.held[h, 1, 0]
    swap_out.start()
    sum_one[1].arrive()
    local_one(1)
    swap_in[1].start()
    for unit in range(units):
        plane_q.final(unit)
        return_q.send(unit)
    for part in (return_g, return_d, return_q):
        part.finish()
    for part in swap_in + [swap_block, swap_out]:
        part.wait()
        part.drain()
    for part in sum_one + [plane_g, plane_d, plane_q, plane_o]:
        part.drain()


def backward(
    part_two,
    part_out,
    residual,
    cot,
    gain_rows,
    own_tok,
    full_q,
    full_o,
    qkv,
    attended,
    normed_one,
    cosines,
    sines,
    g_part,
    d_part,
):
    _, rows, width = part_two.shape
    own, here = full_o.shape[1], attended.shape[1]
    units = g_part.shape[0] // 8
    vmem = lambda shape, dtype=LOW: pltpu.VMEM(shape, dtype)
    step_g, step_d = g_part.shape[2], d_part.shape[2]
    return kernel_call(
        backward_kernel,
        "backward",
        2,
        (
            part_two,
            part_out,
            residual,
            cot,
            gain_rows,
            own_tok,
            full_q,
            full_o,
            qkv,
            attended,
            normed_one,
            cosines,
            sines,
            g_part,
            d_part,
        ),
        [ANYWHERE] * 2
        + [IN_VMEM]
        + [ANYWHERE]
        + [IN_VMEM] * 6
        + [ANYWHERE]
        + [IN_VMEM] * 2
        + [ANYWHERE] * 2,
        [
            ((rows, width), WIDE),
            ((rows, width), LOW),
            ((own, 24 * here), LOW),
            ((own, 8 * step_g), LOW),
            ((own, 8 * step_d), LOW),
            ((own, width), LOW),
        ],
        [ANYWHERE] * 6,
        [
            vmem((8, rows, width)),
            vmem((8, rows, width)),
            vmem((rows, width)),
            vmem((rows, width)),
            vmem((rows, width), WIDE),
            vmem((8 * rows, here)),
            vmem((3, 8 * rows, here), WIDE),
            vmem((8 * rows, 3 * here)),
            vmem((32, own, 3 * here)),
            vmem((4, own, width)),
            vmem((own, width)),
        ]
        + LineScatter.buffers(rows, width)
        + PlaneScatter.scratch(units, own, step_g)
        + PlaneScatter.scratch(units, own, step_d)
        + PlaneScatter.scratch(units, own, 3 * here)
        + PlaneScatter.scratch(1, own // 2, width)
        + [DMA(LineScatter.SEMS)] * 5
        + [DMA(LineGather.SEMS)] * 2
        + [DMA(LineReturn.SEMS)] * 3
        + [DMA((3,))] * 4
        + [DMA((2,)), pltpu.SemaphoreType.REGULAR((3,))],
    )


def grid_shards(
    tokens,
    cotangent,
    qkv_weight,
    out_weight,
    gate_up_weight,
    down_weight,
    gains,
    qkv_first,
    out_first,
    gate_up_first,
    down_first,
    gains_first,
    qkv_second,
    out_second,
    gate_up_second,
    down_second,
    gains_second,
):
    rows, width = tokens.shape[1:]
    seq_len = 8 * rows
    gain_columns = jnp.pad(gains.astype(LOW).T, ((0, 0), (0, 126)))
    cosines, sines = rope_tables(jnp.arange(seq_len, dtype=jnp.int32))
    cosines, sines = (
        jnp.tile(cosines[:, 0], (1, 4)),
        jnp.tile(jnp.concatenate([-sines[:, 0], sines[:, 0]], axis=1), (1, 2)),
    )
    (
        grad_out,
        normed_two,
        gate_up_full,
        down_full,
        qkv_full,
        out_full,
        normed_one,
        qkv_heads,
        attended,
        residual,
        gain_full,
        own_tokens,
    ) = forward(
        tokens[0],
        cotangent[0],
        qkv_weight.astype(LOW),
        gain_columns,
        gate_up_weight.astype(LOW),
        down_weight.astype(LOW),
        out_weight.astype(LOW),
        cosines,
        sines,
    )
    all_grad = grad_out
    grad_out, normed_two = grad_out.reshape(-1, width), normed_two.reshape(-1, width)
    gate_up_full = gate_up_full.reshape(width, -1)
    down_full = down_full.reshape(width, -1)
    gate_up = jnp.dot(normed_two, gate_up_full, preferred_element_type=WIDE)
    ff_here = gate_up.shape[1] // 2
    gate_vals = gate_up[:, :ff_here]
    up_vals = gate_up[:, ff_here:]
    sigmoid_gate = jax.nn.sigmoid(gate_vals)
    activated = (gate_vals * sigmoid_gate * up_vals).astype(LOW)
    mlp_out = lax.dot_general(
        activated, down_full, CONTRACT_LAST, preferred_element_type=WIDE
    ).astype(LOW)

    grad_act = jnp.dot(grad_out, down_full, preferred_element_type=WIDE)
    grad_gate = grad_act * up_vals * sigmoid_gate * (1.0 + gate_vals * (1.0 - sigmoid_gate))
    grad_up = grad_act * gate_vals * sigmoid_gate
    grad_gate_up = jnp.concatenate([grad_gate, grad_up], axis=1).astype(LOW)
    grad_normed_two = lax.dot_general(
        grad_gate_up, gate_up_full, CONTRACT_LAST, preferred_element_type=WIDE
    ).astype(LOW)
    gate_up_part = lax.dot_general(
        normed_two, grad_gate_up, CONTRACT_FIRST, preferred_element_type=WIDE
    ).astype(LOW)
    down_part = lax.dot_general(
        grad_out, activated, CONTRACT_FIRST, preferred_element_type=WIDE
    ).astype(LOW)
    own_rows = qkv_weight.shape[0]
    input_grad, block_out, qkv_sum, gate_up_sum, down_sum, out_sum = backward(
        grad_normed_two.reshape(8, rows, width),
        mlp_out.reshape(8, rows, width),
        residual,
        all_grad,
        gain_full,
        own_tokens,
        qkv_full,
        out_full,
        qkv_heads,
        attended,
        normed_one.reshape(8, rows, width),
        cosines,
        sines,
        gate_up_part.reshape(32, own_rows, -1),
        down_part.reshape(32, own_rows, -1),
    )
    qkv_sum, gate_up_sum, down_sum, out_sum = (
        total.astype(WIDE) for total in (qkv_sum, gate_up_sum, down_sum, out_sum)
    )
    gains_sum = jnp.stack(
        [
            jnp.sum(weight.astype(LOW).astype(WIDE) * total, axis=1)
            for weight, total in ((qkv_weight, qkv_sum), (gate_up_weight, gate_up_sum))
        ],
        axis=0,
    ) / gains.astype(LOW).astype(WIDE)
    wide_rate = 2.5 * D ** (-0.5)
    out_rate = 2.5 * max(D // 512, 1) ** (-0.5)
    down_rate = 2.5 * FF ** (-0.5)
    qkv_new = adam_step(qkv_weight, qkv_sum, qkv_first, qkv_second, wide_rate, WEIGHT_DECAY)
    out_new = adam_step(out_weight, out_sum, out_first, out_second, out_rate, WEIGHT_DECAY)
    gate_up_new = adam_step(
        gate_up_weight, gate_up_sum, gate_up_first, gate_up_second, wide_rate, WEIGHT_DECAY
    )
    down_new = adam_step(
        down_weight, down_sum, down_first, down_second, down_rate, WEIGHT_DECAY
    )
    gains_new = adam_step(gains, gains_sum, gains_first, gains_second, 0.5, 0.0)
    return (
        block_out[None],
        input_grad[None],
        qkv_new[0],
        out_new[0],
        gate_up_new[0],
        down_new[0],
        gains_new[0],
        qkv_new[1],
        out_new[1],
        gate_up_new[1],
        down_new[1],
        gains_new[1],
        qkv_new[2],
        out_new[2],
        gate_up_new[2],
        down_new[2],
        gains_new[2],
    )


def mapped(body, mesh, token_spec, row_spec, gain_spec):
    one_set = (row_spec, row_spec, row_spec, row_spec, gain_spec)
    return jax.shard_map(
        body,
        mesh=mesh,
        in_specs=(token_spec, token_spec) + one_set * 3,
        out_specs=(token_spec, token_spec) + one_set * 3,
        check_vma=False,
    )


def solution(mesh):
    if mesh.shape["seq"] == 8 and mesh.shape["dp"] == 4:
        grid_mesh = Mesh(mesh.devices.reshape(4, 2, 2, 2), GRID)
        return mapped(
            grid_shards,
            grid_mesh,
            P(("y", "c"), ("z", "x"), None),
            P(GRID, None),
            P(None, GRID),
        )
    return mapped(
        shards, mesh, P("dp", "seq", None), P(("seq", "dp"), None), P(None, ("seq", "dp"))
    )
```

```python
import jax
import jax.numpy as jnp
from jax import lax
from jax.experimental import pallas as pl
from jax.experimental.pallas import tpu as pltpu
from jax.sharding import Mesh
from jax.sharding import PartitionSpec as P

D = 2048
HEADS = 32
HEAD_DIM = 64
FF = 8192
BLOCK = 512
STEP = 10


NORM_EPS = 1e-05
ROPE_BASE = 130000.0
BETA_ONE = 0.9
BETA_TWO = 0.999
ADAM_EPS = 1e-08
WEIGHT_DECAY = 0.1
MASKED = -1e30


def rms_parts(values):
    inverse = lax.rsqrt(jnp.mean(values * values, axis=-1, keepdims=True) + NORM_EPS)
    return (values * inverse, inverse)


def rope_tables(positions):
    half_dim = HEAD_DIM // 2
    exponent = jnp.arange(half_dim, dtype=jnp.float32) * (2.0 / HEAD_DIM)
    frequency = ROPE_BASE ** (-exponent)
    angles = positions.astype(jnp.float32)[:, None] * frequency[None, :]
    return (jnp.cos(angles)[:, None, :], jnp.sin(angles)[:, None, :])


def rotate(tensor, cosines, sines):
    half_dim = HEAD_DIM // 2
    lower_half = tensor[..., :half_dim]
    upper_half = tensor[..., half_dim:]
    return jnp.concatenate(
        [lower_half * cosines - upper_half * sines, upper_half * cosines + lower_half * sines],
        axis=-1,
    )


def unrotate(tensor, cosines, sines):
    half_dim = HEAD_DIM // 2
    lower_half = tensor[..., :half_dim]
    upper_half = tensor[..., half_dim:]
    return jnp.concatenate(
        [lower_half * cosines + upper_half * sines, upper_half * cosines - lower_half * sines],
        axis=-1,
    )


def block_scores(query_rows, key_heads, key_id, block_id):
    key_rows = lax.dynamic_slice_in_dim(key_heads, key_id * BLOCK, BLOCK, 0)
    products = jnp.einsum(
        "qhd,khd->hqk", query_rows, key_rows, preferred_element_type=jnp.float32
    ) * HEAD_DIM ** (-0.5)
    local_ids = jnp.arange(BLOCK, dtype=jnp.int32)
    allowed = (key_id < block_id) | (local_ids[None, :] <= local_ids[:, None])
    return jnp.where(allowed[None], products, MASKED)


def row_normalizer(query_rows, key_heads, block_id):
    row_shape = (query_rows.shape[1], BLOCK, 1)

    def absorb(key_id, state):
        running_max, running_total = state
        scores = block_scores(query_rows, key_heads, key_id, block_id)
        new_max = jnp.maximum(running_max, jnp.max(scores, axis=-1, keepdims=True))
        running_total = running_total * jnp.exp(running_max - new_max) + jnp.sum(
            jnp.exp(scores - new_max), axis=-1, keepdims=True
        )
        return (new_max, running_total)

    start_state = (jnp.full(row_shape, MASKED, jnp.float32), jnp.zeros(row_shape, jnp.float32))
    final_max, final_total = lax.fori_loop(0, block_id + 1, absorb, start_state)
    return final_max + jnp.log(final_total)


def attend_forward(query_heads, key_heads, value_heads):
    seq_len, heads_here, head_dim = query_heads.shape

    def one_block(block_id, carry):
        out_all, lse_all = carry
        row_start = block_id * BLOCK
        query_rows = lax.dynamic_slice_in_dim(query_heads, row_start, BLOCK, 0)
        row_lse = row_normalizer(query_rows, key_heads, block_id)

        def weigh_values(key_id, running):
            scores = block_scores(query_rows, key_heads, key_id, block_id)
            weights_low = jnp.exp(scores - row_lse).astype(jnp.bfloat16)
            value_rows = lax.dynamic_slice_in_dim(value_heads, key_id * BLOCK, BLOCK, 0)
            return running + jnp.einsum(
                "hqk,khd->qhd", weights_low, value_rows, preferred_element_type=jnp.float32
            )

        attended = lax.fori_loop(
            0, block_id + 1, weigh_values, jnp.zeros((BLOCK, heads_here, head_dim), jnp.float32)
        )
        out_all = lax.dynamic_update_slice_in_dim(
            out_all, attended.astype(jnp.bfloat16), row_start, 0
        )
        lse_all = lax.dynamic_update_slice_in_dim(lse_all, row_lse, row_start, 1)
        return (out_all, lse_all)

    start_carry = (
        jnp.zeros((seq_len, heads_here, head_dim), jnp.bfloat16),
        jnp.zeros((heads_here, seq_len, 1), jnp.float32),
    )
    return lax.fori_loop(0, seq_len // BLOCK, one_block, start_carry)


def attend_backward(query_heads, key_heads, value_heads, grad_heads, lse_all):
    seq_len, heads_here, head_dim = query_heads.shape
    score_scale = HEAD_DIM ** (-0.5)

    def one_block(block_id, carry):
        grad_q_all, grad_k_all, grad_v_all = carry
        row_start = block_id * BLOCK
        query_rows = lax.dynamic_slice_in_dim(query_heads, row_start, BLOCK, 0)
        grad_rows = lax.dynamic_slice_in_dim(grad_heads, row_start, BLOCK, 0)
        row_lse = lax.dynamic_slice_in_dim(lse_all, row_start, BLOCK, 1)

        def probs_and_grads(key_id):
            scores = block_scores(query_rows, key_heads, key_id, block_id)
            probs = jnp.exp(scores - row_lse)
            value_rows = lax.dynamic_slice_in_dim(value_heads, key_id * BLOCK, BLOCK, 0)
            grad_probs = jnp.einsum(
                "qhd,khd->hqk", grad_rows, value_rows, preferred_element_type=jnp.float32
            )
            return (probs, grad_probs)

        def add_delta(key_id, running):
            probs, grad_probs = probs_and_grads(key_id)
            return running + jnp.sum(probs * grad_probs, axis=-1, keepdims=True)

        row_delta = lax.fori_loop(
            0, block_id + 1, add_delta, jnp.zeros((heads_here, BLOCK, 1), jnp.float32)
        )

        def spread(key_id, inner):
            grad_q_rows, grad_k_acc, grad_v_acc = inner
            probs, grad_probs = probs_and_grads(key_id)
            key_start = key_id * BLOCK
            key_rows = lax.dynamic_slice_in_dim(key_heads, key_start, BLOCK, 0)
            grad_scores = (probs * (grad_probs - row_delta) * score_scale).astype(jnp.bfloat16)
            grad_q_rows = grad_q_rows + jnp.einsum(
                "hqk,khd->qhd", grad_scores, key_rows, preferred_element_type=jnp.float32
            )
            grad_k_part = jnp.einsum(
                "hqk,qhd->khd", grad_scores, query_rows, preferred_element_type=jnp.float32
            )
            grad_v_part = jnp.einsum(
                "hqk,qhd->khd",
                probs.astype(jnp.bfloat16),
                grad_rows,
                preferred_element_type=jnp.float32,
            )
            grad_k_acc = lax.dynamic_update_slice_in_dim(
                grad_k_acc,
                lax.dynamic_slice_in_dim(grad_k_acc, key_start, BLOCK, 0) + grad_k_part,
                key_start,
                0,
            )
            grad_v_acc = lax.dynamic_update_slice_in_dim(
                grad_v_acc,
                lax.dynamic_slice_in_dim(grad_v_acc, key_start, BLOCK, 0) + grad_v_part,
                key_start,
                0,
            )
            return (grad_q_rows, grad_k_acc, grad_v_acc)

        start_inner = (
            jnp.zeros((BLOCK, heads_here, head_dim), jnp.float32),
            grad_k_all,
            grad_v_all,
        )
        grad_q_rows, grad_k_all, grad_v_all = lax.fori_loop(0, block_id + 1, spread, start_inner)
        grad_q_all = lax.dynamic_update_slice_in_dim(grad_q_all, grad_q_rows, row_start, 0)
        return (grad_q_all, grad_k_all, grad_v_all)

    zeros_all = jnp.zeros((seq_len, heads_here, head_dim), jnp.float32)
    return lax.fori_loop(0, seq_len // BLOCK, one_block, (zeros_all, zeros_all, zeros_all))


def adam_step(weight, gradient, first, second, rate, decay):
    new_first = BETA_ONE * first + (1.0 - BETA_ONE) * gradient
    new_second = BETA_TWO * second + (1.0 - BETA_TWO) * gradient * gradient
    first_hat = new_first / (1.0 - BETA_ONE**STEP)
    second_hat = new_second / (1.0 - BETA_TWO**STEP)
    new_weight = weight - rate * (first_hat / (jnp.sqrt(second_hat) + ADAM_EPS) + decay * weight)
    return (new_weight, new_first, new_second)


def shards(
    tokens,
    cotangent,
    qkv_weight,
    out_weight,
    gate_up_weight,
    down_weight,
    gains,
    qkv_first,
    out_first,
    gate_up_first,
    down_first,
    gains_first,
    qkv_second,
    out_second,
    gate_up_second,
    down_second,
    gains_second,
):
    seq_count = lax.axis_size("seq")
    tok_rows = tokens.shape[1]
    width = tokens.shape[2]
    seq_len = tok_rows * seq_count
    heads_here = HEADS // seq_count
    width_here = heads_here * HEAD_DIM
    contract_last = (((1,), (1,)), ((), ()))
    contract_first = (((0,), (0,)), ((), ()))
    qkv_full, proj_full, gain_full = (
        lax.all_gather(qkv_weight.astype(jnp.bfloat16), ("seq", "dp"), axis=0, tiled=True),
        lax.all_gather(out_weight.astype(jnp.bfloat16), ("seq", "dp"), axis=0, tiled=True),
        lax.all_gather(gains.astype(jnp.bfloat16), ("seq", "dp"), axis=1, tiled=True),
    )
    up_full, down_full = (
        lax.all_gather(gate_up_weight.astype(jnp.bfloat16), ("seq", "dp"), axis=0, tiled=True),
        lax.all_gather(down_weight.astype(jnp.bfloat16), ("seq", "dp"), axis=0, tiled=True),
    )
    hidden_in = tokens[0].astype(jnp.float32)
    unit_one, inverse_one = rms_parts(hidden_in)
    normed_one = (unit_one * gain_full[0].astype(jnp.float32)).astype(jnp.bfloat16)
    projected = jnp.einsum(
        "te,ecd->ctd",
        normed_one,
        qkv_full.reshape(width, 3, width),
        preferred_element_type=jnp.float32,
    )
    positions = lax.axis_index("seq") * tok_rows + jnp.arange(tok_rows, dtype=jnp.int32)
    cos_local, sin_local = rope_tables(positions)
    turned = rotate(projected[:2].reshape(2, tok_rows, HEADS, HEAD_DIM), cos_local, sin_local)
    packed = jnp.concatenate([turned.reshape(2, tok_rows, width), projected[2:]], axis=0).astype(
        jnp.bfloat16
    )
    by_heads = lax.all_to_all(packed, "seq", split_axis=2, concat_axis=1, tiled=True)
    query_heads = by_heads[0].reshape(seq_len, heads_here, HEAD_DIM)
    key_heads = by_heads[1].reshape(seq_len, heads_here, HEAD_DIM)
    value_heads = by_heads[2].reshape(seq_len, heads_here, HEAD_DIM)
    out_heads, lse_all = attend_forward(query_heads, key_heads, value_heads)
    attended = lax.all_to_all(
        out_heads.reshape(seq_len, width_here), "seq", split_axis=0, concat_axis=1, tiled=True
    )
    residual = hidden_in + jnp.dot(attended, proj_full, preferred_element_type=jnp.float32)
    unit_two, inverse_two = rms_parts(residual)
    normed_two = (unit_two * gain_full[1].astype(jnp.float32)).astype(jnp.bfloat16)
    gate_up = jnp.dot(normed_two, up_full, preferred_element_type=jnp.float32)
    gate_vals = gate_up[:, :FF]
    up_vals = gate_up[:, FF:]
    sigmoid_gate = jax.nn.sigmoid(gate_vals)
    activated = (gate_vals * sigmoid_gate * up_vals).astype(jnp.bfloat16)
    mlp_out = lax.dot_general(
        activated, down_full, contract_last, preferred_element_type=jnp.float32
    )
    block_out = (residual + mlp_out).astype(jnp.bfloat16)[None]
    back_up, back_down, back_gain = (
        lax.all_gather(gate_up_weight.astype(jnp.bfloat16), ("seq", "dp"), axis=0, tiled=True),
        lax.all_gather(down_weight.astype(jnp.bfloat16), ("seq", "dp"), axis=0, tiled=True),
        lax.all_gather(gains.astype(jnp.bfloat16), ("seq", "dp"), axis=1, tiled=True),
    )
    grad_out = cotangent[0]
    grad_act = jnp.dot(grad_out, back_down, preferred_element_type=jnp.float32)
    grad_gate = grad_act * up_vals * sigmoid_gate * (1.0 + gate_vals * (1.0 - sigmoid_gate))
    grad_up = grad_act * gate_vals * sigmoid_gate
    grad_gate_up = jnp.concatenate([grad_gate, grad_up], axis=1).astype(jnp.bfloat16)
    grad_normed_two = lax.dot_general(
        grad_gate_up, back_up, contract_last, preferred_element_type=jnp.float32
    )
    gain_two_grad = jnp.sum(grad_normed_two * unit_two, axis=0)
    grad_unit_two = grad_normed_two * back_gain[1].astype(jnp.float32)
    grad_residual = grad_out.astype(jnp.float32) + inverse_two * (
        grad_unit_two - unit_two * jnp.mean(grad_unit_two * unit_two, axis=-1, keepdims=True)
    )
    gate_up_rows = lax.dot_general(
        normed_two, grad_gate_up, contract_first, preferred_element_type=jnp.float32
    )
    down_rows = lax.dot_general(
        grad_out, activated, contract_first, preferred_element_type=jnp.float32
    )
    mlp_grad = lax.psum_scatter(
        jnp.concatenate([gate_up_rows, down_rows], axis=1),
        ("seq", "dp"),
        scatter_dimension=0,
        tiled=True,
    )
    back_qkv, back_proj = (
        lax.all_gather(qkv_weight.astype(jnp.bfloat16), ("seq", "dp"), axis=0, tiled=True),
        lax.all_gather(out_weight.astype(jnp.bfloat16), ("seq", "dp"), axis=0, tiled=True),
    )
    grad_branch = grad_residual.astype(jnp.bfloat16)
    proj_grad = lax.dot_general(
        attended, grad_branch, contract_first, preferred_element_type=jnp.float32
    )
    grad_attended = lax.dot_general(
        grad_branch, back_proj, contract_last, preferred_element_type=jnp.float32
    ).astype(jnp.bfloat16)
    grad_heads = lax.all_to_all(
        grad_attended, "seq", split_axis=1, concat_axis=0, tiled=True
    ).reshape(seq_len, heads_here, HEAD_DIM)
    grad_q_all, grad_k_all, grad_v_all = attend_backward(
        query_heads, key_heads, value_heads, grad_heads, lse_all
    )
    cos_whole, sin_whole = rope_tables(jnp.arange(seq_len, dtype=jnp.int32))
    grad_pack = jnp.stack(
        [
            unrotate(grad_q_all, cos_whole, sin_whole).reshape(seq_len, width_here),
            unrotate(grad_k_all, cos_whole, sin_whole).reshape(seq_len, width_here),
            grad_v_all.reshape(seq_len, width_here),
        ],
        axis=0,
    ).astype(jnp.bfloat16)
    grad_projected = lax.all_to_all(grad_pack, "seq", split_axis=1, concat_axis=2, tiled=True)
    qkv_cube = back_qkv.reshape(width, 3, width)
    grad_normed_one = jnp.einsum(
        "ctd,ecd->te", grad_projected, qkv_cube, preferred_element_type=jnp.float32
    )
    qkv_grad = jnp.einsum(
        "te,ctd->ecd", normed_one, grad_projected, preferred_element_type=jnp.float32
    ).reshape(width, 3 * width)
    gain_one_grad = jnp.sum(grad_normed_one * unit_one, axis=0)
    grad_unit_one = grad_normed_one * back_gain[0].astype(jnp.float32)
    input_grad = grad_residual + inverse_one * (
        grad_unit_one - unit_one * jnp.mean(grad_unit_one * unit_one, axis=-1, keepdims=True)
    )
    gains_grad = jnp.stack([gain_one_grad, gain_two_grad], axis=0)
    qkv_sum, proj_sum, gains_sum = (
        lax.psum_scatter(qkv_grad, ("seq", "dp"), scatter_dimension=0, tiled=True),
        lax.psum_scatter(proj_grad, ("seq", "dp"), scatter_dimension=0, tiled=True),
        lax.psum_scatter(gains_grad, ("seq", "dp"), scatter_dimension=1, tiled=True),
    )
    wide_rate = 2.5 * D ** (-0.5)
    out_rate = 2.5 * max(D // 512, 1) ** (-0.5)
    down_rate = 2.5 * FF ** (-0.5)
    qkv_new = adam_step(qkv_weight, qkv_sum, qkv_first, qkv_second, wide_rate, WEIGHT_DECAY)
    out_new = adam_step(out_weight, proj_sum, out_first, out_second, out_rate, WEIGHT_DECAY)
    gate_up_new = adam_step(
        gate_up_weight,
        mlp_grad[:, : 2 * FF],
        gate_up_first,
        gate_up_second,
        wide_rate,
        WEIGHT_DECAY,
    )
    down_new = adam_step(
        down_weight, mlp_grad[:, 2 * FF :], down_first, down_second, down_rate, WEIGHT_DECAY
    )
    gains_new = adam_step(gains, gains_sum, gains_first, gains_second, 0.5, 0.0)
    return (
        block_out,
        input_grad[None],
        qkv_new[0],
        out_new[0],
        gate_up_new[0],
        down_new[0],
        gains_new[0],
        qkv_new[1],
        out_new[1],
        gate_up_new[1],
        down_new[1],
        gains_new[1],
        qkv_new[2],
        out_new[2],
        gate_up_new[2],
        down_new[2],
        gains_new[2],
    )


GRID = ("z", "x", "y", "c")
RING = ("z", "c")
PLANE = ("x", "y")
LOW = jnp.bfloat16
WIDE = jnp.float32
CONTRACT_LAST = (((1,), (1,)), ((), ()))
CONTRACT_FIRST = (((0,), (0,)), ((), ()))
DMA = pltpu.SemaphoreType.DMA
ANYWHERE = pl.BlockSpec(memory_space=pl.ANY)
IN_VMEM = pl.BlockSpec(memory_space=pltpu.VMEM)


def remote(source, target, send, receive, **place):
    return pltpu.make_async_remote_copy(
        src_ref=source,
        dst_ref=target,
        send_sem=send,
        recv_sem=receive,
        device_id=place,
        device_id_type=pl.DeviceIdType.MESH,
    )


def lanes(start, size):
    return pl.ds(pl.multiple_of(start, 128), size)


class Place:
    def __init__(self):
        self.z, self.x, self.y, self.c = (lax.axis_index(name) for name in GRID)
        self.slot = 2 * self.z + self.c
        self.block_here = self.block(self.slot, self.x, self.y)

    def block(self, slot, x, y):
        return (((slot // 2) * 2 + x) * 2 + y) * 2 + lax.rem(slot, 2)

    def meet(self, plane):
        barrier = pltpu.get_barrier_semaphore()
        others = [
            {"z": slot // 2, "c": lax.rem(slot, 2)}
            for slot in (lax.rem(self.slot + step, 8) for step in range(1, 8))
        ]
        if plane:
            others += [{"x": 1 - self.x}, {"y": 1 - self.y}, {"x": 1 - self.x, "c": 1 - self.c}]
        for other in others:
            pl.semaphore_signal(
                barrier, inc=1, device_id=other, device_id_type=pl.DeviceIdType.MESH
            )
        pl.semaphore_wait(barrier, len(others))


class Swap:
    def __init__(self, place, source, spot_there, spot_here, sems):
        p = self.place = place
        self.away = lambda: remote(
            source, spot_there, sems.at[0], sems.at[1], x=1 - p.x, c=1 - p.c
        )
        self.here = lambda: pltpu.make_async_copy(source, spot_here, sems.at[2])

    def start(self):
        p = self.place
        pl.when(p.x != p.c)(lambda: self.away().start())
        pl.when(p.x == p.c)(lambda: self.here().start())

    def wait(self):
        p = self.place
        pl.when(p.x != p.c)(lambda: self.away().wait_recv())
        pl.when(p.x == p.c)(lambda: self.here().wait())

    def drain(self):
        p = self.place
        pl.when(p.x != p.c)(lambda: self.away().wait_send())


class LineGather:
    SEMS = (4, 8)

    def __init__(self, place, buffer, sems, mine=None, rows=None):
        self.place, self.sems, self.mine = place, sems, mine
        self.spot = (lambda slot: buffer.at[slot]) if rows is None else (lambda slot: buffer.at[slot, rows])

    def copy(self, slot, way, own=False):
        p, block = self.place, self.spot(slot)
        if way == 0:
            where = {"z": jnp.minimum(p.z + 1, 3)}
        elif way == 1:
            where = {"z": jnp.maximum(p.z - 1, 0)}
        else:
            where = {"c": 1 - p.c}
        source = self.mine if own and self.mine is not None else block
        return remote(source, block, self.sems.at[way, slot], self.sems.at[3, slot], **where)

    def _pass_on(self, slot, way, own=False):
        p = self.place
        if way == 0:
            pl.when(p.z < 3)(lambda: self.copy(slot, 0, own).start())
        elif way == 1:
            pl.when(p.z > 0)(lambda: self.copy(slot, 1, own).start())

    def start(self):
        slot = self.place.slot
        self._pass_on(slot, 0, True)
        self._pass_on(slot, 1, True)
        self.copy(slot, 2, True).start()
        if self.mine is not None:
            self.keep().start()

    def keep(self):
        slot = self.place.slot
        return pltpu.make_async_copy(self.mine, self.spot(slot), self.sems.at[3, slot])

    def step(self, distance):
        p = self.place

        @pl.when(p.z + distance <= 3)
        def _():
            slot = p.slot + 2 * distance
            self.copy(slot, 2).wait_recv()
            self._pass_on(slot, 1)
            self.copy(slot, 2).start()

        @pl.when(p.z >= distance)
        def _():
            slot = p.slot - 2 * distance
            self.copy(slot, 2).wait_recv()
            self._pass_on(slot, 0)
            self.copy(slot, 2).start()

    def finish(self):
        p = self.place
        if self.mine is not None:
            self.keep().wait()
        for z in range(4):
            self.copy(2 * z + 1 - p.c, 2).wait_recv()

    def drain(self):
        p = self.place
        for z in range(4):
            slot = 2 * z + p.c
            self.copy(slot, 2).wait_send()
            pl.when((z <= p.z) & (p.z < 3))(lambda: self.copy(slot, 0).wait_send())
            pl.when((z >= p.z) & (p.z > 0))(lambda: self.copy(slot, 1).wait_send())


def add_blocks(target, sources):
    def some(step, carry):
        rows = pl.ds(pl.multiple_of(step * 16, 16), 16)
        total = sources[0][rows, :].astype(WIDE)
        for source in sources[1:]:
            total = total + source[rows, :].astype(WIDE)
        target[rows, :] = total.astype(target.dtype)
        return carry

    lax.fori_loop(0, target.shape[0] // 16, some, 0)


class LineScatter:
    SEMS = (6, 4)

    @staticmethod
    def buffers(rows, width):
        return [pltpu.VMEM((4, rows, width), LOW), pltpu.VMEM((5, rows, width), LOW)]

    def __init__(self, place, partial, across, passing, sems, rows):
        self.place, self.partial, self.sems, self.rows = place, partial, sems, rows
        self.across, self.passing = across, passing

    def cross(self, z):
        p = self.place
        return remote(
            self.partial.at[2 * z + 1 - p.c, self.rows],
            self.across.at[z, self.rows],
            self.sems.at[0, z],
            self.sems.at[1, z],
            c=1 - p.c,
        )

    def hop(self, z, way, landing):
        p = self.place
        there = jnp.minimum(p.z + 1, 3) if way == 0 else jnp.maximum(p.z - 1, 0)
        return remote(
            self.across.at[z, self.rows],
            self.passing.at[landing, self.rows],
            self.sems.at[2 + 2 * way, z],
            self.sems.at[3 + 2 * way, z],
            z=there,
        )

    def send(self, z, way):
        p = self.place
        if way == 0:
            self.hop(z, 0, z).start()
        else:
            pl.when(p.z - 1 == z)(lambda: self.hop(z, 1, 4).start())
            pl.when(p.z - 1 != z)(lambda: self.hop(z, 1, z).start())

    def start(self):
        for z in range(4):
            self.cross(z).start()

    def head(self):
        p = self.place
        for z in range(4):
            self.cross(z).wait_recv()
        for way, end in ((0, 0), (1, 3)):

            @pl.when(p.z == end)
            def _():
                for index in range(3):
                    z = 3 - index if way == 0 else index
                    spot = self.across.at[z, self.rows]
                    add_blocks(spot, [self.partial.at[2 * z + p.c, self.rows], spot])
                    self.send(z, way)

    def step(self, index):
        p = self.place
        for way, z in ((0, 3 - index), (1, index)):
            inside = (p.z < z) & (p.z > 0) if way == 0 else (p.z > z) & (p.z < 3)

            @pl.when(inside)
            def _():
                self.hop(z, way, z).wait_recv()
                spot = self.across.at[z, self.rows]
                add_blocks(
                    spot,
                    [
                        self.partial.at[2 * z + p.c, self.rows],
                        spot,
                        self.passing.at[z, self.rows],
                    ],
                )
                self.send(z, way)

    def arrive(self):
        p = self.place
        pl.when(p.z > 0)(lambda: self.hop(p.z, 0, p.z).wait_recv())
        pl.when(p.z < 3)(lambda: self.hop(p.z, 1, 4).wait_recv())
        for end, landing in ((0, 0), (3, 4)):

            @pl.when(p.z == end)
            def _():
                spot = self.passing.at[landing, self.rows]
                spot[...] = jnp.zeros(spot.shape, LOW)

    def total(self, rows):
        p = self.place
        parts = (
            self.partial[p.slot, rows, :],
            self.across[p.z, rows, :],
            self.passing[p.z, rows, :],
            self.passing[4, rows, :],
        )
        return sum(part.astype(WIDE) for part in parts)

    def drain(self):
        p = self.place
        for z in range(4):
            self.cross(z).wait_send()
            pl.when(p.z < z)(lambda: self.hop(z, 0, z).wait_send())
            pl.when(p.z > z)(lambda: self.hop(z, 1, z).wait_send())


class Relayout:
    SEMS = (8, 8)

    def __init__(self, place, parts, target, sems):
        self.place, self.parts, self.target, self.sems = place, parts, target, sems

    def sem(self, kind, slot):
        return self.sems.at[kind, slot]

    def line(self, step):
        p = self.place
        slot = lax.rem(p.slot + step, 8)
        copies = []
        for source, first, size, there in self.parts:
            same_for_all = source.shape[1] == size
            columns = lanes(first if same_for_all else first + size * slot, size)
            piece = source.at[:, columns]
            spot = self.target.at[p.block_here, :, pl.ds(there, size)]
            if step == 0:
                copies.append(pltpu.make_async_copy(piece, spot, self.sem(1, p.slot)))
            else:
                copies.append(
                    remote(
                        piece,
                        spot,
                        self.sem(0, slot),
                        self.sem(1, p.slot),
                        z=slot // 2,
                        c=lax.rem(slot, 2),
                    )
                )
        return copies

    def whole(self, slot):
        p = self.place
        spot = self.target.at[p.block(slot, p.x, p.y)]
        return remote(spot, spot, self.sem(0, slot), self.sem(1, slot), c=1 - p.c)

    def plane(self, slot, x, y, way, send, receive):
        p = self.place
        spot = self.target.at[p.block(slot, x, y)]
        where = {"x": 1 - p.x} if way == 0 else {"y": 1 - p.y}
        return remote(spot, spot, self.sem(send, slot), self.sem(receive, slot), **where)

    def from_own(self, slot, way):
        p = self.place
        return self.plane(slot, p.x, p.y, way, 2 + 2 * way, 3 + 2 * way)

    def corner(self, slot, way):
        p = self.place
        x, y = (p.x, 1 - p.y) if way == 0 else (1 - p.x, p.y)
        return self.plane(slot, x, y, way, 6, 7)

    def start(self, steps=range(8)):
        for step in steps:
            for copy in self.line(step):
                copy.start()

    def spread(self, step):
        p = self.place
        slot = lax.rem(p.slot + 8 - step, 8)
        if isinstance(step, int) and step == 0:
            spot = self.target.at[p.block_here]
            pltpu.make_async_copy(spot, spot, self.sem(1, p.slot)).wait()
        else:
            self.whole(slot).wait_recv()
        for way in range(2):
            self.from_own(slot, way).start()

    def corners(self, z):
        self.from_own(2 * z, 0).wait_recv()
        self.corner(2 * z, 1).start()
        self.from_own(2 * z + 1, 1).wait_recv()
        self.corner(2 * z + 1, 0).start()

    def finish(self):
        for z in range(4):
            self.from_own(2 * z, 1).wait_recv()
            self.from_own(2 * z + 1, 0).wait_recv()
            self.corner(2 * z, 1).wait_recv()
            self.corner(2 * z + 1, 0).wait_recv()

    def drain(self):
        for step in range(1, 8):
            self.whole(lax.rem(self.place.slot + step, 8)).wait_send()
        for z in range(4):
            self.corner(2 * z, 1).wait_send()
            self.corner(2 * z + 1, 0).wait_send()
        for slot in range(8):
            for way in range(2):
                self.from_own(slot, way).wait_send()


class PlaneScatter:
    @staticmethod
    def scratch(units, rows, width):
        shape = (rows, width)
        return [
            pltpu.VMEM((2, 2, units) + shape, LOW),
            pltpu.VMEM((2, units) + shape, LOW),
            DMA((4, 2, 2, units)),
        ]

    def __init__(self, place, part, units, got, last, sems):
        self.place, self.part, self.units = place, part, units
        self.got, self.last, self.sems = got, last, sems

    def pair(self, near):
        p = self.place
        x, y = (p.x, p.y) if near else (1 - p.x, 1 - p.y)
        return ((p.x, y), (x, p.y))

    def own(self, half, near, unit):
        x, y = self.pair(near)[half]
        return self.part(half, unit, x, y)

    def sums(self, half, unit):
        return self.own(half, 1, unit)

    def first(self, half, near, unit):
        p = self.place
        x, y = self.pair(near)[half]
        x, y = (1 - x, y) if half == 0 else (x, 1 - y)
        where = {"x": 1 - p.x} if half == 0 else {"y": 1 - p.y}
        return remote(
            self.part(half, unit, x, y),
            self.got.at[half, near, unit],
            self.sems.at[0, half, near, unit],
            self.sems.at[1, half, near, unit],
            **where,
        )

    def second(self, half, unit):
        p = self.place
        where = {"y": 1 - p.y} if half == 0 else {"x": 1 - p.x}
        return remote(
            self.own(half, 0, unit),
            self.last.at[half, unit],
            self.sems.at[2, half, 0, unit],
            self.sems.at[3, half, 0, unit],
            **where,
        )

    def each(self, call):
        lax.fori_loop(0, self.units, lambda unit, carry: (call(unit), carry)[1], 0)

    def start_unit(self, unit):
        for near in range(2):
            for half in range(2):
                self.first(half, near, unit).start()

    def start(self):
        for near in range(2):

            def begin(unit):
                for half in range(2):
                    self.first(half, near, unit).start()

            self.each(begin)

    def middle(self, unit):
        for half in range(2):
            self.first(half, 0, unit).wait_recv()
            spot = self.own(half, 0, unit)
            add_blocks(spot, [spot, self.got.at[half, 0, unit]])
            self.second(half, unit).start()

    def final(self, unit):
        for half in range(2):
            self.first(half, 1, unit).wait_recv()
            self.second(half, unit).wait_recv()
            spot = self.own(half, 1, unit)
            add_blocks(spot, [spot, self.got.at[half, 1, unit], self.last.at[half, unit]])

    def drain(self):
        def end(unit):
            for half in range(2):
                for near in range(2):
                    self.first(half, near, unit).wait_send()
                self.second(half, unit).wait_send()

        self.each(end)


class LineReturn:
    SEMS = (2, 8)

    def __init__(self, place, sums, parts, target, sems):
        self.place, self.sums, self.parts = place, sums, parts
        self.target, self.sems = target, sems

    def copies(self, z, c, local):
        p = self.place
        made = []
        for here, size, first in self.parts:
            piece = self.sums(c, z).at[:, pl.ds(here, size)]
            spot = self.target.at[:, lanes(first + size * p.slot, size)]
            if local:
                made.append(pltpu.make_async_copy(piece, spot, self.sems.at[1, p.slot]))
            else:
                made.append(
                    remote(
                        piece, spot, self.sems.at[0, 2 * z + c], self.sems.at[1, p.slot], z=z, c=c
                    )
                )
        return made

    def send(self, z):
        p = self.place
        for c in range(2):
            mine = (z == p.z) & (c == p.c)

            @pl.when(mine)
            def _():
                for copy in self.copies(z, c, True):
                    copy.start()

            @pl.when(jnp.logical_not(mine))
            def _():
                for copy in self.copies(z, c, False):
                    copy.start()

    def finish(self):
        p = self.place
        spot = self.sums(0, 0)
        pltpu.make_async_copy(spot, spot, self.sems.at[1, p.slot]).wait()
        for step in range(1, 8):
            slot = lax.rem(p.slot + step, 8)
            whole = remote(
                spot, spot, self.sems.at[0, slot], self.sems.at[1, slot], c=1 - p.c
            )
            whole.wait_recv()
            whole.wait_send()


def kernel_call(kernel, name, number, inputs, in_specs, outputs, out_specs, scratch):
    return pl.pallas_call(
        kernel,
        out_shape=[jax.ShapeDtypeStruct(shape, dtype) for shape, dtype in outputs],
        in_specs=in_specs,
        out_specs=out_specs,
        scratch_shapes=scratch,
        compiler_params=pltpu.CompilerParams(
            collective_id=number, has_side_effects=True, vmem_limit_bytes=60 * 2**20
        ),
        name=name,
    )(*inputs)


CHUNK = 16


def by_rows(count, call):
    def some(step, carry):
        call(pl.ds(pl.multiple_of(step * CHUNK, CHUNK), CHUNK))
        return carry

    lax.fori_loop(0, count // CHUNK, some, 0)


def normed_back(grad_normed, unit, inverse, gain):
    grad_unit = grad_normed * gain
    return inverse * (grad_unit - unit * jnp.mean(grad_unit * unit, axis=-1, keepdims=True))


def turn(values, cosines, sines):
    lane = lax.broadcasted_iota(jnp.int32, values.shape, 1)
    half_dim = HEAD_DIM // 2
    width = values.shape[1]
    partner = jnp.where(
        lax.rem(lane, HEAD_DIM) < half_dim,
        pltpu.roll(values, width - half_dim, 1),
        pltpu.roll(values, half_dim, 1),
    )
    return values * cosines + partner * sines


def head_mask(head):
    lane = lax.broadcasted_iota(jnp.int32, (1, 128), 1)
    return (lane // HEAD_DIM == lax.rem(head, 2)).astype(WIDE).astype(LOW)


def scaled_probs(queries, keys, first_row):
    scores = lax.dot_general(queries, keys, CONTRACT_LAST, preferred_element_type=WIDE)
    scores = scores * HEAD_DIM ** (-0.5)
    row = lax.broadcasted_iota(jnp.int32, scores.shape, 0) + first_row
    column = lax.broadcasted_iota(jnp.int32, scores.shape, 1)
    scores = jnp.where(column <= row, scores, MASKED)
    expo = jnp.exp(scores - jnp.max(scores, axis=1, keepdims=True))
    return expo * (1.0 / jnp.sum(expo, axis=1, keepdims=True))


QUERY_ROWS = 256


def attend_head(head, qkv, total):
    pair = lanes(head // 2 * 128, 128)
    mask = head_mask(head)
    for block in range(qkv.shape[1] // QUERY_ROWS):
        rows = pl.ds(block * QUERY_ROWS, QUERY_ROWS)
        keys = pl.ds(0, (block + 1) * QUERY_ROWS)
        probs = scaled_probs(qkv[0, rows, pair] * mask, qkv[1, keys, pair], block * QUERY_ROWS)
        total[rows, pair] += jnp.dot(
            probs.astype(LOW), qkv[2, keys, pair] * mask, preferred_element_type=WIDE
        )


def forward_kernel(
    tok,
    cot,
    wq,
    gain,
    wg,
    wd,
    wo,
    cosines,
    sines,
    all_cot,
    normed_two,
    full_g,
    full_d,
    out_q,
    out_o,
    out_normed,
    out_qkv,
    out_attended,
    out_residual,
    out_gains,
    out_tok,
    all_tok,
    full_q,
    full_o,
    normed_one,
    qkv,
    heads,
    attended,
    residual,
    gain_rows,
    mine,
    partial,
    *scratch,
):
    buffers, sems = scratch[:2], scratch[2:]
    tok_swap, cot_swap, out_swap, tok_sems, cot_sems, q_sems, g_sems, d_sems = sems[:8]
    o_sems, sum_a, sum_b, gather_a, gather_b, keep_sems = sems[8:]
    p = Place()
    p.meet(True)
    rows_own = tok.shape[0]
    seq_len = 8 * rows_own
    step_q, step_g, step_d = wq.shape[1] // 24, wg.shape[1] // 16, wd.shape[1] // 8
    q_parts = [(wq, i * 8 * step_q, step_q, i * step_q) for i in range(3)]
    q_parts.append((gain, 0, gain.shape[1], 3 * step_q))
    move_q = Relayout(p, q_parts, full_q, q_sems)
    move_g = Relayout(
        p, [(wg, i * 8 * step_g, step_g, i * step_g) for i in range(2)], full_g, g_sems
    )
    move_d = Relayout(p, [(wd, 0, step_d, 0)], full_d, d_sems)
    tokens, cotangents = LineGather(p, all_tok, tok_sems), LineGather(p, all_cot, cot_sems)
    away = 2 * p.z + 1 - p.c
    swap_tok = Swap(p, tok, all_tok.at[away], all_tok.at[p.slot], tok_swap)
    swap_cot = Swap(p, cot, all_cot.at[away], all_cot.at[p.slot], cot_swap)
    swap_out = Swap(p, wo, full_o.at[2 * p.y + 1 - p.x], full_o.at[2 * p.y + p.x], out_swap)
    half = wo.shape[0] // 2

    def out_copy(kind):
        own, beside, above = 2 * p.y + p.x, 2 * p.y + 1 - p.x, 2 * (1 - p.y) + p.x
        send, got = o_sems.at[0, kind], o_sems.at[1, kind]
        if kind < 2:
            where = {"x": 1 - p.x} if kind == 0 else {"y": 1 - p.y}
            return remote(full_o.at[own], full_o.at[own], send, got, **where)
        spot = full_o.at[beside if kind == 2 else above, pl.ds((kind - 2) * half, half)]
        where = {"y": 1 - p.y} if kind == 2 else {"x": 1 - p.x}
        return remote(spot, spot, send, got, **where)

    kept = []

    def keep(source, target):
        copy = pltpu.make_async_copy(source, target, keep_sems.at[len(kept)])
        copy.start()
        kept.append(copy)

    swap_tok.start()
    move_q.start()
    swap_tok.wait()
    tokens.start()
    swap_out.start()
    swap_cot.start()
    for step in range(8):
        move_q.spread(step)
    tokens.step(1)
    swap_out.wait()
    out_copy(0).start()
    out_copy(1).start()
    move_g.start(range(4))
    tokens.step(2)
    for z in range(4):
        move_q.corners(z)
    out_copy(0).wait_recv()
    out_copy(2).start()
    out_copy(1).wait_recv()
    out_copy(3).start()
    tokens.step(3)
    move_g.start(range(4, 8))
    move_g.spread(0)
    move_q.finish()
    columns = full_q.shape[2]
    gain_block = full_q[:, :, pl.ds(3 * step_q, columns - 3 * step_q)].reshape(-1, 128)
    pick = lax.broadcasted_iota(jnp.int32, (8, 128), 0) == lax.broadcasted_iota(
        jnp.int32, (8, 128), 1
    )
    gain_rows[...] = lax.dot_general(
        pick.astype(WIDE).astype(LOW), gain_block, CONTRACT_LAST, preferred_element_type=WIDE
    )
    keep(full_q, out_q)
    keep(gain_rows, out_gains)
    tokens.finish()
    swap_cot.wait()
    cotangents.start()
    keep(all_tok.at[p.slot], out_tok)

    def norm_slot(slot, carry):
        def some(rows):
            unit, _ = rms_parts(all_tok[slot, rows, :].astype(WIDE))
            there = pl.ds(pl.multiple_of(slot * rows_own + rows.start, CHUNK), CHUNK)
            normed_one[there, :] = (unit * gain_rows[pl.ds(0, 1), :]).astype(LOW)

        by_rows(rows_own, some)
        return carry

    lax.fori_loop(0, 8, norm_slot, 0)
    keep(normed_one, out_normed)
    move_g.spread(1)
    move_g.spread(2)

    def project(part, carry):
        rows = pl.ds(pl.multiple_of(part * 512, 512), 512)
        for kind in range(3):
            weight = full_q[:, :, pl.ds(kind * step_q, step_q)].reshape(-1, step_q)
            made = jnp.dot(normed_one[rows, :], weight, preferred_element_type=WIDE)
            if kind < 2:
                made = turn(
                    made,
                    jnp.concatenate([cosines[rows, :]] * 2, axis=1),
                    jnp.concatenate([sines[rows, :]] * 2, axis=1),
                )
            qkv[kind, rows, :] = made.astype(LOW)
        return carry

    lax.fori_loop(0, seq_len // 512, project, 0)
    keep(qkv, out_qkv)
    move_g.spread(3)
    heads[...] = jnp.zeros_like(heads)

    def one_head(head, carry):
        attend_head(head, qkv, heads)
        return carry

    lax.fori_loop(0, 4, one_head, 0)
    attended[...] = heads[...].astype(LOW)
    keep(attended, out_attended)
    out_copy(2).wait_recv()
    out_copy(3).wait_recv()
    keep(full_o, out_o)
    out_weight = lambda: full_o[...].reshape(-1, full_o.shape[2])

    def project_out(part, carry):
        rows = pl.ds(pl.multiple_of(part * 256, 256), 256)
        made = jnp.dot(attended[rows, :], out_weight(), preferred_element_type=WIDE)
        partial[pl.ds(2 * part, 2)] = made.astype(LOW).reshape(2, rows_own, -1)
        return carry

    lax.fori_loop(0, seq_len // 256, project_out, 0)

    part_rows = [pl.ds(0, rows_own // 2), pl.ds(rows_own // 2, rows_own // 2)]
    sums = [
        LineScatter(p, partial, *buffers, sem, rows) for sem, rows in zip((sum_a, sum_b), part_rows)
    ]
    gathers = [
        LineGather(p, normed_two, sem, mine.at[rows], rows)
        for sem, rows in zip((gather_a, gather_b), part_rows)
    ]

    def local(part):
        def some(rows):
            there = pl.ds(pl.multiple_of(part * (rows_own // 2) + rows.start, CHUNK), CHUNK)
            total = all_tok[p.slot, there, :].astype(WIDE) + sums[part].total(there)
            residual[there, :] = total
            unit, _ = rms_parts(total)
            mine[there, :] = (unit * gain_rows[pl.ds(1, 1), :]).astype(LOW)

        by_rows(rows_own // 2, some)

    for part in sums:
        part.start()
    for part in sums:
        part.head()
    cotangents.step(1)
    for step in range(4, 8):
        move_g.spread(step)
    move_d.start()
    for index in range(3):
        sums[0].step(index)
    sums[0].arrive()
    local(0)
    gathers[0].start()
    move_g.corners(0)
    move_g.corners(1)
    cotangents.step(2)
    for index in range(3):
        sums[1].step(index)
        gathers[0].step(index + 1)
    cotangents.step(3)
    sums[1].arrive()
    local(1)
    gathers[1].start()
    keep(residual, out_residual)
    for step in range(8):
        move_d.spread(step)
    for z in range(2, 4):
        move_g.corners(z)
    for distance in range(1, 4):
        gathers[1].step(distance)
    for z in range(4):
        move_d.corners(z)
    for kind in range(4):
        out_copy(kind).wait_send()
    for part in (swap_tok, swap_cot, swap_out):
        part.drain()
    for part in gathers + [cotangents, move_g, move_d]:
        part.finish()
    for part in gathers + sums + [tokens, cotangents, move_q, move_g, move_d]:
        part.drain()
    for copy in kept:
        copy.wait()


def forward(tokens, cotangent, qkv, gain_columns, gate_up, down, out_rows, cosines, sines):
    rows, width = tokens.shape
    own = qkv.shape[0]
    here = qkv.shape[1] // 24
    q_shape = (32, own, 3 * here + gain_columns.shape[1])
    vmem = lambda shape, dtype=LOW: pltpu.VMEM(shape, dtype)
    outputs = [
        ((8, rows, width), LOW),
        ((8, rows, width), LOW),
        ((32, own, gate_up.shape[1] // 8), LOW),
        ((32, own, down.shape[1] // 8), LOW),
        (q_shape, LOW),
        ((4, own, width), LOW),
        ((8 * rows, width), LOW),
        ((3, 8 * rows, here), LOW),
        ((8 * rows, here), LOW),
        ((rows, width), WIDE),
        ((8, width), WIDE),
        ((rows, width), LOW),
    ]
    return kernel_call(
        forward_kernel,
        "forward",
        1,
        (tokens, cotangent, qkv, gain_columns, gate_up, down, out_rows, cosines, sines),
        [ANYWHERE] * 7 + [IN_VMEM] * 2,
        outputs,
        [ANYWHERE] * len(outputs),
        [
            vmem((8, rows, width)),
            vmem(q_shape),
            vmem((4, own, width)),
            vmem((8 * rows, width)),
            vmem((3, 8 * rows, here)),
            vmem((8 * rows, here), WIDE),
            vmem((8 * rows, here)),
            vmem((rows, width), WIDE),
            vmem((8, width), WIDE),
            vmem((rows, width)),
            vmem((8, rows, width)),
        ]
        + LineScatter.buffers(rows, width)
        + [DMA((3,))] * 3
        + [DMA(LineGather.SEMS)] * 2
        + [DMA(Relayout.SEMS)] * 3
        + [DMA((2, 4))]
        + [DMA(LineScatter.SEMS)] * 2
        + [DMA(LineGather.SEMS)] * 2
        + [DMA((8,))],
    )


def weight_part(place, ref):
    return lambda half, unit, x, y: ref.at[place.block(2 * unit + half, x, y)]


def attend_back(head, qkv, grad_heads, grads):
    pair = lanes(head // 2 * 128, 128)
    mask = head_mask(head)
    for block in range(qkv.shape[1] // QUERY_ROWS):
        rows = pl.ds(block * QUERY_ROWS, QUERY_ROWS)
        keys = pl.ds(0, (block + 1) * QUERY_ROWS)
        queries, grad_rows = qkv[0, rows, pair] * mask, grad_heads[rows, pair] * mask
        key_rows = qkv[1, keys, pair]
        probs = scaled_probs(queries, key_rows, block * QUERY_ROWS)
        grad_probs = lax.dot_general(
            grad_rows, qkv[2, keys, pair], CONTRACT_LAST, preferred_element_type=WIDE
        )
        delta = jnp.sum(probs * grad_probs, axis=1, keepdims=True)
        grad_scores = (probs * (grad_probs - delta) * HEAD_DIM ** (-0.5)).astype(LOW)
        grads[0, rows, pair] += jnp.dot(grad_scores, key_rows * mask, preferred_element_type=WIDE)
        grads[1, keys, pair] += lax.dot_general(
            grad_scores, queries, CONTRACT_FIRST, preferred_element_type=WIDE
        )
        grads[2, keys, pair] += lax.dot_general(
            probs.astype(LOW), grad_rows, CONTRACT_FIRST, preferred_element_type=WIDE
        )


def mlp_kernel(
    normed,
    wg,
    wd,
    cot,
    residual,
    gain_rows,
    branch,
    g_sum,
    d_part,
    block_out,
    out_grad,
    nt,
    full_g,
    full_d,
    ct,
    active,
    grad_wide,
    part_two,
    part_out,
    grad_residual,
    mine,
    *scratch,
):
    p = Place()
    rows_own, width = residual.shape
    seq_len = 8 * rows_own
    own, ff = wd.shape[1], wd.shape[2]
    units = wd.shape[0] // 8
    block_rows, slots = seq_len // 2, 4
    part = ff // 4
    wide = width // 4
    blocks = wide // own
    load_sems, sum_a, sum_b, sum_c, gather_a, gather_b, swap_sems, keep_sems = scratch[7:]
    part_rows = [pl.ds(0, rows_own // 2), pl.ds(rows_own // 2, rows_own // 2)]
    sum_two = [
        LineScatter(p, part_two, *scratch[:2], sem, rows)
        for sem, rows in zip((sum_a, sum_b), part_rows)
    ]
    sum_out = LineScatter(p, part_out, *scratch[2:4], sum_c, pl.ds(0, rows_own))
    plane = PlaneScatter(p, weight_part(p, full_g), units, *scratch[4:7])
    gathers = [
        LineGather(p, branch, sem, mine.at[rows], rows)
        for sem, rows in zip((gather_a, gather_b), part_rows)
    ]

    def load(index):
        if index == 0:
            return pltpu.make_async_copy(normed, nt, load_sems.at[0])
        if index == 1:
            return pltpu.make_async_copy(cot, ct, load_sems.at[1])
        return pltpu.make_async_copy(wd, full_d, load_sems.at[2])

    def load_wide(index, side):
        columns = lanes(side * ff + index * part, part)
        return pltpu.make_async_copy(
            wg.at[:, :, columns], full_g.at[:, :, columns], load_sems.at[3 + 2 * index + side]
        )

    load(0).start()
    for index in range(4):
        for side in range(2):
            load_wide(index, side).start()
        if index == 0:
            load(1).start()
            load(2).start()
    p.meet(True)
    for index in range(3):
        load(index).wait()

    def stage_one(index, carry):
        load_wide(index, 0).wait()
        load_wide(index, 1).wait()
        here, there = lanes(index * part, part), lanes(ff + index * part, part)

        def some(block, carry):
            rows = pl.ds(pl.multiple_of(block * block_rows, block_rows), block_rows)
            these = pl.ds(block * slots, slots)
            left = nt[these].reshape(block_rows, width)
            gate = jnp.dot(left, full_g[:, :, here].reshape(width, part), preferred_element_type=WIDE)
            up = jnp.dot(left, full_g[:, :, there].reshape(width, part), preferred_element_type=WIDE)
            grad = jnp.dot(
                ct[these].reshape(block_rows, width),
                full_d[:, :, here].reshape(width, part),
                preferred_element_type=WIDE,
            )
            sigmoid_gate = jax.nn.sigmoid(gate)
            active[rows, here] = (gate * sigmoid_gate * up).astype(LOW)
            grad_wide[rows, here] = (
                grad * up * sigmoid_gate * (1.0 + gate * (1.0 - sigmoid_gate))
            ).astype(LOW)
            grad_wide[rows, there] = (grad * gate * sigmoid_gate).astype(LOW)
            return carry

        return lax.fori_loop(0, seq_len // block_rows, some, carry)

    lax.fori_loop(0, 4, stage_one, 0)

    def rows_times(left, weight, target, index):
        def some(block, carry):
            made = lax.dot_general(
                left[pl.ds(pl.multiple_of(block * block_rows, block_rows), block_rows), :],
                weight[pl.ds(index * blocks, blocks)].reshape(wide, -1),
                CONTRACT_LAST,
                preferred_element_type=WIDE,
            )
            target[pl.ds(block * slots, slots), :, lanes(index * wide, wide)] = made.astype(
                LOW
            ).reshape(slots, rows_own, wide)
            return carry

        lax.fori_loop(0, seq_len // block_rows, some, 0)

    def each_part(call):
        lax.fori_loop(0, 4, lambda index, carry: (call(index), carry)[1], 0)

    def down_grad(index, carry):
        made = lax.dot_general(
            ct[:, :, lanes(index * wide, wide)].reshape(seq_len, wide),
            active[...],
            CONTRACT_FIRST,
            preferred_element_type=WIDE,
        )
        full_d[pl.ds(index * blocks, blocks)] = made.astype(LOW).reshape(blocks, own, ff)
        return carry

    def wide_grad(index):
        for side in range(2):
            made = lax.dot_general(
                nt[:, :, pl.ds(index * wide, wide)].reshape(seq_len, wide),
                grad_wide[:, pl.ds(side * ff, ff)],
                CONTRACT_FIRST,
                preferred_element_type=WIDE,
            )
            full_g[pl.ds(index * blocks, blocks), :, pl.ds(side * ff, ff)] = made.astype(
                LOW
            ).reshape(blocks, own, ff)
        plane.start_unit(index)

    def local_two(part):
        def some(rows):
            spot = pl.ds(pl.multiple_of(part * (rows_own // 2) + rows.start, CHUNK), CHUNK)
            unit, inverse = rms_parts(residual[spot, :])
            total = ct[p.slot, spot, :].astype(WIDE) + normed_back(
                sum_two[part].total(spot), unit, inverse, gain_rows[pl.ds(1, 1), :]
            )
            grad_residual[spot, :] = total
            mine[spot, :] = total.astype(LOW)

        by_rows(rows_own // 2, some)

    each_part(lambda index: rows_times(grad_wide, full_g, part_two, index))
    for half in sum_two:
        half.start()
    for half in sum_two:
        half.head()
    each_part(lambda index: rows_times(active, full_d, part_out, index))
    sum_two[0].step(0)
    sum_out.start()
    lax.fori_loop(0, 2, down_grad, 0)
    sum_two[0].step(1)
    lax.fori_loop(2, 4, down_grad, 0)
    keep_d = pltpu.make_async_copy(full_d, d_part, keep_sems.at[0])
    keep_d.start()
    sum_two[0].step(2)
    wide_grad(0)
    sum_two[0].arrive()
    local_two(0)
    gathers[0].start()
    sum_out.head()
    wide_grad(1)
    sum_two[1].step(0)
    wide_grad(2)
    sum_two[1].step(1)
    gathers[0].step(1)
    wide_grad(3)
    sum_two[1].step(2)
    gathers[0].step(2)
    plane.middle(0)
    sum_two[1].arrive()
    local_two(1)
    gathers[1].start()
    keep_grad = pltpu.make_async_copy(grad_residual, out_grad, keep_sems.at[1])
    keep_grad.start()
    plane.middle(1)
    gathers[0].step(3)
    sum_out.step(0)
    gathers[1].step(1)
    plane.middle(2)
    plane.middle(3)
    sum_out.step(1)
    gathers[1].step(2)
    sum_out.step(2)
    gathers[1].step(3)
    for gather in gathers:
        gather.finish()
    for gather in gathers:
        gather.drain()
    sum_out.arrive()

    def local_out(rows):
        mine[rows, :] = (residual[rows, :] + sum_out.total(rows)).astype(LOW)

    by_rows(rows_own, local_out)
    swap = Swap(p, mine, block_out, block_out, swap_sems)
    swap.start()

    def keep_g(half, unit):
        return pltpu.make_async_copy(
            plane.sums(half, unit), g_sum.at[half, unit], keep_sems.at[2 + 4 * half + unit]
        )

    for unit in range(units):
        plane.final(unit)
        for half in range(2):
            keep_g(half, unit).start()
    swap.wait()
    swap.drain()
    for part in sum_two + [sum_out, plane]:
        part.drain()
    keep_d.wait()
    keep_grad.wait()
    for unit in range(units):
        for half in range(2):
            keep_g(half, unit).wait()


def mlp(normed, wg, wd, cot, residual, gain_rows):
    _, rows, width = normed.shape
    own, ff = wd.shape[1:]
    units = wd.shape[0] // 8
    vmem = lambda shape, dtype=LOW: pltpu.VMEM(shape, dtype)
    return kernel_call(
        mlp_kernel,
        "mlp",
        2,
        (normed, wg, wd, cot, residual, gain_rows),
        [ANYWHERE] * 4 + [IN_VMEM] * 2,
        [
            (normed.shape, LOW),
            ((2, units, own, 2 * ff), LOW),
            (wd.shape, LOW),
            ((rows, width), LOW),
            ((rows, width), WIDE),
        ],
        [ANYWHERE] * 5,
        [
            vmem(normed.shape),
            vmem(wg.shape),
            vmem(wd.shape),
            vmem(cot.shape),
            vmem((8 * rows, ff)),
            vmem((8 * rows, 2 * ff)),
            vmem(normed.shape),
            vmem(normed.shape),
            vmem((rows, width), WIDE),
            vmem((rows, width)),
        ]
        + LineScatter.buffers(rows, width) * 2
        + PlaneScatter.scratch(units, own, 2 * ff)
        + [DMA((11,))]
        + [DMA(LineScatter.SEMS)] * 3
        + [DMA(LineGather.SEMS)] * 2
        + [DMA((3,)), DMA((2 + 2 * units,))],
    )


def backward_kernel(
    branch_all,
    grad_in,
    gain_rows,
    own_tok,
    full_q,
    full_o,
    qkv,
    attended,
    normed_one,
    cosines,
    sines,
    g_sum,
    d_part,
    input_grad,
    q_out,
    g_out,
    d_out,
    o_out,
    work,
    branch,
    grad_residual,
    grad_heads,
    grads,
    grad_projected,
    q_part,
    o_part,
    o_sum,
    d_here,
    *scratch,
):
    buffers, rest = scratch[:2], scratch[2:]
    p = Place()
    rows_own, width = grad_residual.shape
    seq_len = 8 * rows_own
    own = full_o.shape[1]
    units = g_sum.shape[1]
    half = own // 2
    step_q, step_g, step_d = q_part.shape[2] // 3, g_sum.shape[3] // 2, d_part.shape[2]
    plane_d = PlaneScatter(p, weight_part(p, d_here), units, *rest[:3])
    plane_q = PlaneScatter(p, weight_part(p, q_part), units, *rest[3:6])
    plane_o = PlaneScatter(
        p, lambda h, u, x, y: o_part.at[2 * y + x, pl.ds(h * half, half)], 1, *rest[6:9]
    )
    sum_sems, return_sems, swap_sems, load_sems = rest[9:11], rest[11:14], rest[14:17], rest[17]
    part_rows = [pl.ds(0, rows_own // 2), pl.ds(rows_own // 2, rows_own // 2)]
    sum_one = [
        LineScatter(p, branch, *buffers, sem, rows) for sem, rows in zip(sum_sems, part_rows)
    ]
    return_q = LineReturn(
        p, plane_q.sums, [(i * step_q, step_q, i * 8 * step_q) for i in range(3)], q_out, return_sems[0]
    )
    return_g = LineReturn(
        p,
        lambda c, z: g_sum.at[c, z],
        [(i * step_g, step_g, i * 8 * step_g) for i in range(2)],
        g_out,
        return_sems[1],
    )
    return_d = LineReturn(p, plane_d.sums, [(0, step_d, 0)], d_out, return_sems[2])
    swap_in = [
        Swap(p, grad_residual.at[rows], input_grad.at[rows], input_grad.at[rows], sem)
        for sem, rows in zip(swap_sems[:2], part_rows)
    ]
    swap_out = Swap(p, o_sum, o_out, o_out, swap_sems[2])

    def load(source, target, index):
        return pltpu.make_async_copy(source, target, load_sems.at[index])

    loads = [
        load(branch_all, branch, 0),
        load(d_part, d_here, 1),
        load(normed_one, work, 2),
        load(grad_in, grad_residual, 3),
    ]
    for copy in loads:
        copy.start()
    p.meet(True)
    for z in range(4):
        return_g.send(z)
    loads[0].wait()

    def back_out(part, carry):
        rows = pl.ds(pl.multiple_of(part * 256, 256), 256)
        made = lax.dot_general(
            branch[pl.ds(2 * part, 2)].reshape(256, width),
            full_o[...].reshape(-1, width),
            CONTRACT_LAST,
            preferred_element_type=WIDE,
        )
        grad_heads[rows, :] = made.astype(LOW)
        return carry

    lax.fori_loop(0, seq_len // 256, back_out, 0)
    loads[1].wait()
    plane_d.start()

    def out_grad(part, carry):
        columns = lanes(part * 512, 512)
        made = lax.dot_general(
            attended[...],
            branch[:, :, columns].reshape(seq_len, 512),
            CONTRACT_FIRST,
            preferred_element_type=WIDE,
        )
        o_part[:, :, columns] = made.astype(LOW).reshape(4, own, 512)
        return carry

    lax.fori_loop(0, width // 512, out_grad, 0)
    plane_o.start()
    grads[...] = jnp.zeros_like(grads)

    def one_head(head, carry):
        attend_back(head, qkv, grad_heads, grads)
        plane_d.middle(head)
        return carry

    lax.fori_loop(0, 4, one_head, 0)

    def back_turn(part, carry):
        rows = pl.ds(pl.multiple_of(part * 256, 256), 256)
        for kind in range(3):
            made = grads[kind, rows, :]
            if kind < 2:
                made = turn(
                    made,
                    jnp.concatenate([cosines[rows, :]] * 2, axis=1),
                    jnp.concatenate([-sines[rows, :]] * 2, axis=1),
                )
            grad_projected[rows, pl.ds(kind * step_q, step_q)] = made.astype(LOW)
        return carry

    lax.fori_loop(0, seq_len // 256, back_turn, 0)

    def back_qkv(part, carry):
        weight = full_q[pl.ds(part * 8, 8), :, pl.ds(0, 3 * step_q)].reshape(8 * own, 3 * step_q)
        for block in range(seq_len // 512):
            made = lax.dot_general(
                grad_projected[pl.ds(block * 512, 512), :],
                weight,
                CONTRACT_LAST,
                preferred_element_type=WIDE,
            )
            branch[pl.ds(block * 4, 4), :, lanes(part * 8 * own, 8 * own)] = made.astype(
                LOW
            ).reshape(4, rows_own, 8 * own)
        return carry

    lax.fori_loop(0, 4, back_qkv, 0)
    for part in sum_one:
        part.start()
    loads[2].wait()
    loads[3].wait()
    for part in sum_one:
        part.head()

    def qkv_grad(part, carry):
        made = lax.dot_general(
            work[:, :, lanes(part * 8 * own, 8 * own)].reshape(seq_len, 8 * own),
            grad_projected[...],
            CONTRACT_FIRST,
            preferred_element_type=WIDE,
        )
        q_part[pl.ds(part * 8, 8)] = made.astype(LOW).reshape(8, own, 3 * step_q)
        plane_q.start_unit(part)
        return carry

    lax.fori_loop(0, 4, qkv_grad, 0)

    def local_one(part):
        def some(rows):
            spot = pl.ds(pl.multiple_of(part * (rows_own // 2) + rows.start, CHUNK), CHUNK)
            unit, inverse = rms_parts(own_tok[spot, :].astype(WIDE))
            grad_residual[spot, :] = grad_residual[spot, :] + normed_back(
                sum_one[part].total(spot), unit, inverse, gain_rows[pl.ds(0, 1), :]
            )

        by_rows(rows_own // 2, some)

    for unit in range(units):
        plane_d.final(unit)
        return_d.send(unit)
    plane_o.middle(0)
    for index in range(3):
        sum_one[0].step(index)
    for unit in range(units):
        plane_q.middle(unit)
    sum_one[0].arrive()
    local_one(0)
    swap_in[0].start()
    plane_o.final(0)
    for h in range(2):
        o_sum[pl.ds(h * half, half), :] = plane_o.sums(h, 0)[...]
    swap_out.start()
    for unit in range(units):
        plane_q.final(unit)
        return_q.send(unit)
    for index in range(3):
        sum_one[1].step(index)
    sum_one[1].arrive()
    local_one(1)
    swap_in[1].start()
    for part in (return_g, return_d, return_q):
        part.finish()
    for part in swap_in + [swap_out]:
        part.wait()
        part.drain()
    for part in sum_one + [plane_d, plane_q, plane_o]:
        part.drain()


def backward(
    branch,
    grad_residual,
    gain_rows,
    own_tok,
    full_q,
    full_o,
    qkv,
    attended,
    normed_one,
    cosines,
    sines,
    g_sum,
    d_part,
):
    _, rows, width = branch.shape
    own, here = full_o.shape[1], attended.shape[1]
    units = g_sum.shape[1]
    vmem = lambda shape, dtype=LOW: pltpu.VMEM(shape, dtype)
    step_g, step_d = g_sum.shape[3], d_part.shape[2]
    return kernel_call(
        backward_kernel,
        "backward",
        3,
        (
            branch,
            grad_residual,
            gain_rows,
            own_tok,
            full_q,
            full_o,
            qkv,
            attended,
            normed_one,
            cosines,
            sines,
            g_sum,
            d_part,
        ),
        [ANYWHERE] * 2 + [IN_VMEM] * 6 + [ANYWHERE] + [IN_VMEM] * 2 + [ANYWHERE] * 2,
        [
            ((rows, width), WIDE),
            ((own, 24 * here), LOW),
            ((own, 8 * step_g), LOW),
            ((own, 8 * step_d), LOW),
            ((own, width), LOW),
        ],
        [ANYWHERE] * 5,
        [
            vmem((8, rows, width)),
            vmem((8, rows, width)),
            vmem((rows, width), WIDE),
            vmem((8 * rows, here)),
            vmem((3, 8 * rows, here), WIDE),
            vmem((8 * rows, 3 * here)),
            vmem((32, own, 3 * here)),
            vmem((4, own, width)),
            vmem((own, width)),
            vmem(d_part.shape),
        ]
        + LineScatter.buffers(rows, width)
        + PlaneScatter.scratch(units, own, step_d)
        + PlaneScatter.scratch(units, own, 3 * here)
        + PlaneScatter.scratch(1, own // 2, width)
        + [DMA(LineScatter.SEMS)] * 2
        + [DMA(LineReturn.SEMS)] * 3
        + [DMA((3,))] * 3
        + [DMA((4,))],
    )


def grid_shards(
    tokens,
    cotangent,
    qkv_weight,
    out_weight,
    gate_up_weight,
    down_weight,
    gains,
    qkv_first,
    out_first,
    gate_up_first,
    down_first,
    gains_first,
    qkv_second,
    out_second,
    gate_up_second,
    down_second,
    gains_second,
):
    rows, width = tokens.shape[1:]
    seq_len = 8 * rows
    gain_columns = jnp.pad(gains.astype(LOW).T, ((0, 0), (0, 126)))
    cosines, sines = rope_tables(jnp.arange(seq_len, dtype=jnp.int32))
    cosines, sines = (
        jnp.tile(cosines[:, 0], (1, 4)),
        jnp.tile(jnp.concatenate([-sines[:, 0], sines[:, 0]], axis=1), (1, 2)),
    )
    (
        grad_out,
        normed_two,
        gate_up_full,
        down_full,
        qkv_full,
        out_full,
        normed_one,
        qkv_heads,
        attended,
        residual,
        gain_full,
        own_tokens,
    ) = forward(
        tokens[0],
        cotangent[0],
        qkv_weight.astype(LOW),
        gain_columns,
        gate_up_weight.astype(LOW),
        down_weight.astype(LOW),
        out_weight.astype(LOW),
        cosines,
        sines,
    )
    grad_branch, gate_up_half, down_part, block_out, grad_residual = mlp(
        normed_two, gate_up_full, down_full, grad_out, residual, gain_full
    )
    input_grad, qkv_sum, gate_up_sum, down_sum, out_sum = backward(
        grad_branch,
        grad_residual,
        gain_full,
        own_tokens,
        qkv_full,
        out_full,
        qkv_heads,
        attended,
        normed_one.reshape(8, rows, width),
        cosines,
        sines,
        gate_up_half,
        down_part,
    )
    qkv_sum, gate_up_sum, down_sum, out_sum = (
        total.astype(WIDE) for total in (qkv_sum, gate_up_sum, down_sum, out_sum)
    )
    gains_sum = jnp.stack(
        [
            jnp.sum(weight.astype(LOW).astype(WIDE) * total, axis=1)
            for weight, total in ((qkv_weight, qkv_sum), (gate_up_weight, gate_up_sum))
        ],
        axis=0,
    ) / gains.astype(LOW).astype(WIDE)
    wide_rate = 2.5 * D ** (-0.5)
    out_rate = 2.5 * max(D // 512, 1) ** (-0.5)
    down_rate = 2.5 * FF ** (-0.5)
    qkv_new = adam_step(qkv_weight, qkv_sum, qkv_first, qkv_second, wide_rate, WEIGHT_DECAY)
    out_new = adam_step(out_weight, out_sum, out_first, out_second, out_rate, WEIGHT_DECAY)
    gate_up_new = adam_step(
        gate_up_weight, gate_up_sum, gate_up_first, gate_up_second, wide_rate, WEIGHT_DECAY
    )
    down_new = adam_step(
        down_weight, down_sum, down_first, down_second, down_rate, WEIGHT_DECAY
    )
    gains_new = adam_step(gains, gains_sum, gains_first, gains_second, 0.5, 0.0)
    return (
        block_out[None],
        input_grad[None],
        qkv_new[0],
        out_new[0],
        gate_up_new[0],
        down_new[0],
        gains_new[0],
        qkv_new[1],
        out_new[1],
        gate_up_new[1],
        down_new[1],
        gains_new[1],
        qkv_new[2],
        out_new[2],
        gate_up_new[2],
        down_new[2],
        gains_new[2],
    )


def mapped(body, mesh, token_spec, row_spec, gain_spec):
    one_set = (row_spec, row_spec, row_spec, row_spec, gain_spec)
    return jax.shard_map(
        body,
        mesh=mesh,
        in_specs=(token_spec, token_spec) + one_set * 3,
        out_specs=(token_spec, token_spec) + one_set * 3,
        check_vma=False,
    )


def solution(mesh):
    if mesh.shape["seq"] == 8 and mesh.shape["dp"] == 4:
        grid_mesh = Mesh(mesh.devices.reshape(4, 2, 2, 2), GRID)
        return mapped(
            grid_shards,
            grid_mesh,
            P(("y", "c"), ("z", "x"), None),
            P(GRID, None),
            P(None, GRID),
        )
    return mapped(
        shards, mesh, P("dp", "seq", None), P(("seq", "dp"), None), P(None, ("seq", "dp"))
    )
```

```python
import jax
import jax.numpy as jnp
from jax import lax
from jax.experimental import pallas as pl
from jax.experimental.pallas import tpu as pltpu
from jax.sharding import Mesh
from jax.sharding import PartitionSpec as P

D = 2048
HEADS = 32
HEAD_DIM = 64
FF = 8192
BLOCK = 512
STEP = 10


NORM_EPS = 1e-05
ROPE_BASE = 130000.0
BETA_ONE = 0.9
BETA_TWO = 0.999
ADAM_EPS = 1e-08
WEIGHT_DECAY = 0.1
MASKED = -1e30


def rms_parts(values):
    inverse = lax.rsqrt(jnp.mean(values * values, axis=-1, keepdims=True) + NORM_EPS)
    return (values * inverse, inverse)


def rope_tables(positions):
    half_dim = HEAD_DIM // 2
    exponent = jnp.arange(half_dim, dtype=jnp.float32) * (2.0 / HEAD_DIM)
    frequency = ROPE_BASE ** (-exponent)
    angles = positions.astype(jnp.float32)[:, None] * frequency[None, :]
    return (jnp.cos(angles)[:, None, :], jnp.sin(angles)[:, None, :])


def rotate(tensor, cosines, sines):
    half_dim = HEAD_DIM // 2
    lower_half = tensor[..., :half_dim]
    upper_half = tensor[..., half_dim:]
    return jnp.concatenate(
        [lower_half * cosines - upper_half * sines, upper_half * cosines + lower_half * sines],
        axis=-1,
    )


def unrotate(tensor, cosines, sines):
    half_dim = HEAD_DIM // 2
    lower_half = tensor[..., :half_dim]
    upper_half = tensor[..., half_dim:]
    return jnp.concatenate(
        [lower_half * cosines + upper_half * sines, upper_half * cosines - lower_half * sines],
        axis=-1,
    )


def block_scores(query_rows, key_heads, key_id, block_id):
    key_rows = lax.dynamic_slice_in_dim(key_heads, key_id * BLOCK, BLOCK, 0)
    products = jnp.einsum(
        "qhd,khd->hqk", query_rows, key_rows, preferred_element_type=jnp.float32
    ) * HEAD_DIM ** (-0.5)
    local_ids = jnp.arange(BLOCK, dtype=jnp.int32)
    allowed = (key_id < block_id) | (local_ids[None, :] <= local_ids[:, None])
    return jnp.where(allowed[None], products, MASKED)


def row_normalizer(query_rows, key_heads, block_id):
    row_shape = (query_rows.shape[1], BLOCK, 1)

    def absorb(key_id, state):
        running_max, running_total = state
        scores = block_scores(query_rows, key_heads, key_id, block_id)
        new_max = jnp.maximum(running_max, jnp.max(scores, axis=-1, keepdims=True))
        running_total = running_total * jnp.exp(running_max - new_max) + jnp.sum(
            jnp.exp(scores - new_max), axis=-1, keepdims=True
        )
        return (new_max, running_total)

    start_state = (jnp.full(row_shape, MASKED, jnp.float32), jnp.zeros(row_shape, jnp.float32))
    final_max, final_total = lax.fori_loop(0, block_id + 1, absorb, start_state)
    return final_max + jnp.log(final_total)


def attend_forward(query_heads, key_heads, value_heads):
    seq_len, heads_here, head_dim = query_heads.shape

    def one_block(block_id, carry):
        out_all, lse_all = carry
        row_start = block_id * BLOCK
        query_rows = lax.dynamic_slice_in_dim(query_heads, row_start, BLOCK, 0)
        row_lse = row_normalizer(query_rows, key_heads, block_id)

        def weigh_values(key_id, running):
            scores = block_scores(query_rows, key_heads, key_id, block_id)
            weights_low = jnp.exp(scores - row_lse).astype(jnp.bfloat16)
            value_rows = lax.dynamic_slice_in_dim(value_heads, key_id * BLOCK, BLOCK, 0)
            return running + jnp.einsum(
                "hqk,khd->qhd", weights_low, value_rows, preferred_element_type=jnp.float32
            )

        attended = lax.fori_loop(
            0, block_id + 1, weigh_values, jnp.zeros((BLOCK, heads_here, head_dim), jnp.float32)
        )
        out_all = lax.dynamic_update_slice_in_dim(
            out_all, attended.astype(jnp.bfloat16), row_start, 0
        )
        lse_all = lax.dynamic_update_slice_in_dim(lse_all, row_lse, row_start, 1)
        return (out_all, lse_all)

    start_carry = (
        jnp.zeros((seq_len, heads_here, head_dim), jnp.bfloat16),
        jnp.zeros((heads_here, seq_len, 1), jnp.float32),
    )
    return lax.fori_loop(0, seq_len // BLOCK, one_block, start_carry)


def attend_backward(query_heads, key_heads, value_heads, grad_heads, lse_all):
    seq_len, heads_here, head_dim = query_heads.shape
    score_scale = HEAD_DIM ** (-0.5)

    def one_block(block_id, carry):
        grad_q_all, grad_k_all, grad_v_all = carry
        row_start = block_id * BLOCK
        query_rows = lax.dynamic_slice_in_dim(query_heads, row_start, BLOCK, 0)
        grad_rows = lax.dynamic_slice_in_dim(grad_heads, row_start, BLOCK, 0)
        row_lse = lax.dynamic_slice_in_dim(lse_all, row_start, BLOCK, 1)

        def probs_and_grads(key_id):
            scores = block_scores(query_rows, key_heads, key_id, block_id)
            probs = jnp.exp(scores - row_lse)
            value_rows = lax.dynamic_slice_in_dim(value_heads, key_id * BLOCK, BLOCK, 0)
            grad_probs = jnp.einsum(
                "qhd,khd->hqk", grad_rows, value_rows, preferred_element_type=jnp.float32
            )
            return (probs, grad_probs)

        def add_delta(key_id, running):
            probs, grad_probs = probs_and_grads(key_id)
            return running + jnp.sum(probs * grad_probs, axis=-1, keepdims=True)

        row_delta = lax.fori_loop(
            0, block_id + 1, add_delta, jnp.zeros((heads_here, BLOCK, 1), jnp.float32)
        )

        def spread(key_id, inner):
            grad_q_rows, grad_k_acc, grad_v_acc = inner
            probs, grad_probs = probs_and_grads(key_id)
            key_start = key_id * BLOCK
            key_rows = lax.dynamic_slice_in_dim(key_heads, key_start, BLOCK, 0)
            grad_scores = (probs * (grad_probs - row_delta) * score_scale).astype(jnp.bfloat16)
            grad_q_rows = grad_q_rows + jnp.einsum(
                "hqk,khd->qhd", grad_scores, key_rows, preferred_element_type=jnp.float32
            )
            grad_k_part = jnp.einsum(
                "hqk,qhd->khd", grad_scores, query_rows, preferred_element_type=jnp.float32
            )
            grad_v_part = jnp.einsum(
                "hqk,qhd->khd",
                probs.astype(jnp.bfloat16),
                grad_rows,
                preferred_element_type=jnp.float32,
            )
            grad_k_acc = lax.dynamic_update_slice_in_dim(
                grad_k_acc,
                lax.dynamic_slice_in_dim(grad_k_acc, key_start, BLOCK, 0) + grad_k_part,
                key_start,
                0,
            )
            grad_v_acc = lax.dynamic_update_slice_in_dim(
                grad_v_acc,
                lax.dynamic_slice_in_dim(grad_v_acc, key_start, BLOCK, 0) + grad_v_part,
                key_start,
                0,
            )
            return (grad_q_rows, grad_k_acc, grad_v_acc)

        start_inner = (
            jnp.zeros((BLOCK, heads_here, head_dim), jnp.float32),
            grad_k_all,
            grad_v_all,
        )
        grad_q_rows, grad_k_all, grad_v_all = lax.fori_loop(0, block_id + 1, spread, start_inner)
        grad_q_all = lax.dynamic_update_slice_in_dim(grad_q_all, grad_q_rows, row_start, 0)
        return (grad_q_all, grad_k_all, grad_v_all)

    zeros_all = jnp.zeros((seq_len, heads_here, head_dim), jnp.float32)
    return lax.fori_loop(0, seq_len // BLOCK, one_block, (zeros_all, zeros_all, zeros_all))


def adam_step(weight, gradient, first, second, rate, decay):
    new_first = BETA_ONE * first + (1.0 - BETA_ONE) * gradient
    new_second = BETA_TWO * second + (1.0 - BETA_TWO) * gradient * gradient
    first_hat = new_first / (1.0 - BETA_ONE**STEP)
    second_hat = new_second / (1.0 - BETA_TWO**STEP)
    new_weight = weight - rate * (first_hat / (jnp.sqrt(second_hat) + ADAM_EPS) + decay * weight)
    return (new_weight, new_first, new_second)


def shards(
    tokens,
    cotangent,
    qkv_weight,
    out_weight,
    gate_up_weight,
    down_weight,
    gains,
    qkv_first,
    out_first,
    gate_up_first,
    down_first,
    gains_first,
    qkv_second,
    out_second,
    gate_up_second,
    down_second,
    gains_second,
):
    seq_count = lax.axis_size("seq")
    tok_rows = tokens.shape[1]
    width = tokens.shape[2]
    seq_len = tok_rows * seq_count
    heads_here = HEADS // seq_count
    width_here = heads_here * HEAD_DIM
    contract_last = (((1,), (1,)), ((), ()))
    contract_first = (((0,), (0,)), ((), ()))
    qkv_full, proj_full, gain_full = (
        lax.all_gather(qkv_weight.astype(jnp.bfloat16), ("seq", "dp"), axis=0, tiled=True),
        lax.all_gather(out_weight.astype(jnp.bfloat16), ("seq", "dp"), axis=0, tiled=True),
        lax.all_gather(gains.astype(jnp.bfloat16), ("seq", "dp"), axis=1, tiled=True),
    )
    up_full, down_full = (
        lax.all_gather(gate_up_weight.astype(jnp.bfloat16), ("seq", "dp"), axis=0, tiled=True),
        lax.all_gather(down_weight.astype(jnp.bfloat16), ("seq", "dp"), axis=0, tiled=True),
    )
    hidden_in = tokens[0].astype(jnp.float32)
    unit_one, inverse_one = rms_parts(hidden_in)
    normed_one = (unit_one * gain_full[0].astype(jnp.float32)).astype(jnp.bfloat16)
    projected = jnp.einsum(
        "te,ecd->ctd",
        normed_one,
        qkv_full.reshape(width, 3, width),
        preferred_element_type=jnp.float32,
    )
    positions = lax.axis_index("seq") * tok_rows + jnp.arange(tok_rows, dtype=jnp.int32)
    cos_local, sin_local = rope_tables(positions)
    turned = rotate(projected[:2].reshape(2, tok_rows, HEADS, HEAD_DIM), cos_local, sin_local)
    packed = jnp.concatenate([turned.reshape(2, tok_rows, width), projected[2:]], axis=0).astype(
        jnp.bfloat16
    )
    by_heads = lax.all_to_all(packed, "seq", split_axis=2, concat_axis=1, tiled=True)
    query_heads = by_heads[0].reshape(seq_len, heads_here, HEAD_DIM)
    key_heads = by_heads[1].reshape(seq_len, heads_here, HEAD_DIM)
    value_heads = by_heads[2].reshape(seq_len, heads_here, HEAD_DIM)
    out_heads, lse_all = attend_forward(query_heads, key_heads, value_heads)
    attended = lax.all_to_all(
        out_heads.reshape(seq_len, width_here), "seq", split_axis=0, concat_axis=1, tiled=True
    )
    residual = hidden_in + jnp.dot(attended, proj_full, preferred_element_type=jnp.float32)
    unit_two, inverse_two = rms_parts(residual)
    normed_two = (unit_two * gain_full[1].astype(jnp.float32)).astype(jnp.bfloat16)
    gate_up = jnp.dot(normed_two, up_full, preferred_element_type=jnp.float32)
    gate_vals = gate_up[:, :FF]
    up_vals = gate_up[:, FF:]
    sigmoid_gate = jax.nn.sigmoid(gate_vals)
    activated = (gate_vals * sigmoid_gate * up_vals).astype(jnp.bfloat16)
    mlp_out = lax.dot_general(
        activated, down_full, contract_last, preferred_element_type=jnp.float32
    )
    block_out = (residual + mlp_out).astype(jnp.bfloat16)[None]
    back_up, back_down, back_gain = (
        lax.all_gather(gate_up_weight.astype(jnp.bfloat16), ("seq", "dp"), axis=0, tiled=True),
        lax.all_gather(down_weight.astype(jnp.bfloat16), ("seq", "dp"), axis=0, tiled=True),
        lax.all_gather(gains.astype(jnp.bfloat16), ("seq", "dp"), axis=1, tiled=True),
    )
    grad_out = cotangent[0]
    grad_act = jnp.dot(grad_out, back_down, preferred_element_type=jnp.float32)
    grad_gate = grad_act * up_vals * sigmoid_gate * (1.0 + gate_vals * (1.0 - sigmoid_gate))
    grad_up = grad_act * gate_vals * sigmoid_gate
    grad_gate_up = jnp.concatenate([grad_gate, grad_up], axis=1).astype(jnp.bfloat16)
    grad_normed_two = lax.dot_general(
        grad_gate_up, back_up, contract_last, preferred_element_type=jnp.float32
    )
    gain_two_grad = jnp.sum(grad_normed_two * unit_two, axis=0)
    grad_unit_two = grad_normed_two * back_gain[1].astype(jnp.float32)
    grad_residual = grad_out.astype(jnp.float32) + inverse_two * (
        grad_unit_two - unit_two * jnp.mean(grad_unit_two * unit_two, axis=-1, keepdims=True)
    )
    gate_up_rows = lax.dot_general(
        normed_two, grad_gate_up, contract_first, preferred_element_type=jnp.float32
    )
    down_rows = lax.dot_general(
        grad_out, activated, contract_first, preferred_element_type=jnp.float32
    )
    mlp_grad = lax.psum_scatter(
        jnp.concatenate([gate_up_rows, down_rows], axis=1),
        ("seq", "dp"),
        scatter_dimension=0,
        tiled=True,
    )
    back_qkv, back_proj = (
        lax.all_gather(qkv_weight.astype(jnp.bfloat16), ("seq", "dp"), axis=0, tiled=True),
        lax.all_gather(out_weight.astype(jnp.bfloat16), ("seq", "dp"), axis=0, tiled=True),
    )
    grad_branch = grad_residual.astype(jnp.bfloat16)
    proj_grad = lax.dot_general(
        attended, grad_branch, contract_first, preferred_element_type=jnp.float32
    )
    grad_attended = lax.dot_general(
        grad_branch, back_proj, contract_last, preferred_element_type=jnp.float32
    ).astype(jnp.bfloat16)
    grad_heads = lax.all_to_all(
        grad_attended, "seq", split_axis=1, concat_axis=0, tiled=True
    ).reshape(seq_len, heads_here, HEAD_DIM)
    grad_q_all, grad_k_all, grad_v_all = attend_backward(
        query_heads, key_heads, value_heads, grad_heads, lse_all
    )
    cos_whole, sin_whole = rope_tables(jnp.arange(seq_len, dtype=jnp.int32))
    grad_pack = jnp.stack(
        [
            unrotate(grad_q_all, cos_whole, sin_whole).reshape(seq_len, width_here),
            unrotate(grad_k_all, cos_whole, sin_whole).reshape(seq_len, width_here),
            grad_v_all.reshape(seq_len, width_here),
        ],
        axis=0,
    ).astype(jnp.bfloat16)
    grad_projected = lax.all_to_all(grad_pack, "seq", split_axis=1, concat_axis=2, tiled=True)
    qkv_cube = back_qkv.reshape(width, 3, width)
    grad_normed_one = jnp.einsum(
        "ctd,ecd->te", grad_projected, qkv_cube, preferred_element_type=jnp.float32
    )
    qkv_grad = jnp.einsum(
        "te,ctd->ecd", normed_one, grad_projected, preferred_element_type=jnp.float32
    ).reshape(width, 3 * width)
    gain_one_grad = jnp.sum(grad_normed_one * unit_one, axis=0)
    grad_unit_one = grad_normed_one * back_gain[0].astype(jnp.float32)
    input_grad = grad_residual + inverse_one * (
        grad_unit_one - unit_one * jnp.mean(grad_unit_one * unit_one, axis=-1, keepdims=True)
    )
    gains_grad = jnp.stack([gain_one_grad, gain_two_grad], axis=0)
    qkv_sum, proj_sum, gains_sum = (
        lax.psum_scatter(qkv_grad, ("seq", "dp"), scatter_dimension=0, tiled=True),
        lax.psum_scatter(proj_grad, ("seq", "dp"), scatter_dimension=0, tiled=True),
        lax.psum_scatter(gains_grad, ("seq", "dp"), scatter_dimension=1, tiled=True),
    )
    wide_rate = 2.5 * D ** (-0.5)
    out_rate = 2.5 * max(D // 512, 1) ** (-0.5)
    down_rate = 2.5 * FF ** (-0.5)
    qkv_new = adam_step(qkv_weight, qkv_sum, qkv_first, qkv_second, wide_rate, WEIGHT_DECAY)
    out_new = adam_step(out_weight, proj_sum, out_first, out_second, out_rate, WEIGHT_DECAY)
    gate_up_new = adam_step(
        gate_up_weight,
        mlp_grad[:, : 2 * FF],
        gate_up_first,
        gate_up_second,
        wide_rate,
        WEIGHT_DECAY,
    )
    down_new = adam_step(
        down_weight, mlp_grad[:, 2 * FF :], down_first, down_second, down_rate, WEIGHT_DECAY
    )
    gains_new = adam_step(gains, gains_sum, gains_first, gains_second, 0.5, 0.0)
    return (
        block_out,
        input_grad[None],
        qkv_new[0],
        out_new[0],
        gate_up_new[0],
        down_new[0],
        gains_new[0],
        qkv_new[1],
        out_new[1],
        gate_up_new[1],
        down_new[1],
        gains_new[1],
        qkv_new[2],
        out_new[2],
        gate_up_new[2],
        down_new[2],
        gains_new[2],
    )


GRID = ("z", "x", "y", "c")
RING = ("z", "c")
PLANE = ("x", "y")
LOW = jnp.bfloat16
WIDE = jnp.float32
CONTRACT_LAST = (((1,), (1,)), ((), ()))
CONTRACT_FIRST = (((0,), (0,)), ((), ()))
DMA = pltpu.SemaphoreType.DMA
ANYWHERE = pl.BlockSpec(memory_space=pl.ANY)
IN_VMEM = pl.BlockSpec(memory_space=pltpu.VMEM)


def remote(source, target, send, receive, **place):
    return pltpu.make_async_remote_copy(
        src_ref=source,
        dst_ref=target,
        send_sem=send,
        recv_sem=receive,
        device_id=place,
        device_id_type=pl.DeviceIdType.MESH,
    )


def lanes(start, size):
    return pl.ds(pl.multiple_of(start, 128), size)


class Place:
    def __init__(self):
        self.z, self.x, self.y, self.c = (lax.axis_index(name) for name in GRID)
        self.slot = 2 * self.z + self.c
        self.block_here = self.block(self.slot, self.x, self.y)

    def block(self, slot, x, y):
        return (((slot // 2) * 2 + x) * 2 + y) * 2 + lax.rem(slot, 2)

    def meet(self, plane):
        barrier = pltpu.get_barrier_semaphore()
        others = [
            {"z": slot // 2, "c": lax.rem(slot, 2)}
            for slot in (lax.rem(self.slot + step, 8) for step in range(1, 8))
        ]
        if plane:
            others += [{"x": 1 - self.x}, {"y": 1 - self.y}, {"x": 1 - self.x, "c": 1 - self.c}]
        for other in others:
            pl.semaphore_signal(
                barrier, inc=1, device_id=other, device_id_type=pl.DeviceIdType.MESH
            )
        pl.semaphore_wait(barrier, len(others))


class Swap:
    def __init__(self, place, source, spot_there, spot_here, sems):
        p = self.place = place
        self.away = lambda: remote(
            source, spot_there, sems.at[0], sems.at[1], x=1 - p.x, c=1 - p.c
        )
        self.here = lambda: pltpu.make_async_copy(source, spot_here, sems.at[2])

    def start(self):
        p = self.place
        pl.when(p.x != p.c)(lambda: self.away().start())
        pl.when(p.x == p.c)(lambda: self.here().start())

    def wait(self):
        p = self.place
        pl.when(p.x != p.c)(lambda: self.away().wait_recv())
        pl.when(p.x == p.c)(lambda: self.here().wait())

    def drain(self):
        p = self.place
        pl.when(p.x != p.c)(lambda: self.away().wait_send())


class LineGather:
    SEMS = (4, 8)

    def __init__(self, place, buffer, sems, mine=None, rows=None):
        self.place, self.sems, self.mine = place, sems, mine
        self.spot = (lambda slot: buffer.at[slot]) if rows is None else (lambda slot: buffer.at[slot, rows])

    def copy(self, slot, way, own=False):
        p, block = self.place, self.spot(slot)
        if way == 0:
            where = {"z": jnp.minimum(p.z + 1, 3)}
        elif way == 1:
            where = {"z": jnp.maximum(p.z - 1, 0)}
        else:
            where = {"c": 1 - p.c}
        source = self.mine if own and self.mine is not None else block
        return remote(source, block, self.sems.at[way, slot], self.sems.at[3, slot], **where)

    def _pass_on(self, slot, way, own=False):
        p = self.place
        if way == 0:
            pl.when(p.z < 3)(lambda: self.copy(slot, 0, own).start())
        elif way == 1:
            pl.when(p.z > 0)(lambda: self.copy(slot, 1, own).start())

    def start(self):
        slot = self.place.slot
        self._pass_on(slot, 0, True)
        self._pass_on(slot, 1, True)
        self.copy(slot, 2, True).start()
        if self.mine is not None:
            self.keep().start()

    def keep(self):
        slot = self.place.slot
        return pltpu.make_async_copy(self.mine, self.spot(slot), self.sems.at[3, slot])

    def inner(self, distance):
        p = self.place
        side = 1 - 2 * (p.z // 2)
        source = p.z + distance * side

        @pl.when((source >= 0) & (source <= 3))
        def _():
            slot = 2 * source + p.c
            self.copy(slot, 2).wait_recv()
            pl.when(p.z == 1)(lambda: self.copy(slot, 1).start())
            pl.when(p.z == 2)(lambda: self.copy(slot, 0).start())
            self.copy(slot, 2).start()

    def outer(self):
        p = self.place
        for here, way in ((1, 0), (2, 1)):

            @pl.when(p.z == here)
            def _():
                slot = p.slot - 2 + 4 * way
                self.copy(slot, 2).wait_recv()
                self.copy(slot, way).start()
                self.copy(slot, 2).start()

    def steps(self):
        self.inner(1)
        self.outer()
        self.inner(2)
        self.inner(3)

    def finish(self):
        p = self.place
        if self.mine is not None:
            self.keep().wait()
        for z in range(4):
            self.copy(2 * z + 1 - p.c, 2).wait_recv()

    def drain(self):
        p = self.place
        for z in range(4):
            slot = 2 * z + p.c
            self.copy(slot, 2).wait_send()
            pl.when((z <= p.z) & (p.z < 3))(lambda: self.copy(slot, 0).wait_send())
            pl.when((z >= p.z) & (p.z > 0))(lambda: self.copy(slot, 1).wait_send())


def add_blocks(target, sources):
    def some(step, carry):
        rows = pl.ds(pl.multiple_of(step * 16, 16), 16)
        total = sources[0][rows, :].astype(WIDE)
        for source in sources[1:]:
            total = total + source[rows, :].astype(WIDE)
        target[rows, :] = total.astype(target.dtype)
        return carry

    lax.fori_loop(0, target.shape[0] // 16, some, 0)


class LineScatter:
    SEMS = (6, 4)

    @staticmethod
    def buffers(rows, width):
        return [pltpu.VMEM((4, rows, width), LOW), pltpu.VMEM((5, rows, width), LOW)]

    def __init__(self, place, partial, across, passing, sems, rows):
        self.place, self.partial, self.sems, self.rows = place, partial, sems, rows
        self.across, self.passing = across, passing

    def cross(self, z):
        p = self.place
        return remote(
            self.partial.at[2 * z + 1 - p.c, self.rows],
            self.across.at[z, self.rows],
            self.sems.at[0, z],
            self.sems.at[1, z],
            c=1 - p.c,
        )

    def hop(self, z, way, landing):
        p = self.place
        there = jnp.minimum(p.z + 1, 3) if way == 0 else jnp.maximum(p.z - 1, 0)
        return remote(
            self.across.at[z, self.rows],
            self.passing.at[landing, self.rows],
            self.sems.at[2 + 2 * way, z],
            self.sems.at[3 + 2 * way, z],
            z=there,
        )

    def send(self, z, way):
        p = self.place
        if way == 0:
            self.hop(z, 0, z).start()
        else:
            pl.when(p.z - 1 == z)(lambda: self.hop(z, 1, 4).start())
            pl.when(p.z - 1 != z)(lambda: self.hop(z, 1, z).start())

    def start(self):
        for z in range(4):
            self.cross(z).start()

    def head(self):
        p = self.place
        for z in range(4):
            self.cross(z).wait_recv()
        for way, end in ((0, 0), (1, 3)):

            @pl.when(p.z == end)
            def _():
                for index in range(3):
                    z = 3 - index if way == 0 else index
                    spot = self.across.at[z, self.rows]
                    add_blocks(spot, [self.partial.at[2 * z + p.c, self.rows], spot])
                    self.send(z, way)

    def step(self, index):
        p = self.place
        for here, way, z in ((1, index // 2, (3, 2, 0)[index]), (2, 1 - index // 2, (0, 1, 3)[index])):

            @pl.when(p.z == here)
            def _():
                self.hop(z, way, z).wait_recv()
                spot = self.across.at[z, self.rows]
                add_blocks(
                    spot,
                    [
                        self.partial.at[2 * z + p.c, self.rows],
                        spot,
                        self.passing.at[z, self.rows],
                    ],
                )
                self.send(z, way)

    def steps(self):
        for index in range(3):
            self.step(index)

    def arrive(self):
        p = self.place
        pl.when(p.z > 0)(lambda: self.hop(p.z, 0, p.z).wait_recv())
        pl.when(p.z < 3)(lambda: self.hop(p.z, 1, 4).wait_recv())
        for end, landing in ((0, 0), (3, 4)):

            @pl.when(p.z == end)
            def _():
                spot = self.passing.at[landing, self.rows]
                spot[...] = jnp.zeros(spot.shape, LOW)

    def total(self, rows):
        p = self.place
        parts = (
            self.partial[p.slot, rows, :],
            self.across[p.z, rows, :],
            self.passing[p.z, rows, :],
            self.passing[4, rows, :],
        )
        return sum(part.astype(WIDE) for part in parts)

    def drain(self):
        p = self.place
        for z in range(4):
            self.cross(z).wait_send()
            pl.when(p.z < z)(lambda: self.hop(z, 0, z).wait_send())
            pl.when(p.z > z)(lambda: self.hop(z, 1, z).wait_send())


class Relayout:
    SEMS = (8, 8)

    def __init__(self, place, parts, target, sems):
        self.place, self.parts, self.target, self.sems = place, parts, target, sems

    def sem(self, kind, slot):
        return self.sems.at[kind, slot]

    def line(self, step):
        p = self.place
        slot = lax.rem(p.slot + step, 8)
        copies = []
        for source, first, size, there in self.parts:
            same_for_all = source.shape[1] == size
            columns = lanes(first if same_for_all else first + size * slot, size)
            piece = source.at[:, columns]
            spot = self.target.at[p.block_here, :, pl.ds(there, size)]
            if step == 0:
                copies.append(pltpu.make_async_copy(piece, spot, self.sem(1, p.slot)))
            else:
                copies.append(
                    remote(
                        piece,
                        spot,
                        self.sem(0, slot),
                        self.sem(1, p.slot),
                        z=slot // 2,
                        c=lax.rem(slot, 2),
                    )
                )
        return copies

    def whole(self, slot):
        p = self.place
        spot = self.target.at[p.block(slot, p.x, p.y)]
        return remote(spot, spot, self.sem(0, slot), self.sem(1, slot), c=1 - p.c)

    def plane(self, slot, x, y, way, send, receive):
        p = self.place
        spot = self.target.at[p.block(slot, x, y)]
        where = {"x": 1 - p.x} if way == 0 else {"y": 1 - p.y}
        return remote(spot, spot, self.sem(send, slot), self.sem(receive, slot), **where)

    def from_own(self, slot, way):
        p = self.place
        return self.plane(slot, p.x, p.y, way, 2 + 2 * way, 3 + 2 * way)

    def corner(self, slot, way):
        p = self.place
        x, y = (p.x, 1 - p.y) if way == 0 else (1 - p.x, p.y)
        return self.plane(slot, x, y, way, 6, 7)

    def start(self, steps=range(8)):
        for step in steps:
            for copy in self.line(step):
                copy.start()

    def spread(self, step):
        p = self.place
        slot = lax.rem(p.slot + 8 - step, 8)
        if isinstance(step, int) and step == 0:
            spot = self.target.at[p.block_here]
            pltpu.make_async_copy(spot, spot, self.sem(1, p.slot)).wait()
        else:
            self.whole(slot).wait_recv()
        for way in range(2):
            self.from_own(slot, way).start()

    def corners(self, z):
        self.from_own(2 * z, 0).wait_recv()
        self.corner(2 * z, 1).start()
        self.from_own(2 * z + 1, 1).wait_recv()
        self.corner(2 * z + 1, 0).start()

    def finish(self):
        for z in range(4):
            self.from_own(2 * z, 1).wait_recv()
            self.from_own(2 * z + 1, 0).wait_recv()
            self.corner(2 * z, 1).wait_recv()
            self.corner(2 * z + 1, 0).wait_recv()

    def drain(self):
        for step in range(1, 8):
            self.whole(lax.rem(self.place.slot + step, 8)).wait_send()
        for z in range(4):
            self.corner(2 * z, 1).wait_send()
            self.corner(2 * z + 1, 0).wait_send()
        for slot in range(8):
            for way in range(2):
                self.from_own(slot, way).wait_send()


class PlaneScatter:
    @staticmethod
    def scratch(units, rows, width):
        shape = (rows, width)
        return [
            pltpu.VMEM((2, 2, units) + shape, LOW),
            pltpu.VMEM((2, units) + shape, LOW),
            DMA((4, 2, 2, units)),
        ]

    def __init__(self, place, part, units, got, last, sems):
        self.place, self.part, self.units = place, part, units
        self.got, self.last, self.sems = got, last, sems

    def pair(self, near):
        p = self.place
        x, y = (p.x, p.y) if near else (1 - p.x, 1 - p.y)
        return ((p.x, y), (x, p.y))

    def own(self, half, near, unit):
        x, y = self.pair(near)[half]
        return self.part(half, unit, x, y)

    def sums(self, half, unit):
        return self.own(half, 1, unit)

    def first(self, half, near, unit):
        p = self.place
        x, y = self.pair(near)[half]
        x, y = (1 - x, y) if half == 0 else (x, 1 - y)
        where = {"x": 1 - p.x} if half == 0 else {"y": 1 - p.y}
        return remote(
            self.part(half, unit, x, y),
            self.got.at[half, near, unit],
            self.sems.at[0, half, near, unit],
            self.sems.at[1, half, near, unit],
            **where,
        )

    def second(self, half, unit):
        p = self.place
        where = {"y": 1 - p.y} if half == 0 else {"x": 1 - p.x}
        return remote(
            self.own(half, 0, unit),
            self.last.at[half, unit],
            self.sems.at[2, half, 0, unit],
            self.sems.at[3, half, 0, unit],
            **where,
        )

    def each(self, call):
        lax.fori_loop(0, self.units, lambda unit, carry: (call(unit), carry)[1], 0)

    def start_unit(self, unit):
        for near in range(2):
            for half in range(2):
                self.first(half, near, unit).start()

    def start(self):
        for near in range(2):

            def begin(unit):
                for half in range(2):
                    self.first(half, near, unit).start()

            self.each(begin)

    def middle(self, unit):
        for half in range(2):
            self.first(half, 0, unit).wait_recv()
            spot = self.own(half, 0, unit)
            add_blocks(spot, [spot, self.got.at[half, 0, unit]])
            self.second(half, unit).start()

    def final(self, unit):
        for half in range(2):
            self.first(half, 1, unit).wait_recv()
            self.second(half, unit).wait_recv()
            spot = self.own(half, 1, unit)
            add_blocks(spot, [spot, self.got.at[half, 1, unit], self.last.at[half, unit]])

    def drain(self):
        def end(unit):
            for half in range(2):
                for near in range(2):
                    self.first(half, near, unit).wait_send()
                self.second(half, unit).wait_send()

        self.each(end)


class LineReturn:
    SEMS = (2, 8)

    def __init__(self, place, sums, parts, target, sems):
        self.place, self.sums, self.parts = place, sums, parts
        self.target, self.sems = target, sems

    def copies(self, z, c, local):
        p = self.place
        made = []
        for here, size, first in self.parts:
            piece = self.sums(c, z).at[:, pl.ds(here, size)]
            spot = self.target.at[:, lanes(first + size * p.slot, size)]
            if local:
                made.append(pltpu.make_async_copy(piece, spot, self.sems.at[1, p.slot]))
            else:
                made.append(
                    remote(
                        piece, spot, self.sems.at[0, 2 * z + c], self.sems.at[1, p.slot], z=z, c=c
                    )
                )
        return made

    def send(self, z):
        p = self.place
        for c in range(2):
            mine = (z == p.z) & (c == p.c)

            @pl.when(mine)
            def _():
                for copy in self.copies(z, c, True):
                    copy.start()

            @pl.when(jnp.logical_not(mine))
            def _():
                for copy in self.copies(z, c, False):
                    copy.start()

    def finish(self):
        p = self.place
        spot = self.sums(0, 0)
        pltpu.make_async_copy(spot, spot, self.sems.at[1, p.slot]).wait()
        for step in range(1, 8):
            slot = lax.rem(p.slot + step, 8)
            whole = remote(
                spot, spot, self.sems.at[0, slot], self.sems.at[1, slot], c=1 - p.c
            )
            whole.wait_recv()
            whole.wait_send()


def kernel_call(kernel, name, number, inputs, in_specs, outputs, out_specs, scratch):
    return pl.pallas_call(
        kernel,
        out_shape=[jax.ShapeDtypeStruct(shape, dtype) for shape, dtype in outputs],
        in_specs=in_specs,
        out_specs=out_specs,
        scratch_shapes=scratch,
        compiler_params=pltpu.CompilerParams(
            collective_id=number, has_side_effects=True, vmem_limit_bytes=60 * 2**20
        ),
        name=name,
    )(*inputs)


CHUNK = 16


def by_rows(count, call):
    def some(step, carry):
        call(pl.ds(pl.multiple_of(step * CHUNK, CHUNK), CHUNK))
        return carry

    lax.fori_loop(0, count // CHUNK, some, 0)


def normed_back(grad_normed, unit, inverse, gain):
    grad_unit = grad_normed * gain
    return inverse * (grad_unit - unit * jnp.mean(grad_unit * unit, axis=-1, keepdims=True))


def turn(values, cosines, sines):
    lane = lax.broadcasted_iota(jnp.int32, values.shape, 1)
    half_dim = HEAD_DIM // 2
    width = values.shape[1]
    partner = jnp.where(
        lax.rem(lane, HEAD_DIM) < half_dim,
        pltpu.roll(values, width - half_dim, 1),
        pltpu.roll(values, half_dim, 1),
    )
    return values * cosines + partner * sines


def head_mask(head):
    lane = lax.broadcasted_iota(jnp.int32, (1, 128), 1)
    return (lane // HEAD_DIM == lax.rem(head, 2)).astype(WIDE).astype(LOW)


def scaled_probs(queries, keys, first_row):
    scores = lax.dot_general(queries, keys, CONTRACT_LAST, preferred_element_type=WIDE)
    scores = scores * HEAD_DIM ** (-0.5)
    row = lax.broadcasted_iota(jnp.int32, scores.shape, 0) + first_row
    column = lax.broadcasted_iota(jnp.int32, scores.shape, 1)
    scores = jnp.where(column <= row, scores, MASKED)
    expo = jnp.exp(scores - jnp.max(scores, axis=1, keepdims=True))
    return expo * (1.0 / jnp.sum(expo, axis=1, keepdims=True))


QUERY_ROWS = 256


def attend_head(head, qkv, total):
    pair = lanes(head // 2 * 128, 128)
    mask = head_mask(head)
    for block in range(qkv.shape[1] // QUERY_ROWS):
        rows = pl.ds(block * QUERY_ROWS, QUERY_ROWS)
        keys = pl.ds(0, (block + 1) * QUERY_ROWS)
        probs = scaled_probs(qkv[0, rows, pair] * mask, qkv[1, keys, pair], block * QUERY_ROWS)
        total[rows, pair] += jnp.dot(
            probs.astype(LOW), qkv[2, keys, pair] * mask, preferred_element_type=WIDE
        )


def forward_kernel(
    tok,
    cot,
    wq,
    gain,
    wg,
    wd,
    wo,
    cosines,
    sines,
    all_cot,
    normed_two,
    full_g,
    full_d,
    out_q,
    out_o,
    out_normed,
    out_qkv,
    out_attended,
    out_residual,
    out_gains,
    out_tok,
    all_tok,
    full_q,
    full_o,
    normed_one,
    qkv,
    heads,
    attended,
    residual,
    gain_rows,
    mine,
    partial,
    *scratch,
):
    buffers, sems = scratch[:2], scratch[2:]
    tok_swap, cot_swap, out_swap, tok_sems, cot_sems, q_sems, g_sems, d_sems = sems[:8]
    o_sems, sum_a, sum_b, gather_a, gather_b, keep_sems = sems[8:]
    p = Place()
    p.meet(True)
    rows_own = tok.shape[0]
    seq_len = 8 * rows_own
    step_q, step_g, step_d = wq.shape[1] // 24, wg.shape[1] // 16, wd.shape[1] // 8
    q_parts = [(wq, i * 8 * step_q, step_q, i * step_q) for i in range(3)]
    q_parts.append((gain, 0, gain.shape[1], 3 * step_q))
    move_q = Relayout(p, q_parts, full_q, q_sems)
    move_g = Relayout(
        p, [(wg, i * 8 * step_g, step_g, i * step_g) for i in range(2)], full_g, g_sems
    )
    move_d = Relayout(p, [(wd, 0, step_d, 0)], full_d, d_sems)
    tokens, cotangents = LineGather(p, all_tok, tok_sems), LineGather(p, all_cot, cot_sems)
    away = 2 * p.z + 1 - p.c
    swap_tok = Swap(p, tok, all_tok.at[away], all_tok.at[p.slot], tok_swap)
    swap_cot = Swap(p, cot, all_cot.at[away], all_cot.at[p.slot], cot_swap)
    swap_out = Swap(p, wo, full_o.at[2 * p.y + 1 - p.x], full_o.at[2 * p.y + p.x], out_swap)
    half = wo.shape[0] // 2

    def out_copy(kind):
        own, beside, above = 2 * p.y + p.x, 2 * p.y + 1 - p.x, 2 * (1 - p.y) + p.x
        send, got = o_sems.at[0, kind], o_sems.at[1, kind]
        if kind < 2:
            where = {"x": 1 - p.x} if kind == 0 else {"y": 1 - p.y}
            return remote(full_o.at[own], full_o.at[own], send, got, **where)
        spot = full_o.at[beside if kind == 2 else above, pl.ds((kind - 2) * half, half)]
        where = {"y": 1 - p.y} if kind == 2 else {"x": 1 - p.x}
        return remote(spot, spot, send, got, **where)

    kept = []

    def keep(source, target):
        copy = pltpu.make_async_copy(source, target, keep_sems.at[len(kept)])
        copy.start()
        kept.append(copy)

    swap_tok.start()
    move_q.start()
    swap_tok.wait()
    tokens.start()
    swap_out.start()
    swap_cot.start()
    for step in range(8):
        move_q.spread(step)
    tokens.inner(1)
    tokens.outer()
    tokens.inner(2)
    swap_out.wait()
    out_copy(0).start()
    out_copy(1).start()
    for z in range(4):
        move_q.corners(z)
    out_copy(0).wait_recv()
    out_copy(2).start()
    out_copy(1).wait_recv()
    out_copy(3).start()
    tokens.inner(3)
    tokens.drain()
    move_g.start()
    move_q.finish()
    columns = full_q.shape[2]
    gain_block = full_q[:, :, pl.ds(3 * step_q, columns - 3 * step_q)].reshape(-1, 128)
    pick = lax.broadcasted_iota(jnp.int32, (8, 128), 0) == lax.broadcasted_iota(
        jnp.int32, (8, 128), 1
    )
    gain_rows[...] = lax.dot_general(
        pick.astype(WIDE).astype(LOW), gain_block, CONTRACT_LAST, preferred_element_type=WIDE
    )
    keep(full_q, out_q)
    keep(gain_rows, out_gains)
    tokens.finish()
    keep(all_tok.at[p.slot], out_tok)

    def norm_slot(slot, carry):
        def some(rows):
            unit, _ = rms_parts(all_tok[slot, rows, :].astype(WIDE))
            there = pl.ds(pl.multiple_of(slot * rows_own + rows.start, CHUNK), CHUNK)
            normed_one[there, :] = (unit * gain_rows[pl.ds(0, 1), :]).astype(LOW)

        by_rows(rows_own, some)
        return carry

    lax.fori_loop(0, 8, norm_slot, 0)
    keep(normed_one, out_normed)

    def project(part, carry):
        rows = pl.ds(pl.multiple_of(part * 512, 512), 512)
        for kind in range(3):
            weight = full_q[:, :, pl.ds(kind * step_q, step_q)].reshape(-1, step_q)
            made = jnp.dot(normed_one[rows, :], weight, preferred_element_type=WIDE)
            if kind < 2:
                made = turn(
                    made,
                    jnp.concatenate([cosines[rows, :]] * 2, axis=1),
                    jnp.concatenate([sines[rows, :]] * 2, axis=1),
                )
            qkv[kind, rows, :] = made.astype(LOW)
        return carry

    lax.fori_loop(0, seq_len // 512, project, 0)
    keep(qkv, out_qkv)
    move_g.spread(0)
    move_g.spread(1)
    heads[...] = jnp.zeros_like(heads)

    def one_head(head, carry):
        attend_head(head, qkv, heads)
        return carry

    lax.fori_loop(0, 4, one_head, 0)
    move_g.spread(2)
    move_g.spread(3)
    attended[...] = heads[...].astype(LOW)
    keep(attended, out_attended)
    out_copy(2).wait_recv()
    out_copy(3).wait_recv()
    keep(full_o, out_o)
    out_weight = lambda: full_o[...].reshape(-1, full_o.shape[2])

    def project_out(part, carry):
        rows = pl.ds(pl.multiple_of(part * 256, 256), 256)
        made = jnp.dot(attended[rows, :], out_weight(), preferred_element_type=WIDE)
        partial[pl.ds(2 * part, 2)] = made.astype(LOW).reshape(2, rows_own, -1)
        return carry

    lax.fori_loop(0, seq_len // 256, project_out, 0)

    part_rows = [pl.ds(0, rows_own // 2), pl.ds(rows_own // 2, rows_own // 2)]
    sums = [
        LineScatter(p, partial, *buffers, sem, rows) for sem, rows in zip((sum_a, sum_b), part_rows)
    ]
    gathers = [
        LineGather(p, normed_two, sem, mine.at[rows], rows)
        for sem, rows in zip((gather_a, gather_b), part_rows)
    ]

    def local(part):
        def some(rows):
            there = pl.ds(pl.multiple_of(part * (rows_own // 2) + rows.start, CHUNK), CHUNK)
            total = all_tok[p.slot, there, :].astype(WIDE) + sums[part].total(there)
            residual[there, :] = total
            unit, _ = rms_parts(total)
            mine[there, :] = (unit * gain_rows[pl.ds(1, 1), :]).astype(LOW)

        by_rows(rows_own // 2, some)

    for part in sums:
        part.start()
    for part in sums:
        part.head()
    move_g.spread(4)
    move_g.spread(5)
    sums[0].steps()
    move_g.spread(6)
    move_g.spread(7)
    swap_cot.wait()
    sums[0].arrive()
    local(0)
    gathers[0].start()
    sums[1].steps()
    gathers[0].inner(1)
    sums[1].arrive()
    local(1)
    gathers[1].start()
    keep(residual, out_residual)
    move_d.start()
    cotangents.start()
    gathers[0].outer()
    gathers[1].inner(1)
    for z in range(4):
        move_g.corners(z)
    for step in range(8):
        move_d.spread(step)
    gathers[0].inner(2)
    gathers[1].outer()
    gathers[1].inner(2)
    cotangents.inner(1)
    cotangents.outer()
    cotangents.inner(2)
    for z in range(4):
        move_d.corners(z)
    gathers[0].inner(3)
    gathers[1].inner(3)
    cotangents.inner(3)
    for kind in range(4):
        out_copy(kind).wait_send()
    for part in (swap_tok, swap_cot, swap_out):
        part.drain()
    for part in gathers + [cotangents, move_g, move_d]:
        part.finish()
    for part in gathers + sums + [cotangents, move_q, move_g, move_d]:
        part.drain()
    for copy in kept:
        copy.wait()


def forward(tokens, cotangent, qkv, gain_columns, gate_up, down, out_rows, cosines, sines):
    rows, width = tokens.shape
    own = qkv.shape[0]
    here = qkv.shape[1] // 24
    q_shape = (32, own, 3 * here + gain_columns.shape[1])
    vmem = lambda shape, dtype=LOW: pltpu.VMEM(shape, dtype)
    outputs = [
        ((8, rows, width), LOW),
        ((8, rows, width), LOW),
        ((32, own, gate_up.shape[1] // 8), LOW),
        ((32, own, down.shape[1] // 8), LOW),
        (q_shape, LOW),
        ((4, own, width), LOW),
        ((8 * rows, width), LOW),
        ((3, 8 * rows, here), LOW),
        ((8 * rows, here), LOW),
        ((rows, width), WIDE),
        ((8, width), WIDE),
        ((rows, width), LOW),
    ]
    return kernel_call(
        forward_kernel,
        "forward",
        1,
        (tokens, cotangent, qkv, gain_columns, gate_up, down, out_rows, cosines, sines),
        [ANYWHERE] * 7 + [IN_VMEM] * 2,
        outputs,
        [ANYWHERE] * len(outputs),
        [
            vmem((8, rows, width)),
            vmem(q_shape),
            vmem((4, own, width)),
            vmem((8 * rows, width)),
            vmem((3, 8 * rows, here)),
            vmem((8 * rows, here), WIDE),
            vmem((8 * rows, here)),
            vmem((rows, width), WIDE),
            vmem((8, width), WIDE),
            vmem((rows, width)),
            vmem((8, rows, width)),
        ]
        + LineScatter.buffers(rows, width)
        + [DMA((3,))] * 3
        + [DMA(LineGather.SEMS)] * 2
        + [DMA(Relayout.SEMS)] * 3
        + [DMA((2, 4))]
        + [DMA(LineScatter.SEMS)] * 2
        + [DMA(LineGather.SEMS)] * 2
        + [DMA((8,))],
    )


def weight_part(place, ref):
    return lambda half, unit, x, y: ref.at[place.block(2 * unit + half, x, y)]


def attend_back(head, qkv, grad_heads, grads):
    pair = lanes(head // 2 * 128, 128)
    mask = head_mask(head)
    for block in range(qkv.shape[1] // QUERY_ROWS):
        rows = pl.ds(block * QUERY_ROWS, QUERY_ROWS)
        keys = pl.ds(0, (block + 1) * QUERY_ROWS)
        queries, grad_rows = qkv[0, rows, pair] * mask, grad_heads[rows, pair] * mask
        key_rows = qkv[1, keys, pair]
        probs = scaled_probs(queries, key_rows, block * QUERY_ROWS)
        grad_probs = lax.dot_general(
            grad_rows, qkv[2, keys, pair], CONTRACT_LAST, preferred_element_type=WIDE
        )
        delta = jnp.sum(probs * grad_probs, axis=1, keepdims=True)
        grad_scores = (probs * (grad_probs - delta) * HEAD_DIM ** (-0.5)).astype(LOW)
        grads[0, rows, pair] += jnp.dot(grad_scores, key_rows * mask, preferred_element_type=WIDE)
        grads[1, keys, pair] += lax.dot_general(
            grad_scores, queries, CONTRACT_FIRST, preferred_element_type=WIDE
        )
        grads[2, keys, pair] += lax.dot_general(
            probs.astype(LOW), grad_rows, CONTRACT_FIRST, preferred_element_type=WIDE
        )


def mlp_kernel(
    normed,
    wg,
    wd,
    cot,
    residual,
    gain_rows,
    branch,
    g_sum,
    d_part,
    block_out,
    out_grad,
    nt,
    full_g,
    full_d,
    ct,
    active,
    grad_wide,
    part_two,
    part_out,
    grad_residual,
    mine,
    *scratch,
):
    p = Place()
    rows_own, width = residual.shape
    seq_len = 8 * rows_own
    own, ff = wd.shape[1], wd.shape[2]
    units = wd.shape[0] // 8
    block_rows, slots = seq_len // 2, 4
    part = ff // 4
    wide = width // 4
    blocks = wide // own
    load_sems, sum_a, sum_b, sum_c, gather_a, gather_b, swap_sems, keep_sems = scratch[7:]
    part_rows = [pl.ds(0, rows_own // 2), pl.ds(rows_own // 2, rows_own // 2)]
    sum_two = [
        LineScatter(p, part_two, *scratch[:2], sem, rows)
        for sem, rows in zip((sum_a, sum_b), part_rows)
    ]
    sum_out = LineScatter(p, part_out, *scratch[2:4], sum_c, pl.ds(0, rows_own))
    plane = PlaneScatter(p, weight_part(p, full_g), units, *scratch[4:7])
    gathers = [
        LineGather(p, branch, sem, mine.at[rows], rows)
        for sem, rows in zip((gather_a, gather_b), part_rows)
    ]

    def load(index):
        if index == 0:
            return pltpu.make_async_copy(normed, nt, load_sems.at[0])
        if index == 1:
            return pltpu.make_async_copy(cot, ct, load_sems.at[1])
        return pltpu.make_async_copy(wd, full_d, load_sems.at[2])

    def load_wide(index, side):
        columns = lanes(side * ff + index * part, part)
        return pltpu.make_async_copy(
            wg.at[:, :, columns], full_g.at[:, :, columns], load_sems.at[3 + 2 * index + side]
        )

    load(0).start()
    for index in range(4):
        for side in range(2):
            load_wide(index, side).start()
        if index == 0:
            load(1).start()
            load(2).start()
    p.meet(True)
    for index in range(3):
        load(index).wait()

    def stage_one(index, carry):
        load_wide(index, 0).wait()
        load_wide(index, 1).wait()
        here, there = lanes(index * part, part), lanes(ff + index * part, part)

        def some(block, carry):
            rows = pl.ds(pl.multiple_of(block * block_rows, block_rows), block_rows)
            these = pl.ds(block * slots, slots)
            left = nt[these].reshape(block_rows, width)
            gate = jnp.dot(left, full_g[:, :, here].reshape(width, part), preferred_element_type=WIDE)
            up = jnp.dot(left, full_g[:, :, there].reshape(width, part), preferred_element_type=WIDE)
            grad = jnp.dot(
                ct[these].reshape(block_rows, width),
                full_d[:, :, here].reshape(width, part),
                preferred_element_type=WIDE,
            )
            sigmoid_gate = jax.nn.sigmoid(gate)
            active[rows, here] = (gate * sigmoid_gate * up).astype(LOW)
            grad_wide[rows, here] = (
                grad * up * sigmoid_gate * (1.0 + gate * (1.0 - sigmoid_gate))
            ).astype(LOW)
            grad_wide[rows, there] = (grad * gate * sigmoid_gate).astype(LOW)
            return carry

        return lax.fori_loop(0, seq_len // block_rows, some, carry)

    lax.fori_loop(0, 4, stage_one, 0)

    def rows_times(left, weight, target, index):
        def some(block, carry):
            made = lax.dot_general(
                left[pl.ds(pl.multiple_of(block * block_rows, block_rows), block_rows), :],
                weight[pl.ds(index * blocks, blocks)].reshape(wide, -1),
                CONTRACT_LAST,
                preferred_element_type=WIDE,
            )
            target[pl.ds(block * slots, slots), :, lanes(index * wide, wide)] = made.astype(
                LOW
            ).reshape(slots, rows_own, wide)
            return carry

        lax.fori_loop(0, seq_len // block_rows, some, 0)

    def each_part(call):
        lax.fori_loop(0, 4, lambda index, carry: (call(index), carry)[1], 0)

    def down_grad(index, carry):
        made = lax.dot_general(
            ct[:, :, lanes(index * wide, wide)].reshape(seq_len, wide),
            active[...],
            CONTRACT_FIRST,
            preferred_element_type=WIDE,
        )
        full_d[pl.ds(index * blocks, blocks)] = made.astype(LOW).reshape(blocks, own, ff)
        return carry

    def wide_grad(index):
        for side in range(2):
            made = lax.dot_general(
                nt[:, :, pl.ds(index * wide, wide)].reshape(seq_len, wide),
                grad_wide[:, pl.ds(side * ff, ff)],
                CONTRACT_FIRST,
                preferred_element_type=WIDE,
            )
            full_g[pl.ds(index * blocks, blocks), :, pl.ds(side * ff, ff)] = made.astype(
                LOW
            ).reshape(blocks, own, ff)
        plane.start_unit(index)

    def local_two(part):
        def some(rows):
            spot = pl.ds(pl.multiple_of(part * (rows_own // 2) + rows.start, CHUNK), CHUNK)
            unit, inverse = rms_parts(residual[spot, :])
            total = ct[p.slot, spot, :].astype(WIDE) + normed_back(
                sum_two[part].total(spot), unit, inverse, gain_rows[pl.ds(1, 1), :]
            )
            grad_residual[spot, :] = total
            mine[spot, :] = total.astype(LOW)

        by_rows(rows_own // 2, some)

    each_part(lambda index: rows_times(grad_wide, full_g, part_two, index))
    for half in sum_two:
        half.start()
    for half in sum_two:
        half.head()
    each_part(lambda index: rows_times(active, full_d, part_out, index))
    sum_two[0].step(0)
    sum_out.start()
    lax.fori_loop(0, 2, down_grad, 0)
    sum_two[0].step(1)
    sum_two[0].step(2)
    lax.fori_loop(2, 4, down_grad, 0)
    keep_d = pltpu.make_async_copy(full_d, d_part, keep_sems.at[0])
    keep_d.start()
    sum_two[0].arrive()
    local_two(0)
    gathers[0].start()
    wide_grad(0)
    sum_two[1].step(0)
    wide_grad(1)
    sum_two[1].step(1)
    sum_two[1].step(2)
    gathers[0].inner(1)
    wide_grad(2)
    sum_two[1].arrive()
    local_two(1)
    gathers[1].start()
    sum_out.head()
    keep_grad = pltpu.make_async_copy(grad_residual, out_grad, keep_sems.at[1])
    keep_grad.start()
    wide_grad(3)
    gathers[0].outer()
    gathers[1].inner(1)
    gathers[0].inner(2)
    gathers[1].outer()
    gathers[1].inner(2)
    plane.middle(0)
    plane.middle(1)
    sum_out.step(0)
    gathers[0].inner(3)
    gathers[1].inner(3)
    sum_out.step(1)
    sum_out.step(2)
    plane.middle(2)
    plane.middle(3)
    for gather in gathers:
        gather.finish()
    for gather in gathers:
        gather.drain()
    sum_out.arrive()

    def local_out(rows):
        mine[rows, :] = (residual[rows, :] + sum_out.total(rows)).astype(LOW)

    by_rows(rows_own, local_out)
    swap = Swap(p, mine, block_out, block_out, swap_sems)
    swap.start()

    def keep_g(half, unit):
        return pltpu.make_async_copy(
            plane.sums(half, unit), g_sum.at[half, unit], keep_sems.at[2 + 4 * half + unit]
        )

    for unit in range(units):
        plane.final(unit)
        for half in range(2):
            keep_g(half, unit).start()
    swap.wait()
    swap.drain()
    for part in sum_two + [sum_out, plane]:
        part.drain()
    keep_d.wait()
    keep_grad.wait()
    for unit in range(units):
        for half in range(2):
            keep_g(half, unit).wait()


def mlp(normed, wg, wd, cot, residual, gain_rows):
    _, rows, width = normed.shape
    own, ff = wd.shape[1:]
    units = wd.shape[0] // 8
    vmem = lambda shape, dtype=LOW: pltpu.VMEM(shape, dtype)
    return kernel_call(
        mlp_kernel,
        "mlp",
        2,
        (normed, wg, wd, cot, residual, gain_rows),
        [ANYWHERE] * 4 + [IN_VMEM] * 2,
        [
            (normed.shape, LOW),
            ((2, units, own, 2 * ff), LOW),
            (wd.shape, LOW),
            ((rows, width), LOW),
            ((rows, width), WIDE),
        ],
        [ANYWHERE] * 5,
        [
            vmem(normed.shape),
            vmem(wg.shape),
            vmem(wd.shape),
            vmem(cot.shape),
            vmem((8 * rows, ff)),
            vmem((8 * rows, 2 * ff)),
            vmem(normed.shape),
            vmem(normed.shape),
            vmem((rows, width), WIDE),
            vmem((rows, width)),
        ]
        + LineScatter.buffers(rows, width) * 2
        + PlaneScatter.scratch(units, own, 2 * ff)
        + [DMA((11,))]
        + [DMA(LineScatter.SEMS)] * 3
        + [DMA(LineGather.SEMS)] * 2
        + [DMA((3,)), DMA((2 + 2 * units,))],
    )


def backward_kernel(
    branch_all,
    grad_in,
    gain_rows,
    own_tok,
    full_q,
    full_o,
    qkv,
    attended,
    normed_one,
    cosines,
    sines,
    g_sum,
    d_part,
    input_grad,
    q_out,
    g_out,
    d_out,
    o_out,
    work,
    branch,
    grad_residual,
    grad_heads,
    grads,
    grad_projected,
    q_part,
    o_part,
    o_sum,
    d_here,
    *scratch,
):
    buffers, rest = scratch[:2], scratch[2:]
    p = Place()
    rows_own, width = grad_residual.shape
    seq_len = 8 * rows_own
    own = full_o.shape[1]
    units = g_sum.shape[1]
    half = own // 2
    step_q, step_g, step_d = q_part.shape[2] // 3, g_sum.shape[3] // 2, d_part.shape[2]
    plane_d = PlaneScatter(p, weight_part(p, d_here), units, *rest[:3])
    plane_q = PlaneScatter(p, weight_part(p, q_part), units, *rest[3:6])
    plane_o = PlaneScatter(
        p, lambda h, u, x, y: o_part.at[2 * y + x, pl.ds(h * half, half)], 1, *rest[6:9]
    )
    sum_sems, return_sems, swap_sems, load_sems = rest[9:11], rest[11:14], rest[14:17], rest[17]
    part_rows = [pl.ds(0, rows_own // 2), pl.ds(rows_own // 2, rows_own // 2)]
    sum_one = [
        LineScatter(p, branch, *buffers, sem, rows) for sem, rows in zip(sum_sems, part_rows)
    ]
    return_q = LineReturn(
        p, plane_q.sums, [(i * step_q, step_q, i * 8 * step_q) for i in range(3)], q_out, return_sems[0]
    )
    return_g = LineReturn(
        p,
        lambda c, z: g_sum.at[c, z],
        [(i * step_g, step_g, i * 8 * step_g) for i in range(2)],
        g_out,
        return_sems[1],
    )
    return_d = LineReturn(p, plane_d.sums, [(0, step_d, 0)], d_out, return_sems[2])
    swap_in = [
        Swap(p, grad_residual.at[rows], input_grad.at[rows], input_grad.at[rows], sem)
        for sem, rows in zip(swap_sems[:2], part_rows)
    ]
    swap_out = Swap(p, o_sum, o_out, o_out, swap_sems[2])

    def load(source, target, index):
        return pltpu.make_async_copy(source, target, load_sems.at[index])

    loads = [
        load(branch_all, branch, 0),
        load(d_part, d_here, 1),
        load(normed_one, work, 2),
        load(grad_in, grad_residual, 3),
    ]
    for copy in loads:
        copy.start()
    p.meet(True)
    for z in range(4):
        return_g.send(z)
    loads[0].wait()

    def back_out(part, carry):
        rows = pl.ds(pl.multiple_of(part * 256, 256), 256)
        made = lax.dot_general(
            branch[pl.ds(2 * part, 2)].reshape(256, width),
            full_o[...].reshape(-1, width),
            CONTRACT_LAST,
            preferred_element_type=WIDE,
        )
        grad_heads[rows, :] = made.astype(LOW)
        return carry

    lax.fori_loop(0, seq_len // 256, back_out, 0)
    loads[1].wait()
    plane_d.start()

    def out_grad(part, carry):
        columns = lanes(part * 512, 512)
        made = lax.dot_general(
            attended[...],
            branch[:, :, columns].reshape(seq_len, 512),
            CONTRACT_FIRST,
            preferred_element_type=WIDE,
        )
        o_part[:, :, columns] = made.astype(LOW).reshape(4, own, 512)
        return carry

    lax.fori_loop(0, width // 512, out_grad, 0)
    plane_o.start()
    grads[...] = jnp.zeros_like(grads)

    def one_head(head, carry):
        attend_back(head, qkv, grad_heads, grads)
        plane_d.middle(head)
        return carry

    lax.fori_loop(0, 4, one_head, 0)

    def back_turn(part, carry):
        rows = pl.ds(pl.multiple_of(part * 256, 256), 256)
        for kind in range(3):
            made = grads[kind, rows, :]
            if kind < 2:
                made = turn(
                    made,
                    jnp.concatenate([cosines[rows, :]] * 2, axis=1),
                    jnp.concatenate([-sines[rows, :]] * 2, axis=1),
                )
            grad_projected[rows, pl.ds(kind * step_q, step_q)] = made.astype(LOW)
        return carry

    lax.fori_loop(0, seq_len // 256, back_turn, 0)

    def back_qkv(part, carry):
        weight = full_q[pl.ds(part * 8, 8), :, pl.ds(0, 3 * step_q)].reshape(8 * own, 3 * step_q)
        for block in range(seq_len // 512):
            made = lax.dot_general(
                grad_projected[pl.ds(block * 512, 512), :],
                weight,
                CONTRACT_LAST,
                preferred_element_type=WIDE,
            )
            branch[pl.ds(block * 4, 4), :, lanes(part * 8 * own, 8 * own)] = made.astype(
                LOW
            ).reshape(4, rows_own, 8 * own)
        return carry

    lax.fori_loop(0, 4, back_qkv, 0)
    for part in sum_one:
        part.start()
    loads[2].wait()
    loads[3].wait()
    for part in sum_one:
        part.head()

    def qkv_grad(part, carry):
        made = lax.dot_general(
            work[:, :, lanes(part * 8 * own, 8 * own)].reshape(seq_len, 8 * own),
            grad_projected[...],
            CONTRACT_FIRST,
            preferred_element_type=WIDE,
        )
        q_part[pl.ds(part * 8, 8)] = made.astype(LOW).reshape(8, own, 3 * step_q)
        plane_q.start_unit(part)
        return carry

    lax.fori_loop(0, 4, qkv_grad, 0)

    def local_one(part):
        def some(rows):
            spot = pl.ds(pl.multiple_of(part * (rows_own // 2) + rows.start, CHUNK), CHUNK)
            unit, inverse = rms_parts(own_tok[spot, :].astype(WIDE))
            grad_residual[spot, :] = grad_residual[spot, :] + normed_back(
                sum_one[part].total(spot), unit, inverse, gain_rows[pl.ds(0, 1), :]
            )

        by_rows(rows_own // 2, some)

    for part in sum_one:
        part.steps()
    for unit in range(units):
        plane_d.final(unit)
        return_d.send(unit)
    plane_o.middle(0)
    for unit in range(units):
        plane_q.middle(unit)
    for part in range(2):
        sum_one[part].arrive()
        local_one(part)
        swap_in[part].start()
    plane_o.final(0)
    for h in range(2):
        o_sum[pl.ds(h * half, half), :] = plane_o.sums(h, 0)[...]
    swap_out.start()
    for unit in range(units):
        plane_q.final(unit)
        return_q.send(unit)
    for part in (return_g, return_d, return_q):
        part.finish()
    for part in swap_in + [swap_out]:
        part.wait()
        part.drain()
    for part in sum_one + [plane_d, plane_q, plane_o]:
        part.drain()


def backward(
    branch,
    grad_residual,
    gain_rows,
    own_tok,
    full_q,
    full_o,
    qkv,
    attended,
    normed_one,
    cosines,
    sines,
    g_sum,
    d_part,
):
    _, rows, width = branch.shape
    own, here = full_o.shape[1], attended.shape[1]
    units = g_sum.shape[1]
    vmem = lambda shape, dtype=LOW: pltpu.VMEM(shape, dtype)
    step_g, step_d = g_sum.shape[3], d_part.shape[2]
    return kernel_call(
        backward_kernel,
        "backward",
        3,
        (
            branch,
            grad_residual,
            gain_rows,
            own_tok,
            full_q,
            full_o,
            qkv,
            attended,
            normed_one,
            cosines,
            sines,
            g_sum,
            d_part,
        ),
        [ANYWHERE] * 2 + [IN_VMEM] * 6 + [ANYWHERE] + [IN_VMEM] * 2 + [ANYWHERE] * 2,
        [
            ((rows, width), WIDE),
            ((own, 24 * here), LOW),
            ((own, 8 * step_g), LOW),
            ((own, 8 * step_d), LOW),
            ((own, width), LOW),
        ],
        [ANYWHERE] * 5,
        [
            vmem((8, rows, width)),
            vmem((8, rows, width)),
            vmem((rows, width), WIDE),
            vmem((8 * rows, here)),
            vmem((3, 8 * rows, here), WIDE),
            vmem((8 * rows, 3 * here)),
            vmem((32, own, 3 * here)),
            vmem((4, own, width)),
            vmem((own, width)),
            vmem(d_part.shape),
        ]
        + LineScatter.buffers(rows, width)
        + PlaneScatter.scratch(units, own, step_d)
        + PlaneScatter.scratch(units, own, 3 * here)
        + PlaneScatter.scratch(1, own // 2, width)
        + [DMA(LineScatter.SEMS)] * 2
        + [DMA(LineReturn.SEMS)] * 3
        + [DMA((3,))] * 3
        + [DMA((4,))],
    )


def grid_shards(
    tokens,
    cotangent,
    qkv_weight,
    out_weight,
    gate_up_weight,
    down_weight,
    gains,
    qkv_first,
    out_first,
    gate_up_first,
    down_first,
    gains_first,
    qkv_second,
    out_second,
    gate_up_second,
    down_second,
    gains_second,
):
    rows, width = tokens.shape[1:]
    seq_len = 8 * rows
    gain_columns = jnp.pad(gains.astype(LOW).T, ((0, 0), (0, 126)))
    cosines, sines = rope_tables(jnp.arange(seq_len, dtype=jnp.int32))
    cosines, sines = (
        jnp.tile(cosines[:, 0], (1, 4)),
        jnp.tile(jnp.concatenate([-sines[:, 0], sines[:, 0]], axis=1), (1, 2)),
    )
    (
        grad_out,
        normed_two,
        gate_up_full,
        down_full,
        qkv_full,
        out_full,
        normed_one,
        qkv_heads,
        attended,
        residual,
        gain_full,
        own_tokens,
    ) = forward(
        tokens[0],
        cotangent[0],
        qkv_weight.astype(LOW),
        gain_columns,
        gate_up_weight.astype(LOW),
        down_weight.astype(LOW),
        out_weight.astype(LOW),
        cosines,
        sines,
    )
    grad_branch, gate_up_half, down_part, block_out, grad_residual = mlp(
        normed_two, gate_up_full, down_full, grad_out, residual, gain_full
    )
    input_grad, qkv_sum, gate_up_sum, down_sum, out_sum = backward(
        grad_branch,
        grad_residual,
        gain_full,
        own_tokens,
        qkv_full,
        out_full,
        qkv_heads,
        attended,
        normed_one.reshape(8, rows, width),
        cosines,
        sines,
        gate_up_half,
        down_part,
    )
    qkv_sum, gate_up_sum, down_sum, out_sum = (
        total.astype(WIDE) for total in (qkv_sum, gate_up_sum, down_sum, out_sum)
    )
    gains_sum = jnp.stack(
        [
            jnp.sum(weight.astype(LOW).astype(WIDE) * total, axis=1)
            for weight, total in ((qkv_weight, qkv_sum), (gate_up_weight, gate_up_sum))
        ],
        axis=0,
    ) / gains.astype(LOW).astype(WIDE)
    wide_rate = 2.5 * D ** (-0.5)
    out_rate = 2.5 * max(D // 512, 1) ** (-0.5)
    down_rate = 2.5 * FF ** (-0.5)
    qkv_new = adam_step(qkv_weight, qkv_sum, qkv_first, qkv_second, wide_rate, WEIGHT_DECAY)
    out_new = adam_step(out_weight, out_sum, out_first, out_second, out_rate, WEIGHT_DECAY)
    gate_up_new = adam_step(
        gate_up_weight, gate_up_sum, gate_up_first, gate_up_second, wide_rate, WEIGHT_DECAY
    )
    down_new = adam_step(
        down_weight, down_sum, down_first, down_second, down_rate, WEIGHT_DECAY
    )
    gains_new = adam_step(gains, gains_sum, gains_first, gains_second, 0.5, 0.0)
    return (
        block_out[None],
        input_grad[None],
        qkv_new[0],
        out_new[0],
        gate_up_new[0],
        down_new[0],
        gains_new[0],
        qkv_new[1],
        out_new[1],
        gate_up_new[1],
        down_new[1],
        gains_new[1],
        qkv_new[2],
        out_new[2],
        gate_up_new[2],
        down_new[2],
        gains_new[2],
    )


def mapped(body, mesh, token_spec, row_spec, gain_spec):
    one_set = (row_spec, row_spec, row_spec, row_spec, gain_spec)
    return jax.shard_map(
        body,
        mesh=mesh,
        in_specs=(token_spec, token_spec) + one_set * 3,
        out_specs=(token_spec, token_spec) + one_set * 3,
        check_vma=False,
    )


def solution(mesh):
    if mesh.shape["seq"] == 8 and mesh.shape["dp"] == 4:
        grid_mesh = Mesh(mesh.devices.reshape(4, 2, 2, 2), GRID)
        return mapped(
            grid_shards,
            grid_mesh,
            P(("y", "c"), ("z", "x"), None),
            P(GRID, None),
            P(None, GRID),
        )
    return mapped(
        shards, mesh, P("dp", "seq", None), P(("seq", "dp"), None), P(None, ("seq", "dp"))
    )
```

```python
import jax
import jax.numpy as jnp
import numpy as np
from jax import lax
from jax.experimental import pallas as pl
from jax.experimental.pallas import tpu as pltpu
from jax.sharding import Mesh
from jax.sharding import PartitionSpec as P

D = 2048
HEADS = 32
HEAD_DIM = 64
FF = 8192
BLOCK = 512
STEP = 10


NORM_EPS = 1e-05
ROPE_BASE = 130000.0
BETA_ONE = 0.9
BETA_TWO = 0.999
ADAM_EPS = 1e-08
WEIGHT_DECAY = 0.1
MASKED = -1e30


def rms_parts(values):
    inverse = lax.rsqrt(jnp.mean(values * values, axis=-1, keepdims=True) + NORM_EPS)
    return (values * inverse, inverse)


def rope_tables(positions):
    half_dim = HEAD_DIM // 2
    exponent = jnp.arange(half_dim, dtype=jnp.float32) * (2.0 / HEAD_DIM)
    frequency = ROPE_BASE ** (-exponent)
    angles = positions.astype(jnp.float32)[:, None] * frequency[None, :]
    return (jnp.cos(angles)[:, None, :], jnp.sin(angles)[:, None, :])


def rotate(tensor, cosines, sines):
    half_dim = HEAD_DIM // 2
    lower_half = tensor[..., :half_dim]
    upper_half = tensor[..., half_dim:]
    return jnp.concatenate(
        [lower_half * cosines - upper_half * sines, upper_half * cosines + lower_half * sines],
        axis=-1,
    )


def unrotate(tensor, cosines, sines):
    half_dim = HEAD_DIM // 2
    lower_half = tensor[..., :half_dim]
    upper_half = tensor[..., half_dim:]
    return jnp.concatenate(
        [lower_half * cosines + upper_half * sines, upper_half * cosines - lower_half * sines],
        axis=-1,
    )


def block_scores(query_rows, key_heads, key_id, block_id):
    key_rows = lax.dynamic_slice_in_dim(key_heads, key_id * BLOCK, BLOCK, 0)
    products = jnp.einsum(
        "qhd,khd->hqk", query_rows, key_rows, preferred_element_type=jnp.float32
    ) * HEAD_DIM ** (-0.5)
    local_ids = jnp.arange(BLOCK, dtype=jnp.int32)
    allowed = (key_id < block_id) | (local_ids[None, :] <= local_ids[:, None])
    return jnp.where(allowed[None], products, MASKED)


def row_normalizer(query_rows, key_heads, block_id):
    row_shape = (query_rows.shape[1], BLOCK, 1)

    def absorb(key_id, state):
        running_max, running_total = state
        scores = block_scores(query_rows, key_heads, key_id, block_id)
        new_max = jnp.maximum(running_max, jnp.max(scores, axis=-1, keepdims=True))
        running_total = running_total * jnp.exp(running_max - new_max) + jnp.sum(
            jnp.exp(scores - new_max), axis=-1, keepdims=True
        )
        return (new_max, running_total)

    start_state = (jnp.full(row_shape, MASKED, jnp.float32), jnp.zeros(row_shape, jnp.float32))
    final_max, final_total = lax.fori_loop(0, block_id + 1, absorb, start_state)
    return final_max + jnp.log(final_total)


def attend_forward(query_heads, key_heads, value_heads):
    seq_len, heads_here, head_dim = query_heads.shape

    def one_block(block_id, carry):
        out_all, lse_all = carry
        row_start = block_id * BLOCK
        query_rows = lax.dynamic_slice_in_dim(query_heads, row_start, BLOCK, 0)
        row_lse = row_normalizer(query_rows, key_heads, block_id)

        def weigh_values(key_id, running):
            scores = block_scores(query_rows, key_heads, key_id, block_id)
            weights_low = jnp.exp(scores - row_lse).astype(jnp.bfloat16)
            value_rows = lax.dynamic_slice_in_dim(value_heads, key_id * BLOCK, BLOCK, 0)
            return running + jnp.einsum(
                "hqk,khd->qhd", weights_low, value_rows, preferred_element_type=jnp.float32
            )

        attended = lax.fori_loop(
            0, block_id + 1, weigh_values, jnp.zeros((BLOCK, heads_here, head_dim), jnp.float32)
        )
        out_all = lax.dynamic_update_slice_in_dim(
            out_all, attended.astype(jnp.bfloat16), row_start, 0
        )
        lse_all = lax.dynamic_update_slice_in_dim(lse_all, row_lse, row_start, 1)
        return (out_all, lse_all)

    start_carry = (
        jnp.zeros((seq_len, heads_here, head_dim), jnp.bfloat16),
        jnp.zeros((heads_here, seq_len, 1), jnp.float32),
    )
    return lax.fori_loop(0, seq_len // BLOCK, one_block, start_carry)


def attend_backward(query_heads, key_heads, value_heads, grad_heads, lse_all):
    seq_len, heads_here, head_dim = query_heads.shape
    score_scale = HEAD_DIM ** (-0.5)

    def one_block(block_id, carry):
        grad_q_all, grad_k_all, grad_v_all = carry
        row_start = block_id * BLOCK
        query_rows = lax.dynamic_slice_in_dim(query_heads, row_start, BLOCK, 0)
        grad_rows = lax.dynamic_slice_in_dim(grad_heads, row_start, BLOCK, 0)
        row_lse = lax.dynamic_slice_in_dim(lse_all, row_start, BLOCK, 1)

        def probs_and_grads(key_id):
            scores = block_scores(query_rows, key_heads, key_id, block_id)
            probs = jnp.exp(scores - row_lse)
            value_rows = lax.dynamic_slice_in_dim(value_heads, key_id * BLOCK, BLOCK, 0)
            grad_probs = jnp.einsum(
                "qhd,khd->hqk", grad_rows, value_rows, preferred_element_type=jnp.float32
            )
            return (probs, grad_probs)

        def add_delta(key_id, running):
            probs, grad_probs = probs_and_grads(key_id)
            return running + jnp.sum(probs * grad_probs, axis=-1, keepdims=True)

        row_delta = lax.fori_loop(
            0, block_id + 1, add_delta, jnp.zeros((heads_here, BLOCK, 1), jnp.float32)
        )

        def spread(key_id, inner):
            grad_q_rows, grad_k_acc, grad_v_acc = inner
            probs, grad_probs = probs_and_grads(key_id)
            key_start = key_id * BLOCK
            key_rows = lax.dynamic_slice_in_dim(key_heads, key_start, BLOCK, 0)
            grad_scores = (probs * (grad_probs - row_delta) * score_scale).astype(jnp.bfloat16)
            grad_q_rows = grad_q_rows + jnp.einsum(
                "hqk,khd->qhd", grad_scores, key_rows, preferred_element_type=jnp.float32
            )
            grad_k_part = jnp.einsum(
                "hqk,qhd->khd", grad_scores, query_rows, preferred_element_type=jnp.float32
            )
            grad_v_part = jnp.einsum(
                "hqk,qhd->khd",
                probs.astype(jnp.bfloat16),
                grad_rows,
                preferred_element_type=jnp.float32,
            )
            grad_k_acc = lax.dynamic_update_slice_in_dim(
                grad_k_acc,
                lax.dynamic_slice_in_dim(grad_k_acc, key_start, BLOCK, 0) + grad_k_part,
                key_start,
                0,
            )
            grad_v_acc = lax.dynamic_update_slice_in_dim(
                grad_v_acc,
                lax.dynamic_slice_in_dim(grad_v_acc, key_start, BLOCK, 0) + grad_v_part,
                key_start,
                0,
            )
            return (grad_q_rows, grad_k_acc, grad_v_acc)

        start_inner = (
            jnp.zeros((BLOCK, heads_here, head_dim), jnp.float32),
            grad_k_all,
            grad_v_all,
        )
        grad_q_rows, grad_k_all, grad_v_all = lax.fori_loop(0, block_id + 1, spread, start_inner)
        grad_q_all = lax.dynamic_update_slice_in_dim(grad_q_all, grad_q_rows, row_start, 0)
        return (grad_q_all, grad_k_all, grad_v_all)

    zeros_all = jnp.zeros((seq_len, heads_here, head_dim), jnp.float32)
    return lax.fori_loop(0, seq_len // BLOCK, one_block, (zeros_all, zeros_all, zeros_all))


def adam_step(weight, gradient, first, second, rate, decay):
    new_first = BETA_ONE * first + (1.0 - BETA_ONE) * gradient
    new_second = BETA_TWO * second + (1.0 - BETA_TWO) * gradient * gradient
    first_hat = new_first / (1.0 - BETA_ONE**STEP)
    second_hat = new_second / (1.0 - BETA_TWO**STEP)
    new_weight = weight - rate * (first_hat / (jnp.sqrt(second_hat) + ADAM_EPS) + decay * weight)
    return (new_weight, new_first, new_second)


def shards(
    tokens,
    cotangent,
    qkv_weight,
    out_weight,
    gate_up_weight,
    down_weight,
    gains,
    qkv_first,
    out_first,
    gate_up_first,
    down_first,
    gains_first,
    qkv_second,
    out_second,
    gate_up_second,
    down_second,
    gains_second,
):
    seq_count = lax.axis_size("seq")
    tok_rows = tokens.shape[1]
    width = tokens.shape[2]
    seq_len = tok_rows * seq_count
    heads_here = HEADS // seq_count
    width_here = heads_here * HEAD_DIM
    contract_last = (((1,), (1,)), ((), ()))
    contract_first = (((0,), (0,)), ((), ()))
    qkv_full, proj_full, gain_full = (
        lax.all_gather(qkv_weight.astype(jnp.bfloat16), ("seq", "dp"), axis=0, tiled=True),
        lax.all_gather(out_weight.astype(jnp.bfloat16), ("seq", "dp"), axis=0, tiled=True),
        lax.all_gather(gains.astype(jnp.bfloat16), ("seq", "dp"), axis=1, tiled=True),
    )
    up_full, down_full = (
        lax.all_gather(gate_up_weight.astype(jnp.bfloat16), ("seq", "dp"), axis=0, tiled=True),
        lax.all_gather(down_weight.astype(jnp.bfloat16), ("seq", "dp"), axis=0, tiled=True),
    )
    hidden_in = tokens[0].astype(jnp.float32)
    unit_one, inverse_one = rms_parts(hidden_in)
    normed_one = (unit_one * gain_full[0].astype(jnp.float32)).astype(jnp.bfloat16)
    projected = jnp.einsum(
        "te,ecd->ctd",
        normed_one,
        qkv_full.reshape(width, 3, width),
        preferred_element_type=jnp.float32,
    )
    positions = lax.axis_index("seq") * tok_rows + jnp.arange(tok_rows, dtype=jnp.int32)
    cos_local, sin_local = rope_tables(positions)
    turned = rotate(projected[:2].reshape(2, tok_rows, HEADS, HEAD_DIM), cos_local, sin_local)
    packed = jnp.concatenate([turned.reshape(2, tok_rows, width), projected[2:]], axis=0).astype(
        jnp.bfloat16
    )
    by_heads = lax.all_to_all(packed, "seq", split_axis=2, concat_axis=1, tiled=True)
    query_heads = by_heads[0].reshape(seq_len, heads_here, HEAD_DIM)
    key_heads = by_heads[1].reshape(seq_len, heads_here, HEAD_DIM)
    value_heads = by_heads[2].reshape(seq_len, heads_here, HEAD_DIM)
    out_heads, lse_all = attend_forward(query_heads, key_heads, value_heads)
    attended = lax.all_to_all(
        out_heads.reshape(seq_len, width_here), "seq", split_axis=0, concat_axis=1, tiled=True
    )
    residual = hidden_in + jnp.dot(attended, proj_full, preferred_element_type=jnp.float32)
    unit_two, inverse_two = rms_parts(residual)
    normed_two = (unit_two * gain_full[1].astype(jnp.float32)).astype(jnp.bfloat16)
    gate_up = jnp.dot(normed_two, up_full, preferred_element_type=jnp.float32)
    gate_vals = gate_up[:, :FF]
    up_vals = gate_up[:, FF:]
    sigmoid_gate = jax.nn.sigmoid(gate_vals)
    activated = (gate_vals * sigmoid_gate * up_vals).astype(jnp.bfloat16)
    mlp_out = lax.dot_general(
        activated, down_full, contract_last, preferred_element_type=jnp.float32
    )
    block_out = (residual + mlp_out).astype(jnp.bfloat16)[None]
    back_up, back_down, back_gain = (
        lax.all_gather(gate_up_weight.astype(jnp.bfloat16), ("seq", "dp"), axis=0, tiled=True),
        lax.all_gather(down_weight.astype(jnp.bfloat16), ("seq", "dp"), axis=0, tiled=True),
        lax.all_gather(gains.astype(jnp.bfloat16), ("seq", "dp"), axis=1, tiled=True),
    )
    grad_out = cotangent[0]
    grad_act = jnp.dot(grad_out, back_down, preferred_element_type=jnp.float32)
    grad_gate = grad_act * up_vals * sigmoid_gate * (1.0 + gate_vals * (1.0 - sigmoid_gate))
    grad_up = grad_act * gate_vals * sigmoid_gate
    grad_gate_up = jnp.concatenate([grad_gate, grad_up], axis=1).astype(jnp.bfloat16)
    grad_normed_two = lax.dot_general(
        grad_gate_up, back_up, contract_last, preferred_element_type=jnp.float32
    )
    gain_two_grad = jnp.sum(grad_normed_two * unit_two, axis=0)
    grad_unit_two = grad_normed_two * back_gain[1].astype(jnp.float32)
    grad_residual = grad_out.astype(jnp.float32) + inverse_two * (
        grad_unit_two - unit_two * jnp.mean(grad_unit_two * unit_two, axis=-1, keepdims=True)
    )
    gate_up_rows = lax.dot_general(
        normed_two, grad_gate_up, contract_first, preferred_element_type=jnp.float32
    )
    down_rows = lax.dot_general(
        grad_out, activated, contract_first, preferred_element_type=jnp.float32
    )
    mlp_grad = lax.psum_scatter(
        jnp.concatenate([gate_up_rows, down_rows], axis=1),
        ("seq", "dp"),
        scatter_dimension=0,
        tiled=True,
    )
    back_qkv, back_proj = (
        lax.all_gather(qkv_weight.astype(jnp.bfloat16), ("seq", "dp"), axis=0, tiled=True),
        lax.all_gather(out_weight.astype(jnp.bfloat16), ("seq", "dp"), axis=0, tiled=True),
    )
    grad_branch = grad_residual.astype(jnp.bfloat16)
    proj_grad = lax.dot_general(
        attended, grad_branch, contract_first, preferred_element_type=jnp.float32
    )
    grad_attended = lax.dot_general(
        grad_branch, back_proj, contract_last, preferred_element_type=jnp.float32
    ).astype(jnp.bfloat16)
    grad_heads = lax.all_to_all(
        grad_attended, "seq", split_axis=1, concat_axis=0, tiled=True
    ).reshape(seq_len, heads_here, HEAD_DIM)
    grad_q_all, grad_k_all, grad_v_all = attend_backward(
        query_heads, key_heads, value_heads, grad_heads, lse_all
    )
    cos_whole, sin_whole = rope_tables(jnp.arange(seq_len, dtype=jnp.int32))
    grad_pack = jnp.stack(
        [
            unrotate(grad_q_all, cos_whole, sin_whole).reshape(seq_len, width_here),
            unrotate(grad_k_all, cos_whole, sin_whole).reshape(seq_len, width_here),
            grad_v_all.reshape(seq_len, width_here),
        ],
        axis=0,
    ).astype(jnp.bfloat16)
    grad_projected = lax.all_to_all(grad_pack, "seq", split_axis=1, concat_axis=2, tiled=True)
    qkv_cube = back_qkv.reshape(width, 3, width)
    grad_normed_one = jnp.einsum(
        "ctd,ecd->te", grad_projected, qkv_cube, preferred_element_type=jnp.float32
    )
    qkv_grad = jnp.einsum(
        "te,ctd->ecd", normed_one, grad_projected, preferred_element_type=jnp.float32
    ).reshape(width, 3 * width)
    gain_one_grad = jnp.sum(grad_normed_one * unit_one, axis=0)
    grad_unit_one = grad_normed_one * back_gain[0].astype(jnp.float32)
    input_grad = grad_residual + inverse_one * (
        grad_unit_one - unit_one * jnp.mean(grad_unit_one * unit_one, axis=-1, keepdims=True)
    )
    gains_grad = jnp.stack([gain_one_grad, gain_two_grad], axis=0)
    qkv_sum, proj_sum, gains_sum = (
        lax.psum_scatter(qkv_grad, ("seq", "dp"), scatter_dimension=0, tiled=True),
        lax.psum_scatter(proj_grad, ("seq", "dp"), scatter_dimension=0, tiled=True),
        lax.psum_scatter(gains_grad, ("seq", "dp"), scatter_dimension=1, tiled=True),
    )
    wide_rate = 2.5 * D ** (-0.5)
    out_rate = 2.5 * max(D // 512, 1) ** (-0.5)
    down_rate = 2.5 * FF ** (-0.5)
    qkv_new = adam_step(qkv_weight, qkv_sum, qkv_first, qkv_second, wide_rate, WEIGHT_DECAY)
    out_new = adam_step(out_weight, proj_sum, out_first, out_second, out_rate, WEIGHT_DECAY)
    gate_up_new = adam_step(
        gate_up_weight,
        mlp_grad[:, : 2 * FF],
        gate_up_first,
        gate_up_second,
        wide_rate,
        WEIGHT_DECAY,
    )
    down_new = adam_step(
        down_weight, mlp_grad[:, 2 * FF :], down_first, down_second, down_rate, WEIGHT_DECAY
    )
    gains_new = adam_step(gains, gains_sum, gains_first, gains_second, 0.5, 0.0)
    return (
        block_out,
        input_grad[None],
        qkv_new[0],
        out_new[0],
        gate_up_new[0],
        down_new[0],
        gains_new[0],
        qkv_new[1],
        out_new[1],
        gate_up_new[1],
        down_new[1],
        gains_new[1],
        qkv_new[2],
        out_new[2],
        gate_up_new[2],
        down_new[2],
        gains_new[2],
    )


GRID = ("z", "x", "y", "c")
RING = ("z", "c")
PLANE = ("x", "y")
LOW = jnp.bfloat16
WIDE = jnp.float32
CONTRACT_LAST = (((1,), (1,)), ((), ()))
CONTRACT_FIRST = (((0,), (0,)), ((), ()))
DMA = pltpu.SemaphoreType.DMA
ANYWHERE = pl.BlockSpec(memory_space=pl.ANY)
IN_VMEM = pl.BlockSpec(memory_space=pltpu.VMEM)


def remote(source, target, send, receive, **place):
    return pltpu.make_async_remote_copy(
        src_ref=source,
        dst_ref=target,
        send_sem=send,
        recv_sem=receive,
        device_id=place,
        device_id_type=pl.DeviceIdType.MESH,
    )


def lanes(start, size):
    return pl.ds(pl.multiple_of(start, 128), size)


class Place:
    def __init__(self):
        self.z, self.x, self.y, self.c = (lax.axis_index(name) for name in GRID)
        self.slot = 2 * self.z + self.c
        self.block_here = self.block(self.slot, self.x, self.y)

    def block(self, slot, x, y):
        return (((slot // 2) * 2 + x) * 2 + y) * 2 + lax.rem(slot, 2)

    def meet(self, plane):
        barrier = pltpu.get_barrier_semaphore()
        others = [
            {"z": slot // 2, "c": lax.rem(slot, 2)}
            for slot in (lax.rem(self.slot + step, 8) for step in range(1, 8))
        ]
        if plane:
            others += [{"x": 1 - self.x}, {"y": 1 - self.y}, {"x": 1 - self.x, "c": 1 - self.c}]
        for other in others:
            pl.semaphore_signal(
                barrier, inc=1, device_id=other, device_id_type=pl.DeviceIdType.MESH
            )
        pl.semaphore_wait(barrier, len(others))


class Swap:
    def __init__(self, place, source, spot_there, spot_here, sems):
        p = self.place = place
        self.away = lambda: remote(
            source, spot_there, sems.at[0], sems.at[1], x=1 - p.x, c=1 - p.c
        )
        self.here = lambda: pltpu.make_async_copy(source, spot_here, sems.at[2])

    def start(self):
        p = self.place
        pl.when(p.x != p.c)(lambda: self.away().start())
        pl.when(p.x == p.c)(lambda: self.here().start())

    def wait(self):
        p = self.place
        pl.when(p.x != p.c)(lambda: self.away().wait_recv())
        pl.when(p.x == p.c)(lambda: self.here().wait())

    def drain(self):
        p = self.place
        pl.when(p.x != p.c)(lambda: self.away().wait_send())


class LineGather:
    SEMS = (4, 8)

    def __init__(self, place, buffer, sems, mine=None, rows=None):
        self.place, self.sems, self.mine = place, sems, mine
        self.spot = (lambda slot: buffer.at[slot]) if rows is None else (lambda slot: buffer.at[slot, rows])

    def copy(self, slot, way, own=False):
        p, block = self.place, self.spot(slot)
        if way == 0:
            where = {"z": jnp.minimum(p.z + 1, 3)}
        elif way == 1:
            where = {"z": jnp.maximum(p.z - 1, 0)}
        else:
            where = {"c": 1 - p.c}
        source = self.mine if own and self.mine is not None else block
        return remote(source, block, self.sems.at[way, slot], self.sems.at[3, slot], **where)

    def _pass_on(self, slot, way, own=False):
        p = self.place
        if way == 0:
            pl.when(p.z < 3)(lambda: self.copy(slot, 0, own).start())
        elif way == 1:
            pl.when(p.z > 0)(lambda: self.copy(slot, 1, own).start())

    def start(self):
        slot = self.place.slot
        self._pass_on(slot, 0, True)
        self._pass_on(slot, 1, True)
        self.copy(slot, 2, True).start()
        if self.mine is not None:
            self.keep().start()

    def keep(self):
        slot = self.place.slot
        return pltpu.make_async_copy(self.mine, self.spot(slot), self.sems.at[3, slot])

    def inner(self, distance):
        p = self.place
        side = 1 - 2 * (p.z // 2)
        source = p.z + distance * side

        @pl.when((source >= 0) & (source <= 3))
        def _():
            slot = 2 * source + p.c
            self.copy(slot, 2).wait_recv()
            pl.when(p.z == 1)(lambda: self.copy(slot, 1).start())
            pl.when(p.z == 2)(lambda: self.copy(slot, 0).start())
            self.copy(slot, 2).start()

    def outer(self):
        p = self.place
        for here, way in ((1, 0), (2, 1)):

            @pl.when(p.z == here)
            def _():
                slot = p.slot - 2 + 4 * way
                self.copy(slot, 2).wait_recv()
                self.copy(slot, way).start()
                self.copy(slot, 2).start()

    def steps(self):
        self.inner(1)
        self.outer()
        self.inner(2)
        self.inner(3)

    def finish(self):
        p = self.place
        if self.mine is not None:
            self.keep().wait()
        for z in range(4):
            self.copy(2 * z + 1 - p.c, 2).wait_recv()

    def drain(self):
        p = self.place
        for z in range(4):
            slot = 2 * z + p.c
            self.copy(slot, 2).wait_send()
            pl.when((z <= p.z) & (p.z < 3))(lambda: self.copy(slot, 0).wait_send())
            pl.when((z >= p.z) & (p.z > 0))(lambda: self.copy(slot, 1).wait_send())


def add_blocks(target, sources):
    def some(step, carry):
        rows = pl.ds(pl.multiple_of(step * 16, 16), 16)
        total = sources[0][rows, :].astype(WIDE)
        for source in sources[1:]:
            total = total + source[rows, :].astype(WIDE)
        target[rows, :] = total.astype(target.dtype)
        return carry

    lax.fori_loop(0, target.shape[0] // 16, some, 0)


class LineScatter:
    SEMS = (6, 4)

    @staticmethod
    def buffers(rows, width):
        return [pltpu.VMEM((4, rows, width), LOW), pltpu.VMEM((5, rows, width), LOW)]

    def __init__(self, place, partial, across, passing, sems, rows):
        self.place, self.partial, self.sems, self.rows = place, partial, sems, rows
        self.across, self.passing = across, passing

    def cross(self, z):
        p = self.place
        return remote(
            self.partial.at[2 * z + 1 - p.c, self.rows],
            self.across.at[z, self.rows],
            self.sems.at[0, z],
            self.sems.at[1, z],
            c=1 - p.c,
        )

    def hop(self, z, way, landing):
        p = self.place
        there = jnp.minimum(p.z + 1, 3) if way == 0 else jnp.maximum(p.z - 1, 0)
        return remote(
            self.across.at[z, self.rows],
            self.passing.at[landing, self.rows],
            self.sems.at[2 + 2 * way, z],
            self.sems.at[3 + 2 * way, z],
            z=there,
        )

    def send(self, z, way):
        p = self.place
        if way == 0:
            self.hop(z, 0, z).start()
        else:
            pl.when(p.z - 1 == z)(lambda: self.hop(z, 1, 4).start())
            pl.when(p.z - 1 != z)(lambda: self.hop(z, 1, z).start())

    def start(self):
        for z in range(4):
            self.cross(z).start()

    def head(self):
        p = self.place
        for z in range(4):
            self.cross(z).wait_recv()
        for way, end in ((0, 0), (1, 3)):

            @pl.when(p.z == end)
            def _():
                for index in range(3):
                    z = 3 - index if way == 0 else index
                    spot = self.across.at[z, self.rows]
                    add_blocks(spot, [self.partial.at[2 * z + p.c, self.rows], spot])
                    self.send(z, way)

    def step(self, index):
        p = self.place
        for here, way, z in ((1, index // 2, (3, 2, 0)[index]), (2, 1 - index // 2, (0, 1, 3)[index])):

            @pl.when(p.z == here)
            def _():
                self.hop(z, way, z).wait_recv()
                spot = self.across.at[z, self.rows]
                add_blocks(
                    spot,
                    [
                        self.partial.at[2 * z + p.c, self.rows],
                        spot,
                        self.passing.at[z, self.rows],
                    ],
                )
                self.send(z, way)

    def steps(self):
        for index in range(3):
            self.step(index)

    def arrive(self):
        p = self.place
        pl.when(p.z > 0)(lambda: self.hop(p.z, 0, p.z).wait_recv())
        pl.when(p.z < 3)(lambda: self.hop(p.z, 1, 4).wait_recv())
        for end, landing in ((0, 0), (3, 4)):

            @pl.when(p.z == end)
            def _():
                spot = self.passing.at[landing, self.rows]
                spot[...] = jnp.zeros(spot.shape, LOW)

    def total(self, rows):
        p = self.place
        parts = (
            self.partial[p.slot, rows, :],
            self.across[p.z, rows, :],
            self.passing[p.z, rows, :],
            self.passing[4, rows, :],
        )
        return sum(part.astype(WIDE) for part in parts)

    def drain(self):
        p = self.place
        for z in range(4):
            self.cross(z).wait_send()
            pl.when(p.z < z)(lambda: self.hop(z, 0, z).wait_send())
            pl.when(p.z > z)(lambda: self.hop(z, 1, z).wait_send())


class Relayout:
    SEMS = (8, 8)

    def __init__(self, place, parts, target, sems):
        self.place, self.parts, self.target, self.sems = place, parts, target, sems

    def sem(self, kind, slot):
        return self.sems.at[kind, slot]

    def line(self, step):
        p = self.place
        slot = lax.rem(p.slot + step, 8)
        copies = []
        for source, first, size, there in self.parts:
            same_for_all = source.shape[1] == size
            columns = lanes(first if same_for_all else first + size * slot, size)
            piece = source.at[:, columns]
            spot = self.target.at[p.block_here, :, pl.ds(there, size)]
            if step == 0:
                copies.append(pltpu.make_async_copy(piece, spot, self.sem(1, p.slot)))
            else:
                copies.append(
                    remote(
                        piece,
                        spot,
                        self.sem(0, slot),
                        self.sem(1, p.slot),
                        z=slot // 2,
                        c=lax.rem(slot, 2),
                    )
                )
        return copies

    def whole(self, slot):
        p = self.place
        spot = self.target.at[p.block(slot, p.x, p.y)]
        return remote(spot, spot, self.sem(0, slot), self.sem(1, slot), c=1 - p.c)

    def plane(self, slot, x, y, way, send, receive):
        p = self.place
        spot = self.target.at[p.block(slot, x, y)]
        where = {"x": 1 - p.x} if way == 0 else {"y": 1 - p.y}
        return remote(spot, spot, self.sem(send, slot), self.sem(receive, slot), **where)

    def from_own(self, slot, way):
        p = self.place
        return self.plane(slot, p.x, p.y, way, 2 + 2 * way, 3 + 2 * way)

    def corner(self, slot, way):
        p = self.place
        x, y = (p.x, 1 - p.y) if way == 0 else (1 - p.x, p.y)
        return self.plane(slot, x, y, way, 6, 7)

    def start(self, steps=range(8)):
        for step in steps:
            for copy in self.line(step):
                copy.start()

    def spread(self, step):
        p = self.place
        slot = lax.rem(p.slot + 8 - step, 8)
        if isinstance(step, int) and step == 0:
            spot = self.target.at[p.block_here]
            pltpu.make_async_copy(spot, spot, self.sem(1, p.slot)).wait()
        else:
            self.whole(slot).wait_recv()
        for way in range(2):
            self.from_own(slot, way).start()

    def corners(self, z):
        self.from_own(2 * z, 0).wait_recv()
        self.corner(2 * z, 1).start()
        self.from_own(2 * z + 1, 1).wait_recv()
        self.corner(2 * z + 1, 0).start()

    def finish(self):
        for z in range(4):
            self.from_own(2 * z, 1).wait_recv()
            self.from_own(2 * z + 1, 0).wait_recv()
            self.corner(2 * z, 1).wait_recv()
            self.corner(2 * z + 1, 0).wait_recv()

    def drain(self):
        for step in range(1, 8):
            self.whole(lax.rem(self.place.slot + step, 8)).wait_send()
        for z in range(4):
            self.corner(2 * z, 1).wait_send()
            self.corner(2 * z + 1, 0).wait_send()
        for slot in range(8):
            for way in range(2):
                self.from_own(slot, way).wait_send()


class PlaneScatter:
    @staticmethod
    def scratch(units, rows, width):
        shape = (rows, width)
        return [
            pltpu.VMEM((2, 2, units) + shape, LOW),
            pltpu.VMEM((2, units) + shape, LOW),
            DMA((4, 2, 2, units)),
        ]

    def __init__(self, place, part, units, got, last, sems):
        self.place, self.part, self.units = place, part, units
        self.got, self.last, self.sems = got, last, sems

    def pair(self, near):
        p = self.place
        x, y = (p.x, p.y) if near else (1 - p.x, 1 - p.y)
        return ((p.x, y), (x, p.y))

    def own(self, half, near, unit):
        x, y = self.pair(near)[half]
        return self.part(half, unit, x, y)

    def sums(self, half, unit):
        return self.own(half, 1, unit)

    def first(self, half, near, unit):
        p = self.place
        x, y = self.pair(near)[half]
        x, y = (1 - x, y) if half == 0 else (x, 1 - y)
        where = {"x": 1 - p.x} if half == 0 else {"y": 1 - p.y}
        return remote(
            self.part(half, unit, x, y),
            self.got.at[half, near, unit],
            self.sems.at[0, half, near, unit],
            self.sems.at[1, half, near, unit],
            **where,
        )

    def second(self, half, unit):
        p = self.place
        where = {"y": 1 - p.y} if half == 0 else {"x": 1 - p.x}
        return remote(
            self.own(half, 0, unit),
            self.last.at[half, unit],
            self.sems.at[2, half, 0, unit],
            self.sems.at[3, half, 0, unit],
            **where,
        )

    def each(self, call):
        lax.fori_loop(0, self.units, lambda unit, carry: (call(unit), carry)[1], 0)

    def start_unit(self, unit):
        for near in range(2):
            for half in range(2):
                self.first(half, near, unit).start()

    def start(self):
        for near in range(2):

            def begin(unit):
                for half in range(2):
                    self.first(half, near, unit).start()

            self.each(begin)

    def middle(self, unit):
        for half in range(2):
            self.first(half, 0, unit).wait_recv()
            spot = self.own(half, 0, unit)
            add_blocks(spot, [spot, self.got.at[half, 0, unit]])
            self.second(half, unit).start()

    def final(self, unit):
        for half in range(2):
            self.first(half, 1, unit).wait_recv()
            self.second(half, unit).wait_recv()
            spot = self.own(half, 1, unit)
            add_blocks(spot, [spot, self.got.at[half, 1, unit], self.last.at[half, unit]])

    def drain(self):
        def end(unit):
            for half in range(2):
                for near in range(2):
                    self.first(half, near, unit).wait_send()
                self.second(half, unit).wait_send()

        self.each(end)


class LineReturn:
    SEMS = (2, 8)

    def __init__(self, place, sums, parts, target, sems):
        self.place, self.sums, self.parts = place, sums, parts
        self.target, self.sems = target, sems

    def copies(self, z, c, local):
        p = self.place
        made = []
        for here, size, first in self.parts:
            piece = self.sums(c, z).at[:, pl.ds(here, size)]
            spot = self.target.at[:, lanes(first + size * p.slot, size)]
            if local:
                made.append(pltpu.make_async_copy(piece, spot, self.sems.at[1, p.slot]))
            else:
                made.append(
                    remote(
                        piece, spot, self.sems.at[0, 2 * z + c], self.sems.at[1, p.slot], z=z, c=c
                    )
                )
        return made

    def send(self, z):
        p = self.place
        for c in range(2):
            mine = (z == p.z) & (c == p.c)

            @pl.when(mine)
            def _():
                for copy in self.copies(z, c, True):
                    copy.start()

            @pl.when(jnp.logical_not(mine))
            def _():
                for copy in self.copies(z, c, False):
                    copy.start()

    def finish(self):
        p = self.place
        spot = self.sums(0, 0)
        pltpu.make_async_copy(spot, spot, self.sems.at[1, p.slot]).wait()
        for step in range(1, 8):
            slot = lax.rem(p.slot + step, 8)
            whole = remote(
                spot, spot, self.sems.at[0, slot], self.sems.at[1, slot], c=1 - p.c
            )
            whole.wait_recv()
            whole.wait_send()


def kernel_call(kernel, name, number, inputs, in_specs, outputs, out_specs, scratch):
    return pl.pallas_call(
        kernel,
        out_shape=[jax.ShapeDtypeStruct(shape, dtype) for shape, dtype in outputs],
        in_specs=in_specs,
        out_specs=out_specs,
        scratch_shapes=scratch,
        compiler_params=pltpu.CompilerParams(
            collective_id=number, has_side_effects=True, vmem_limit_bytes=60 * 2**20
        ),
        name=name,
    )(*inputs)


CHUNK = 16


def by_rows(count, call):
    def some(step, carry):
        call(pl.ds(pl.multiple_of(step * CHUNK, CHUNK), CHUNK))
        return carry

    lax.fori_loop(0, count // CHUNK, some, 0)


def normed_back(grad_normed, unit, inverse, gain):
    grad_unit = grad_normed * gain
    return inverse * (grad_unit - unit * jnp.mean(grad_unit * unit, axis=-1, keepdims=True))


def turn_tables(length):
    half_dim = HEAD_DIM // 2
    exponent = np.arange(half_dim, dtype=np.float32) * np.float32(2.0 / HEAD_DIM)
    frequency = np.float32(ROPE_BASE) ** (-exponent)
    angles = np.arange(length, dtype=np.float32)[:, None] * frequency[None, :]
    angles = angles.astype(np.float64)
    cosines, sines = np.cos(angles).astype(np.float32), np.sin(angles).astype(np.float32)
    return (
        jnp.asarray(np.tile(cosines, (1, 4))),
        jnp.asarray(np.tile(np.concatenate([-sines, sines], axis=1), (1, 2))),
    )


def turn(values, cosines, sines):
    lane = lax.broadcasted_iota(jnp.int32, values.shape, 1)
    half_dim = HEAD_DIM // 2
    width = values.shape[1]
    partner = jnp.where(
        lax.rem(lane, HEAD_DIM) < half_dim,
        pltpu.roll(values, width - half_dim, 1),
        pltpu.roll(values, half_dim, 1),
    )
    return values * cosines + partner * sines


def head_mask(head):
    lane = lax.broadcasted_iota(jnp.int32, (1, 128), 1)
    return (lane // HEAD_DIM == lax.rem(head, 2)).astype(WIDE).astype(LOW)


def scaled_probs(queries, keys, first_row):
    scores = lax.dot_general(queries, keys, CONTRACT_LAST, preferred_element_type=WIDE)
    scores = scores * HEAD_DIM ** (-0.5)
    row = lax.broadcasted_iota(jnp.int32, scores.shape, 0) + first_row
    column = lax.broadcasted_iota(jnp.int32, scores.shape, 1)
    scores = jnp.where(column <= row, scores, MASKED)
    expo = jnp.exp(scores - jnp.max(scores, axis=1, keepdims=True))
    return expo * (1.0 / jnp.sum(expo, axis=1, keepdims=True))


QUERY_ROWS = 256


def attend_head(head, qkv, total):
    pair = lanes(head // 2 * 128, 128)
    mask = head_mask(head)
    for block in range(qkv.shape[1] // QUERY_ROWS):
        rows = pl.ds(block * QUERY_ROWS, QUERY_ROWS)
        keys = pl.ds(0, (block + 1) * QUERY_ROWS)
        probs = scaled_probs(qkv[0, rows, pair] * mask, qkv[1, keys, pair], block * QUERY_ROWS)
        total[rows, pair] += jnp.dot(
            probs.astype(LOW), qkv[2, keys, pair] * mask, preferred_element_type=WIDE
        )


def forward_kernel(
    tok,
    cot,
    wide_q,
    gain,
    wide_g,
    wide_d,
    wide_o,
    cosines,
    sines,
    all_cot,
    normed_two,
    full_g,
    full_d,
    out_q,
    out_o,
    out_normed,
    out_qkv,
    out_attended,
    out_residual,
    out_gains,
    out_tok,
    all_tok,
    full_q,
    full_o,
    normed_one,
    qkv,
    heads,
    attended,
    residual,
    gain_rows,
    mine,
    partial,
    from_q,
    from_g,
    from_d,
    from_o,
    wq,
    wg,
    wd,
    wo,
    *scratch,
):
    buffers, sems = scratch[:2], scratch[2:]
    tok_swap, cot_swap, out_swap, tok_sems, cot_sems, q_sems, g_sems, d_sems = sems[:8]
    o_sems, sum_a, sum_b, gather_a, gather_b, keep_sems, cast_sems = sems[8:]
    casts = [
        (wide_q, from_q, wq),
        (wide_o, from_o, wo),
        (wide_g, from_g, wg),
        (wide_d, from_d, wd),
    ]
    loads = [
        pltpu.make_async_copy(source, target, cast_sems.at[index])
        for index, (source, target, _) in enumerate(casts)
    ]
    for copy in loads:
        copy.start()

    def cast(index):
        _, source, target = casts[index]
        loads[index].wait()
        parts = source.shape[1] // 2048

        def some(step, carry):
            rows = pl.ds(pl.multiple_of(step // parts * CHUNK, CHUNK), CHUNK)
            columns = lanes(lax.rem(step, parts) * 2048, 2048)
            target[rows, columns] = source[rows, columns].astype(LOW)
            return carry

        lax.fori_loop(0, source.shape[0] // CHUNK * parts, some, 0)

    p = Place()
    p.meet(True)
    rows_own = tok.shape[0]
    seq_len = 8 * rows_own
    step_q, step_g, step_d = wq.shape[1] // 24, wg.shape[1] // 16, wd.shape[1] // 8
    q_parts = [(wq, i * 8 * step_q, step_q, i * step_q) for i in range(3)]
    q_parts.append((gain, 0, gain.shape[1], 3 * step_q))
    move_q = Relayout(p, q_parts, full_q, q_sems)
    move_g = Relayout(
        p, [(wg, i * 8 * step_g, step_g, i * step_g) for i in range(2)], full_g, g_sems
    )
    move_d = Relayout(p, [(wd, 0, step_d, 0)], full_d, d_sems)
    tokens, cotangents = LineGather(p, all_tok, tok_sems), LineGather(p, all_cot, cot_sems)
    away = 2 * p.z + 1 - p.c
    swap_tok = Swap(p, tok, all_tok.at[away], all_tok.at[p.slot], tok_swap)
    swap_cot = Swap(p, cot, all_cot.at[away], all_cot.at[p.slot], cot_swap)
    swap_out = Swap(p, wo, full_o.at[2 * p.y + 1 - p.x], full_o.at[2 * p.y + p.x], out_swap)
    half = wo.shape[0] // 2

    def out_copy(kind):
        own, beside, above = 2 * p.y + p.x, 2 * p.y + 1 - p.x, 2 * (1 - p.y) + p.x
        send, got = o_sems.at[0, kind], o_sems.at[1, kind]
        if kind < 2:
            where = {"x": 1 - p.x} if kind == 0 else {"y": 1 - p.y}
            return remote(full_o.at[own], full_o.at[own], send, got, **where)
        spot = full_o.at[beside if kind == 2 else above, pl.ds((kind - 2) * half, half)]
        where = {"y": 1 - p.y} if kind == 2 else {"x": 1 - p.x}
        return remote(spot, spot, send, got, **where)

    kept = []

    def keep(source, target):
        copy = pltpu.make_async_copy(source, target, keep_sems.at[len(kept)])
        copy.start()
        kept.append(copy)

    swap_tok.start()
    cast(0)
    move_q.start()
    cast(1)
    swap_tok.wait()
    tokens.start()
    swap_out.start()
    swap_cot.start()
    cast(2)
    cast(3)
    for step in range(8):
        move_q.spread(step)
    tokens.inner(1)
    tokens.outer()
    tokens.inner(2)
    swap_out.wait()
    out_copy(0).start()
    out_copy(1).start()
    for z in range(4):
        move_q.corners(z)
    out_copy(0).wait_recv()
    out_copy(2).start()
    out_copy(1).wait_recv()
    out_copy(3).start()
    tokens.inner(3)
    tokens.drain()
    move_g.start()
    move_q.finish()
    columns = full_q.shape[2]
    gain_block = full_q[:, :, pl.ds(3 * step_q, columns - 3 * step_q)].reshape(-1, 128)
    pick = lax.broadcasted_iota(jnp.int32, (8, 128), 0) == lax.broadcasted_iota(
        jnp.int32, (8, 128), 1
    )
    gain_rows[...] = lax.dot_general(
        pick.astype(WIDE).astype(LOW), gain_block, CONTRACT_LAST, preferred_element_type=WIDE
    )
    keep(full_q, out_q)
    keep(gain_rows, out_gains)
    tokens.finish()
    keep(all_tok.at[p.slot], out_tok)

    def norm_slot(slot, carry):
        def some(rows):
            unit, _ = rms_parts(all_tok[slot, rows, :].astype(WIDE))
            there = pl.ds(pl.multiple_of(slot * rows_own + rows.start, CHUNK), CHUNK)
            normed_one[there, :] = (unit * gain_rows[pl.ds(0, 1), :]).astype(LOW)

        by_rows(rows_own, some)
        return carry

    lax.fori_loop(0, 8, norm_slot, 0)
    keep(normed_one, out_normed)

    def project(part, carry):
        rows = pl.ds(pl.multiple_of(part * 512, 512), 512)
        for kind in range(3):
            weight = full_q[:, :, pl.ds(kind * step_q, step_q)].reshape(-1, step_q)
            made = jnp.dot(normed_one[rows, :], weight, preferred_element_type=WIDE)
            if kind < 2:
                made = turn(
                    made,
                    jnp.concatenate([cosines[rows, :]] * 2, axis=1),
                    jnp.concatenate([sines[rows, :]] * 2, axis=1),
                )
            qkv[kind, rows, :] = made.astype(LOW)
        return carry

    lax.fori_loop(0, seq_len // 512, project, 0)
    keep(qkv, out_qkv)
    move_g.spread(0)
    move_g.spread(1)
    heads[...] = jnp.zeros_like(heads)

    def one_head(head, carry):
        attend_head(head, qkv, heads)
        return carry

    lax.fori_loop(0, 4, one_head, 0)
    move_g.spread(2)
    move_g.spread(3)
    attended[...] = heads[...].astype(LOW)
    keep(attended, out_attended)
    out_copy(2).wait_recv()
    out_copy(3).wait_recv()
    keep(full_o, out_o)
    out_weight = lambda: full_o[...].reshape(-1, full_o.shape[2])

    def project_out(part, carry):
        rows = pl.ds(pl.multiple_of(part * 256, 256), 256)
        made = jnp.dot(attended[rows, :], out_weight(), preferred_element_type=WIDE)
        partial[pl.ds(2 * part, 2)] = made.astype(LOW).reshape(2, rows_own, -1)
        return carry

    lax.fori_loop(0, seq_len // 256, project_out, 0)

    part_rows = [pl.ds(0, rows_own // 2), pl.ds(rows_own // 2, rows_own // 2)]
    sums = [
        LineScatter(p, partial, *buffers, sem, rows) for sem, rows in zip((sum_a, sum_b), part_rows)
    ]
    gathers = [
        LineGather(p, normed_two, sem, mine.at[rows], rows)
        for sem, rows in zip((gather_a, gather_b), part_rows)
    ]

    def local(part):
        def some(rows):
            there = pl.ds(pl.multiple_of(part * (rows_own // 2) + rows.start, CHUNK), CHUNK)
            total = all_tok[p.slot, there, :].astype(WIDE) + sums[part].total(there)
            residual[there, :] = total
            unit, _ = rms_parts(total)
            mine[there, :] = (unit * gain_rows[pl.ds(1, 1), :]).astype(LOW)

        by_rows(rows_own // 2, some)

    for part in sums:
        part.start()
    for part in sums:
        part.head()
    move_g.spread(4)
    move_g.spread(5)
    sums[0].steps()
    move_g.spread(6)
    move_g.spread(7)
    swap_cot.wait()
    sums[0].arrive()
    local(0)
    gathers[0].start()
    sums[1].steps()
    gathers[0].inner(1)
    sums[1].arrive()
    local(1)
    gathers[1].start()
    keep(residual, out_residual)
    move_d.start()
    cotangents.start()
    gathers[0].outer()
    gathers[1].inner(1)
    for z in range(4):
        move_g.corners(z)
    for step in range(8):
        move_d.spread(step)
    gathers[0].inner(2)
    gathers[1].outer()
    gathers[1].inner(2)
    cotangents.inner(1)
    cotangents.outer()
    cotangents.inner(2)
    for z in range(4):
        move_d.corners(z)
    gathers[0].inner(3)
    gathers[1].inner(3)
    cotangents.inner(3)
    for kind in range(4):
        out_copy(kind).wait_send()
    for part in (swap_tok, swap_cot, swap_out):
        part.drain()
    for part in gathers + [cotangents, move_g, move_d]:
        part.finish()
    for part in gathers + sums + [cotangents, move_q, move_g, move_d]:
        part.drain()
    for copy in kept:
        copy.wait()


def forward(tokens, cotangent, qkv, gain_columns, gate_up, down, out_rows, cosines, sines):
    rows, width = tokens.shape
    own = qkv.shape[0]
    here = qkv.shape[1] // 24
    q_shape = (32, own, 3 * here + gain_columns.shape[1])
    vmem = lambda shape, dtype=LOW: pltpu.VMEM(shape, dtype)
    outputs = [
        ((8, rows, width), LOW),
        ((8, rows, width), LOW),
        ((32, own, gate_up.shape[1] // 8), LOW),
        ((32, own, down.shape[1] // 8), LOW),
        (q_shape, LOW),
        ((4, own, width), LOW),
        ((8 * rows, width), LOW),
        ((3, 8 * rows, here), LOW),
        ((8 * rows, here), LOW),
        ((rows, width), WIDE),
        ((8, width), WIDE),
        ((rows, width), LOW),
    ]
    return kernel_call(
        forward_kernel,
        "forward",
        1,
        (tokens, cotangent, qkv, gain_columns, gate_up, down, out_rows, cosines, sines),
        [ANYWHERE] * 7 + [IN_VMEM] * 2,
        outputs,
        [ANYWHERE] * len(outputs),
        [
            vmem((8, rows, width)),
            vmem(q_shape),
            vmem((4, own, width)),
            vmem((8 * rows, width)),
            vmem((3, 8 * rows, here)),
            vmem((8 * rows, here), WIDE),
            vmem((8 * rows, here)),
            vmem((rows, width), WIDE),
            vmem((8, width), WIDE),
            vmem((rows, width)),
            vmem((8, rows, width)),
        ]
        + [vmem(array.shape, WIDE) for array in (qkv, gate_up, down, out_rows)]
        + [vmem(array.shape) for array in (qkv, gate_up, down, out_rows)]
        + LineScatter.buffers(rows, width)
        + [DMA((3,))] * 3
        + [DMA(LineGather.SEMS)] * 2
        + [DMA(Relayout.SEMS)] * 3
        + [DMA((2, 4))]
        + [DMA(LineScatter.SEMS)] * 2
        + [DMA(LineGather.SEMS)] * 2
        + [DMA((8,)), DMA((4,))],
    )


def weight_part(place, ref):
    return lambda half, unit, x, y: ref.at[place.block(2 * unit + half, x, y)]


def attend_back(head, qkv, grad_heads, grads):
    pair = lanes(head // 2 * 128, 128)
    mask = head_mask(head)
    for block in range(qkv.shape[1] // QUERY_ROWS):
        rows = pl.ds(block * QUERY_ROWS, QUERY_ROWS)
        keys = pl.ds(0, (block + 1) * QUERY_ROWS)
        queries, grad_rows = qkv[0, rows, pair] * mask, grad_heads[rows, pair] * mask
        key_rows = qkv[1, keys, pair]
        probs = scaled_probs(queries, key_rows, block * QUERY_ROWS)
        grad_probs = lax.dot_general(
            grad_rows, qkv[2, keys, pair], CONTRACT_LAST, preferred_element_type=WIDE
        )
        delta = jnp.sum(probs * grad_probs, axis=1, keepdims=True)
        grad_scores = (probs * (grad_probs - delta) * HEAD_DIM ** (-0.5)).astype(LOW)
        grads[0, rows, pair] += jnp.dot(grad_scores, key_rows * mask, preferred_element_type=WIDE)
        grads[1, keys, pair] += lax.dot_general(
            grad_scores, queries, CONTRACT_FIRST, preferred_element_type=WIDE
        )
        grads[2, keys, pair] += lax.dot_general(
            probs.astype(LOW), grad_rows, CONTRACT_FIRST, preferred_element_type=WIDE
        )


def mlp_kernel(
    normed,
    wg,
    wd,
    cot,
    residual,
    gain_rows,
    branch,
    g_sum,
    d_part,
    block_out,
    out_grad,
    nt,
    full_g,
    full_d,
    ct,
    active,
    grad_wide,
    part_two,
    part_out,
    grad_residual,
    mine,
    *scratch,
):
    p = Place()
    rows_own, width = residual.shape
    seq_len = 8 * rows_own
    own, ff = wd.shape[1], wd.shape[2]
    units = wd.shape[0] // 8
    block_rows = seq_len // 2
    part = ff // 4
    wide = width // 4
    blocks = wide // own
    load_sems, sum_a, sum_b, sum_c, gather_a, gather_b, swap_sems, keep_sems = scratch[7:]
    part_rows = [pl.ds(0, rows_own // 2), pl.ds(rows_own // 2, rows_own // 2)]
    sum_two = [
        LineScatter(p, part_two, *scratch[:2], sem, rows)
        for sem, rows in zip((sum_a, sum_b), part_rows)
    ]
    sum_out = LineScatter(p, part_out, *scratch[2:4], sum_c, pl.ds(0, rows_own))
    plane = PlaneScatter(p, weight_part(p, full_g), units, *scratch[4:7])
    gathers = [
        LineGather(p, branch, sem, mine.at[rows], rows)
        for sem, rows in zip((gather_a, gather_b), part_rows)
    ]

    def load(index):
        if index < 4:
            source, target = ((normed, nt), (cot, ct))[index // 2]
            return pltpu.make_async_copy(
                source.at[:, part_rows[index % 2]], target.at[index % 2], load_sems.at[index]
            )
        return pltpu.make_async_copy(wd, full_d, load_sems.at[4])

    def load_wide(index, side):
        columns = lanes(side * ff + index * part, part)
        return pltpu.make_async_copy(
            wg.at[:, :, columns], full_g.at[:, :, columns], load_sems.at[5 + 2 * index + side]
        )

    load(0).start()
    for index in range(4):
        for side in range(2):
            load_wide(index, side).start()
        if index == 0:
            for other in (2, 4, 1, 3):
                load(other).start()
    p.meet(True)
    for index in (0, 2, 4):
        load(index).wait()

    def stage_one(half, first, last):
        rows = pl.ds(half * block_rows, block_rows)

        def some(index, carry):
            if half == 0:
                load_wide(index, 0).wait()
                load_wide(index, 1).wait()
            here, there = lanes(index * part, part), lanes(ff + index * part, part)
            left = nt[half].reshape(block_rows, width)
            gate = jnp.dot(left, full_g[:, :, here].reshape(width, part), preferred_element_type=WIDE)
            up = jnp.dot(left, full_g[:, :, there].reshape(width, part), preferred_element_type=WIDE)
            grad = jnp.dot(
                ct[half].reshape(block_rows, width),
                full_d[:, :, here].reshape(width, part),
                preferred_element_type=WIDE,
            )
            sigmoid_gate = jax.nn.sigmoid(gate)
            active[rows, here] = (gate * sigmoid_gate * up).astype(LOW)
            grad_wide[rows, here] = (
                grad * up * sigmoid_gate * (1.0 + gate * (1.0 - sigmoid_gate))
            ).astype(LOW)
            grad_wide[rows, there] = (grad * gate * sigmoid_gate).astype(LOW)
            return carry

        lax.fori_loop(first, last, some, 0)

    def rows_times(left, weight, target, half, first, last):
        def some(index, carry):
            made = lax.dot_general(
                left[pl.ds(half * block_rows, block_rows), :],
                weight[pl.ds(index * blocks, blocks)].reshape(wide, -1),
                CONTRACT_LAST,
                preferred_element_type=WIDE,
            )
            target[:, part_rows[half], lanes(index * wide, wide)] = made.astype(LOW).reshape(
                8, rows_own // 2, wide
            )
            return carry

        lax.fori_loop(first, last, some, 0)

    def down_grad(index, carry):
        made = lax.dot_general(
            ct[:, :, :, lanes(index * wide, wide)].reshape(seq_len, wide),
            active[...],
            CONTRACT_FIRST,
            preferred_element_type=WIDE,
        )
        full_d[pl.ds(index * blocks, blocks)] = made.astype(LOW).reshape(blocks, own, ff)
        return carry

    def wide_grad(index):
        for side in range(2):
            made = lax.dot_general(
                nt[:, :, :, pl.ds(index * wide, wide)].reshape(seq_len, wide),
                grad_wide[:, pl.ds(side * ff, ff)],
                CONTRACT_FIRST,
                preferred_element_type=WIDE,
            )
            full_g[pl.ds(index * blocks, blocks), :, pl.ds(side * ff, ff)] = made.astype(
                LOW
            ).reshape(blocks, own, ff)
        plane.start_unit(index)

    def local_two(part):
        def some(rows):
            spot = pl.ds(pl.multiple_of(part * (rows_own // 2) + rows.start, CHUNK), CHUNK)
            unit, inverse = rms_parts(residual[spot, :])
            total = ct[part, p.slot, rows, :].astype(WIDE) + normed_back(
                sum_two[part].total(spot), unit, inverse, gain_rows[pl.ds(1, 1), :]
            )
            grad_residual[spot, :] = total
            mine[spot, :] = total.astype(LOW)

        by_rows(rows_own // 2, some)

    stage_one(0, 0, 4)
    rows_times(grad_wide, full_g, part_two, 0, 0, 4)
    sum_two[0].start()
    load(1).wait()
    load(3).wait()
    stage_one(1, 0, 2)
    sum_two[0].head()
    stage_one(1, 2, 4)
    sum_two[0].step(0)
    sum_two[0].step(1)
    rows_times(grad_wide, full_g, part_two, 1, 0, 4)
    sum_two[1].start()
    sum_two[0].step(2)
    wide_grad(0)
    sum_two[1].head()
    sum_two[0].arrive()
    local_two(0)
    gathers[0].start()
    rows_times(active, full_d, part_out, 0, 0, 4)
    sum_two[1].step(0)
    rows_times(active, full_d, part_out, 1, 0, 4)
    sum_out.start()
    sum_two[1].step(1)
    sum_two[1].step(2)
    wide_grad(1)
    gathers[0].inner(1)
    sum_two[1].arrive()
    local_two(1)
    gathers[1].start()
    sum_out.head()
    keep_grad = pltpu.make_async_copy(grad_residual, out_grad, keep_sems.at[1])
    keep_grad.start()
    wide_grad(2)
    gathers[0].outer()
    gathers[1].inner(1)
    wide_grad(3)
    gathers[0].inner(2)
    gathers[1].outer()
    plane.middle(0)
    lax.fori_loop(0, 2, down_grad, 0)
    gathers[1].inner(2)
    lax.fori_loop(2, 4, down_grad, 0)
    keep_d = pltpu.make_async_copy(full_d, d_part, keep_sems.at[0])
    keep_d.start()
    plane.middle(1)
    sum_out.step(0)
    gathers[0].inner(3)
    gathers[1].inner(3)
    plane.middle(2)
    sum_out.step(1)
    sum_out.step(2)
    plane.middle(3)
    for gather in gathers:
        gather.finish()
    for gather in gathers:
        gather.drain()
    sum_out.arrive()

    def local_out(rows):
        mine[rows, :] = (residual[rows, :] + sum_out.total(rows)).astype(LOW)

    by_rows(rows_own, local_out)
    keep_block = pltpu.make_async_copy(mine, block_out, swap_sems.at[0])
    keep_block.start()

    def keep_g(half, unit):
        return pltpu.make_async_copy(
            plane.sums(half, unit), g_sum.at[half, unit], keep_sems.at[2 + 4 * half + unit]
        )

    for unit in range(units):
        plane.final(unit)
        for half in range(2):
            keep_g(half, unit).start()
    keep_block.wait()
    for part in sum_two + [sum_out, plane]:
        part.drain()
    keep_d.wait()
    keep_grad.wait()
    for unit in range(units):
        for half in range(2):
            keep_g(half, unit).wait()


def mlp(normed, wg, wd, cot, residual, gain_rows):
    _, rows, width = normed.shape
    own, ff = wd.shape[1:]
    units = wd.shape[0] // 8
    vmem = lambda shape, dtype=LOW: pltpu.VMEM(shape, dtype)
    return kernel_call(
        mlp_kernel,
        "mlp",
        2,
        (normed, wg, wd, cot, residual, gain_rows),
        [ANYWHERE] * 4 + [IN_VMEM] * 2,
        [
            (normed.shape, LOW),
            ((2, units, own, 2 * ff), LOW),
            (wd.shape, LOW),
            ((rows, width), LOW),
            ((rows, width), WIDE),
        ],
        [ANYWHERE] * 5,
        [
            vmem((2, 8, rows // 2, width)),
            vmem(wg.shape),
            vmem(wd.shape),
            vmem((2, 8, rows // 2, width)),
            vmem((8 * rows, ff)),
            vmem((8 * rows, 2 * ff)),
            vmem(normed.shape),
            vmem(normed.shape),
            vmem((rows, width), WIDE),
            vmem((rows, width)),
        ]
        + LineScatter.buffers(rows, width) * 2
        + PlaneScatter.scratch(units, own, 2 * ff)
        + [DMA((13,))]
        + [DMA(LineScatter.SEMS)] * 3
        + [DMA(LineGather.SEMS)] * 2
        + [DMA((3,)), DMA((2 + 2 * units,))],
    )


def backward_kernel(
    branch_all,
    grad_in,
    gain_rows,
    own_tok,
    full_q,
    full_o,
    qkv,
    attended,
    normed_one,
    cosines,
    sines,
    g_sum,
    d_part,
    block,
    input_grad,
    block_out,
    q_out,
    g_out,
    d_out,
    o_out,
    work,
    branch,
    grad_residual,
    grad_heads,
    grads,
    grad_projected,
    q_part,
    o_part,
    o_sum,
    d_here,
    *scratch,
):
    buffers, rest = scratch[:2], scratch[2:]
    p = Place()
    rows_own, width = grad_residual.shape
    seq_len = 8 * rows_own
    own = full_o.shape[1]
    units = g_sum.shape[1]
    half = own // 2
    step_q, step_g, step_d = q_part.shape[2] // 3, g_sum.shape[3] // 2, d_part.shape[2]
    plane_d = PlaneScatter(p, weight_part(p, d_here), units, *rest[:3])
    plane_q = PlaneScatter(p, weight_part(p, q_part), units, *rest[3:6])
    plane_o = PlaneScatter(
        p, lambda h, u, x, y: o_part.at[2 * y + x, pl.ds(h * half, half)], 1, *rest[6:9]
    )
    sum_sems, return_sems, swap_sems, load_sems = rest[9:11], rest[11:14], rest[14:18], rest[18]
    part_rows = [pl.ds(0, rows_own // 2), pl.ds(rows_own // 2, rows_own // 2)]
    sum_one = [
        LineScatter(p, branch, *buffers, sem, rows) for sem, rows in zip(sum_sems, part_rows)
    ]
    return_q = LineReturn(
        p, plane_q.sums, [(i * step_q, step_q, i * 8 * step_q) for i in range(3)], q_out, return_sems[0]
    )
    return_g = LineReturn(
        p,
        lambda c, z: g_sum.at[c, z],
        [(i * step_g, step_g, i * 8 * step_g) for i in range(2)],
        g_out,
        return_sems[1],
    )
    return_d = LineReturn(p, plane_d.sums, [(0, step_d, 0)], d_out, return_sems[2])
    swap_in = [
        Swap(p, grad_residual.at[rows], input_grad.at[rows], input_grad.at[rows], sem)
        for sem, rows in zip(swap_sems[:2], part_rows)
    ]
    swap_out = Swap(p, o_sum, o_out, o_out, swap_sems[2])
    swap_block = Swap(p, block, block_out, block_out, swap_sems[3])

    def load(source, target, index):
        return pltpu.make_async_copy(source, target, load_sems.at[index])

    loads = [
        load(branch_all, branch, 0),
        load(d_part, d_here, 1),
        load(normed_one, work, 2),
        load(grad_in, grad_residual, 3),
    ]
    for copy in loads:
        copy.start()
    p.meet(True)
    swap_block.start()
    for z in range(4):
        return_g.send(z)
    loads[0].wait()

    def back_out(part, carry):
        rows = pl.ds(pl.multiple_of(part * 256, 256), 256)
        made = lax.dot_general(
            branch[pl.ds(2 * part, 2)].reshape(256, width),
            full_o[...].reshape(-1, width),
            CONTRACT_LAST,
            preferred_element_type=WIDE,
        )
        grad_heads[rows, :] = made.astype(LOW)
        return carry

    lax.fori_loop(0, seq_len // 256, back_out, 0)
    loads[1].wait()
    plane_d.start()

    def out_grad(part, carry):
        columns = lanes(part * 512, 512)
        made = lax.dot_general(
            attended[...],
            branch[:, :, columns].reshape(seq_len, 512),
            CONTRACT_FIRST,
            preferred_element_type=WIDE,
        )
        o_part[:, :, columns] = made.astype(LOW).reshape(4, own, 512)
        return carry

    lax.fori_loop(0, width // 512, out_grad, 0)
    plane_o.start()
    grads[...] = jnp.zeros_like(grads)

    def one_head(head, carry):
        attend_back(head, qkv, grad_heads, grads)
        plane_d.middle(head)
        return carry

    lax.fori_loop(0, 4, one_head, 0)

    def back_turn(part, carry):
        rows = pl.ds(pl.multiple_of(part * 256, 256), 256)
        for kind in range(3):
            made = grads[kind, rows, :]
            if kind < 2:
                made = turn(
                    made,
                    jnp.concatenate([cosines[rows, :]] * 2, axis=1),
                    jnp.concatenate([-sines[rows, :]] * 2, axis=1),
                )
            grad_projected[rows, pl.ds(kind * step_q, step_q)] = made.astype(LOW)
        return carry

    lax.fori_loop(0, seq_len // 256, back_turn, 0)

    def back_qkv(part, carry):
        weight = full_q[pl.ds(part * 8, 8), :, pl.ds(0, 3 * step_q)].reshape(8 * own, 3 * step_q)
        for block in range(seq_len // 512):
            made = lax.dot_general(
                grad_projected[pl.ds(block * 512, 512), :],
                weight,
                CONTRACT_LAST,
                preferred_element_type=WIDE,
            )
            branch[pl.ds(block * 4, 4), :, lanes(part * 8 * own, 8 * own)] = made.astype(
                LOW
            ).reshape(4, rows_own, 8 * own)
        return carry

    lax.fori_loop(0, 4, back_qkv, 0)
    for part in sum_one:
        part.start()
    loads[2].wait()
    loads[3].wait()
    for part in sum_one:
        part.head()

    def qkv_grad(part, carry):
        made = lax.dot_general(
            work[:, :, lanes(part * 8 * own, 8 * own)].reshape(seq_len, 8 * own),
            grad_projected[...],
            CONTRACT_FIRST,
            preferred_element_type=WIDE,
        )
        q_part[pl.ds(part * 8, 8)] = made.astype(LOW).reshape(8, own, 3 * step_q)
        plane_q.start_unit(part)
        return carry

    lax.fori_loop(0, 4, qkv_grad, 0)

    def local_one(part):
        def some(rows):
            spot = pl.ds(pl.multiple_of(part * (rows_own // 2) + rows.start, CHUNK), CHUNK)
            unit, inverse = rms_parts(own_tok[spot, :].astype(WIDE))
            grad_residual[spot, :] = grad_residual[spot, :] + normed_back(
                sum_one[part].total(spot), unit, inverse, gain_rows[pl.ds(0, 1), :]
            )

        by_rows(rows_own // 2, some)

    for part in sum_one:
        part.steps()
    for unit in range(units):
        plane_d.final(unit)
        return_d.send(unit)
    plane_o.middle(0)
    for unit in range(units):
        plane_q.middle(unit)
    for part in range(2):
        sum_one[part].arrive()
        local_one(part)
        swap_in[part].start()
    plane_o.final(0)
    for h in range(2):
        o_sum[pl.ds(h * half, half), :] = plane_o.sums(h, 0)[...]
    swap_out.start()
    for unit in range(units):
        plane_q.final(unit)
        return_q.send(unit)
    for part in (return_g, return_d, return_q):
        part.finish()
    for part in swap_in + [swap_out, swap_block]:
        part.wait()
        part.drain()
    for part in sum_one + [plane_d, plane_q, plane_o]:
        part.drain()


def backward(
    branch,
    grad_residual,
    gain_rows,
    own_tok,
    full_q,
    full_o,
    qkv,
    attended,
    normed_one,
    cosines,
    sines,
    g_sum,
    d_part,
    block,
):
    _, rows, width = branch.shape
    own, here = full_o.shape[1], attended.shape[1]
    units = g_sum.shape[1]
    vmem = lambda shape, dtype=LOW: pltpu.VMEM(shape, dtype)
    step_g, step_d = g_sum.shape[3], d_part.shape[2]
    return kernel_call(
        backward_kernel,
        "backward",
        3,
        (
            branch,
            grad_residual,
            gain_rows,
            own_tok,
            full_q,
            full_o,
            qkv,
            attended,
            normed_one,
            cosines,
            sines,
            g_sum,
            d_part,
            block,
        ),
        [ANYWHERE] * 2 + [IN_VMEM] * 6 + [ANYWHERE] + [IN_VMEM] * 2 + [ANYWHERE] * 3,
        [
            ((rows, width), WIDE),
            ((rows, width), LOW),
            ((own, 24 * here), LOW),
            ((own, 8 * step_g), LOW),
            ((own, 8 * step_d), LOW),
            ((own, width), LOW),
        ],
        [ANYWHERE] * 6,
        [
            vmem((8, rows, width)),
            vmem((8, rows, width)),
            vmem((rows, width), WIDE),
            vmem((8 * rows, here)),
            vmem((3, 8 * rows, here), WIDE),
            vmem((8 * rows, 3 * here)),
            vmem((32, own, 3 * here)),
            vmem((4, own, width)),
            vmem((own, width)),
            vmem(d_part.shape),
        ]
        + LineScatter.buffers(rows, width)
        + PlaneScatter.scratch(units, own, step_d)
        + PlaneScatter.scratch(units, own, 3 * here)
        + PlaneScatter.scratch(1, own // 2, width)
        + [DMA(LineScatter.SEMS)] * 2
        + [DMA(LineReturn.SEMS)] * 3
        + [DMA((3,))] * 4
        + [DMA((4,))],
    )


ADAM_STEPS = 8
WIDE_RATE = 2.5 * D ** (-0.5)
OUT_RATE = 2.5 * max(D // 512, 1) ** (-0.5)
DOWN_RATE = 2.5 * FF ** (-0.5)


def adam_kernel(*refs):
    inputs, outputs, sums = refs[:16], refs[16:28], refs[28:]

    @pl.when(pl.program_id(0) == 0)
    def _():
        for total in sums:
            total[...] = jnp.zeros_like(total)

    for index, rate in enumerate((WIDE_RATE, OUT_RATE, WIDE_RATE, DOWN_RATE)):
        weight, first, second, low_gradient = (ref[...] for ref in inputs[4 * index : 4 * index + 4])
        gradient = low_gradient.astype(WIDE)
        made = adam_step(weight, gradient, first, second, rate, WEIGHT_DECAY)
        for target, value in zip(outputs[3 * index : 3 * index + 3], made):
            target[...] = value
        if index % 2 == 0:
            total = jnp.sum(weight.astype(LOW).astype(WIDE) * gradient, axis=1, keepdims=True)
            sums[index // 2][...] += jnp.broadcast_to(total, sums[index // 2].shape)


def adam_all(groups):
    specs, out_specs, out_shape = [], [], []
    rows = groups[0][0].shape[0]
    for group in groups:
        spec = pl.BlockSpec((rows, group[0].shape[1] // ADAM_STEPS), lambda step: (0, step))
        specs += [spec] * 4
        out_specs += [spec] * 3
        out_shape += [jax.ShapeDtypeStruct(group[0].shape, WIDE)] * 3
    whole = pl.BlockSpec((rows, 128), lambda step: (0, 0))
    return pl.pallas_call(
        adam_kernel,
        grid=(ADAM_STEPS,),
        in_specs=specs,
        out_specs=out_specs + [whole] * 2,
        out_shape=out_shape + [jax.ShapeDtypeStruct((rows, 128), WIDE)] * 2,
        compiler_params=pltpu.CompilerParams(vmem_limit_bytes=56 * 2**20),
        name="adam",
    )(*[array for group in groups for array in group])


def grid_shards(
    tokens,
    cotangent,
    qkv_weight,
    out_weight,
    gate_up_weight,
    down_weight,
    gains,
    qkv_first,
    out_first,
    gate_up_first,
    down_first,
    gains_first,
    qkv_second,
    out_second,
    gate_up_second,
    down_second,
    gains_second,
):
    rows, width = tokens.shape[1:]
    seq_len = 8 * rows
    gain_columns = jnp.pad(gains.astype(LOW).T, ((0, 0), (0, 126)))
    cosines, sines = turn_tables(seq_len)
    (
        grad_out,
        normed_two,
        gate_up_full,
        down_full,
        qkv_full,
        out_full,
        normed_one,
        qkv_heads,
        attended,
        residual,
        gain_full,
        own_tokens,
    ) = forward(
        tokens[0],
        cotangent[0],
        qkv_weight,
        gain_columns,
        gate_up_weight,
        down_weight,
        out_weight,
        cosines,
        sines,
    )
    grad_branch, gate_up_half, down_part, block_own, grad_residual = mlp(
        normed_two, gate_up_full, down_full, grad_out, residual, gain_full
    )
    input_grad, block_out, qkv_sum, gate_up_sum, down_sum, out_sum = backward(
        grad_branch,
        grad_residual,
        gain_full,
        own_tokens,
        qkv_full,
        out_full,
        qkv_heads,
        attended,
        normed_one.reshape(8, rows, width),
        cosines,
        sines,
        gate_up_half,
        down_part,
        block_own,
    )
    made = adam_all(
        [
            (qkv_weight, qkv_first, qkv_second, qkv_sum),
            (out_weight, out_first, out_second, out_sum),
            (gate_up_weight, gate_up_first, gate_up_second, gate_up_sum),
            (down_weight, down_first, down_second, down_sum),
        ]
    )
    qkv_new, out_new, gate_up_new, down_new = (made[3 * i : 3 * i + 3] for i in range(4))
    gains_sum = jnp.stack([made[12][:, 0], made[13][:, 0]], axis=0) / gains.astype(LOW).astype(WIDE)
    gains_new = adam_step(gains, gains_sum, gains_first, gains_second, 0.5, 0.0)
    return (
        block_out[None],
        input_grad[None],
        qkv_new[0],
        out_new[0],
        gate_up_new[0],
        down_new[0],
        gains_new[0],
        qkv_new[1],
        out_new[1],
        gate_up_new[1],
        down_new[1],
        gains_new[1],
        qkv_new[2],
        out_new[2],
        gate_up_new[2],
        down_new[2],
        gains_new[2],
    )


def mapped(body, mesh, token_spec, row_spec, gain_spec):
    one_set = (row_spec, row_spec, row_spec, row_spec, gain_spec)
    return jax.shard_map(
        body,
        mesh=mesh,
        in_specs=(token_spec, token_spec) + one_set * 3,
        out_specs=(token_spec, token_spec) + one_set * 3,
        check_vma=False,
    )


def solution(mesh):
    if mesh.shape["seq"] == 8 and mesh.shape["dp"] == 4:
        grid_mesh = Mesh(mesh.devices.reshape(4, 2, 2, 2), GRID)
        return mapped(
            grid_shards,
            grid_mesh,
            P(("y", "c"), ("z", "x"), None),
            P(GRID, None),
            P(None, GRID),
        )
    return mapped(
        shards, mesh, P("dp", "seq", None), P(("seq", "dp"), None), P(None, ("seq", "dp"))
    )
```

```python
import jax
import jax.numpy as jnp
import numpy as np
from jax import lax
from jax.experimental import pallas as pl
from jax.experimental.pallas import tpu as pltpu
from jax.sharding import Mesh
from jax.sharding import PartitionSpec as P

D = 2048
HEADS = 32
HEAD_DIM = 64
FF = 8192
BLOCK = 512
STEP = 10


NORM_EPS = 1e-05
ROPE_BASE = 130000.0
BETA_ONE = 0.9
BETA_TWO = 0.999
ADAM_EPS = 1e-08
WEIGHT_DECAY = 0.1
MASKED = -1e30


def rms_parts(values):
    inverse = lax.rsqrt(jnp.mean(values * values, axis=-1, keepdims=True) + NORM_EPS)
    return (values * inverse, inverse)


def rope_tables(positions):
    half_dim = HEAD_DIM // 2
    exponent = jnp.arange(half_dim, dtype=jnp.float32) * (2.0 / HEAD_DIM)
    frequency = ROPE_BASE ** (-exponent)
    angles = positions.astype(jnp.float32)[:, None] * frequency[None, :]
    return (jnp.cos(angles)[:, None, :], jnp.sin(angles)[:, None, :])


def rotate(tensor, cosines, sines):
    half_dim = HEAD_DIM // 2
    lower_half = tensor[..., :half_dim]
    upper_half = tensor[..., half_dim:]
    return jnp.concatenate(
        [lower_half * cosines - upper_half * sines, upper_half * cosines + lower_half * sines],
        axis=-1,
    )


def unrotate(tensor, cosines, sines):
    half_dim = HEAD_DIM // 2
    lower_half = tensor[..., :half_dim]
    upper_half = tensor[..., half_dim:]
    return jnp.concatenate(
        [lower_half * cosines + upper_half * sines, upper_half * cosines - lower_half * sines],
        axis=-1,
    )


def block_scores(query_rows, key_heads, key_id, block_id):
    key_rows = lax.dynamic_slice_in_dim(key_heads, key_id * BLOCK, BLOCK, 0)
    products = jnp.einsum(
        "qhd,khd->hqk", query_rows, key_rows, preferred_element_type=jnp.float32
    ) * HEAD_DIM ** (-0.5)
    local_ids = jnp.arange(BLOCK, dtype=jnp.int32)
    allowed = (key_id < block_id) | (local_ids[None, :] <= local_ids[:, None])
    return jnp.where(allowed[None], products, MASKED)


def row_normalizer(query_rows, key_heads, block_id):
    row_shape = (query_rows.shape[1], BLOCK, 1)

    def absorb(key_id, state):
        running_max, running_total = state
        scores = block_scores(query_rows, key_heads, key_id, block_id)
        new_max = jnp.maximum(running_max, jnp.max(scores, axis=-1, keepdims=True))
        running_total = running_total * jnp.exp(running_max - new_max) + jnp.sum(
            jnp.exp(scores - new_max), axis=-1, keepdims=True
        )
        return (new_max, running_total)

    start_state = (jnp.full(row_shape, MASKED, jnp.float32), jnp.zeros(row_shape, jnp.float32))
    final_max, final_total = lax.fori_loop(0, block_id + 1, absorb, start_state)
    return final_max + jnp.log(final_total)


def attend_forward(query_heads, key_heads, value_heads):
    seq_len, heads_here, head_dim = query_heads.shape

    def one_block(block_id, carry):
        out_all, lse_all = carry
        row_start = block_id * BLOCK
        query_rows = lax.dynamic_slice_in_dim(query_heads, row_start, BLOCK, 0)
        row_lse = row_normalizer(query_rows, key_heads, block_id)

        def weigh_values(key_id, running):
            scores = block_scores(query_rows, key_heads, key_id, block_id)
            weights_low = jnp.exp(scores - row_lse).astype(jnp.bfloat16)
            value_rows = lax.dynamic_slice_in_dim(value_heads, key_id * BLOCK, BLOCK, 0)
            return running + jnp.einsum(
                "hqk,khd->qhd", weights_low, value_rows, preferred_element_type=jnp.float32
            )

        attended = lax.fori_loop(
            0, block_id + 1, weigh_values, jnp.zeros((BLOCK, heads_here, head_dim), jnp.float32)
        )
        out_all = lax.dynamic_update_slice_in_dim(
            out_all, attended.astype(jnp.bfloat16), row_start, 0
        )
        lse_all = lax.dynamic_update_slice_in_dim(lse_all, row_lse, row_start, 1)
        return (out_all, lse_all)

    start_carry = (
        jnp.zeros((seq_len, heads_here, head_dim), jnp.bfloat16),
        jnp.zeros((heads_here, seq_len, 1), jnp.float32),
    )
    return lax.fori_loop(0, seq_len // BLOCK, one_block, start_carry)


def attend_backward(query_heads, key_heads, value_heads, grad_heads, lse_all):
    seq_len, heads_here, head_dim = query_heads.shape
    score_scale = HEAD_DIM ** (-0.5)

    def one_block(block_id, carry):
        grad_q_all, grad_k_all, grad_v_all = carry
        row_start = block_id * BLOCK
        query_rows = lax.dynamic_slice_in_dim(query_heads, row_start, BLOCK, 0)
        grad_rows = lax.dynamic_slice_in_dim(grad_heads, row_start, BLOCK, 0)
        row_lse = lax.dynamic_slice_in_dim(lse_all, row_start, BLOCK, 1)

        def probs_and_grads(key_id):
            scores = block_scores(query_rows, key_heads, key_id, block_id)
            probs = jnp.exp(scores - row_lse)
            value_rows = lax.dynamic_slice_in_dim(value_heads, key_id * BLOCK, BLOCK, 0)
            grad_probs = jnp.einsum(
                "qhd,khd->hqk", grad_rows, value_rows, preferred_element_type=jnp.float32
            )
            return (probs, grad_probs)

        def add_delta(key_id, running):
            probs, grad_probs = probs_and_grads(key_id)
            return running + jnp.sum(probs * grad_probs, axis=-1, keepdims=True)

        row_delta = lax.fori_loop(
            0, block_id + 1, add_delta, jnp.zeros((heads_here, BLOCK, 1), jnp.float32)
        )

        def spread(key_id, inner):
            grad_q_rows, grad_k_acc, grad_v_acc = inner
            probs, grad_probs = probs_and_grads(key_id)
            key_start = key_id * BLOCK
            key_rows = lax.dynamic_slice_in_dim(key_heads, key_start, BLOCK, 0)
            grad_scores = (probs * (grad_probs - row_delta) * score_scale).astype(jnp.bfloat16)
            grad_q_rows = grad_q_rows + jnp.einsum(
                "hqk,khd->qhd", grad_scores, key_rows, preferred_element_type=jnp.float32
            )
            grad_k_part = jnp.einsum(
                "hqk,qhd->khd", grad_scores, query_rows, preferred_element_type=jnp.float32
            )
            grad_v_part = jnp.einsum(
                "hqk,qhd->khd",
                probs.astype(jnp.bfloat16),
                grad_rows,
                preferred_element_type=jnp.float32,
            )
            grad_k_acc = lax.dynamic_update_slice_in_dim(
                grad_k_acc,
                lax.dynamic_slice_in_dim(grad_k_acc, key_start, BLOCK, 0) + grad_k_part,
                key_start,
                0,
            )
            grad_v_acc = lax.dynamic_update_slice_in_dim(
                grad_v_acc,
                lax.dynamic_slice_in_dim(grad_v_acc, key_start, BLOCK, 0) + grad_v_part,
                key_start,
                0,
            )
            return (grad_q_rows, grad_k_acc, grad_v_acc)

        start_inner = (
            jnp.zeros((BLOCK, heads_here, head_dim), jnp.float32),
            grad_k_all,
            grad_v_all,
        )
        grad_q_rows, grad_k_all, grad_v_all = lax.fori_loop(0, block_id + 1, spread, start_inner)
        grad_q_all = lax.dynamic_update_slice_in_dim(grad_q_all, grad_q_rows, row_start, 0)
        return (grad_q_all, grad_k_all, grad_v_all)

    zeros_all = jnp.zeros((seq_len, heads_here, head_dim), jnp.float32)
    return lax.fori_loop(0, seq_len // BLOCK, one_block, (zeros_all, zeros_all, zeros_all))


def adam_step(weight, gradient, first, second, rate, decay):
    new_first = BETA_ONE * first + (1.0 - BETA_ONE) * gradient
    new_second = BETA_TWO * second + (1.0 - BETA_TWO) * gradient * gradient
    first_hat = new_first / (1.0 - BETA_ONE**STEP)
    second_hat = new_second / (1.0 - BETA_TWO**STEP)
    new_weight = weight - rate * (first_hat / (jnp.sqrt(second_hat) + ADAM_EPS) + decay * weight)
    return (new_weight, new_first, new_second)


def shards(
    tokens,
    cotangent,
    qkv_weight,
    out_weight,
    gate_up_weight,
    down_weight,
    gains,
    qkv_first,
    out_first,
    gate_up_first,
    down_first,
    gains_first,
    qkv_second,
    out_second,
    gate_up_second,
    down_second,
    gains_second,
):
    seq_count = lax.axis_size("seq")
    tok_rows = tokens.shape[1]
    width = tokens.shape[2]
    seq_len = tok_rows * seq_count
    heads_here = HEADS // seq_count
    width_here = heads_here * HEAD_DIM
    contract_last = (((1,), (1,)), ((), ()))
    contract_first = (((0,), (0,)), ((), ()))
    qkv_full, proj_full, gain_full = (
        lax.all_gather(qkv_weight.astype(jnp.bfloat16), ("seq", "dp"), axis=0, tiled=True),
        lax.all_gather(out_weight.astype(jnp.bfloat16), ("seq", "dp"), axis=0, tiled=True),
        lax.all_gather(gains.astype(jnp.bfloat16), ("seq", "dp"), axis=1, tiled=True),
    )
    up_full, down_full = (
        lax.all_gather(gate_up_weight.astype(jnp.bfloat16), ("seq", "dp"), axis=0, tiled=True),
        lax.all_gather(down_weight.astype(jnp.bfloat16), ("seq", "dp"), axis=0, tiled=True),
    )
    hidden_in = tokens[0].astype(jnp.float32)
    unit_one, inverse_one = rms_parts(hidden_in)
    normed_one = (unit_one * gain_full[0].astype(jnp.float32)).astype(jnp.bfloat16)
    projected = jnp.einsum(
        "te,ecd->ctd",
        normed_one,
        qkv_full.reshape(width, 3, width),
        preferred_element_type=jnp.float32,
    )
    positions = lax.axis_index("seq") * tok_rows + jnp.arange(tok_rows, dtype=jnp.int32)
    cos_local, sin_local = rope_tables(positions)
    turned = rotate(projected[:2].reshape(2, tok_rows, HEADS, HEAD_DIM), cos_local, sin_local)
    packed = jnp.concatenate([turned.reshape(2, tok_rows, width), projected[2:]], axis=0).astype(
        jnp.bfloat16
    )
    by_heads = lax.all_to_all(packed, "seq", split_axis=2, concat_axis=1, tiled=True)
    query_heads = by_heads[0].reshape(seq_len, heads_here, HEAD_DIM)
    key_heads = by_heads[1].reshape(seq_len, heads_here, HEAD_DIM)
    value_heads = by_heads[2].reshape(seq_len, heads_here, HEAD_DIM)
    out_heads, lse_all = attend_forward(query_heads, key_heads, value_heads)
    attended = lax.all_to_all(
        out_heads.reshape(seq_len, width_here), "seq", split_axis=0, concat_axis=1, tiled=True
    )
    residual = hidden_in + jnp.dot(attended, proj_full, preferred_element_type=jnp.float32)
    unit_two, inverse_two = rms_parts(residual)
    normed_two = (unit_two * gain_full[1].astype(jnp.float32)).astype(jnp.bfloat16)
    gate_up = jnp.dot(normed_two, up_full, preferred_element_type=jnp.float32)
    gate_vals = gate_up[:, :FF]
    up_vals = gate_up[:, FF:]
    sigmoid_gate = jax.nn.sigmoid(gate_vals)
    activated = (gate_vals * sigmoid_gate * up_vals).astype(jnp.bfloat16)
    mlp_out = lax.dot_general(
        activated, down_full, contract_last, preferred_element_type=jnp.float32
    )
    block_out = (residual + mlp_out).astype(jnp.bfloat16)[None]
    back_up, back_down, back_gain = (
        lax.all_gather(gate_up_weight.astype(jnp.bfloat16), ("seq", "dp"), axis=0, tiled=True),
        lax.all_gather(down_weight.astype(jnp.bfloat16), ("seq", "dp"), axis=0, tiled=True),
        lax.all_gather(gains.astype(jnp.bfloat16), ("seq", "dp"), axis=1, tiled=True),
    )
    grad_out = cotangent[0]
    grad_act = jnp.dot(grad_out, back_down, preferred_element_type=jnp.float32)
    grad_gate = grad_act * up_vals * sigmoid_gate * (1.0 + gate_vals * (1.0 - sigmoid_gate))
    grad_up = grad_act * gate_vals * sigmoid_gate
    grad_gate_up = jnp.concatenate([grad_gate, grad_up], axis=1).astype(jnp.bfloat16)
    grad_normed_two = lax.dot_general(
        grad_gate_up, back_up, contract_last, preferred_element_type=jnp.float32
    )
    gain_two_grad = jnp.sum(grad_normed_two * unit_two, axis=0)
    grad_unit_two = grad_normed_two * back_gain[1].astype(jnp.float32)
    grad_residual = grad_out.astype(jnp.float32) + inverse_two * (
        grad_unit_two - unit_two * jnp.mean(grad_unit_two * unit_two, axis=-1, keepdims=True)
    )
    gate_up_rows = lax.dot_general(
        normed_two, grad_gate_up, contract_first, preferred_element_type=jnp.float32
    )
    down_rows = lax.dot_general(
        grad_out, activated, contract_first, preferred_element_type=jnp.float32
    )
    mlp_grad = lax.psum_scatter(
        jnp.concatenate([gate_up_rows, down_rows], axis=1),
        ("seq", "dp"),
        scatter_dimension=0,
        tiled=True,
    )
    back_qkv, back_proj = (
        lax.all_gather(qkv_weight.astype(jnp.bfloat16), ("seq", "dp"), axis=0, tiled=True),
        lax.all_gather(out_weight.astype(jnp.bfloat16), ("seq", "dp"), axis=0, tiled=True),
    )
    grad_branch = grad_residual.astype(jnp.bfloat16)
    proj_grad = lax.dot_general(
        attended, grad_branch, contract_first, preferred_element_type=jnp.float32
    )
    grad_attended = lax.dot_general(
        grad_branch, back_proj, contract_last, preferred_element_type=jnp.float32
    ).astype(jnp.bfloat16)
    grad_heads = lax.all_to_all(
        grad_attended, "seq", split_axis=1, concat_axis=0, tiled=True
    ).reshape(seq_len, heads_here, HEAD_DIM)
    grad_q_all, grad_k_all, grad_v_all = attend_backward(
        query_heads, key_heads, value_heads, grad_heads, lse_all
    )
    cos_whole, sin_whole = rope_tables(jnp.arange(seq_len, dtype=jnp.int32))
    grad_pack = jnp.stack(
        [
            unrotate(grad_q_all, cos_whole, sin_whole).reshape(seq_len, width_here),
            unrotate(grad_k_all, cos_whole, sin_whole).reshape(seq_len, width_here),
            grad_v_all.reshape(seq_len, width_here),
        ],
        axis=0,
    ).astype(jnp.bfloat16)
    grad_projected = lax.all_to_all(grad_pack, "seq", split_axis=1, concat_axis=2, tiled=True)
    qkv_cube = back_qkv.reshape(width, 3, width)
    grad_normed_one = jnp.einsum(
        "ctd,ecd->te", grad_projected, qkv_cube, preferred_element_type=jnp.float32
    )
    qkv_grad = jnp.einsum(
        "te,ctd->ecd", normed_one, grad_projected, preferred_element_type=jnp.float32
    ).reshape(width, 3 * width)
    gain_one_grad = jnp.sum(grad_normed_one * unit_one, axis=0)
    grad_unit_one = grad_normed_one * back_gain[0].astype(jnp.float32)
    input_grad = grad_residual + inverse_one * (
        grad_unit_one - unit_one * jnp.mean(grad_unit_one * unit_one, axis=-1, keepdims=True)
    )
    gains_grad = jnp.stack([gain_one_grad, gain_two_grad], axis=0)
    qkv_sum, proj_sum, gains_sum = (
        lax.psum_scatter(qkv_grad, ("seq", "dp"), scatter_dimension=0, tiled=True),
        lax.psum_scatter(proj_grad, ("seq", "dp"), scatter_dimension=0, tiled=True),
        lax.psum_scatter(gains_grad, ("seq", "dp"), scatter_dimension=1, tiled=True),
    )
    wide_rate = 2.5 * D ** (-0.5)
    out_rate = 2.5 * max(D // 512, 1) ** (-0.5)
    down_rate = 2.5 * FF ** (-0.5)
    qkv_new = adam_step(qkv_weight, qkv_sum, qkv_first, qkv_second, wide_rate, WEIGHT_DECAY)
    out_new = adam_step(out_weight, proj_sum, out_first, out_second, out_rate, WEIGHT_DECAY)
    gate_up_new = adam_step(
        gate_up_weight,
        mlp_grad[:, : 2 * FF],
        gate_up_first,
        gate_up_second,
        wide_rate,
        WEIGHT_DECAY,
    )
    down_new = adam_step(
        down_weight, mlp_grad[:, 2 * FF :], down_first, down_second, down_rate, WEIGHT_DECAY
    )
    gains_new = adam_step(gains, gains_sum, gains_first, gains_second, 0.5, 0.0)
    return (
        block_out,
        input_grad[None],
        qkv_new[0],
        out_new[0],
        gate_up_new[0],
        down_new[0],
        gains_new[0],
        qkv_new[1],
        out_new[1],
        gate_up_new[1],
        down_new[1],
        gains_new[1],
        qkv_new[2],
        out_new[2],
        gate_up_new[2],
        down_new[2],
        gains_new[2],
    )


GRID = ("z", "x", "y", "c")
RING = ("z", "c")
PLANE = ("x", "y")
LOW = jnp.bfloat16
WIDE = jnp.float32
CONTRACT_LAST = (((1,), (1,)), ((), ()))
CONTRACT_FIRST = (((0,), (0,)), ((), ()))
DMA = pltpu.SemaphoreType.DMA
ANYWHERE = pl.BlockSpec(memory_space=pl.ANY)
IN_VMEM = pl.BlockSpec(memory_space=pltpu.VMEM)


def remote(source, target, send, receive, **place):
    return pltpu.make_async_remote_copy(
        src_ref=source,
        dst_ref=target,
        send_sem=send,
        recv_sem=receive,
        device_id=place,
        device_id_type=pl.DeviceIdType.MESH,
    )


def lanes(start, size):
    return pl.ds(pl.multiple_of(start, 128), size)


class Place:
    def __init__(self):
        self.z, self.x, self.y, self.c = (lax.axis_index(name) for name in GRID)
        self.slot = 2 * self.z + self.c
        self.block_here = self.block(self.slot, self.x, self.y)

    def block(self, slot, x, y):
        return (((slot // 2) * 2 + x) * 2 + y) * 2 + lax.rem(slot, 2)

    def meet(self, plane):
        barrier = pltpu.get_barrier_semaphore()
        others = [
            {"z": slot // 2, "c": lax.rem(slot, 2)}
            for slot in (lax.rem(self.slot + step, 8) for step in range(1, 8))
        ]
        if plane:
            others += [{"x": 1 - self.x}, {"y": 1 - self.y}, {"x": 1 - self.x, "c": 1 - self.c}]
        for other in others:
            pl.semaphore_signal(
                barrier, inc=1, device_id=other, device_id_type=pl.DeviceIdType.MESH
            )
        pl.semaphore_wait(barrier, len(others))


class Swap:
    def __init__(self, place, source, spot_there, spot_here, sems):
        p = self.place = place
        self.away = lambda: remote(
            source, spot_there, sems.at[0], sems.at[1], x=1 - p.x, c=1 - p.c
        )
        self.here = lambda: pltpu.make_async_copy(source, spot_here, sems.at[2])

    def start(self):
        p = self.place
        pl.when(p.x != p.c)(lambda: self.away().start())
        pl.when(p.x == p.c)(lambda: self.here().start())

    def wait(self):
        p = self.place
        pl.when(p.x != p.c)(lambda: self.away().wait_recv())
        pl.when(p.x == p.c)(lambda: self.here().wait())

    def drain(self):
        p = self.place
        pl.when(p.x != p.c)(lambda: self.away().wait_send())


class LineGather:
    SEMS = (4, 8)

    def __init__(self, place, buffer, sems, mine=None, rows=None):
        self.place, self.sems, self.mine = place, sems, mine
        self.spot = (lambda slot: buffer.at[slot]) if rows is None else (lambda slot: buffer.at[slot, rows])

    def copy(self, slot, way, own=False):
        p, block = self.place, self.spot(slot)
        if way == 0:
            where = {"z": jnp.minimum(p.z + 1, 3)}
        elif way == 1:
            where = {"z": jnp.maximum(p.z - 1, 0)}
        else:
            where = {"c": 1 - p.c}
        source = self.mine if own and self.mine is not None else block
        return remote(source, block, self.sems.at[way, slot], self.sems.at[3, slot], **where)

    def _pass_on(self, slot, way, own=False):
        p = self.place
        if way == 0:
            pl.when(p.z < 3)(lambda: self.copy(slot, 0, own).start())
        elif way == 1:
            pl.when(p.z > 0)(lambda: self.copy(slot, 1, own).start())

    def start(self):
        slot = self.place.slot
        self._pass_on(slot, 0, True)
        self._pass_on(slot, 1, True)
        self.copy(slot, 2, True).start()
        if self.mine is not None:
            self.keep().start()

    def start_part(self, inside):
        p = self.place
        in_line = (p.z == 1) | (p.z == 2)
        pl.when(in_line if inside else jnp.logical_not(in_line))(self.start)

    def keep(self):
        slot = self.place.slot
        return pltpu.make_async_copy(self.mine, self.spot(slot), self.sems.at[3, slot])

    def inner(self, distance):
        p = self.place
        side = 1 - 2 * (p.z // 2)
        source = p.z + distance * side

        @pl.when((source >= 0) & (source <= 3))
        def _():
            slot = 2 * source + p.c
            self.copy(slot, 2).wait_recv()
            pl.when(p.z == 1)(lambda: self.copy(slot, 1).start())
            pl.when(p.z == 2)(lambda: self.copy(slot, 0).start())
            self.copy(slot, 2).start()

    def outer(self):
        p = self.place
        for here, way in ((1, 0), (2, 1)):

            @pl.when(p.z == here)
            def _():
                slot = p.slot - 2 + 4 * way
                self.copy(slot, 2).wait_recv()
                self.copy(slot, way).start()
                self.copy(slot, 2).start()

    def steps(self):
        self.inner(1)
        self.outer()
        self.inner(2)
        self.inner(3)

    def finish(self):
        p = self.place
        if self.mine is not None:
            self.keep().wait()
        for z in range(4):
            self.copy(2 * z + 1 - p.c, 2).wait_recv()

    def drain(self):
        p = self.place
        for z in range(4):
            slot = 2 * z + p.c
            self.copy(slot, 2).wait_send()
            pl.when((z <= p.z) & (p.z < 3))(lambda: self.copy(slot, 0).wait_send())
            pl.when((z >= p.z) & (p.z > 0))(lambda: self.copy(slot, 1).wait_send())


def add_blocks(target, sources):
    def some(step, carry):
        rows = pl.ds(pl.multiple_of(step * 16, 16), 16)
        total = sources[0][rows, :].astype(WIDE)
        for source in sources[1:]:
            total = total + source[rows, :].astype(WIDE)
        target[rows, :] = total.astype(target.dtype)
        return carry

    lax.fori_loop(0, target.shape[0] // 16, some, 0)


class LineScatter:
    SEMS = (6, 4)

    @staticmethod
    def buffers(rows, width):
        return [pltpu.VMEM((4, rows, width), LOW), pltpu.VMEM((5, rows, width), LOW)]

    def __init__(self, place, partial, across, passing, sems, rows):
        self.place, self.partial, self.sems, self.rows = place, partial, sems, rows
        self.across, self.passing = across, passing

    def cross(self, z):
        p = self.place
        return remote(
            self.partial.at[2 * z + 1 - p.c, self.rows],
            self.across.at[z, self.rows],
            self.sems.at[0, z],
            self.sems.at[1, z],
            c=1 - p.c,
        )

    def hop(self, z, way, landing):
        p = self.place
        there = jnp.minimum(p.z + 1, 3) if way == 0 else jnp.maximum(p.z - 1, 0)
        return remote(
            self.across.at[z, self.rows],
            self.passing.at[landing, self.rows],
            self.sems.at[2 + 2 * way, z],
            self.sems.at[3 + 2 * way, z],
            z=there,
        )

    def send(self, z, way):
        p = self.place
        if way == 0:
            self.hop(z, 0, z).start()
        else:
            pl.when(p.z - 1 == z)(lambda: self.hop(z, 1, 4).start())
            pl.when(p.z - 1 != z)(lambda: self.hop(z, 1, z).start())

    def start(self):
        for z in range(4):
            self.cross(z).start()

    def head(self):
        p = self.place
        for z in range(4):
            self.cross(z).wait_recv()
        for way, end in ((0, 0), (1, 3)):

            @pl.when(p.z == end)
            def _():
                for index in range(3):
                    z = 3 - index if way == 0 else index
                    spot = self.across.at[z, self.rows]
                    add_blocks(spot, [self.partial.at[2 * z + p.c, self.rows], spot])
                    self.send(z, way)

    def step(self, index):
        p = self.place
        for here, way, z in ((1, index // 2, (3, 2, 0)[index]), (2, 1 - index // 2, (0, 1, 3)[index])):

            @pl.when(p.z == here)
            def _():
                self.hop(z, way, z).wait_recv()
                spot = self.across.at[z, self.rows]
                add_blocks(
                    spot,
                    [
                        self.partial.at[2 * z + p.c, self.rows],
                        spot,
                        self.passing.at[z, self.rows],
                    ],
                )
                self.send(z, way)

    def steps(self):
        for index in range(3):
            self.step(index)

    def arrive(self):
        p = self.place
        pl.when(p.z > 0)(lambda: self.hop(p.z, 0, p.z).wait_recv())
        pl.when(p.z < 3)(lambda: self.hop(p.z, 1, 4).wait_recv())
        for end, landing in ((0, 0), (3, 4)):

            @pl.when(p.z == end)
            def _():
                spot = self.passing.at[landing, self.rows]
                spot[...] = jnp.zeros(spot.shape, LOW)

    def total(self, rows):
        p = self.place
        parts = (
            self.partial[p.slot, rows, :],
            self.across[p.z, rows, :],
            self.passing[p.z, rows, :],
            self.passing[4, rows, :],
        )
        return sum(part.astype(WIDE) for part in parts)

    def drain(self):
        p = self.place
        for z in range(4):
            self.cross(z).wait_send()
            pl.when(p.z < z)(lambda: self.hop(z, 0, z).wait_send())
            pl.when(p.z > z)(lambda: self.hop(z, 1, z).wait_send())


class Relayout:
    SEMS = (8, 8)

    def __init__(self, place, parts, target, sems):
        self.place, self.parts, self.target, self.sems = place, parts, target, sems

    def sem(self, kind, slot):
        return self.sems.at[kind, slot]

    def line(self, step):
        p = self.place
        slot = lax.rem(p.slot + step, 8)
        copies = []
        for source, first, size, there in self.parts:
            same_for_all = source.shape[1] == size
            columns = lanes(first if same_for_all else first + size * slot, size)
            piece = source.at[:, columns]
            spot = self.target.at[p.block_here, :, pl.ds(there, size)]
            if step == 0:
                copies.append(pltpu.make_async_copy(piece, spot, self.sem(1, p.slot)))
            else:
                copies.append(
                    remote(
                        piece,
                        spot,
                        self.sem(0, slot),
                        self.sem(1, p.slot),
                        z=slot // 2,
                        c=lax.rem(slot, 2),
                    )
                )
        return copies

    def whole(self, slot):
        p = self.place
        spot = self.target.at[p.block(slot, p.x, p.y)]
        return remote(spot, spot, self.sem(0, slot), self.sem(1, slot), c=1 - p.c)

    def plane(self, slot, x, y, way, send, receive):
        p = self.place
        spot = self.target.at[p.block(slot, x, y)]
        where = {"x": 1 - p.x} if way == 0 else {"y": 1 - p.y}
        return remote(spot, spot, self.sem(send, slot), self.sem(receive, slot), **where)

    def from_own(self, slot, way):
        p = self.place
        return self.plane(slot, p.x, p.y, way, 2 + 2 * way, 3 + 2 * way)

    def corner(self, slot, way):
        p = self.place
        x, y = (p.x, 1 - p.y) if way == 0 else (1 - p.x, p.y)
        return self.plane(slot, x, y, way, 6, 7)

    def start(self, steps=range(8)):
        for step in steps:
            for copy in self.line(step):
                copy.start()

    def spread(self, step):
        p = self.place
        slot = lax.rem(p.slot + 8 - step, 8)
        if isinstance(step, int) and step == 0:
            spot = self.target.at[p.block_here]
            pltpu.make_async_copy(spot, spot, self.sem(1, p.slot)).wait()
        else:
            self.whole(slot).wait_recv()
        for way in range(2):
            self.from_own(slot, way).start()

    def spread_from(self, slot):
        p = self.place

        @pl.when(p.slot == slot)
        def _():
            spot = self.target.at[p.block_here]
            pltpu.make_async_copy(spot, spot, self.sem(1, p.slot)).wait()

        pl.when(p.slot != slot)(lambda: self.whole(slot).wait_recv())
        for way in range(2):
            self.from_own(slot, way).start()

    def corners(self, z):
        self.from_own(2 * z, 0).wait_recv()
        self.corner(2 * z, 1).start()
        self.from_own(2 * z + 1, 1).wait_recv()
        self.corner(2 * z + 1, 0).start()

    def finish(self):
        for z in range(4):
            self.from_own(2 * z, 1).wait_recv()
            self.from_own(2 * z + 1, 0).wait_recv()
            self.corner(2 * z, 1).wait_recv()
            self.corner(2 * z + 1, 0).wait_recv()

    def drain(self):
        for step in range(1, 8):
            self.whole(lax.rem(self.place.slot + step, 8)).wait_send()
        for z in range(4):
            self.corner(2 * z, 1).wait_send()
            self.corner(2 * z + 1, 0).wait_send()
        for slot in range(8):
            for way in range(2):
                self.from_own(slot, way).wait_send()


class PlaneScatter:
    @staticmethod
    def scratch(units, rows, width):
        shape = (rows, width)
        return [
            pltpu.VMEM((2, 2, units) + shape, LOW),
            pltpu.VMEM((2, units) + shape, LOW),
            DMA((4, 2, 2, units)),
        ]

    def __init__(self, place, part, units, got, last, sems):
        self.place, self.part, self.units = place, part, units
        self.got, self.last, self.sems = got, last, sems

    def pair(self, near):
        p = self.place
        x, y = (p.x, p.y) if near else (1 - p.x, 1 - p.y)
        return ((p.x, y), (x, p.y))

    def own(self, half, near, unit):
        x, y = self.pair(near)[half]
        return self.part(half, unit, x, y)

    def sums(self, half, unit):
        return self.own(half, 1, unit)

    def first(self, half, near, unit):
        p = self.place
        x, y = self.pair(near)[half]
        x, y = (1 - x, y) if half == 0 else (x, 1 - y)
        where = {"x": 1 - p.x} if half == 0 else {"y": 1 - p.y}
        return remote(
            self.part(half, unit, x, y),
            self.got.at[half, near, unit],
            self.sems.at[0, half, near, unit],
            self.sems.at[1, half, near, unit],
            **where,
        )

    def second(self, half, unit):
        p = self.place
        where = {"y": 1 - p.y} if half == 0 else {"x": 1 - p.x}
        return remote(
            self.own(half, 0, unit),
            self.last.at[half, unit],
            self.sems.at[2, half, 0, unit],
            self.sems.at[3, half, 0, unit],
            **where,
        )

    def each(self, call):
        lax.fori_loop(0, self.units, lambda unit, carry: (call(unit), carry)[1], 0)

    def start_unit(self, unit):
        for near in range(2):
            for half in range(2):
                self.first(half, near, unit).start()

    def start(self):
        for near in range(2):

            def begin(unit):
                for half in range(2):
                    self.first(half, near, unit).start()

            self.each(begin)

    def middle(self, unit):
        for half in range(2):
            self.first(half, 0, unit).wait_recv()
            spot = self.own(half, 0, unit)
            add_blocks(spot, [spot, self.got.at[half, 0, unit]])
            self.second(half, unit).start()

    def final(self, unit):
        for half in range(2):
            self.first(half, 1, unit).wait_recv()
            self.second(half, unit).wait_recv()
            spot = self.own(half, 1, unit)
            add_blocks(spot, [spot, self.got.at[half, 1, unit], self.last.at[half, unit]])

    def drain(self):
        def end(unit):
            for half in range(2):
                for near in range(2):
                    self.first(half, near, unit).wait_send()
                self.second(half, unit).wait_send()

        self.each(end)


class LineReturn:
    SEMS = (2, 8)

    def __init__(self, place, sums, parts, target, sems):
        self.place, self.sums, self.parts = place, sums, parts
        self.target, self.sems = target, sems

    def copies(self, z, c, local):
        p = self.place
        made = []
        for here, size, first in self.parts:
            piece = self.sums(c, z).at[:, pl.ds(here, size)]
            spot = self.target.at[:, lanes(first + size * p.slot, size)]
            if local:
                made.append(pltpu.make_async_copy(piece, spot, self.sems.at[1, p.slot]))
            else:
                made.append(
                    remote(
                        piece, spot, self.sems.at[0, 2 * z + c], self.sems.at[1, p.slot], z=z, c=c
                    )
                )
        return made

    def send(self, z):
        p = self.place
        for c in range(2):
            mine = (z == p.z) & (c == p.c)

            @pl.when(mine)
            def _():
                for copy in self.copies(z, c, True):
                    copy.start()

            @pl.when(jnp.logical_not(mine))
            def _():
                for copy in self.copies(z, c, False):
                    copy.start()

    def finish(self):
        p = self.place
        spot = self.sums(0, 0)
        pltpu.make_async_copy(spot, spot, self.sems.at[1, p.slot]).wait()
        for step in range(1, 8):
            slot = lax.rem(p.slot + step, 8)
            whole = remote(
                spot, spot, self.sems.at[0, slot], self.sems.at[1, slot], c=1 - p.c
            )
            whole.wait_recv()
            whole.wait_send()


def kernel_call(kernel, name, number, inputs, in_specs, outputs, out_specs, scratch):
    return pl.pallas_call(
        kernel,
        out_shape=[jax.ShapeDtypeStruct(shape, dtype) for shape, dtype in outputs],
        in_specs=in_specs,
        out_specs=out_specs,
        scratch_shapes=scratch,
        compiler_params=pltpu.CompilerParams(
            collective_id=number, has_side_effects=True, vmem_limit_bytes=60 * 2**20
        ),
        name=name,
    )(*inputs)


CHUNK = 16


def by_rows(count, call):
    def some(step, carry):
        call(pl.ds(pl.multiple_of(step * CHUNK, CHUNK), CHUNK))
        return carry

    lax.fori_loop(0, count // CHUNK, some, 0)


def normed_back(grad_normed, unit, inverse, gain):
    grad_unit = grad_normed * gain
    return inverse * (grad_unit - unit * jnp.mean(grad_unit * unit, axis=-1, keepdims=True))


def turn_tables(length):
    half_dim = HEAD_DIM // 2
    exponent = np.arange(half_dim, dtype=np.float32) * np.float32(2.0 / HEAD_DIM)
    frequency = np.float32(ROPE_BASE) ** (-exponent)
    angles = np.arange(length, dtype=np.float32)[:, None] * frequency[None, :]
    angles = angles.astype(np.float64)
    cosines, sines = np.cos(angles).astype(np.float32), np.sin(angles).astype(np.float32)
    return (
        jnp.asarray(np.tile(cosines, (1, 4))),
        jnp.asarray(np.tile(np.concatenate([-sines, sines], axis=1), (1, 2))),
    )


def turn(values, cosines, sines):
    lane = lax.broadcasted_iota(jnp.int32, values.shape, 1)
    half_dim = HEAD_DIM // 2
    width = values.shape[1]
    partner = jnp.where(
        lax.rem(lane, HEAD_DIM) < half_dim,
        pltpu.roll(values, width - half_dim, 1),
        pltpu.roll(values, half_dim, 1),
    )
    return values * cosines + partner * sines


def head_mask(head):
    lane = lax.broadcasted_iota(jnp.int32, (1, 128), 1)
    return (lane // HEAD_DIM == lax.rem(head, 2)).astype(WIDE).astype(LOW)


def scaled_probs(queries, keys, first_row):
    scores = lax.dot_general(queries, keys, CONTRACT_LAST, preferred_element_type=WIDE)
    scores = scores * HEAD_DIM ** (-0.5)
    row = lax.broadcasted_iota(jnp.int32, scores.shape, 0) + first_row
    column = lax.broadcasted_iota(jnp.int32, scores.shape, 1)
    scores = jnp.where(column <= row, scores, MASKED)
    expo = jnp.exp(scores - jnp.max(scores, axis=1, keepdims=True))
    return expo * (1.0 / jnp.sum(expo, axis=1, keepdims=True))


QUERY_ROWS = 256


def attend_head(head, qkv, total):
    pair = lanes(head // 2 * 128, 128)
    mask = head_mask(head)
    for block in range(qkv.shape[1] // QUERY_ROWS):
        rows = pl.ds(block * QUERY_ROWS, QUERY_ROWS)
        keys = pl.ds(0, (block + 1) * QUERY_ROWS)
        probs = scaled_probs(qkv[0, rows, pair] * mask, qkv[1, keys, pair], block * QUERY_ROWS)
        total[rows, pair] += jnp.dot(
            probs.astype(LOW), qkv[2, keys, pair] * mask, preferred_element_type=WIDE
        )


def forward_kernel(
    tok,
    cot,
    wide_q,
    gain,
    wide_g,
    wide_d,
    wide_o,
    cosines,
    sines,
    all_cot,
    normed_two,
    full_g,
    full_d,
    out_q,
    out_o,
    out_normed,
    out_qkv,
    out_attended,
    out_residual,
    out_gains,
    out_tok,
    all_tok,
    full_q,
    full_o,
    normed_one,
    qkv,
    heads,
    attended,
    residual,
    gain_rows,
    mine,
    partial,
    from_q,
    from_g,
    from_d,
    from_o,
    wq,
    wg,
    wd,
    wo,
    *scratch,
):
    buffers, sems = scratch[:2], scratch[2:]
    tok_swap, cot_swap, out_swap, tok_sems, cot_sems, q_sems, g_sems, d_sems = sems[:8]
    o_sems, sum_a, sum_b, gather_a, gather_b, keep_sems, cast_sems = sems[8:]
    casts = [
        (wide_q, from_q, wq),
        (wide_o, from_o, wo),
        (wide_g, from_g, wg),
        (wide_d, from_d, wd),
    ]
    loads = [
        pltpu.make_async_copy(source, target, cast_sems.at[index])
        for index, (source, target, _) in enumerate(casts)
    ]
    for copy in loads:
        copy.start()

    def cast(index):
        _, source, target = casts[index]
        loads[index].wait()
        parts = source.shape[1] // 2048

        def some(step, carry):
            rows = pl.ds(pl.multiple_of(step // parts * CHUNK, CHUNK), CHUNK)
            columns = lanes(lax.rem(step, parts) * 2048, 2048)
            target[rows, columns] = source[rows, columns].astype(LOW)
            return carry

        lax.fori_loop(0, source.shape[0] // CHUNK * parts, some, 0)

    p = Place()
    p.meet(True)
    rows_own = tok.shape[0]
    seq_len = 8 * rows_own
    step_q, step_g, step_d = wq.shape[1] // 24, wg.shape[1] // 16, wd.shape[1] // 8
    q_parts = [(wq, i * 8 * step_q, step_q, i * step_q) for i in range(3)]
    q_parts.append((gain, 0, gain.shape[1], 3 * step_q))
    move_q = Relayout(p, q_parts, full_q, q_sems)
    move_g = Relayout(
        p, [(wg, i * 8 * step_g, step_g, i * step_g) for i in range(2)], full_g, g_sems
    )
    move_d = Relayout(p, [(wd, 0, step_d, 0)], full_d, d_sems)
    tokens, cotangents = LineGather(p, all_tok, tok_sems), LineGather(p, all_cot, cot_sems)
    away = 2 * p.z + 1 - p.c
    swap_tok = Swap(p, tok, all_tok.at[away], all_tok.at[p.slot], tok_swap)
    swap_cot = Swap(p, cot, all_cot.at[away], all_cot.at[p.slot], cot_swap)
    swap_out = Swap(p, wo, full_o.at[2 * p.y + 1 - p.x], full_o.at[2 * p.y + p.x], out_swap)
    half = wo.shape[0] // 2

    def out_copy(kind):
        own, beside, above = 2 * p.y + p.x, 2 * p.y + 1 - p.x, 2 * (1 - p.y) + p.x
        send, got = o_sems.at[0, kind], o_sems.at[1, kind]
        if kind < 2:
            where = {"x": 1 - p.x} if kind == 0 else {"y": 1 - p.y}
            return remote(full_o.at[own], full_o.at[own], send, got, **where)
        spot = full_o.at[beside if kind == 2 else above, pl.ds((kind - 2) * half, half)]
        where = {"y": 1 - p.y} if kind == 2 else {"x": 1 - p.x}
        return remote(spot, spot, send, got, **where)

    kept = []

    def keep(source, target):
        copy = pltpu.make_async_copy(source, target, keep_sems.at[len(kept)])
        copy.start()
        kept.append(copy)

    swap_tok.start()
    cast(0)
    move_q.start()
    cast(1)
    swap_tok.wait()
    tokens.start()
    swap_out.start()
    swap_cot.start()
    cast(2)
    cast(3)
    for step in range(8):
        move_q.spread(step)
    tokens.inner(1)
    tokens.outer()
    move_g.start(range(3))
    tokens.inner(2)
    swap_out.wait()
    out_copy(0).start()
    out_copy(1).start()
    for z in range(4):
        move_q.corners(z)
    out_copy(0).wait_recv()
    out_copy(2).start()
    out_copy(1).wait_recv()
    out_copy(3).start()
    tokens.inner(3)
    tokens.drain()
    move_g.start(range(3, 8))
    move_q.finish()
    for step in range(3):
        move_g.spread(step)
    columns = full_q.shape[2]
    gain_block = full_q[:, :, pl.ds(3 * step_q, columns - 3 * step_q)].reshape(-1, 128)
    pick = lax.broadcasted_iota(jnp.int32, (8, 128), 0) == lax.broadcasted_iota(
        jnp.int32, (8, 128), 1
    )
    gain_rows[...] = lax.dot_general(
        pick.astype(WIDE).astype(LOW), gain_block, CONTRACT_LAST, preferred_element_type=WIDE
    )
    keep(full_q, out_q)
    keep(gain_rows, out_gains)
    tokens.finish()
    keep(all_tok.at[p.slot], out_tok)

    def norm_slot(slot, carry):
        def some(rows):
            unit, _ = rms_parts(all_tok[slot, rows, :].astype(WIDE))
            there = pl.ds(pl.multiple_of(slot * rows_own + rows.start, CHUNK), CHUNK)
            normed_one[there, :] = (unit * gain_rows[pl.ds(0, 1), :]).astype(LOW)

        by_rows(rows_own, some)
        return carry

    lax.fori_loop(0, 8, norm_slot, 0)
    keep(normed_one, out_normed)

    def project(part, carry):
        rows = pl.ds(pl.multiple_of(part * 512, 512), 512)
        for kind in range(3):
            weight = full_q[:, :, pl.ds(kind * step_q, step_q)].reshape(-1, step_q)
            made = jnp.dot(normed_one[rows, :], weight, preferred_element_type=WIDE)
            if kind < 2:
                made = turn(
                    made,
                    jnp.concatenate([cosines[rows, :]] * 2, axis=1),
                    jnp.concatenate([sines[rows, :]] * 2, axis=1),
                )
            qkv[kind, rows, :] = made.astype(LOW)
        return carry

    lax.fori_loop(0, seq_len // 512, project, 0)
    keep(qkv, out_qkv)
    heads[...] = jnp.zeros_like(heads)

    def one_head(head, carry):
        attend_head(head, qkv, heads)
        return carry

    lax.fori_loop(0, 4, one_head, 0)
    move_g.spread(3)
    attended[...] = heads[...].astype(LOW)
    keep(attended, out_attended)
    out_copy(2).wait_recv()
    out_copy(3).wait_recv()
    keep(full_o, out_o)
    out_weight = lambda: full_o[...].reshape(-1, full_o.shape[2])

    def project_out(part, carry):
        rows = pl.ds(pl.multiple_of(part * 256, 256), 256)
        made = jnp.dot(attended[rows, :], out_weight(), preferred_element_type=WIDE)
        partial[pl.ds(2 * part, 2)] = made.astype(LOW).reshape(2, rows_own, -1)
        return carry

    lax.fori_loop(0, seq_len // 256, project_out, 0)

    part_rows = [pl.ds(0, rows_own // 2), pl.ds(rows_own // 2, rows_own // 2)]
    sums = [
        LineScatter(p, partial, *buffers, sem, rows) for sem, rows in zip((sum_a, sum_b), part_rows)
    ]
    gathers = [
        LineGather(p, normed_two, sem, mine.at[rows], rows)
        for sem, rows in zip((gather_a, gather_b), part_rows)
    ]

    def local(part):
        def some(rows):
            there = pl.ds(pl.multiple_of(part * (rows_own // 2) + rows.start, CHUNK), CHUNK)
            total = all_tok[p.slot, there, :].astype(WIDE) + sums[part].total(there)
            residual[there, :] = total
            unit, _ = rms_parts(total)
            mine[there, :] = (unit * gain_rows[pl.ds(1, 1), :]).astype(LOW)

        by_rows(rows_own // 2, some)

    for part in sums:
        part.start()
    swap_cot.wait()
    cotangents.start_part(True)
    for part in sums:
        part.head()
    move_g.spread(4)
    move_g.spread(5)
    sums[0].steps()
    move_g.spread(6)
    move_g.spread(7)
    cotangents.inner(1)
    in_line = (p.z == 1) | (p.z == 2)
    pl.when(in_line)(move_d.start)
    sums[0].arrive()
    local(0)
    gathers[0].start()
    move_g.corners(0)
    move_g.corners(1)
    sums[1].steps()
    move_g.corners(2)
    move_g.corners(3)
    gathers[0].inner(1)
    sums[1].arrive()
    local(1)
    gathers[1].start()
    keep(residual, out_residual)
    cotangents.start_part(False)
    pl.when(jnp.logical_not(in_line))(move_d.start)
    for slot in range(2, 6):
        move_d.spread_from(slot)
    gathers[0].outer()
    gathers[1].inner(1)
    gathers[0].inner(2)
    gathers[1].outer()
    gathers[1].inner(2)
    cotangents.outer()
    for slot in (0, 1, 6, 7):
        move_d.spread_from(slot)
    cotangents.inner(2)
    for z in range(4):
        move_d.corners(z)
    gathers[0].inner(3)
    gathers[1].inner(3)
    cotangents.inner(3)
    for kind in range(4):
        out_copy(kind).wait_send()
    for part in (swap_tok, swap_cot, swap_out):
        part.drain()
    for part in gathers + [cotangents, move_g, move_d]:
        part.finish()
    for part in gathers + sums + [cotangents, move_q, move_g, move_d]:
        part.drain()
    for copy in kept:
        copy.wait()


def forward(tokens, cotangent, qkv, gain_columns, gate_up, down, out_rows, cosines, sines):
    rows, width = tokens.shape
    own = qkv.shape[0]
    here = qkv.shape[1] // 24
    q_shape = (32, own, 3 * here + gain_columns.shape[1])
    vmem = lambda shape, dtype=LOW: pltpu.VMEM(shape, dtype)
    outputs = [
        ((8, rows, width), LOW),
        ((8, rows, width), LOW),
        ((32, own, gate_up.shape[1] // 8), LOW),
        ((32, own, down.shape[1] // 8), LOW),
        (q_shape, LOW),
        ((4, own, width), LOW),
        ((8 * rows, width), LOW),
        ((3, 8 * rows, here), LOW),
        ((8 * rows, here), LOW),
        ((rows, width), WIDE),
        ((8, width), WIDE),
        ((rows, width), LOW),
    ]
    return kernel_call(
        forward_kernel,
        "forward",
        1,
        (tokens, cotangent, qkv, gain_columns, gate_up, down, out_rows, cosines, sines),
        [ANYWHERE] * 7 + [IN_VMEM] * 2,
        outputs,
        [ANYWHERE] * len(outputs),
        [
            vmem((8, rows, width)),
            vmem(q_shape),
            vmem((4, own, width)),
            vmem((8 * rows, width)),
            vmem((3, 8 * rows, here)),
            vmem((8 * rows, here), WIDE),
            vmem((8 * rows, here)),
            vmem((rows, width), WIDE),
            vmem((8, width), WIDE),
            vmem((rows, width)),
            vmem((8, rows, width)),
        ]
        + [vmem(array.shape, WIDE) for array in (qkv, gate_up, down, out_rows)]
        + [vmem(array.shape) for array in (qkv, gate_up, down, out_rows)]
        + LineScatter.buffers(rows, width)
        + [DMA((3,))] * 3
        + [DMA(LineGather.SEMS)] * 2
        + [DMA(Relayout.SEMS)] * 3
        + [DMA((2, 4))]
        + [DMA(LineScatter.SEMS)] * 2
        + [DMA(LineGather.SEMS)] * 2
        + [DMA((8,)), DMA((4,))],
    )


def weight_part(place, ref):
    return lambda half, unit, x, y: ref.at[place.block(2 * unit + half, x, y)]


def attend_back(head, qkv, grad_heads, grads):
    pair = lanes(head // 2 * 128, 128)
    mask = head_mask(head)
    for block in range(qkv.shape[1] // QUERY_ROWS):
        rows = pl.ds(block * QUERY_ROWS, QUERY_ROWS)
        keys = pl.ds(0, (block + 1) * QUERY_ROWS)
        queries, grad_rows = qkv[0, rows, pair] * mask, grad_heads[rows, pair] * mask
        key_rows = qkv[1, keys, pair]
        probs = scaled_probs(queries, key_rows, block * QUERY_ROWS)
        grad_probs = lax.dot_general(
            grad_rows, qkv[2, keys, pair], CONTRACT_LAST, preferred_element_type=WIDE
        )
        delta = jnp.sum(probs * grad_probs, axis=1, keepdims=True)
        grad_scores = (probs * (grad_probs - delta) * HEAD_DIM ** (-0.5)).astype(LOW)
        grads[0, rows, pair] += jnp.dot(grad_scores, key_rows * mask, preferred_element_type=WIDE)
        grads[1, keys, pair] += lax.dot_general(
            grad_scores, queries, CONTRACT_FIRST, preferred_element_type=WIDE
        )
        grads[2, keys, pair] += lax.dot_general(
            probs.astype(LOW), grad_rows, CONTRACT_FIRST, preferred_element_type=WIDE
        )


def mlp_kernel(
    normed,
    wg,
    wd,
    cot,
    residual,
    gain_rows,
    branch,
    g_sum,
    d_part,
    block_out,
    out_grad,
    nt,
    full_g,
    full_d,
    ct,
    active,
    grad_wide,
    part_two,
    part_out,
    grad_residual,
    mine,
    *scratch,
):
    p = Place()
    rows_own, width = residual.shape
    seq_len = 8 * rows_own
    own, ff = wd.shape[1], wd.shape[2]
    units = wd.shape[0] // 8
    block_rows = seq_len // 2
    part = ff // 4
    wide = width // 4
    blocks = wide // own
    load_sems, sum_a, sum_b, sum_c, gather_a, gather_b, swap_sems, keep_sems = scratch[7:]
    part_rows = [pl.ds(0, rows_own // 2), pl.ds(rows_own // 2, rows_own // 2)]
    sum_two = [
        LineScatter(p, part_two, *scratch[:2], sem, rows)
        for sem, rows in zip((sum_a, sum_b), part_rows)
    ]
    sum_out = LineScatter(p, part_out, *scratch[2:4], sum_c, pl.ds(0, rows_own))
    plane = PlaneScatter(p, weight_part(p, full_g), units, *scratch[4:7])
    gathers = [
        LineGather(p, branch, sem, mine.at[rows], rows)
        for sem, rows in zip((gather_a, gather_b), part_rows)
    ]

    def load(index):
        if index < 4:
            source, target = ((normed, nt), (cot, ct))[index // 2]
            return pltpu.make_async_copy(
                source.at[:, part_rows[index % 2]], target.at[index % 2], load_sems.at[index]
            )
        return pltpu.make_async_copy(wd, full_d, load_sems.at[4])

    def load_wide(index, side):
        columns = lanes(side * ff + index * part, part)
        return pltpu.make_async_copy(
            wg.at[:, :, columns], full_g.at[:, :, columns], load_sems.at[5 + 2 * index + side]
        )

    load(0).start()
    for index in range(4):
        for side in range(2):
            load_wide(index, side).start()
        if index == 0:
            for other in (2, 4, 1, 3):
                load(other).start()
    p.meet(True)
    for index in (0, 2, 4):
        load(index).wait()

    def stage_one(half, first, last):
        rows = pl.ds(half * block_rows, block_rows)

        def some(index, carry):
            if half == 0:
                load_wide(index, 0).wait()
                load_wide(index, 1).wait()
            here, there = lanes(index * part, part), lanes(ff + index * part, part)
            left = nt[half].reshape(block_rows, width)
            gate = jnp.dot(left, full_g[:, :, here].reshape(width, part), preferred_element_type=WIDE)
            up = jnp.dot(left, full_g[:, :, there].reshape(width, part), preferred_element_type=WIDE)
            grad = jnp.dot(
                ct[half].reshape(block_rows, width),
                full_d[:, :, here].reshape(width, part),
                preferred_element_type=WIDE,
            )
            sigmoid_gate = jax.nn.sigmoid(gate)
            active[rows, here] = (gate * sigmoid_gate * up).astype(LOW)
            grad_wide[rows, here] = (
                grad * up * sigmoid_gate * (1.0 + gate * (1.0 - sigmoid_gate))
            ).astype(LOW)
            grad_wide[rows, there] = (grad * gate * sigmoid_gate).astype(LOW)
            return carry

        lax.fori_loop(first, last, some, 0)

    def rows_times(left, weight, target, half, first, last):
        def some(index, carry):
            made = lax.dot_general(
                left[pl.ds(half * block_rows, block_rows), :],
                weight[pl.ds(index * blocks, blocks)].reshape(wide, -1),
                CONTRACT_LAST,
                preferred_element_type=WIDE,
            )
            target[:, part_rows[half], lanes(index * wide, wide)] = made.astype(LOW).reshape(
                8, rows_own // 2, wide
            )
            return carry

        lax.fori_loop(first, last, some, 0)

    def down_grad(index, carry):
        made = lax.dot_general(
            ct[:, :, :, lanes(index * wide, wide)].reshape(seq_len, wide),
            active[...],
            CONTRACT_FIRST,
            preferred_element_type=WIDE,
        )
        full_d[pl.ds(index * blocks, blocks)] = made.astype(LOW).reshape(blocks, own, ff)
        return carry

    def wide_grad(index):
        for side in range(2):
            made = lax.dot_general(
                nt[:, :, :, pl.ds(index * wide, wide)].reshape(seq_len, wide),
                grad_wide[:, pl.ds(side * ff, ff)],
                CONTRACT_FIRST,
                preferred_element_type=WIDE,
            )
            full_g[pl.ds(index * blocks, blocks), :, pl.ds(side * ff, ff)] = made.astype(
                LOW
            ).reshape(blocks, own, ff)
        plane.start_unit(index)

    def local_two(part):
        def some(rows):
            spot = pl.ds(pl.multiple_of(part * (rows_own // 2) + rows.start, CHUNK), CHUNK)
            unit, inverse = rms_parts(residual[spot, :])
            total = ct[part, p.slot, rows, :].astype(WIDE) + normed_back(
                sum_two[part].total(spot), unit, inverse, gain_rows[pl.ds(1, 1), :]
            )
            grad_residual[spot, :] = total
            mine[spot, :] = total.astype(LOW)

        by_rows(rows_own // 2, some)

    stage_one(0, 0, 4)
    rows_times(grad_wide, full_g, part_two, 0, 0, 4)
    sum_two[0].start()
    load(1).wait()
    load(3).wait()
    stage_one(1, 0, 2)
    sum_two[0].head()
    stage_one(1, 2, 4)
    rows_times(grad_wide, full_g, part_two, 1, 0, 2)
    sum_two[0].step(0)
    rows_times(grad_wide, full_g, part_two, 1, 2, 3)
    sum_two[0].step(1)
    rows_times(grad_wide, full_g, part_two, 1, 3, 4)
    sum_two[1].start()
    sum_two[0].step(2)
    wide_grad(0)
    sum_two[1].head()
    sum_two[0].arrive()
    local_two(0)
    gathers[0].start()
    rows_times(active, full_d, part_out, 0, 0, 4)
    sum_two[1].step(0)
    rows_times(active, full_d, part_out, 1, 0, 4)
    sum_out.start()
    sum_two[1].step(1)
    sum_two[1].step(2)
    wide_grad(1)
    gathers[0].inner(1)
    sum_two[1].arrive()
    local_two(1)
    gathers[1].start()
    sum_out.head()
    keep_grad = pltpu.make_async_copy(grad_residual, out_grad, keep_sems.at[1])
    keep_grad.start()
    wide_grad(2)
    gathers[0].outer()
    gathers[1].inner(1)
    wide_grad(3)
    gathers[0].inner(2)
    gathers[1].outer()
    plane.middle(0)
    lax.fori_loop(0, 2, down_grad, 0)
    gathers[1].inner(2)
    lax.fori_loop(2, 4, down_grad, 0)
    keep_d = pltpu.make_async_copy(full_d, d_part, keep_sems.at[0])
    keep_d.start()
    plane.middle(1)
    sum_out.step(0)
    gathers[0].inner(3)
    gathers[1].inner(3)
    plane.middle(2)
    sum_out.step(1)
    sum_out.step(2)
    plane.middle(3)
    for gather in gathers:
        gather.finish()
    for gather in gathers:
        gather.drain()
    sum_out.arrive()

    def local_out(rows):
        mine[rows, :] = (residual[rows, :] + sum_out.total(rows)).astype(LOW)

    by_rows(rows_own, local_out)
    keep_block = pltpu.make_async_copy(mine, block_out, swap_sems.at[0])
    keep_block.start()

    def keep_g(half, unit):
        return pltpu.make_async_copy(
            plane.sums(half, unit), g_sum.at[half, unit], keep_sems.at[2 + 4 * half + unit]
        )

    for unit in range(units):
        plane.final(unit)
        for half in range(2):
            keep_g(half, unit).start()
    keep_block.wait()
    for part in sum_two + [sum_out, plane]:
        part.drain()
    keep_d.wait()
    keep_grad.wait()
    for unit in range(units):
        for half in range(2):
            keep_g(half, unit).wait()


def mlp(normed, wg, wd, cot, residual, gain_rows):
    _, rows, width = normed.shape
    own, ff = wd.shape[1:]
    units = wd.shape[0] // 8
    vmem = lambda shape, dtype=LOW: pltpu.VMEM(shape, dtype)
    return kernel_call(
        mlp_kernel,
        "mlp",
        2,
        (normed, wg, wd, cot, residual, gain_rows),
        [ANYWHERE] * 4 + [IN_VMEM] * 2,
        [
            (normed.shape, LOW),
            ((2, units, own, 2 * ff), LOW),
            (wd.shape, LOW),
            ((rows, width), LOW),
            ((rows, width), WIDE),
        ],
        [ANYWHERE] * 5,
        [
            vmem((2, 8, rows // 2, width)),
            vmem(wg.shape),
            vmem(wd.shape),
            vmem((2, 8, rows // 2, width)),
            vmem((8 * rows, ff)),
            vmem((8 * rows, 2 * ff)),
            vmem(normed.shape),
            vmem(normed.shape),
            vmem((rows, width), WIDE),
            vmem((rows, width)),
        ]
        + LineScatter.buffers(rows, width) * 2
        + PlaneScatter.scratch(units, own, 2 * ff)
        + [DMA((13,))]
        + [DMA(LineScatter.SEMS)] * 3
        + [DMA(LineGather.SEMS)] * 2
        + [DMA((3,)), DMA((2 + 2 * units,))],
    )


def backward_kernel(
    branch_all,
    grad_in,
    gain_rows,
    own_tok,
    full_q,
    full_o,
    qkv,
    attended,
    normed_one,
    cosines,
    sines,
    g_sum,
    d_part,
    block,
    input_grad,
    block_out,
    q_out,
    g_out,
    d_out,
    o_out,
    work,
    branch,
    grad_residual,
    grad_heads,
    grads,
    grad_projected,
    q_part,
    o_part,
    o_sum,
    d_here,
    *scratch,
):
    buffers, rest = scratch[:2], scratch[2:]
    p = Place()
    rows_own, width = grad_residual.shape
    seq_len = 8 * rows_own
    own = full_o.shape[1]
    units = g_sum.shape[1]
    half = own // 2
    step_q, step_g, step_d = q_part.shape[2] // 3, g_sum.shape[3] // 2, d_part.shape[2]
    plane_d = PlaneScatter(p, weight_part(p, d_here), units, *rest[:3])
    plane_q = PlaneScatter(p, weight_part(p, q_part), units, *rest[3:6])
    plane_o = PlaneScatter(
        p, lambda h, u, x, y: o_part.at[2 * y + x, pl.ds(h * half, half)], 1, *rest[6:9]
    )
    sum_sems, return_sems, swap_sems, load_sems = rest[9:11], rest[11:14], rest[14:18], rest[18]
    part_rows = [pl.ds(0, rows_own // 2), pl.ds(rows_own // 2, rows_own // 2)]
    sum_one = [
        LineScatter(p, branch, *buffers, sem, rows) for sem, rows in zip(sum_sems, part_rows)
    ]
    return_q = LineReturn(
        p, plane_q.sums, [(i * step_q, step_q, i * 8 * step_q) for i in range(3)], q_out, return_sems[0]
    )
    return_g = LineReturn(
        p,
        lambda c, z: g_sum.at[c, z],
        [(i * step_g, step_g, i * 8 * step_g) for i in range(2)],
        g_out,
        return_sems[1],
    )
    return_d = LineReturn(p, plane_d.sums, [(0, step_d, 0)], d_out, return_sems[2])
    swap_in = [
        Swap(p, grad_residual.at[rows], input_grad.at[rows], input_grad.at[rows], sem)
        for sem, rows in zip(swap_sems[:2], part_rows)
    ]
    swap_out = Swap(p, o_sum, o_out, o_out, swap_sems[2])
    swap_block = Swap(p, block, block_out, block_out, swap_sems[3])

    def load(source, target, index):
        return pltpu.make_async_copy(source, target, load_sems.at[index])

    loads = [
        load(branch_all, branch, 0),
        load(d_part, d_here, 1),
        load(normed_one, work, 2),
        load(grad_in, grad_residual, 3),
    ]
    for copy in loads:
        copy.start()
    p.meet(True)
    swap_block.start()
    for z in range(4):
        return_g.send(z)
    loads[0].wait()

    def back_out(part, carry):
        rows = pl.ds(pl.multiple_of(part * 256, 256), 256)
        made = lax.dot_general(
            branch[pl.ds(2 * part, 2)].reshape(256, width),
            full_o[...].reshape(-1, width),
            CONTRACT_LAST,
            preferred_element_type=WIDE,
        )
        grad_heads[rows, :] = made.astype(LOW)
        return carry

    lax.fori_loop(0, seq_len // 256, back_out, 0)
    loads[1].wait()
    plane_d.start()

    def out_grad(part, carry):
        columns = lanes(part * 512, 512)
        made = lax.dot_general(
            attended[...],
            branch[:, :, columns].reshape(seq_len, 512),
            CONTRACT_FIRST,
            preferred_element_type=WIDE,
        )
        o_part[:, :, columns] = made.astype(LOW).reshape(4, own, 512)
        return carry

    lax.fori_loop(0, width // 512, out_grad, 0)
    plane_o.start()
    grads[...] = jnp.zeros_like(grads)

    def one_head(head, carry):
        attend_back(head, qkv, grad_heads, grads)
        plane_d.middle(head)
        return carry

    lax.fori_loop(0, 4, one_head, 0)

    def back_turn(part, carry):
        rows = pl.ds(pl.multiple_of(part * 256, 256), 256)
        for kind in range(3):
            made = grads[kind, rows, :]
            if kind < 2:
                made = turn(
                    made,
                    jnp.concatenate([cosines[rows, :]] * 2, axis=1),
                    jnp.concatenate([-sines[rows, :]] * 2, axis=1),
                )
            grad_projected[rows, pl.ds(kind * step_q, step_q)] = made.astype(LOW)
        return carry

    lax.fori_loop(0, seq_len // 256, back_turn, 0)

    def back_qkv(part, carry):
        weight = full_q[pl.ds(part * 8, 8), :, pl.ds(0, 3 * step_q)].reshape(8 * own, 3 * step_q)
        for block in range(seq_len // 512):
            made = lax.dot_general(
                grad_projected[pl.ds(block * 512, 512), :],
                weight,
                CONTRACT_LAST,
                preferred_element_type=WIDE,
            )
            branch[pl.ds(block * 4, 4), :, lanes(part * 8 * own, 8 * own)] = made.astype(
                LOW
            ).reshape(4, rows_own, 8 * own)
        return carry

    lax.fori_loop(0, 4, back_qkv, 0)
    for part in sum_one:
        part.start()
    loads[2].wait()
    loads[3].wait()
    for part in sum_one:
        part.head()

    def qkv_grad(part, carry):
        made = lax.dot_general(
            work[:, :, lanes(part * 8 * own, 8 * own)].reshape(seq_len, 8 * own),
            grad_projected[...],
            CONTRACT_FIRST,
            preferred_element_type=WIDE,
        )
        q_part[pl.ds(part * 8, 8)] = made.astype(LOW).reshape(8, own, 3 * step_q)
        plane_q.start_unit(part)
        return carry

    lax.fori_loop(0, 4, qkv_grad, 0)

    def local_one(part):
        def some(rows):
            spot = pl.ds(pl.multiple_of(part * (rows_own // 2) + rows.start, CHUNK), CHUNK)
            unit, inverse = rms_parts(own_tok[spot, :].astype(WIDE))
            grad_residual[spot, :] = grad_residual[spot, :] + normed_back(
                sum_one[part].total(spot), unit, inverse, gain_rows[pl.ds(0, 1), :]
            )

        by_rows(rows_own // 2, some)

    for part in sum_one:
        part.steps()
    for unit in range(units):
        plane_d.final(unit)
        return_d.send(unit)
    plane_o.middle(0)
    for unit in range(units):
        plane_q.middle(unit)
    for part in range(2):
        sum_one[part].arrive()
        local_one(part)
        swap_in[part].start()
    plane_o.final(0)
    for h in range(2):
        o_sum[pl.ds(h * half, half), :] = plane_o.sums(h, 0)[...]
    swap_out.start()
    for unit in range(units):
        plane_q.final(unit)
        return_q.send(unit)
    for part in (return_g, return_d, return_q):
        part.finish()
    for part in swap_in + [swap_out, swap_block]:
        part.wait()
        part.drain()
    for part in sum_one + [plane_d, plane_q, plane_o]:
        part.drain()


def backward(
    branch,
    grad_residual,
    gain_rows,
    own_tok,
    full_q,
    full_o,
    qkv,
    attended,
    normed_one,
    cosines,
    sines,
    g_sum,
    d_part,
    block,
):
    _, rows, width = branch.shape
    own, here = full_o.shape[1], attended.shape[1]
    units = g_sum.shape[1]
    vmem = lambda shape, dtype=LOW: pltpu.VMEM(shape, dtype)
    step_g, step_d = g_sum.shape[3], d_part.shape[2]
    return kernel_call(
        backward_kernel,
        "backward",
        3,
        (
            branch,
            grad_residual,
            gain_rows,
            own_tok,
            full_q,
            full_o,
            qkv,
            attended,
            normed_one,
            cosines,
            sines,
            g_sum,
            d_part,
            block,
        ),
        [ANYWHERE] * 2 + [IN_VMEM] * 6 + [ANYWHERE] + [IN_VMEM] * 2 + [ANYWHERE] * 3,
        [
            ((rows, width), WIDE),
            ((rows, width), LOW),
            ((own, 24 * here), LOW),
            ((own, 8 * step_g), LOW),
            ((own, 8 * step_d), LOW),
            ((own, width), LOW),
        ],
        [ANYWHERE] * 6,
        [
            vmem((8, rows, width)),
            vmem((8, rows, width)),
            vmem((rows, width), WIDE),
            vmem((8 * rows, here)),
            vmem((3, 8 * rows, here), WIDE),
            vmem((8 * rows, 3 * here)),
            vmem((32, own, 3 * here)),
            vmem((4, own, width)),
            vmem((own, width)),
            vmem(d_part.shape),
        ]
        + LineScatter.buffers(rows, width)
        + PlaneScatter.scratch(units, own, step_d)
        + PlaneScatter.scratch(units, own, 3 * here)
        + PlaneScatter.scratch(1, own // 2, width)
        + [DMA(LineScatter.SEMS)] * 2
        + [DMA(LineReturn.SEMS)] * 3
        + [DMA((3,))] * 4
        + [DMA((4,))],
    )


ADAM_STEPS = 4
WIDE_RATE = 2.5 * D ** (-0.5)
OUT_RATE = 2.5 * max(D // 512, 1) ** (-0.5)
DOWN_RATE = 2.5 * FF ** (-0.5)


def adam_quick(weight, gradient, first, second, rate, decay):
    new_first = BETA_ONE * first + (1.0 - BETA_ONE) * gradient
    new_second = BETA_TWO * second + (1.0 - BETA_TWO) * gradient * gradient
    root = jnp.sqrt(new_second * (1.0 / (1.0 - BETA_TWO**STEP))) + ADAM_EPS
    moved = new_first * (rate / (1.0 - BETA_ONE**STEP)) / root
    return ((1.0 - rate * decay) * weight - moved, new_first, new_second)


def adam_kernel(*refs):
    inputs, gains, handed = refs[:16], refs[16:19], refs[19:21]
    outputs, gains_new, placed = refs[21:33], refs[33:36], refs[36:38]
    sums = refs[38:]
    step = pl.program_id(0)
    for source, target in zip(handed, placed):
        target[...] = source[...]

    @pl.when(step == 0)
    def _():
        for total in sums:
            total[...] = jnp.zeros_like(total)

    for index, rate in enumerate((WIDE_RATE, OUT_RATE, WIDE_RATE, DOWN_RATE)):
        weight, first, second, low_gradient = (ref[...] for ref in inputs[4 * index : 4 * index + 4])
        gradient = low_gradient.astype(WIDE)
        made = adam_quick(weight, gradient, first, second, rate, WEIGHT_DECAY)
        for target, value in zip(outputs[3 * index : 3 * index + 3], made):
            target[...] = value
        if index % 2 == 0:
            total = jnp.sum(weight.astype(LOW).astype(WIDE) * gradient, axis=1, keepdims=True)
            sums[index // 2][...] += jnp.broadcast_to(total, sums[index // 2].shape)

    @pl.when(step == ADAM_STEPS - 1)
    def _():
        rows = [jnp.transpose(total[...])[:1] for total in sums]
        weight, first, second = (ref[...] for ref in gains)
        gradient = jnp.concatenate(rows, axis=0) / weight.astype(LOW).astype(WIDE)
        for target, value in zip(gains_new, adam_quick(weight, gradient, first, second, 0.5, 0.0)):
            target[...] = value


def adam_all(groups, gains, handed):
    specs, out_specs, out_shape = [], [], []
    rows = groups[0][0].shape[0]
    for group in groups:
        spec = pl.BlockSpec((rows, group[0].shape[1] // ADAM_STEPS), lambda step: (0, step))
        specs += [spec] * 4
        out_specs += [spec] * 3
        out_shape += [jax.ShapeDtypeStruct(group[0].shape, WIDE)] * 3
    whole = [pl.BlockSpec(gains[0].shape, lambda step: (0, 0))] * 3
    whole += [
        pl.BlockSpec((a.shape[0], a.shape[1] // ADAM_STEPS), lambda step: (0, step)) for a in handed
    ]
    arrays = list(gains) + list(handed)
    return pl.pallas_call(
        adam_kernel,
        grid=(ADAM_STEPS,),
        in_specs=specs + whole,
        out_specs=out_specs + whole,
        out_shape=out_shape + [jax.ShapeDtypeStruct(a.shape, a.dtype) for a in arrays],
        scratch_shapes=[pltpu.VMEM((rows, 128), WIDE)] * 2,
        compiler_params=pltpu.CompilerParams(vmem_limit_bytes=56 * 2**20),
        name="adam",
    )(*[array for group in groups for array in group], *arrays)


def grid_shards(
    tokens,
    cotangent,
    qkv_weight,
    out_weight,
    gate_up_weight,
    down_weight,
    gains,
    qkv_first,
    out_first,
    gate_up_first,
    down_first,
    gains_first,
    qkv_second,
    out_second,
    gate_up_second,
    down_second,
    gains_second,
):
    rows, width = tokens.shape[1:]
    seq_len = 8 * rows
    gain_columns = jnp.pad(gains.astype(LOW).T, ((0, 0), (0, 126)))
    cosines, sines = turn_tables(seq_len)
    (
        grad_out,
        normed_two,
        gate_up_full,
        down_full,
        qkv_full,
        out_full,
        normed_one,
        qkv_heads,
        attended,
        residual,
        gain_full,
        own_tokens,
    ) = forward(
        tokens[0],
        cotangent[0],
        qkv_weight,
        gain_columns,
        gate_up_weight,
        down_weight,
        out_weight,
        cosines,
        sines,
    )
    grad_branch, gate_up_half, down_part, block_own, grad_residual = mlp(
        normed_two, gate_up_full, down_full, grad_out, residual, gain_full
    )
    input_grad, block_out, qkv_sum, gate_up_sum, down_sum, out_sum = backward(
        grad_branch,
        grad_residual,
        gain_full,
        own_tokens,
        qkv_full,
        out_full,
        qkv_heads,
        attended,
        normed_one.reshape(8, rows, width),
        cosines,
        sines,
        gate_up_half,
        down_part,
        block_own,
    )
    made = adam_all(
        [
            (qkv_weight, qkv_first, qkv_second, qkv_sum),
            (out_weight, out_first, out_second, out_sum),
            (gate_up_weight, gate_up_first, gate_up_second, gate_up_sum),
            (down_weight, down_first, down_second, down_sum),
        ],
        (gains, gains_first, gains_second),
        (input_grad, block_out),
    )
    qkv_new, out_new, gate_up_new, down_new, gains_new = (
        made[3 * i : 3 * i + 3] for i in range(5)
    )
    input_grad, block_out = made[15:]
    return (
        block_out[None],
        input_grad[None],
        qkv_new[0],
        out_new[0],
        gate_up_new[0],
        down_new[0],
        gains_new[0],
        qkv_new[1],
        out_new[1],
        gate_up_new[1],
        down_new[1],
        gains_new[1],
        qkv_new[2],
        out_new[2],
        gate_up_new[2],
        down_new[2],
        gains_new[2],
    )


def mapped(body, mesh, token_spec, row_spec, gain_spec):
    one_set = (row_spec, row_spec, row_spec, row_spec, gain_spec)
    return jax.shard_map(
        body,
        mesh=mesh,
        in_specs=(token_spec, token_spec) + one_set * 3,
        out_specs=(token_spec, token_spec) + one_set * 3,
        check_vma=False,
    )


def solution(mesh):
    if mesh.shape["seq"] == 8 and mesh.shape["dp"] == 4:
        grid_mesh = Mesh(mesh.devices.reshape(4, 2, 2, 2), GRID)
        return mapped(
            grid_shards,
            grid_mesh,
            P(("y", "c"), ("z", "x"), None),
            P(GRID, None),
            P(None, GRID),
        )
    return mapped(
        shards, mesh, P("dp", "seq", None), P(("seq", "dp"), None), P(None, ("seq", "dp"))
    )
```

```python
import jax
import jax.numpy as jnp
import numpy as np
from jax import lax
from jax.experimental import pallas as pl
from jax.experimental.pallas import tpu as pltpu
from jax.sharding import Mesh
from jax.sharding import PartitionSpec as P

D = 2048
HEADS = 32
HEAD_DIM = 64
FF = 8192
BLOCK = 512
STEP = 10


NORM_EPS = 1e-05
ROPE_BASE = 130000.0
BETA_ONE = 0.9
BETA_TWO = 0.999
ADAM_EPS = 1e-08
WEIGHT_DECAY = 0.1
MASKED = -1e30


def rms_parts(values):
    inverse = lax.rsqrt(jnp.mean(values * values, axis=-1, keepdims=True) + NORM_EPS)
    return (values * inverse, inverse)


def rope_tables(positions):
    half_dim = HEAD_DIM // 2
    exponent = jnp.arange(half_dim, dtype=jnp.float32) * (2.0 / HEAD_DIM)
    frequency = ROPE_BASE ** (-exponent)
    angles = positions.astype(jnp.float32)[:, None] * frequency[None, :]
    return (jnp.cos(angles)[:, None, :], jnp.sin(angles)[:, None, :])


def rotate(tensor, cosines, sines):
    half_dim = HEAD_DIM // 2
    lower_half = tensor[..., :half_dim]
    upper_half = tensor[..., half_dim:]
    return jnp.concatenate(
        [lower_half * cosines - upper_half * sines, upper_half * cosines + lower_half * sines],
        axis=-1,
    )


def unrotate(tensor, cosines, sines):
    half_dim = HEAD_DIM // 2
    lower_half = tensor[..., :half_dim]
    upper_half = tensor[..., half_dim:]
    return jnp.concatenate(
        [lower_half * cosines + upper_half * sines, upper_half * cosines - lower_half * sines],
        axis=-1,
    )


def block_scores(query_rows, key_heads, key_id, block_id):
    key_rows = lax.dynamic_slice_in_dim(key_heads, key_id * BLOCK, BLOCK, 0)
    products = jnp.einsum(
        "qhd,khd->hqk", query_rows, key_rows, preferred_element_type=jnp.float32
    ) * HEAD_DIM ** (-0.5)
    local_ids = jnp.arange(BLOCK, dtype=jnp.int32)
    allowed = (key_id < block_id) | (local_ids[None, :] <= local_ids[:, None])
    return jnp.where(allowed[None], products, MASKED)


def row_normalizer(query_rows, key_heads, block_id):
    row_shape = (query_rows.shape[1], BLOCK, 1)

    def absorb(key_id, state):
        running_max, running_total = state
        scores = block_scores(query_rows, key_heads, key_id, block_id)
        new_max = jnp.maximum(running_max, jnp.max(scores, axis=-1, keepdims=True))
        running_total = running_total * jnp.exp(running_max - new_max) + jnp.sum(
            jnp.exp(scores - new_max), axis=-1, keepdims=True
        )
        return (new_max, running_total)

    start_state = (jnp.full(row_shape, MASKED, jnp.float32), jnp.zeros(row_shape, jnp.float32))
    final_max, final_total = lax.fori_loop(0, block_id + 1, absorb, start_state)
    return final_max + jnp.log(final_total)


def attend_forward(query_heads, key_heads, value_heads):
    seq_len, heads_here, head_dim = query_heads.shape

    def one_block(block_id, carry):
        out_all, lse_all = carry
        row_start = block_id * BLOCK
        query_rows = lax.dynamic_slice_in_dim(query_heads, row_start, BLOCK, 0)
        row_lse = row_normalizer(query_rows, key_heads, block_id)

        def weigh_values(key_id, running):
            scores = block_scores(query_rows, key_heads, key_id, block_id)
            weights_low = jnp.exp(scores - row_lse).astype(jnp.bfloat16)
            value_rows = lax.dynamic_slice_in_dim(value_heads, key_id * BLOCK, BLOCK, 0)
            return running + jnp.einsum(
                "hqk,khd->qhd", weights_low, value_rows, preferred_element_type=jnp.float32
            )

        attended = lax.fori_loop(
            0, block_id + 1, weigh_values, jnp.zeros((BLOCK, heads_here, head_dim), jnp.float32)
        )
        out_all = lax.dynamic_update_slice_in_dim(
            out_all, attended.astype(jnp.bfloat16), row_start, 0
        )
        lse_all = lax.dynamic_update_slice_in_dim(lse_all, row_lse, row_start, 1)
        return (out_all, lse_all)

    start_carry = (
        jnp.zeros((seq_len, heads_here, head_dim), jnp.bfloat16),
        jnp.zeros((heads_here, seq_len, 1), jnp.float32),
    )
    return lax.fori_loop(0, seq_len // BLOCK, one_block, start_carry)


def attend_backward(query_heads, key_heads, value_heads, grad_heads, lse_all):
    seq_len, heads_here, head_dim = query_heads.shape
    score_scale = HEAD_DIM ** (-0.5)

    def one_block(block_id, carry):
        grad_q_all, grad_k_all, grad_v_all = carry
        row_start = block_id * BLOCK
        query_rows = lax.dynamic_slice_in_dim(query_heads, row_start, BLOCK, 0)
        grad_rows = lax.dynamic_slice_in_dim(grad_heads, row_start, BLOCK, 0)
        row_lse = lax.dynamic_slice_in_dim(lse_all, row_start, BLOCK, 1)

        def probs_and_grads(key_id):
            scores = block_scores(query_rows, key_heads, key_id, block_id)
            probs = jnp.exp(scores - row_lse)
            value_rows = lax.dynamic_slice_in_dim(value_heads, key_id * BLOCK, BLOCK, 0)
            grad_probs = jnp.einsum(
                "qhd,khd->hqk", grad_rows, value_rows, preferred_element_type=jnp.float32
            )
            return (probs, grad_probs)

        def add_delta(key_id, running):
            probs, grad_probs = probs_and_grads(key_id)
            return running + jnp.sum(probs * grad_probs, axis=-1, keepdims=True)

        row_delta = lax.fori_loop(
            0, block_id + 1, add_delta, jnp.zeros((heads_here, BLOCK, 1), jnp.float32)
        )

        def spread(key_id, inner):
            grad_q_rows, grad_k_acc, grad_v_acc = inner
            probs, grad_probs = probs_and_grads(key_id)
            key_start = key_id * BLOCK
            key_rows = lax.dynamic_slice_in_dim(key_heads, key_start, BLOCK, 0)
            grad_scores = (probs * (grad_probs - row_delta) * score_scale).astype(jnp.bfloat16)
            grad_q_rows = grad_q_rows + jnp.einsum(
                "hqk,khd->qhd", grad_scores, key_rows, preferred_element_type=jnp.float32
            )
            grad_k_part = jnp.einsum(
                "hqk,qhd->khd", grad_scores, query_rows, preferred_element_type=jnp.float32
            )
            grad_v_part = jnp.einsum(
                "hqk,qhd->khd",
                probs.astype(jnp.bfloat16),
                grad_rows,
                preferred_element_type=jnp.float32,
            )
            grad_k_acc = lax.dynamic_update_slice_in_dim(
                grad_k_acc,
                lax.dynamic_slice_in_dim(grad_k_acc, key_start, BLOCK, 0) + grad_k_part,
                key_start,
                0,
            )
            grad_v_acc = lax.dynamic_update_slice_in_dim(
                grad_v_acc,
                lax.dynamic_slice_in_dim(grad_v_acc, key_start, BLOCK, 0) + grad_v_part,
                key_start,
                0,
            )
            return (grad_q_rows, grad_k_acc, grad_v_acc)

        start_inner = (
            jnp.zeros((BLOCK, heads_here, head_dim), jnp.float32),
            grad_k_all,
            grad_v_all,
        )
        grad_q_rows, grad_k_all, grad_v_all = lax.fori_loop(0, block_id + 1, spread, start_inner)
        grad_q_all = lax.dynamic_update_slice_in_dim(grad_q_all, grad_q_rows, row_start, 0)
        return (grad_q_all, grad_k_all, grad_v_all)

    zeros_all = jnp.zeros((seq_len, heads_here, head_dim), jnp.float32)
    return lax.fori_loop(0, seq_len // BLOCK, one_block, (zeros_all, zeros_all, zeros_all))


def adam_step(weight, gradient, first, second, rate, decay):
    new_first = BETA_ONE * first + (1.0 - BETA_ONE) * gradient
    new_second = BETA_TWO * second + (1.0 - BETA_TWO) * gradient * gradient
    first_hat = new_first / (1.0 - BETA_ONE**STEP)
    second_hat = new_second / (1.0 - BETA_TWO**STEP)
    new_weight = weight - rate * (first_hat / (jnp.sqrt(second_hat) + ADAM_EPS) + decay * weight)
    return (new_weight, new_first, new_second)


def shards(
    tokens,
    cotangent,
    qkv_weight,
    out_weight,
    gate_up_weight,
    down_weight,
    gains,
    qkv_first,
    out_first,
    gate_up_first,
    down_first,
    gains_first,
    qkv_second,
    out_second,
    gate_up_second,
    down_second,
    gains_second,
):
    seq_count = lax.axis_size("seq")
    tok_rows = tokens.shape[1]
    width = tokens.shape[2]
    seq_len = tok_rows * seq_count
    heads_here = HEADS // seq_count
    width_here = heads_here * HEAD_DIM
    contract_last = (((1,), (1,)), ((), ()))
    contract_first = (((0,), (0,)), ((), ()))
    qkv_full, proj_full, gain_full = (
        lax.all_gather(qkv_weight.astype(jnp.bfloat16), ("seq", "dp"), axis=0, tiled=True),
        lax.all_gather(out_weight.astype(jnp.bfloat16), ("seq", "dp"), axis=0, tiled=True),
        lax.all_gather(gains.astype(jnp.bfloat16), ("seq", "dp"), axis=1, tiled=True),
    )
    up_full, down_full = (
        lax.all_gather(gate_up_weight.astype(jnp.bfloat16), ("seq", "dp"), axis=0, tiled=True),
        lax.all_gather(down_weight.astype(jnp.bfloat16), ("seq", "dp"), axis=0, tiled=True),
    )
    hidden_in = tokens[0].astype(jnp.float32)
    unit_one, inverse_one = rms_parts(hidden_in)
    normed_one = (unit_one * gain_full[0].astype(jnp.float32)).astype(jnp.bfloat16)
    projected = jnp.einsum(
        "te,ecd->ctd",
        normed_one,
        qkv_full.reshape(width, 3, width),
        preferred_element_type=jnp.float32,
    )
    positions = lax.axis_index("seq") * tok_rows + jnp.arange(tok_rows, dtype=jnp.int32)
    cos_local, sin_local = rope_tables(positions)
    turned = rotate(projected[:2].reshape(2, tok_rows, HEADS, HEAD_DIM), cos_local, sin_local)
    packed = jnp.concatenate([turned.reshape(2, tok_rows, width), projected[2:]], axis=0).astype(
        jnp.bfloat16
    )
    by_heads = lax.all_to_all(packed, "seq", split_axis=2, concat_axis=1, tiled=True)
    query_heads = by_heads[0].reshape(seq_len, heads_here, HEAD_DIM)
    key_heads = by_heads[1].reshape(seq_len, heads_here, HEAD_DIM)
    value_heads = by_heads[2].reshape(seq_len, heads_here, HEAD_DIM)
    out_heads, lse_all = attend_forward(query_heads, key_heads, value_heads)
    attended = lax.all_to_all(
        out_heads.reshape(seq_len, width_here), "seq", split_axis=0, concat_axis=1, tiled=True
    )
    residual = hidden_in + jnp.dot(attended, proj_full, preferred_element_type=jnp.float32)
    unit_two, inverse_two = rms_parts(residual)
    normed_two = (unit_two * gain_full[1].astype(jnp.float32)).astype(jnp.bfloat16)
    gate_up = jnp.dot(normed_two, up_full, preferred_element_type=jnp.float32)
    gate_vals = gate_up[:, :FF]
    up_vals = gate_up[:, FF:]
    sigmoid_gate = jax.nn.sigmoid(gate_vals)
    activated = (gate_vals * sigmoid_gate * up_vals).astype(jnp.bfloat16)
    mlp_out = lax.dot_general(
        activated, down_full, contract_last, preferred_element_type=jnp.float32
    )
    block_out = (residual + mlp_out).astype(jnp.bfloat16)[None]
    back_up, back_down, back_gain = (
        lax.all_gather(gate_up_weight.astype(jnp.bfloat16), ("seq", "dp"), axis=0, tiled=True),
        lax.all_gather(down_weight.astype(jnp.bfloat16), ("seq", "dp"), axis=0, tiled=True),
        lax.all_gather(gains.astype(jnp.bfloat16), ("seq", "dp"), axis=1, tiled=True),
    )
    grad_out = cotangent[0]
    grad_act = jnp.dot(grad_out, back_down, preferred_element_type=jnp.float32)
    grad_gate = grad_act * up_vals * sigmoid_gate * (1.0 + gate_vals * (1.0 - sigmoid_gate))
    grad_up = grad_act * gate_vals * sigmoid_gate
    grad_gate_up = jnp.concatenate([grad_gate, grad_up], axis=1).astype(jnp.bfloat16)
    grad_normed_two = lax.dot_general(
        grad_gate_up, back_up, contract_last, preferred_element_type=jnp.float32
    )
    gain_two_grad = jnp.sum(grad_normed_two * unit_two, axis=0)
    grad_unit_two = grad_normed_two * back_gain[1].astype(jnp.float32)
    grad_residual = grad_out.astype(jnp.float32) + inverse_two * (
        grad_unit_two - unit_two * jnp.mean(grad_unit_two * unit_two, axis=-1, keepdims=True)
    )
    gate_up_rows = lax.dot_general(
        normed_two, grad_gate_up, contract_first, preferred_element_type=jnp.float32
    )
    down_rows = lax.dot_general(
        grad_out, activated, contract_first, preferred_element_type=jnp.float32
    )
    mlp_grad = lax.psum_scatter(
        jnp.concatenate([gate_up_rows, down_rows], axis=1),
        ("seq", "dp"),
        scatter_dimension=0,
        tiled=True,
    )
    back_qkv, back_proj = (
        lax.all_gather(qkv_weight.astype(jnp.bfloat16), ("seq", "dp"), axis=0, tiled=True),
        lax.all_gather(out_weight.astype(jnp.bfloat16), ("seq", "dp"), axis=0, tiled=True),
    )
    grad_branch = grad_residual.astype(jnp.bfloat16)
    proj_grad = lax.dot_general(
        attended, grad_branch, contract_first, preferred_element_type=jnp.float32
    )
    grad_attended = lax.dot_general(
        grad_branch, back_proj, contract_last, preferred_element_type=jnp.float32
    ).astype(jnp.bfloat16)
    grad_heads = lax.all_to_all(
        grad_attended, "seq", split_axis=1, concat_axis=0, tiled=True
    ).reshape(seq_len, heads_here, HEAD_DIM)
    grad_q_all, grad_k_all, grad_v_all = attend_backward(
        query_heads, key_heads, value_heads, grad_heads, lse_all
    )
    cos_whole, sin_whole = rope_tables(jnp.arange(seq_len, dtype=jnp.int32))
    grad_pack = jnp.stack(
        [
            unrotate(grad_q_all, cos_whole, sin_whole).reshape(seq_len, width_here),
            unrotate(grad_k_all, cos_whole, sin_whole).reshape(seq_len, width_here),
            grad_v_all.reshape(seq_len, width_here),
        ],
        axis=0,
    ).astype(jnp.bfloat16)
    grad_projected = lax.all_to_all(grad_pack, "seq", split_axis=1, concat_axis=2, tiled=True)
    qkv_cube = back_qkv.reshape(width, 3, width)
    grad_normed_one = jnp.einsum(
        "ctd,ecd->te", grad_projected, qkv_cube, preferred_element_type=jnp.float32
    )
    qkv_grad = jnp.einsum(
        "te,ctd->ecd", normed_one, grad_projected, preferred_element_type=jnp.float32
    ).reshape(width, 3 * width)
    gain_one_grad = jnp.sum(grad_normed_one * unit_one, axis=0)
    grad_unit_one = grad_normed_one * back_gain[0].astype(jnp.float32)
    input_grad = grad_residual + inverse_one * (
        grad_unit_one - unit_one * jnp.mean(grad_unit_one * unit_one, axis=-1, keepdims=True)
    )
    gains_grad = jnp.stack([gain_one_grad, gain_two_grad], axis=0)
    qkv_sum, proj_sum, gains_sum = (
        lax.psum_scatter(qkv_grad, ("seq", "dp"), scatter_dimension=0, tiled=True),
        lax.psum_scatter(proj_grad, ("seq", "dp"), scatter_dimension=0, tiled=True),
        lax.psum_scatter(gains_grad, ("seq", "dp"), scatter_dimension=1, tiled=True),
    )
    wide_rate = 2.5 * D ** (-0.5)
    out_rate = 2.5 * max(D // 512, 1) ** (-0.5)
    down_rate = 2.5 * FF ** (-0.5)
    qkv_new = adam_step(qkv_weight, qkv_sum, qkv_first, qkv_second, wide_rate, WEIGHT_DECAY)
    out_new = adam_step(out_weight, proj_sum, out_first, out_second, out_rate, WEIGHT_DECAY)
    gate_up_new = adam_step(
        gate_up_weight,
        mlp_grad[:, : 2 * FF],
        gate_up_first,
        gate_up_second,
        wide_rate,
        WEIGHT_DECAY,
    )
    down_new = adam_step(
        down_weight, mlp_grad[:, 2 * FF :], down_first, down_second, down_rate, WEIGHT_DECAY
    )
    gains_new = adam_step(gains, gains_sum, gains_first, gains_second, 0.5, 0.0)
    return (
        block_out,
        input_grad[None],
        qkv_new[0],
        out_new[0],
        gate_up_new[0],
        down_new[0],
        gains_new[0],
        qkv_new[1],
        out_new[1],
        gate_up_new[1],
        down_new[1],
        gains_new[1],
        qkv_new[2],
        out_new[2],
        gate_up_new[2],
        down_new[2],
        gains_new[2],
    )


GRID = ("z", "x", "y", "c")
RING = ("z", "c")
PLANE = ("x", "y")
LOW = jnp.bfloat16
WIDE = jnp.float32
CONTRACT_LAST = (((1,), (1,)), ((), ()))
CONTRACT_FIRST = (((0,), (0,)), ((), ()))
DMA = pltpu.SemaphoreType.DMA
ANYWHERE = pl.BlockSpec(memory_space=pl.ANY)
IN_VMEM = pl.BlockSpec(memory_space=pltpu.VMEM)


def remote(source, target, send, receive, **place):
    return pltpu.make_async_remote_copy(
        src_ref=source,
        dst_ref=target,
        send_sem=send,
        recv_sem=receive,
        device_id=place,
        device_id_type=pl.DeviceIdType.MESH,
    )


def lanes(start, size):
    return pl.ds(pl.multiple_of(start, 128), size)


class Place:
    def __init__(self):
        self.z, self.x, self.y, self.c = (lax.axis_index(name) for name in GRID)
        self.slot = 2 * self.z + self.c
        self.block_here = self.block(self.slot, self.x, self.y)

    def block(self, slot, x, y):
        return (((slot // 2) * 2 + x) * 2 + y) * 2 + lax.rem(slot, 2)

    def meet(self, plane):
        barrier = pltpu.get_barrier_semaphore()
        others = [
            {"z": slot // 2, "c": lax.rem(slot, 2)}
            for slot in (lax.rem(self.slot + step, 8) for step in range(1, 8))
        ]
        if plane:
            others += [{"x": 1 - self.x}, {"y": 1 - self.y}, {"x": 1 - self.x, "c": 1 - self.c}]
        for other in others:
            pl.semaphore_signal(
                barrier, inc=1, device_id=other, device_id_type=pl.DeviceIdType.MESH
            )
        pl.semaphore_wait(barrier, len(others))


class Swap:
    def __init__(self, place, source, spot_there, spot_here, sems):
        p = self.place = place
        self.away = lambda: remote(
            source, spot_there, sems.at[0], sems.at[1], x=1 - p.x, c=1 - p.c
        )
        self.here = lambda: pltpu.make_async_copy(source, spot_here, sems.at[2])

    def start(self):
        p = self.place
        pl.when(p.x != p.c)(lambda: self.away().start())
        pl.when(p.x == p.c)(lambda: self.here().start())

    def wait(self):
        p = self.place
        pl.when(p.x != p.c)(lambda: self.away().wait_recv())
        pl.when(p.x == p.c)(lambda: self.here().wait())

    def drain(self):
        p = self.place
        pl.when(p.x != p.c)(lambda: self.away().wait_send())


class LineGather:
    SEMS = (4, 8)

    def __init__(self, place, buffer, sems, mine=None, rows=None):
        self.place, self.sems, self.mine = place, sems, mine
        self.spot = (lambda slot: buffer.at[slot]) if rows is None else (lambda slot: buffer.at[slot, rows])

    def copy(self, slot, way, own=False):
        p, block = self.place, self.spot(slot)
        if way == 0:
            where = {"z": jnp.minimum(p.z + 1, 3)}
        elif way == 1:
            where = {"z": jnp.maximum(p.z - 1, 0)}
        else:
            where = {"c": 1 - p.c}
        source = self.mine if own and self.mine is not None else block
        return remote(source, block, self.sems.at[way, slot], self.sems.at[3, slot], **where)

    def _pass_on(self, slot, way, own=False):
        p = self.place
        if way == 0:
            pl.when(p.z < 3)(lambda: self.copy(slot, 0, own).start())
        elif way == 1:
            pl.when(p.z > 0)(lambda: self.copy(slot, 1, own).start())

    def start(self):
        slot = self.place.slot
        self._pass_on(slot, 0, True)
        self._pass_on(slot, 1, True)
        self.copy(slot, 2, True).start()
        if self.mine is not None:
            self.keep().start()

    def start_part(self, inside):
        p = self.place
        in_line = (p.z == 1) | (p.z == 2)
        pl.when(in_line if inside else jnp.logical_not(in_line))(self.start)

    def keep(self):
        slot = self.place.slot
        return pltpu.make_async_copy(self.mine, self.spot(slot), self.sems.at[3, slot])

    def inner(self, distance):
        p = self.place
        side = 1 - 2 * (p.z // 2)
        source = p.z + distance * side

        @pl.when((source >= 0) & (source <= 3))
        def _():
            slot = 2 * source + p.c
            self.copy(slot, 2).wait_recv()
            pl.when(p.z == 1)(lambda: self.copy(slot, 1).start())
            pl.when(p.z == 2)(lambda: self.copy(slot, 0).start())
            self.copy(slot, 2).start()

    def outer(self):
        p = self.place
        for here, way in ((1, 0), (2, 1)):

            @pl.when(p.z == here)
            def _():
                slot = p.slot - 2 + 4 * way
                self.copy(slot, 2).wait_recv()
                self.copy(slot, way).start()
                self.copy(slot, 2).start()

    def steps(self):
        self.inner(1)
        self.outer()
        self.inner(2)
        self.inner(3)

    def finish(self):
        p = self.place
        if self.mine is not None:
            self.keep().wait()
        for z in range(4):
            self.copy(2 * z + 1 - p.c, 2).wait_recv()

    def drain(self):
        p = self.place
        for z in range(4):
            slot = 2 * z + p.c
            self.copy(slot, 2).wait_send()
            pl.when((z <= p.z) & (p.z < 3))(lambda: self.copy(slot, 0).wait_send())
            pl.when((z >= p.z) & (p.z > 0))(lambda: self.copy(slot, 1).wait_send())


def add_blocks(target, sources):
    def some(step, carry):
        rows = pl.ds(pl.multiple_of(step * 16, 16), 16)
        total = sources[0][rows, :].astype(WIDE)
        for source in sources[1:]:
            total = total + source[rows, :].astype(WIDE)
        target[rows, :] = total.astype(target.dtype)
        return carry

    lax.fori_loop(0, target.shape[0] // 16, some, 0)


class LineScatter:
    SEMS = (6, 4)

    @staticmethod
    def buffers(rows, width):
        return [pltpu.VMEM((4, rows, width), LOW), pltpu.VMEM((5, rows, width), LOW)]

    def __init__(self, place, partial, across, passing, sems, rows):
        self.place, self.partial, self.sems, self.rows = place, partial, sems, rows
        self.across, self.passing = across, passing

    def cross(self, z):
        p = self.place
        return remote(
            self.partial.at[2 * z + 1 - p.c, self.rows],
            self.across.at[z, self.rows],
            self.sems.at[0, z],
            self.sems.at[1, z],
            c=1 - p.c,
        )

    def hop(self, z, way, landing):
        p = self.place
        there = jnp.minimum(p.z + 1, 3) if way == 0 else jnp.maximum(p.z - 1, 0)
        return remote(
            self.across.at[z, self.rows],
            self.passing.at[landing, self.rows],
            self.sems.at[2 + 2 * way, z],
            self.sems.at[3 + 2 * way, z],
            z=there,
        )

    def send(self, z, way):
        p = self.place
        if way == 0:
            self.hop(z, 0, z).start()
        else:
            pl.when(p.z - 1 == z)(lambda: self.hop(z, 1, 4).start())
            pl.when(p.z - 1 != z)(lambda: self.hop(z, 1, z).start())

    def start(self):
        for z in range(4):
            self.cross(z).start()

    def head(self):
        p = self.place
        for z in range(4):
            self.cross(z).wait_recv()
        for way, end in ((0, 0), (1, 3)):

            @pl.when(p.z == end)
            def _():
                for index in range(3):
                    z = 3 - index if way == 0 else index
                    spot = self.across.at[z, self.rows]
                    add_blocks(spot, [self.partial.at[2 * z + p.c, self.rows], spot])
                    self.send(z, way)

    def step(self, index):
        p = self.place
        for here, way, z in ((1, index // 2, (3, 2, 0)[index]), (2, 1 - index // 2, (0, 1, 3)[index])):

            @pl.when(p.z == here)
            def _():
                self.hop(z, way, z).wait_recv()
                spot = self.across.at[z, self.rows]
                add_blocks(
                    spot,
                    [
                        self.partial.at[2 * z + p.c, self.rows],
                        spot,
                        self.passing.at[z, self.rows],
                    ],
                )
                self.send(z, way)

    def steps(self):
        for index in range(3):
            self.step(index)

    def arrive(self):
        p = self.place
        pl.when(p.z > 0)(lambda: self.hop(p.z, 0, p.z).wait_recv())
        pl.when(p.z < 3)(lambda: self.hop(p.z, 1, 4).wait_recv())
        for end, landing in ((0, 0), (3, 4)):

            @pl.when(p.z == end)
            def _():
                spot = self.passing.at[landing, self.rows]
                spot[...] = jnp.zeros(spot.shape, LOW)

    def total(self, rows):
        p = self.place
        parts = (
            self.partial[p.slot, rows, :],
            self.across[p.z, rows, :],
            self.passing[p.z, rows, :],
            self.passing[4, rows, :],
        )
        return sum(part.astype(WIDE) for part in parts)

    def drain(self):
        p = self.place
        for z in range(4):
            self.cross(z).wait_send()
            pl.when(p.z < z)(lambda: self.hop(z, 0, z).wait_send())
            pl.when(p.z > z)(lambda: self.hop(z, 1, z).wait_send())


class Relayout:
    SEMS = (8, 8)

    def __init__(self, place, parts, target, sems):
        self.place, self.parts, self.target, self.sems = place, parts, target, sems

    def sem(self, kind, slot):
        return self.sems.at[kind, slot]

    def line(self, step):
        p = self.place
        slot = lax.rem(p.slot + step, 8)
        copies = []
        for source, first, size, there in self.parts:
            same_for_all = source.shape[1] == size
            columns = lanes(first if same_for_all else first + size * slot, size)
            piece = source.at[:, columns]
            spot = self.target.at[p.block_here, :, pl.ds(there, size)]
            if step == 0:
                copies.append(pltpu.make_async_copy(piece, spot, self.sem(1, p.slot)))
            else:
                copies.append(
                    remote(
                        piece,
                        spot,
                        self.sem(0, slot),
                        self.sem(1, p.slot),
                        z=slot // 2,
                        c=lax.rem(slot, 2),
                    )
                )
        return copies

    def whole(self, slot):
        p = self.place
        spot = self.target.at[p.block(slot, p.x, p.y)]
        return remote(spot, spot, self.sem(0, slot), self.sem(1, slot), c=1 - p.c)

    def plane(self, slot, x, y, way, send, receive):
        p = self.place
        spot = self.target.at[p.block(slot, x, y)]
        where = {"x": 1 - p.x} if way == 0 else {"y": 1 - p.y}
        return remote(spot, spot, self.sem(send, slot), self.sem(receive, slot), **where)

    def from_own(self, slot, way):
        p = self.place
        return self.plane(slot, p.x, p.y, way, 2 + 2 * way, 3 + 2 * way)

    def corner(self, slot, way):
        p = self.place
        x, y = (p.x, 1 - p.y) if way == 0 else (1 - p.x, p.y)
        return self.plane(slot, x, y, way, 6, 7)

    def start(self, steps=range(8)):
        for step in steps:
            for copy in self.line(step):
                copy.start()

    def spread(self, step):
        p = self.place
        slot = lax.rem(p.slot + 8 - step, 8)
        if isinstance(step, int) and step == 0:
            spot = self.target.at[p.block_here]
            pltpu.make_async_copy(spot, spot, self.sem(1, p.slot)).wait()
        else:
            self.whole(slot).wait_recv()
        for way in range(2):
            self.from_own(slot, way).start()

    def spread_from(self, slot):
        p = self.place

        @pl.when(p.slot == slot)
        def _():
            spot = self.target.at[p.block_here]
            pltpu.make_async_copy(spot, spot, self.sem(1, p.slot)).wait()

        pl.when(p.slot != slot)(lambda: self.whole(slot).wait_recv())
        for way in range(2):
            self.from_own(slot, way).start()

    def corners(self, z):
        self.from_own(2 * z, 0).wait_recv()
        self.corner(2 * z, 1).start()
        self.from_own(2 * z + 1, 1).wait_recv()
        self.corner(2 * z + 1, 0).start()

    def finish(self):
        for z in range(4):
            self.from_own(2 * z, 1).wait_recv()
            self.from_own(2 * z + 1, 0).wait_recv()
            self.corner(2 * z, 1).wait_recv()
            self.corner(2 * z + 1, 0).wait_recv()

    def drain(self):
        for step in range(1, 8):
            self.whole(lax.rem(self.place.slot + step, 8)).wait_send()
        for z in range(4):
            self.corner(2 * z, 1).wait_send()
            self.corner(2 * z + 1, 0).wait_send()
        for slot in range(8):
            for way in range(2):
                self.from_own(slot, way).wait_send()


class PlaneScatter:
    @staticmethod
    def scratch(units, rows, width):
        shape = (rows, width)
        return [
            pltpu.VMEM((2, 2, units) + shape, LOW),
            pltpu.VMEM((2, units) + shape, LOW),
            DMA((4, 2, 2, units)),
        ]

    def __init__(self, place, part, units, got, last, sems):
        self.place, self.part, self.units = place, part, units
        self.got, self.last, self.sems = got, last, sems

    def pair(self, near):
        p = self.place
        x, y = (p.x, p.y) if near else (1 - p.x, 1 - p.y)
        return ((p.x, y), (x, p.y))

    def own(self, half, near, unit):
        x, y = self.pair(near)[half]
        return self.part(half, unit, x, y)

    def sums(self, half, unit):
        return self.own(half, 1, unit)

    def first(self, half, near, unit):
        p = self.place
        x, y = self.pair(near)[half]
        x, y = (1 - x, y) if half == 0 else (x, 1 - y)
        where = {"x": 1 - p.x} if half == 0 else {"y": 1 - p.y}
        return remote(
            self.part(half, unit, x, y),
            self.got.at[half, near, unit],
            self.sems.at[0, half, near, unit],
            self.sems.at[1, half, near, unit],
            **where,
        )

    def second(self, half, unit):
        p = self.place
        where = {"y": 1 - p.y} if half == 0 else {"x": 1 - p.x}
        return remote(
            self.own(half, 0, unit),
            self.last.at[half, unit],
            self.sems.at[2, half, 0, unit],
            self.sems.at[3, half, 0, unit],
            **where,
        )

    def each(self, call):
        lax.fori_loop(0, self.units, lambda unit, carry: (call(unit), carry)[1], 0)

    def start_unit(self, unit):
        for near in range(2):
            for half in range(2):
                self.first(half, near, unit).start()

    def start(self):
        for near in range(2):

            def begin(unit):
                for half in range(2):
                    self.first(half, near, unit).start()

            self.each(begin)

    def middle(self, unit):
        for half in range(2):
            self.first(half, 0, unit).wait_recv()
            spot = self.own(half, 0, unit)
            add_blocks(spot, [spot, self.got.at[half, 0, unit]])
            self.second(half, unit).start()

    def final(self, unit):
        for half in range(2):
            self.first(half, 1, unit).wait_recv()
            self.second(half, unit).wait_recv()
            spot = self.own(half, 1, unit)
            add_blocks(spot, [spot, self.got.at[half, 1, unit], self.last.at[half, unit]])

    def drain(self):
        def end(unit):
            for half in range(2):
                for near in range(2):
                    self.first(half, near, unit).wait_send()
                self.second(half, unit).wait_send()

        self.each(end)


class LineReturn:
    SEMS = (2, 8)

    def __init__(self, place, sums, parts, target, sems):
        self.place, self.sums, self.parts = place, sums, parts
        self.target, self.sems = target, sems

    def copies(self, z, c, local):
        p = self.place
        made = []
        for here, size, first in self.parts:
            piece = self.sums(c, z).at[:, pl.ds(here, size)]
            spot = self.target.at[:, lanes(first + size * p.slot, size)]
            if local:
                made.append(pltpu.make_async_copy(piece, spot, self.sems.at[1, p.slot]))
            else:
                made.append(
                    remote(
                        piece, spot, self.sems.at[0, 2 * z + c], self.sems.at[1, p.slot], z=z, c=c
                    )
                )
        return made

    def send(self, z):
        p = self.place
        for c in range(2):
            mine = (z == p.z) & (c == p.c)

            @pl.when(mine)
            def _():
                for copy in self.copies(z, c, True):
                    copy.start()

            @pl.when(jnp.logical_not(mine))
            def _():
                for copy in self.copies(z, c, False):
                    copy.start()

    def finish(self):
        p = self.place
        spot = self.sums(0, 0)
        pltpu.make_async_copy(spot, spot, self.sems.at[1, p.slot]).wait()
        for step in range(1, 8):
            slot = lax.rem(p.slot + step, 8)
            whole = remote(
                spot, spot, self.sems.at[0, slot], self.sems.at[1, slot], c=1 - p.c
            )
            whole.wait_recv()
            whole.wait_send()


def kernel_call(kernel, name, number, inputs, in_specs, outputs, out_specs, scratch):
    return pl.pallas_call(
        kernel,
        out_shape=[jax.ShapeDtypeStruct(shape, dtype) for shape, dtype in outputs],
        in_specs=in_specs,
        out_specs=out_specs,
        scratch_shapes=scratch,
        compiler_params=pltpu.CompilerParams(
            collective_id=number, has_side_effects=True, vmem_limit_bytes=60 * 2**20
        ),
        name=name,
    )(*inputs)


CHUNK = 16


def by_rows(count, call):
    def some(step, carry):
        call(pl.ds(pl.multiple_of(step * CHUNK, CHUNK), CHUNK))
        return carry

    lax.fori_loop(0, count // CHUNK, some, 0)


def normed_back(grad_normed, unit, inverse, gain):
    grad_unit = grad_normed * gain
    return inverse * (grad_unit - unit * jnp.mean(grad_unit * unit, axis=-1, keepdims=True))


def turn_tables(length):
    half_dim = HEAD_DIM // 2
    exponent = np.arange(half_dim, dtype=np.float32) * np.float32(2.0 / HEAD_DIM)
    frequency = np.float32(ROPE_BASE) ** (-exponent)
    angles = np.arange(length, dtype=np.float32)[:, None] * frequency[None, :]
    angles = angles.astype(np.float64)
    cosines, sines = np.cos(angles).astype(np.float32), np.sin(angles).astype(np.float32)
    return (
        jnp.asarray(np.tile(cosines, (1, 4))),
        jnp.asarray(np.tile(np.concatenate([-sines, sines], axis=1), (1, 2))),
    )


def turn(values, cosines, sines):
    lane = lax.broadcasted_iota(jnp.int32, values.shape, 1)
    half_dim = HEAD_DIM // 2
    width = values.shape[1]
    partner = jnp.where(
        lax.rem(lane, HEAD_DIM) < half_dim,
        pltpu.roll(values, width - half_dim, 1),
        pltpu.roll(values, half_dim, 1),
    )
    return values * cosines + partner * sines


def head_mask(head):
    lane = lax.broadcasted_iota(jnp.int32, (1, 128), 1)
    return (lane // HEAD_DIM == lax.rem(head, 2)).astype(WIDE).astype(LOW)


def scaled_probs(queries, keys, first_row):
    scores = lax.dot_general(queries, keys, CONTRACT_LAST, preferred_element_type=WIDE)
    scores = scores * HEAD_DIM ** (-0.5)
    row = lax.broadcasted_iota(jnp.int32, scores.shape, 0) + first_row
    column = lax.broadcasted_iota(jnp.int32, scores.shape, 1)
    scores = jnp.where(column <= row, scores, MASKED)
    expo = jnp.exp(scores - jnp.max(scores, axis=1, keepdims=True))
    return expo * (1.0 / jnp.sum(expo, axis=1, keepdims=True))


QUERY_ROWS = 256


def attend_head(head, qkv, total):
    pair = lanes(head // 2 * 128, 128)
    mask = head_mask(head)
    for block in range(qkv.shape[1] // QUERY_ROWS):
        rows = pl.ds(block * QUERY_ROWS, QUERY_ROWS)
        keys = pl.ds(0, (block + 1) * QUERY_ROWS)
        probs = scaled_probs(qkv[0, rows, pair] * mask, qkv[1, keys, pair], block * QUERY_ROWS)
        total[rows, pair] += jnp.dot(
            probs.astype(LOW), qkv[2, keys, pair] * mask, preferred_element_type=WIDE
        )


def forward_kernel(
    tok,
    cot,
    wide_q,
    gain,
    wide_g,
    wide_d,
    wide_o,
    cosines,
    sines,
    all_cot,
    normed_two,
    full_g,
    full_d,
    out_q,
    out_o,
    out_normed,
    out_qkv,
    out_attended,
    out_residual,
    out_gains,
    out_tok,
    all_tok,
    full_q,
    full_o,
    normed_one,
    qkv,
    heads,
    attended,
    residual,
    gain_rows,
    mine,
    partial,
    from_q,
    from_g,
    from_d,
    from_o,
    wq,
    wg,
    wd,
    wo,
    *scratch,
):
    buffers, sems = scratch[:2], scratch[2:]
    tok_swap, cot_swap, out_swap, tok_sems, cot_sems, q_sems, g_sems, d_sems = sems[:8]
    o_sems, sum_a, sum_b, gather_a, gather_b, keep_sems, cast_sems = sems[8:]
    casts = [
        (wide_q, from_q, wq),
        (wide_o, from_o, wo),
        (wide_g, from_g, wg),
        (wide_d, from_d, wd),
    ]
    loads = [
        pltpu.make_async_copy(source, target, cast_sems.at[index])
        for index, (source, target, _) in enumerate(casts)
    ]
    for copy in loads:
        copy.start()

    def cast(index):
        _, source, target = casts[index]
        loads[index].wait()
        parts = source.shape[1] // 2048

        def some(step, carry):
            rows = pl.ds(pl.multiple_of(step // parts * CHUNK, CHUNK), CHUNK)
            columns = lanes(lax.rem(step, parts) * 2048, 2048)
            target[rows, columns] = source[rows, columns].astype(LOW)
            return carry

        lax.fori_loop(0, source.shape[0] // CHUNK * parts, some, 0)

    p = Place()
    p.meet(True)
    rows_own = tok.shape[0]
    seq_len = 8 * rows_own
    step_q, step_g, step_d = wq.shape[1] // 24, wg.shape[1] // 16, wd.shape[1] // 8
    q_parts = [(wq, i * 8 * step_q, step_q, i * step_q) for i in range(3)]
    q_parts.append((gain, 0, gain.shape[1], 3 * step_q))
    move_q = Relayout(p, q_parts, full_q, q_sems)
    move_g = Relayout(
        p, [(wg, i * 8 * step_g, step_g, i * step_g) for i in range(2)], full_g, g_sems
    )
    move_d = Relayout(p, [(wd, 0, step_d, 0)], full_d, d_sems)
    tokens, cotangents = LineGather(p, all_tok, tok_sems), LineGather(p, all_cot, cot_sems)
    away = 2 * p.z + 1 - p.c
    swap_tok = Swap(p, tok, all_tok.at[away], all_tok.at[p.slot], tok_swap)
    swap_cot = Swap(p, cot, all_cot.at[away], all_cot.at[p.slot], cot_swap)
    swap_out = Swap(p, wo, full_o.at[2 * p.y + 1 - p.x], full_o.at[2 * p.y + p.x], out_swap)
    half = wo.shape[0] // 2

    def out_copy(kind):
        own, beside, above = 2 * p.y + p.x, 2 * p.y + 1 - p.x, 2 * (1 - p.y) + p.x
        send, got = o_sems.at[0, kind], o_sems.at[1, kind]
        if kind < 2:
            where = {"x": 1 - p.x} if kind == 0 else {"y": 1 - p.y}
            return remote(full_o.at[own], full_o.at[own], send, got, **where)
        spot = full_o.at[beside if kind == 2 else above, pl.ds((kind - 2) * half, half)]
        where = {"y": 1 - p.y} if kind == 2 else {"x": 1 - p.x}
        return remote(spot, spot, send, got, **where)

    kept = []

    def keep(source, target):
        copy = pltpu.make_async_copy(source, target, keep_sems.at[len(kept)])
        copy.start()
        kept.append(copy)

    swap_tok.start()
    cast(0)
    move_q.start()
    cast(1)
    swap_tok.wait()
    tokens.start()
    swap_out.start()
    swap_cot.start()
    cast(2)
    cast(3)
    for step in range(8):
        move_q.spread(step)
    tokens.inner(1)
    tokens.outer()
    move_g.start(range(3))
    tokens.inner(2)
    swap_out.wait()
    out_copy(0).start()
    out_copy(1).start()
    for z in range(4):
        move_q.corners(z)
    out_copy(0).wait_recv()
    out_copy(2).start()
    out_copy(1).wait_recv()
    out_copy(3).start()
    tokens.inner(3)
    tokens.drain()
    move_g.start(range(3, 8))
    swap_cot.wait()
    cotangents.start_part(True)
    move_q.finish()
    for step in range(3):
        move_g.spread(step)
    columns = full_q.shape[2]
    gain_block = full_q[:, :, pl.ds(3 * step_q, columns - 3 * step_q)].reshape(-1, 128)
    pick = lax.broadcasted_iota(jnp.int32, (8, 128), 0) == lax.broadcasted_iota(
        jnp.int32, (8, 128), 1
    )
    gain_rows[...] = lax.dot_general(
        pick.astype(WIDE).astype(LOW), gain_block, CONTRACT_LAST, preferred_element_type=WIDE
    )
    keep(full_q, out_q)
    keep(gain_rows, out_gains)
    tokens.finish()
    keep(all_tok.at[p.slot], out_tok)

    def norm_slot(slot, carry):
        def some(rows):
            unit, _ = rms_parts(all_tok[slot, rows, :].astype(WIDE))
            there = pl.ds(pl.multiple_of(slot * rows_own + rows.start, CHUNK), CHUNK)
            normed_one[there, :] = (unit * gain_rows[pl.ds(0, 1), :]).astype(LOW)

        by_rows(rows_own, some)
        return carry

    lax.fori_loop(0, 8, norm_slot, 0)
    keep(normed_one, out_normed)

    def project(part, carry):
        rows = pl.ds(pl.multiple_of(part * 512, 512), 512)
        for kind in range(3):
            weight = full_q[:, :, pl.ds(kind * step_q, step_q)].reshape(-1, step_q)
            made = jnp.dot(normed_one[rows, :], weight, preferred_element_type=WIDE)
            if kind < 2:
                made = turn(
                    made,
                    jnp.concatenate([cosines[rows, :]] * 2, axis=1),
                    jnp.concatenate([sines[rows, :]] * 2, axis=1),
                )
            qkv[kind, rows, :] = made.astype(LOW)
        return carry

    lax.fori_loop(0, seq_len // 512, project, 0)
    keep(qkv, out_qkv)
    heads[...] = jnp.zeros_like(heads)

    def one_head(head, carry):
        attend_head(head, qkv, heads)
        return carry

    lax.fori_loop(0, 4, one_head, 0)
    move_g.spread(3)
    attended[...] = heads[...].astype(LOW)
    keep(attended, out_attended)
    out_copy(2).wait_recv()
    out_copy(3).wait_recv()
    keep(full_o, out_o)
    out_weight = lambda: full_o[...].reshape(-1, full_o.shape[2])

    def project_out(part, carry):
        rows = pl.ds(pl.multiple_of(part * 256, 256), 256)
        made = jnp.dot(attended[rows, :], out_weight(), preferred_element_type=WIDE)
        partial[pl.ds(2 * part, 2)] = made.astype(LOW).reshape(2, rows_own, -1)
        return carry

    lax.fori_loop(0, seq_len // 256, project_out, 0)

    part_rows = [pl.ds(0, rows_own // 2), pl.ds(rows_own // 2, rows_own // 2)]
    sums = [
        LineScatter(p, partial, *buffers, sem, rows) for sem, rows in zip((sum_a, sum_b), part_rows)
    ]
    gathers = [
        LineGather(p, normed_two, sem, mine.at[rows], rows)
        for sem, rows in zip((gather_a, gather_b), part_rows)
    ]

    def local(part):
        def some(rows):
            there = pl.ds(pl.multiple_of(part * (rows_own // 2) + rows.start, CHUNK), CHUNK)
            total = all_tok[p.slot, there, :].astype(WIDE) + sums[part].total(there)
            residual[there, :] = total
            unit, _ = rms_parts(total)
            mine[there, :] = (unit * gain_rows[pl.ds(1, 1), :]).astype(LOW)

        by_rows(rows_own // 2, some)

    for part in sums:
        part.start()
    for part in sums:
        part.head()
    move_g.spread(4)
    move_g.spread(5)
    in_line = (p.z == 1) | (p.z == 2)
    pl.when(in_line)(lambda: cotangents.inner(1))
    sums[0].steps()
    move_g.spread(6)
    move_g.spread(7)
    pl.when(jnp.logical_not(in_line))(lambda: cotangents.inner(1))
    pl.when(in_line)(move_d.start)
    sums[0].arrive()
    local(0)
    gathers[0].start()
    move_g.corners(0)
    move_g.corners(1)
    sums[1].steps()
    move_g.corners(2)
    move_g.corners(3)
    gathers[0].inner(1)
    sums[1].arrive()
    local(1)
    gathers[1].start()
    keep(residual, out_residual)
    cotangents.start_part(False)
    pl.when(jnp.logical_not(in_line))(move_d.start)
    for slot in range(2, 6):
        move_d.spread_from(slot)
    gathers[0].outer()
    gathers[1].inner(1)
    gathers[0].inner(2)
    gathers[1].outer()
    gathers[1].inner(2)
    cotangents.outer()
    for slot in (0, 1, 6, 7):
        move_d.spread_from(slot)
    cotangents.inner(2)
    for z in range(4):
        move_d.corners(z)
    gathers[0].inner(3)
    gathers[1].inner(3)
    cotangents.inner(3)
    for kind in range(4):
        out_copy(kind).wait_send()
    for part in (swap_tok, swap_cot, swap_out):
        part.drain()
    for part in gathers + [cotangents, move_g, move_d]:
        part.finish()
    for part in gathers + sums + [cotangents, move_q, move_g, move_d]:
        part.drain()
    for copy in kept:
        copy.wait()


def forward(tokens, cotangent, qkv, gain_columns, gate_up, down, out_rows, cosines, sines):
    rows, width = tokens.shape
    own = qkv.shape[0]
    here = qkv.shape[1] // 24
    q_shape = (32, own, 3 * here + gain_columns.shape[1])
    vmem = lambda shape, dtype=LOW: pltpu.VMEM(shape, dtype)
    outputs = [
        ((8, rows, width), LOW),
        ((8, rows, width), LOW),
        ((32, own, gate_up.shape[1] // 8), LOW),
        ((32, own, down.shape[1] // 8), LOW),
        (q_shape, LOW),
        ((4, own, width), LOW),
        ((8 * rows, width), LOW),
        ((3, 8 * rows, here), LOW),
        ((8 * rows, here), LOW),
        ((rows, width), WIDE),
        ((8, width), WIDE),
        ((rows, width), LOW),
    ]
    return kernel_call(
        forward_kernel,
        "forward",
        1,
        (tokens, cotangent, qkv, gain_columns, gate_up, down, out_rows, cosines, sines),
        [ANYWHERE] * 7 + [IN_VMEM] * 2,
        outputs,
        [ANYWHERE] * len(outputs),
        [
            vmem((8, rows, width)),
            vmem(q_shape),
            vmem((4, own, width)),
            vmem((8 * rows, width)),
            vmem((3, 8 * rows, here)),
            vmem((8 * rows, here), WIDE),
            vmem((8 * rows, here)),
            vmem((rows, width), WIDE),
            vmem((8, width), WIDE),
            vmem((rows, width)),
            vmem((8, rows, width)),
        ]
        + [vmem(array.shape, WIDE) for array in (qkv, gate_up, down, out_rows)]
        + [vmem(array.shape) for array in (qkv, gate_up, down, out_rows)]
        + LineScatter.buffers(rows, width)
        + [DMA((3,))] * 3
        + [DMA(LineGather.SEMS)] * 2
        + [DMA(Relayout.SEMS)] * 3
        + [DMA((2, 4))]
        + [DMA(LineScatter.SEMS)] * 2
        + [DMA(LineGather.SEMS)] * 2
        + [DMA((8,)), DMA((4,))],
    )


def weight_part(place, ref):
    return lambda half, unit, x, y: ref.at[place.block(2 * unit + half, x, y)]


def attend_back(head, qkv, grad_heads, grads):
    pair = lanes(head // 2 * 128, 128)
    mask = head_mask(head)
    for block in range(qkv.shape[1] // QUERY_ROWS):
        rows = pl.ds(block * QUERY_ROWS, QUERY_ROWS)
        keys = pl.ds(0, (block + 1) * QUERY_ROWS)
        queries, grad_rows = qkv[0, rows, pair] * mask, grad_heads[rows, pair] * mask
        key_rows = qkv[1, keys, pair]
        probs = scaled_probs(queries, key_rows, block * QUERY_ROWS)
        grad_probs = lax.dot_general(
            grad_rows, qkv[2, keys, pair], CONTRACT_LAST, preferred_element_type=WIDE
        )
        delta = jnp.sum(probs * grad_probs, axis=1, keepdims=True)
        grad_scores = (probs * (grad_probs - delta) * HEAD_DIM ** (-0.5)).astype(LOW)
        grads[0, rows, pair] += jnp.dot(grad_scores, key_rows * mask, preferred_element_type=WIDE)
        grads[1, keys, pair] += lax.dot_general(
            grad_scores, queries, CONTRACT_FIRST, preferred_element_type=WIDE
        )
        grads[2, keys, pair] += lax.dot_general(
            probs.astype(LOW), grad_rows, CONTRACT_FIRST, preferred_element_type=WIDE
        )


def mlp_kernel(
    normed,
    wg,
    wd,
    cot,
    residual,
    gain_rows,
    branch,
    g_sum,
    d_part,
    block_out,
    out_grad,
    nt,
    full_g,
    full_d,
    ct,
    active,
    grad_wide,
    part_two,
    part_out,
    grad_residual,
    mine,
    *scratch,
):
    p = Place()
    rows_own, width = residual.shape
    seq_len = 8 * rows_own
    own, ff = wd.shape[1], wd.shape[2]
    units = wd.shape[0] // 8
    block_rows = seq_len // 2
    part = ff // 4
    wide = width // 4
    blocks = wide // own
    load_sems, sum_a, sum_b, sum_c, gather_a, gather_b, swap_sems, keep_sems = scratch[7:]
    part_rows = [pl.ds(0, rows_own // 2), pl.ds(rows_own // 2, rows_own // 2)]
    sum_two = [
        LineScatter(p, part_two, *scratch[:2], sem, rows)
        for sem, rows in zip((sum_a, sum_b), part_rows)
    ]
    sum_out = LineScatter(p, part_out, *scratch[2:4], sum_c, pl.ds(0, rows_own))
    plane = PlaneScatter(p, weight_part(p, full_g), units, *scratch[4:7])
    gathers = [
        LineGather(p, branch, sem, mine.at[rows], rows)
        for sem, rows in zip((gather_a, gather_b), part_rows)
    ]

    def load(index):
        if index < 4:
            source, target = ((normed, nt), (cot, ct))[index // 2]
            return pltpu.make_async_copy(
                source.at[:, part_rows[index % 2]], target.at[index % 2], load_sems.at[index]
            )
        return pltpu.make_async_copy(wd, full_d, load_sems.at[4])

    def load_wide(index, side):
        columns = lanes(side * ff + index * part, part)
        return pltpu.make_async_copy(
            wg.at[:, :, columns], full_g.at[:, :, columns], load_sems.at[5 + 2 * index + side]
        )

    load(0).start()
    for index in range(4):
        for side in range(2):
            load_wide(index, side).start()
        if index == 0:
            for other in (2, 4, 1, 3):
                load(other).start()
    p.meet(True)
    for index in (0, 2, 4):
        load(index).wait()

    def stage_one(half, first, last):
        rows = pl.ds(half * block_rows, block_rows)

        def some(index, carry):
            if half == 0:
                load_wide(index, 0).wait()
                load_wide(index, 1).wait()
            here, there = lanes(index * part, part), lanes(ff + index * part, part)
            left = nt[half].reshape(block_rows, width)
            gate = jnp.dot(left, full_g[:, :, here].reshape(width, part), preferred_element_type=WIDE)
            up = jnp.dot(left, full_g[:, :, there].reshape(width, part), preferred_element_type=WIDE)
            grad = jnp.dot(
                ct[half].reshape(block_rows, width),
                full_d[:, :, here].reshape(width, part),
                preferred_element_type=WIDE,
            )
            sigmoid_gate = jax.nn.sigmoid(gate)
            active[rows, here] = (gate * sigmoid_gate * up).astype(LOW)
            grad_wide[rows, here] = (
                grad * up * sigmoid_gate * (1.0 + gate * (1.0 - sigmoid_gate))
            ).astype(LOW)
            grad_wide[rows, there] = (grad * gate * sigmoid_gate).astype(LOW)
            return carry

        lax.fori_loop(first, last, some, 0)

    def rows_times(left, weight, target, half, first, last):
        def some(index, carry):
            made = lax.dot_general(
                left[pl.ds(half * block_rows, block_rows), :],
                weight[pl.ds(index * blocks, blocks)].reshape(wide, -1),
                CONTRACT_LAST,
                preferred_element_type=WIDE,
            )
            target[:, part_rows[half], lanes(index * wide, wide)] = made.astype(LOW).reshape(
                8, rows_own // 2, wide
            )
            return carry

        lax.fori_loop(first, last, some, 0)

    def down_grad(index, carry):
        made = lax.dot_general(
            ct[:, :, :, lanes(index * wide, wide)].reshape(seq_len, wide),
            active[...],
            CONTRACT_FIRST,
            preferred_element_type=WIDE,
        )
        full_d[pl.ds(index * blocks, blocks)] = made.astype(LOW).reshape(blocks, own, ff)
        return carry

    def wide_grad(index):
        for side in range(2):
            made = lax.dot_general(
                nt[:, :, :, pl.ds(index * wide, wide)].reshape(seq_len, wide),
                grad_wide[:, pl.ds(side * ff, ff)],
                CONTRACT_FIRST,
                preferred_element_type=WIDE,
            )
            full_g[pl.ds(index * blocks, blocks), :, pl.ds(side * ff, ff)] = made.astype(
                LOW
            ).reshape(blocks, own, ff)
        plane.start_unit(index)

    def local_two(part):
        def some(rows):
            spot = pl.ds(pl.multiple_of(part * (rows_own // 2) + rows.start, CHUNK), CHUNK)
            unit, inverse = rms_parts(residual[spot, :])
            total = ct[part, p.slot, rows, :].astype(WIDE) + normed_back(
                sum_two[part].total(spot), unit, inverse, gain_rows[pl.ds(1, 1), :]
            )
            grad_residual[spot, :] = total
            mine[spot, :] = total.astype(LOW)

        by_rows(rows_own // 2, some)

    stage_one(0, 0, 4)
    rows_times(grad_wide, full_g, part_two, 0, 0, 4)
    sum_two[0].start()
    load(1).wait()
    load(3).wait()
    stage_one(1, 0, 2)
    sum_two[0].head()
    stage_one(1, 2, 4)
    rows_times(grad_wide, full_g, part_two, 1, 0, 2)
    sum_two[0].step(0)
    rows_times(grad_wide, full_g, part_two, 1, 2, 3)
    sum_two[0].step(1)
    rows_times(grad_wide, full_g, part_two, 1, 3, 4)
    sum_two[1].start()
    sum_two[0].step(2)
    wide_grad(0)
    sum_two[1].head()
    sum_two[0].arrive()
    local_two(0)
    gathers[0].start()
    rows_times(active, full_d, part_out, 0, 0, 4)
    sum_two[1].step(0)
    rows_times(active, full_d, part_out, 1, 0, 4)
    sum_out.start()
    sum_two[1].step(1)
    sum_two[1].step(2)
    wide_grad(1)
    gathers[0].inner(1)
    sum_two[1].arrive()
    local_two(1)
    gathers[1].start()
    sum_out.head()
    keep_grad = pltpu.make_async_copy(grad_residual, out_grad, keep_sems.at[1])
    keep_grad.start()
    wide_grad(2)
    gathers[0].outer()
    gathers[1].inner(1)
    wide_grad(3)
    gathers[0].inner(2)
    gathers[1].outer()
    plane.middle(0)
    lax.fori_loop(0, 2, down_grad, 0)
    gathers[1].inner(2)
    lax.fori_loop(2, 4, down_grad, 0)
    keep_d = pltpu.make_async_copy(full_d, d_part, keep_sems.at[0])
    keep_d.start()
    plane.middle(1)
    sum_out.step(0)
    gathers[0].inner(3)
    gathers[1].inner(3)
    plane.middle(2)
    sum_out.step(1)
    sum_out.step(2)
    plane.middle(3)
    for gather in gathers:
        gather.finish()
    for gather in gathers:
        gather.drain()
    def keep_g(half, unit):
        return pltpu.make_async_copy(
            plane.sums(half, unit), g_sum.at[half, unit], keep_sems.at[2 + 4 * half + unit]
        )

    def finish_unit(unit):
        plane.final(unit)
        for half in range(2):
            keep_g(half, unit).start()

    for unit in range(units - 1):
        finish_unit(unit)
    sum_out.arrive()

    def local_out(rows):
        mine[rows, :] = (residual[rows, :] + sum_out.total(rows)).astype(LOW)

    by_rows(rows_own, local_out)
    keep_block = pltpu.make_async_copy(mine, block_out, swap_sems.at[0])
    keep_block.start()
    finish_unit(units - 1)
    keep_block.wait()
    for part in sum_two + [sum_out, plane]:
        part.drain()
    keep_d.wait()
    keep_grad.wait()
    for unit in range(units):
        for half in range(2):
            keep_g(half, unit).wait()


def mlp(normed, wg, wd, cot, residual, gain_rows):
    _, rows, width = normed.shape
    own, ff = wd.shape[1:]
    units = wd.shape[0] // 8
    vmem = lambda shape, dtype=LOW: pltpu.VMEM(shape, dtype)
    return kernel_call(
        mlp_kernel,
        "mlp",
        2,
        (normed, wg, wd, cot, residual, gain_rows),
        [ANYWHERE] * 4 + [IN_VMEM] * 2,
        [
            (normed.shape, LOW),
            ((2, units, own, 2 * ff), LOW),
            (wd.shape, LOW),
            ((rows, width), LOW),
            ((rows, width), WIDE),
        ],
        [ANYWHERE] * 5,
        [
            vmem((2, 8, rows // 2, width)),
            vmem(wg.shape),
            vmem(wd.shape),
            vmem((2, 8, rows // 2, width)),
            vmem((8 * rows, ff)),
            vmem((8 * rows, 2 * ff)),
            vmem(normed.shape),
            vmem(normed.shape),
            vmem((rows, width), WIDE),
            vmem((rows, width)),
        ]
        + LineScatter.buffers(rows, width) * 2
        + PlaneScatter.scratch(units, own, 2 * ff)
        + [DMA((13,))]
        + [DMA(LineScatter.SEMS)] * 3
        + [DMA(LineGather.SEMS)] * 2
        + [DMA((3,)), DMA((2 + 2 * units,))],
    )


def backward_kernel(
    branch_all,
    grad_in,
    gain_rows,
    own_tok,
    full_q,
    full_o,
    qkv,
    attended,
    normed_one,
    cosines,
    sines,
    g_sum,
    d_part,
    block,
    input_grad,
    block_out,
    q_out,
    g_out,
    d_out,
    o_out,
    work,
    branch,
    grad_residual,
    grad_heads,
    grads,
    grad_projected,
    q_part,
    o_part,
    o_sum,
    d_here,
    *scratch,
):
    buffers, rest = scratch[:2], scratch[2:]
    p = Place()
    rows_own, width = grad_residual.shape
    seq_len = 8 * rows_own
    own = full_o.shape[1]
    units = g_sum.shape[1]
    half = own // 2
    step_q, step_g, step_d = q_part.shape[2] // 3, g_sum.shape[3] // 2, d_part.shape[2]
    plane_d = PlaneScatter(p, weight_part(p, d_here), units, *rest[:3])
    plane_q = PlaneScatter(p, weight_part(p, q_part), units, *rest[3:6])
    plane_o = PlaneScatter(
        p, lambda h, u, x, y: o_part.at[2 * y + x, pl.ds(h * half, half)], 1, *rest[6:9]
    )
    sum_sems, return_sems, swap_sems, load_sems = rest[9:11], rest[11:14], rest[14:18], rest[18]
    part_rows = [pl.ds(0, rows_own // 2), pl.ds(rows_own // 2, rows_own // 2)]
    sum_one = [
        LineScatter(p, branch, *buffers, sem, rows) for sem, rows in zip(sum_sems, part_rows)
    ]
    return_q = LineReturn(
        p, plane_q.sums, [(i * step_q, step_q, i * 8 * step_q) for i in range(3)], q_out, return_sems[0]
    )
    return_g = LineReturn(
        p,
        lambda c, z: g_sum.at[c, z],
        [(i * step_g, step_g, i * 8 * step_g) for i in range(2)],
        g_out,
        return_sems[1],
    )
    return_d = LineReturn(p, plane_d.sums, [(0, step_d, 0)], d_out, return_sems[2])
    swap_in = [
        Swap(p, grad_residual.at[rows], input_grad.at[rows], input_grad.at[rows], sem)
        for sem, rows in zip(swap_sems[:2], part_rows)
    ]
    swap_out = Swap(p, o_sum, o_out, o_out, swap_sems[2])
    swap_block = Swap(p, block, block_out, block_out, swap_sems[3])

    def load(source, target, index):
        return pltpu.make_async_copy(source, target, load_sems.at[index])

    loads = [
        load(branch_all, branch, 0),
        load(d_part, d_here, 1),
        load(normed_one, work, 2),
        load(grad_in, grad_residual, 3),
    ]
    for copy in loads:
        copy.start()
    p.meet(True)
    swap_block.start()
    for z in range(4):
        return_g.send(z)
    loads[0].wait()

    def back_out(part, carry):
        rows = pl.ds(pl.multiple_of(part * 256, 256), 256)
        made = lax.dot_general(
            branch[pl.ds(2 * part, 2)].reshape(256, width),
            full_o[...].reshape(-1, width),
            CONTRACT_LAST,
            preferred_element_type=WIDE,
        )
        grad_heads[rows, :] = made.astype(LOW)
        return carry

    lax.fori_loop(0, seq_len // 256, back_out, 0)
    loads[1].wait()
    plane_d.start()

    def out_grad(part, carry):
        columns = lanes(part * 512, 512)
        made = lax.dot_general(
            attended[...],
            branch[:, :, columns].reshape(seq_len, 512),
            CONTRACT_FIRST,
            preferred_element_type=WIDE,
        )
        o_part[:, :, columns] = made.astype(LOW).reshape(4, own, 512)
        return carry

    lax.fori_loop(0, width // 512, out_grad, 0)
    plane_o.start()
    grads[...] = jnp.zeros_like(grads)

    def one_head(head, carry):
        attend_back(head, qkv, grad_heads, grads)
        plane_d.middle(head)
        return carry

    lax.fori_loop(0, 4, one_head, 0)

    def back_turn(part, carry):
        rows = pl.ds(pl.multiple_of(part * 256, 256), 256)
        for kind in range(3):
            made = grads[kind, rows, :]
            if kind < 2:
                made = turn(
                    made,
                    jnp.concatenate([cosines[rows, :]] * 2, axis=1),
                    jnp.concatenate([-sines[rows, :]] * 2, axis=1),
                )
            grad_projected[rows, pl.ds(kind * step_q, step_q)] = made.astype(LOW)
        return carry

    lax.fori_loop(0, seq_len // 256, back_turn, 0)

    def back_qkv(part, carry):
        weight = full_q[pl.ds(part * 8, 8), :, pl.ds(0, 3 * step_q)].reshape(8 * own, 3 * step_q)
        for block in range(seq_len // 512):
            made = lax.dot_general(
                grad_projected[pl.ds(block * 512, 512), :],
                weight,
                CONTRACT_LAST,
                preferred_element_type=WIDE,
            )
            branch[pl.ds(block * 4, 4), :, lanes(part * 8 * own, 8 * own)] = made.astype(
                LOW
            ).reshape(4, rows_own, 8 * own)
        return carry

    lax.fori_loop(0, 4, back_qkv, 0)
    for part in sum_one:
        part.start()
    loads[2].wait()
    loads[3].wait()
    for part in sum_one:
        part.head()

    def qkv_grad(part, carry):
        made = lax.dot_general(
            work[:, :, lanes(part * 8 * own, 8 * own)].reshape(seq_len, 8 * own),
            grad_projected[...],
            CONTRACT_FIRST,
            preferred_element_type=WIDE,
        )
        q_part[pl.ds(part * 8, 8)] = made.astype(LOW).reshape(8, own, 3 * step_q)
        plane_q.start_unit(part)
        return carry

    lax.fori_loop(0, 4, qkv_grad, 0)

    def local_one(part):
        def some(rows):
            spot = pl.ds(pl.multiple_of(part * (rows_own // 2) + rows.start, CHUNK), CHUNK)
            unit, inverse = rms_parts(own_tok[spot, :].astype(WIDE))
            grad_residual[spot, :] = grad_residual[spot, :] + normed_back(
                sum_one[part].total(spot), unit, inverse, gain_rows[pl.ds(0, 1), :]
            )

        by_rows(rows_own // 2, some)

    for part in sum_one:
        part.steps()
    for unit in range(units):
        plane_d.final(unit)
        return_d.send(unit)
    plane_o.middle(0)
    for unit in range(units):
        plane_q.middle(unit)
    for part in range(2):
        sum_one[part].arrive()
        local_one(part)
        swap_in[part].start()
    plane_o.final(0)
    for h in range(2):
        o_sum[pl.ds(h * half, half), :] = plane_o.sums(h, 0)[...]
    swap_out.start()
    for unit in range(units):
        plane_q.final(unit)
        return_q.send(unit)
    for part in (return_g, return_d, return_q):
        part.finish()
    for part in swap_in + [swap_out, swap_block]:
        part.wait()
        part.drain()
    for part in sum_one + [plane_d, plane_q, plane_o]:
        part.drain()


def backward(
    branch,
    grad_residual,
    gain_rows,
    own_tok,
    full_q,
    full_o,
    qkv,
    attended,
    normed_one,
    cosines,
    sines,
    g_sum,
    d_part,
    block,
):
    _, rows, width = branch.shape
    own, here = full_o.shape[1], attended.shape[1]
    units = g_sum.shape[1]
    vmem = lambda shape, dtype=LOW: pltpu.VMEM(shape, dtype)
    step_g, step_d = g_sum.shape[3], d_part.shape[2]
    return kernel_call(
        backward_kernel,
        "backward",
        3,
        (
            branch,
            grad_residual,
            gain_rows,
            own_tok,
            full_q,
            full_o,
            qkv,
            attended,
            normed_one,
            cosines,
            sines,
            g_sum,
            d_part,
            block,
        ),
        [ANYWHERE] * 2 + [IN_VMEM] * 6 + [ANYWHERE] + [IN_VMEM] * 2 + [ANYWHERE] * 3,
        [
            ((rows, width), WIDE),
            ((rows, width), LOW),
            ((own, 24 * here), LOW),
            ((own, 8 * step_g), LOW),
            ((own, 8 * step_d), LOW),
            ((own, width), LOW),
        ],
        [ANYWHERE] * 6,
        [
            vmem((8, rows, width)),
            vmem((8, rows, width)),
            vmem((rows, width), WIDE),
            vmem((8 * rows, here)),
            vmem((3, 8 * rows, here), WIDE),
            vmem((8 * rows, 3 * here)),
            vmem((32, own, 3 * here)),
            vmem((4, own, width)),
            vmem((own, width)),
            vmem(d_part.shape),
        ]
        + LineScatter.buffers(rows, width)
        + PlaneScatter.scratch(units, own, step_d)
        + PlaneScatter.scratch(units, own, 3 * here)
        + PlaneScatter.scratch(1, own // 2, width)
        + [DMA(LineScatter.SEMS)] * 2
        + [DMA(LineReturn.SEMS)] * 3
        + [DMA((3,))] * 4
        + [DMA((4,))],
    )


ADAM_STEPS = 4
WIDE_RATE = 2.5 * D ** (-0.5)
OUT_RATE = 2.5 * max(D // 512, 1) ** (-0.5)
DOWN_RATE = 2.5 * FF ** (-0.5)


def adam_quick(weight, gradient, first, second, rate, decay):
    new_first = BETA_ONE * first + (1.0 - BETA_ONE) * gradient
    new_second = BETA_TWO * second + (1.0 - BETA_TWO) * gradient * gradient
    root = jnp.sqrt(new_second * (1.0 / (1.0 - BETA_TWO**STEP))) + ADAM_EPS
    moved = new_first * (rate / (1.0 - BETA_ONE**STEP)) / root
    return ((1.0 - rate * decay) * weight - moved, new_first, new_second)


def adam_kernel(*refs):
    inputs, gains, handed = refs[:16], refs[16:19], refs[19:21]
    outputs, gains_new, placed = refs[21:33], refs[33:36], refs[36:38]
    sums = refs[38:]
    step = pl.program_id(0)
    for source, target in zip(handed, placed):
        target[...] = source[...]

    @pl.when(step == 0)
    def _():
        for total in sums:
            total[...] = jnp.zeros_like(total)

    for index, rate in enumerate((WIDE_RATE, OUT_RATE, WIDE_RATE, DOWN_RATE)):
        weight, first, second, low_gradient = (ref[...] for ref in inputs[4 * index : 4 * index + 4])
        gradient = low_gradient.astype(WIDE)
        made = adam_quick(weight, gradient, first, second, rate, WEIGHT_DECAY)
        for target, value in zip(outputs[3 * index : 3 * index + 3], made):
            target[...] = value
        if index % 2 == 0:
            total = jnp.sum(weight.astype(LOW).astype(WIDE) * gradient, axis=1, keepdims=True)
            sums[index // 2][...] += jnp.broadcast_to(total, sums[index // 2].shape)

    @pl.when(step == ADAM_STEPS - 1)
    def _():
        rows = [jnp.transpose(total[...])[:1] for total in sums]
        weight, first, second = (ref[...] for ref in gains)
        gradient = jnp.concatenate(rows, axis=0) / weight.astype(LOW).astype(WIDE)
        for target, value in zip(gains_new, adam_quick(weight, gradient, first, second, 0.5, 0.0)):
            target[...] = value


def adam_all(groups, gains, handed):
    specs, out_specs, out_shape = [], [], []
    rows = groups[0][0].shape[0]
    for group in groups:
        spec = pl.BlockSpec((rows, group[0].shape[1] // ADAM_STEPS), lambda step: (0, step))
        specs += [spec] * 4
        out_specs += [spec] * 3
        out_shape += [jax.ShapeDtypeStruct(group[0].shape, WIDE)] * 3
    whole = [pl.BlockSpec(gains[0].shape, lambda step: (0, 0))] * 3
    whole += [
        pl.BlockSpec((a.shape[0], a.shape[1] // ADAM_STEPS), lambda step: (0, step)) for a in handed
    ]
    arrays = list(gains) + list(handed)
    return pl.pallas_call(
        adam_kernel,
        grid=(ADAM_STEPS,),
        in_specs=specs + whole,
        out_specs=out_specs + whole,
        out_shape=out_shape + [jax.ShapeDtypeStruct(a.shape, a.dtype) for a in arrays],
        scratch_shapes=[pltpu.VMEM((rows, 128), WIDE)] * 2,
        compiler_params=pltpu.CompilerParams(vmem_limit_bytes=56 * 2**20),
        name="adam",
    )(*[array for group in groups for array in group], *arrays)


def grid_shards(
    tokens,
    cotangent,
    qkv_weight,
    out_weight,
    gate_up_weight,
    down_weight,
    gains,
    qkv_first,
    out_first,
    gate_up_first,
    down_first,
    gains_first,
    qkv_second,
    out_second,
    gate_up_second,
    down_second,
    gains_second,
):
    rows, width = tokens.shape[1:]
    seq_len = 8 * rows
    gain_columns = jnp.pad(gains.astype(LOW).T, ((0, 0), (0, 126)))
    cosines, sines = turn_tables(seq_len)
    (
        grad_out,
        normed_two,
        gate_up_full,
        down_full,
        qkv_full,
        out_full,
        normed_one,
        qkv_heads,
        attended,
        residual,
        gain_full,
        own_tokens,
    ) = forward(
        tokens[0],
        cotangent[0],
        qkv_weight,
        gain_columns,
        gate_up_weight,
        down_weight,
        out_weight,
        cosines,
        sines,
    )
    grad_branch, gate_up_half, down_part, block_own, grad_residual = mlp(
        normed_two, gate_up_full, down_full, grad_out, residual, gain_full
    )
    input_grad, block_out, qkv_sum, gate_up_sum, down_sum, out_sum = backward(
        grad_branch,
        grad_residual,
        gain_full,
        own_tokens,
        qkv_full,
        out_full,
        qkv_heads,
        attended,
        normed_one.reshape(8, rows, width),
        cosines,
        sines,
        gate_up_half,
        down_part,
        block_own,
    )
    made = adam_all(
        [
            (qkv_weight, qkv_first, qkv_second, qkv_sum),
            (out_weight, out_first, out_second, out_sum),
            (gate_up_weight, gate_up_first, gate_up_second, gate_up_sum),
            (down_weight, down_first, down_second, down_sum),
        ],
        (gains, gains_first, gains_second),
        (input_grad, block_out),
    )
    qkv_new, out_new, gate_up_new, down_new, gains_new = (
        made[3 * i : 3 * i + 3] for i in range(5)
    )
    input_grad, block_out = made[15:]
    return (
        block_out[None],
        input_grad[None],
        qkv_new[0],
        out_new[0],
        gate_up_new[0],
        down_new[0],
        gains_new[0],
        qkv_new[1],
        out_new[1],
        gate_up_new[1],
        down_new[1],
        gains_new[1],
        qkv_new[2],
        out_new[2],
        gate_up_new[2],
        down_new[2],
        gains_new[2],
    )


def mapped(body, mesh, token_spec, row_spec, gain_spec):
    one_set = (row_spec, row_spec, row_spec, row_spec, gain_spec)
    return jax.shard_map(
        body,
        mesh=mesh,
        in_specs=(token_spec, token_spec) + one_set * 3,
        out_specs=(token_spec, token_spec) + one_set * 3,
        check_vma=False,
    )


def solution(mesh):
    if mesh.shape["seq"] == 8 and mesh.shape["dp"] == 4:
        grid_mesh = Mesh(mesh.devices.reshape(4, 2, 2, 2), GRID)
        return mapped(
            grid_shards,
            grid_mesh,
            P(("y", "c"), ("z", "x"), None),
            P(GRID, None),
            P(None, GRID),
        )
    return mapped(
        shards, mesh, P("dp", "seq", None), P(("seq", "dp"), None), P(None, ("seq", "dp"))
    )
```

```python
import jax
import jax.numpy as jnp
import numpy as np
from jax import lax
from jax.experimental import pallas as pl
from jax.experimental.pallas import tpu as pltpu
from jax.sharding import Mesh
from jax.sharding import PartitionSpec as P

D = 2048
HEADS = 32
HEAD_DIM = 64
FF = 8192
BLOCK = 512
STEP = 10


NORM_EPS = 1e-05
ROPE_BASE = 130000.0
BETA_ONE = 0.9
BETA_TWO = 0.999
ADAM_EPS = 1e-08
WEIGHT_DECAY = 0.1
MASKED = -1e30


def rms_parts(values):
    inverse = lax.rsqrt(jnp.mean(values * values, axis=-1, keepdims=True) + NORM_EPS)
    return (values * inverse, inverse)


def rope_tables(positions):
    half_dim = HEAD_DIM // 2
    exponent = jnp.arange(half_dim, dtype=jnp.float32) * (2.0 / HEAD_DIM)
    frequency = ROPE_BASE ** (-exponent)
    angles = positions.astype(jnp.float32)[:, None] * frequency[None, :]
    return (jnp.cos(angles)[:, None, :], jnp.sin(angles)[:, None, :])


def rotate(tensor, cosines, sines):
    half_dim = HEAD_DIM // 2
    lower_half = tensor[..., :half_dim]
    upper_half = tensor[..., half_dim:]
    return jnp.concatenate(
        [lower_half * cosines - upper_half * sines, upper_half * cosines + lower_half * sines],
        axis=-1,
    )


def unrotate(tensor, cosines, sines):
    half_dim = HEAD_DIM // 2
    lower_half = tensor[..., :half_dim]
    upper_half = tensor[..., half_dim:]
    return jnp.concatenate(
        [lower_half * cosines + upper_half * sines, upper_half * cosines - lower_half * sines],
        axis=-1,
    )


def block_scores(query_rows, key_heads, key_id, block_id):
    key_rows = lax.dynamic_slice_in_dim(key_heads, key_id * BLOCK, BLOCK, 0)
    products = jnp.einsum(
        "qhd,khd->hqk", query_rows, key_rows, preferred_element_type=jnp.float32
    ) * HEAD_DIM ** (-0.5)
    local_ids = jnp.arange(BLOCK, dtype=jnp.int32)
    allowed = (key_id < block_id) | (local_ids[None, :] <= local_ids[:, None])
    return jnp.where(allowed[None], products, MASKED)


def row_normalizer(query_rows, key_heads, block_id):
    row_shape = (query_rows.shape[1], BLOCK, 1)

    def absorb(key_id, state):
        running_max, running_total = state
        scores = block_scores(query_rows, key_heads, key_id, block_id)
        new_max = jnp.maximum(running_max, jnp.max(scores, axis=-1, keepdims=True))
        running_total = running_total * jnp.exp(running_max - new_max) + jnp.sum(
            jnp.exp(scores - new_max), axis=-1, keepdims=True
        )
        return (new_max, running_total)

    start_state = (jnp.full(row_shape, MASKED, jnp.float32), jnp.zeros(row_shape, jnp.float32))
    final_max, final_total = lax.fori_loop(0, block_id + 1, absorb, start_state)
    return final_max + jnp.log(final_total)


def attend_forward(query_heads, key_heads, value_heads):
    seq_len, heads_here, head_dim = query_heads.shape

    def one_block(block_id, carry):
        out_all, lse_all = carry
        row_start = block_id * BLOCK
        query_rows = lax.dynamic_slice_in_dim(query_heads, row_start, BLOCK, 0)
        row_lse = row_normalizer(query_rows, key_heads, block_id)

        def weigh_values(key_id, running):
            scores = block_scores(query_rows, key_heads, key_id, block_id)
            weights_low = jnp.exp(scores - row_lse).astype(jnp.bfloat16)
            value_rows = lax.dynamic_slice_in_dim(value_heads, key_id * BLOCK, BLOCK, 0)
            return running + jnp.einsum(
                "hqk,khd->qhd", weights_low, value_rows, preferred_element_type=jnp.float32
            )

        attended = lax.fori_loop(
            0, block_id + 1, weigh_values, jnp.zeros((BLOCK, heads_here, head_dim), jnp.float32)
        )
        out_all = lax.dynamic_update_slice_in_dim(
            out_all, attended.astype(jnp.bfloat16), row_start, 0
        )
        lse_all = lax.dynamic_update_slice_in_dim(lse_all, row_lse, row_start, 1)
        return (out_all, lse_all)

    start_carry = (
        jnp.zeros((seq_len, heads_here, head_dim), jnp.bfloat16),
        jnp.zeros((heads_here, seq_len, 1), jnp.float32),
    )
    return lax.fori_loop(0, seq_len // BLOCK, one_block, start_carry)


def attend_backward(query_heads, key_heads, value_heads, grad_heads, lse_all):
    seq_len, heads_here, head_dim = query_heads.shape
    score_scale = HEAD_DIM ** (-0.5)

    def one_block(block_id, carry):
        grad_q_all, grad_k_all, grad_v_all = carry
        row_start = block_id * BLOCK
        query_rows = lax.dynamic_slice_in_dim(query_heads, row_start, BLOCK, 0)
        grad_rows = lax.dynamic_slice_in_dim(grad_heads, row_start, BLOCK, 0)
        row_lse = lax.dynamic_slice_in_dim(lse_all, row_start, BLOCK, 1)

        def probs_and_grads(key_id):
            scores = block_scores(query_rows, key_heads, key_id, block_id)
            probs = jnp.exp(scores - row_lse)
            value_rows = lax.dynamic_slice_in_dim(value_heads, key_id * BLOCK, BLOCK, 0)
            grad_probs = jnp.einsum(
                "qhd,khd->hqk", grad_rows, value_rows, preferred_element_type=jnp.float32
            )
            return (probs, grad_probs)

        def add_delta(key_id, running):
            probs, grad_probs = probs_and_grads(key_id)
            return running + jnp.sum(probs * grad_probs, axis=-1, keepdims=True)

        row_delta = lax.fori_loop(
            0, block_id + 1, add_delta, jnp.zeros((heads_here, BLOCK, 1), jnp.float32)
        )

        def spread(key_id, inner):
            grad_q_rows, grad_k_acc, grad_v_acc = inner
            probs, grad_probs = probs_and_grads(key_id)
            key_start = key_id * BLOCK
            key_rows = lax.dynamic_slice_in_dim(key_heads, key_start, BLOCK, 0)
            grad_scores = (probs * (grad_probs - row_delta) * score_scale).astype(jnp.bfloat16)
            grad_q_rows = grad_q_rows + jnp.einsum(
                "hqk,khd->qhd", grad_scores, key_rows, preferred_element_type=jnp.float32
            )
            grad_k_part = jnp.einsum(
                "hqk,qhd->khd", grad_scores, query_rows, preferred_element_type=jnp.float32
            )
            grad_v_part = jnp.einsum(
                "hqk,qhd->khd",
                probs.astype(jnp.bfloat16),
                grad_rows,
                preferred_element_type=jnp.float32,
            )
            grad_k_acc = lax.dynamic_update_slice_in_dim(
                grad_k_acc,
                lax.dynamic_slice_in_dim(grad_k_acc, key_start, BLOCK, 0) + grad_k_part,
                key_start,
                0,
            )
            grad_v_acc = lax.dynamic_update_slice_in_dim(
                grad_v_acc,
                lax.dynamic_slice_in_dim(grad_v_acc, key_start, BLOCK, 0) + grad_v_part,
                key_start,
                0,
            )
            return (grad_q_rows, grad_k_acc, grad_v_acc)

        start_inner = (
            jnp.zeros((BLOCK, heads_here, head_dim), jnp.float32),
            grad_k_all,
            grad_v_all,
        )
        grad_q_rows, grad_k_all, grad_v_all = lax.fori_loop(0, block_id + 1, spread, start_inner)
        grad_q_all = lax.dynamic_update_slice_in_dim(grad_q_all, grad_q_rows, row_start, 0)
        return (grad_q_all, grad_k_all, grad_v_all)

    zeros_all = jnp.zeros((seq_len, heads_here, head_dim), jnp.float32)
    return lax.fori_loop(0, seq_len // BLOCK, one_block, (zeros_all, zeros_all, zeros_all))


def adam_step(weight, gradient, first, second, rate, decay):
    new_first = BETA_ONE * first + (1.0 - BETA_ONE) * gradient
    new_second = BETA_TWO * second + (1.0 - BETA_TWO) * gradient * gradient
    first_hat = new_first / (1.0 - BETA_ONE**STEP)
    second_hat = new_second / (1.0 - BETA_TWO**STEP)
    new_weight = weight - rate * (first_hat / (jnp.sqrt(second_hat) + ADAM_EPS) + decay * weight)
    return (new_weight, new_first, new_second)


def shards(
    tokens,
    cotangent,
    qkv_weight,
    out_weight,
    gate_up_weight,
    down_weight,
    gains,
    qkv_first,
    out_first,
    gate_up_first,
    down_first,
    gains_first,
    qkv_second,
    out_second,
    gate_up_second,
    down_second,
    gains_second,
):
    seq_count = lax.axis_size("seq")
    tok_rows = tokens.shape[1]
    width = tokens.shape[2]
    seq_len = tok_rows * seq_count
    heads_here = HEADS // seq_count
    width_here = heads_here * HEAD_DIM
    contract_last = (((1,), (1,)), ((), ()))
    contract_first = (((0,), (0,)), ((), ()))
    qkv_full, proj_full, gain_full = (
        lax.all_gather(qkv_weight.astype(jnp.bfloat16), ("seq", "dp"), axis=0, tiled=True),
        lax.all_gather(out_weight.astype(jnp.bfloat16), ("seq", "dp"), axis=0, tiled=True),
        lax.all_gather(gains.astype(jnp.bfloat16), ("seq", "dp"), axis=1, tiled=True),
    )
    up_full, down_full = (
        lax.all_gather(gate_up_weight.astype(jnp.bfloat16), ("seq", "dp"), axis=0, tiled=True),
        lax.all_gather(down_weight.astype(jnp.bfloat16), ("seq", "dp"), axis=0, tiled=True),
    )
    hidden_in = tokens[0].astype(jnp.float32)
    unit_one, inverse_one = rms_parts(hidden_in)
    normed_one = (unit_one * gain_full[0].astype(jnp.float32)).astype(jnp.bfloat16)
    projected = jnp.einsum(
        "te,ecd->ctd",
        normed_one,
        qkv_full.reshape(width, 3, width),
        preferred_element_type=jnp.float32,
    )
    positions = lax.axis_index("seq") * tok_rows + jnp.arange(tok_rows, dtype=jnp.int32)
    cos_local, sin_local = rope_tables(positions)
    turned = rotate(projected[:2].reshape(2, tok_rows, HEADS, HEAD_DIM), cos_local, sin_local)
    packed = jnp.concatenate([turned.reshape(2, tok_rows, width), projected[2:]], axis=0).astype(
        jnp.bfloat16
    )
    by_heads = lax.all_to_all(packed, "seq", split_axis=2, concat_axis=1, tiled=True)
    query_heads = by_heads[0].reshape(seq_len, heads_here, HEAD_DIM)
    key_heads = by_heads[1].reshape(seq_len, heads_here, HEAD_DIM)
    value_heads = by_heads[2].reshape(seq_len, heads_here, HEAD_DIM)
    out_heads, lse_all = attend_forward(query_heads, key_heads, value_heads)
    attended = lax.all_to_all(
        out_heads.reshape(seq_len, width_here), "seq", split_axis=0, concat_axis=1, tiled=True
    )
    residual = hidden_in + jnp.dot(attended, proj_full, preferred_element_type=jnp.float32)
    unit_two, inverse_two = rms_parts(residual)
    normed_two = (unit_two * gain_full[1].astype(jnp.float32)).astype(jnp.bfloat16)
    gate_up = jnp.dot(normed_two, up_full, preferred_element_type=jnp.float32)
    gate_vals = gate_up[:, :FF]
    up_vals = gate_up[:, FF:]
    sigmoid_gate = jax.nn.sigmoid(gate_vals)
    activated = (gate_vals * sigmoid_gate * up_vals).astype(jnp.bfloat16)
    mlp_out = lax.dot_general(
        activated, down_full, contract_last, preferred_element_type=jnp.float32
    )
    block_out = (residual + mlp_out).astype(jnp.bfloat16)[None]
    back_up, back_down, back_gain = (
        lax.all_gather(gate_up_weight.astype(jnp.bfloat16), ("seq", "dp"), axis=0, tiled=True),
        lax.all_gather(down_weight.astype(jnp.bfloat16), ("seq", "dp"), axis=0, tiled=True),
        lax.all_gather(gains.astype(jnp.bfloat16), ("seq", "dp"), axis=1, tiled=True),
    )
    grad_out = cotangent[0]
    grad_act = jnp.dot(grad_out, back_down, preferred_element_type=jnp.float32)
    grad_gate = grad_act * up_vals * sigmoid_gate * (1.0 + gate_vals * (1.0 - sigmoid_gate))
    grad_up = grad_act * gate_vals * sigmoid_gate
    grad_gate_up = jnp.concatenate([grad_gate, grad_up], axis=1).astype(jnp.bfloat16)
    grad_normed_two = lax.dot_general(
        grad_gate_up, back_up, contract_last, preferred_element_type=jnp.float32
    )
    gain_two_grad = jnp.sum(grad_normed_two * unit_two, axis=0)
    grad_unit_two = grad_normed_two * back_gain[1].astype(jnp.float32)
    grad_residual = grad_out.astype(jnp.float32) + inverse_two * (
        grad_unit_two - unit_two * jnp.mean(grad_unit_two * unit_two, axis=-1, keepdims=True)
    )
    gate_up_rows = lax.dot_general(
        normed_two, grad_gate_up, contract_first, preferred_element_type=jnp.float32
    )
    down_rows = lax.dot_general(
        grad_out, activated, contract_first, preferred_element_type=jnp.float32
    )
    mlp_grad = lax.psum_scatter(
        jnp.concatenate([gate_up_rows, down_rows], axis=1),
        ("seq", "dp"),
        scatter_dimension=0,
        tiled=True,
    )
    back_qkv, back_proj = (
        lax.all_gather(qkv_weight.astype(jnp.bfloat16), ("seq", "dp"), axis=0, tiled=True),
        lax.all_gather(out_weight.astype(jnp.bfloat16), ("seq", "dp"), axis=0, tiled=True),
    )
    grad_branch = grad_residual.astype(jnp.bfloat16)
    proj_grad = lax.dot_general(
        attended, grad_branch, contract_first, preferred_element_type=jnp.float32
    )
    grad_attended = lax.dot_general(
        grad_branch, back_proj, contract_last, preferred_element_type=jnp.float32
    ).astype(jnp.bfloat16)
    grad_heads = lax.all_to_all(
        grad_attended, "seq", split_axis=1, concat_axis=0, tiled=True
    ).reshape(seq_len, heads_here, HEAD_DIM)
    grad_q_all, grad_k_all, grad_v_all = attend_backward(
        query_heads, key_heads, value_heads, grad_heads, lse_all
    )
    cos_whole, sin_whole = rope_tables(jnp.arange(seq_len, dtype=jnp.int32))
    grad_pack = jnp.stack(
        [
            unrotate(grad_q_all, cos_whole, sin_whole).reshape(seq_len, width_here),
            unrotate(grad_k_all, cos_whole, sin_whole).reshape(seq_len, width_here),
            grad_v_all.reshape(seq_len, width_here),
        ],
        axis=0,
    ).astype(jnp.bfloat16)
    grad_projected = lax.all_to_all(grad_pack, "seq", split_axis=1, concat_axis=2, tiled=True)
    qkv_cube = back_qkv.reshape(width, 3, width)
    grad_normed_one = jnp.einsum(
        "ctd,ecd->te", grad_projected, qkv_cube, preferred_element_type=jnp.float32
    )
    qkv_grad = jnp.einsum(
        "te,ctd->ecd", normed_one, grad_projected, preferred_element_type=jnp.float32
    ).reshape(width, 3 * width)
    gain_one_grad = jnp.sum(grad_normed_one * unit_one, axis=0)
    grad_unit_one = grad_normed_one * back_gain[0].astype(jnp.float32)
    input_grad = grad_residual + inverse_one * (
        grad_unit_one - unit_one * jnp.mean(grad_unit_one * unit_one, axis=-1, keepdims=True)
    )
    gains_grad = jnp.stack([gain_one_grad, gain_two_grad], axis=0)
    qkv_sum, proj_sum, gains_sum = (
        lax.psum_scatter(qkv_grad, ("seq", "dp"), scatter_dimension=0, tiled=True),
        lax.psum_scatter(proj_grad, ("seq", "dp"), scatter_dimension=0, tiled=True),
        lax.psum_scatter(gains_grad, ("seq", "dp"), scatter_dimension=1, tiled=True),
    )
    wide_rate = 2.5 * D ** (-0.5)
    out_rate = 2.5 * max(D // 512, 1) ** (-0.5)
    down_rate = 2.5 * FF ** (-0.5)
    qkv_new = adam_step(qkv_weight, qkv_sum, qkv_first, qkv_second, wide_rate, WEIGHT_DECAY)
    out_new = adam_step(out_weight, proj_sum, out_first, out_second, out_rate, WEIGHT_DECAY)
    gate_up_new = adam_step(
        gate_up_weight,
        mlp_grad[:, : 2 * FF],
        gate_up_first,
        gate_up_second,
        wide_rate,
        WEIGHT_DECAY,
    )
    down_new = adam_step(
        down_weight, mlp_grad[:, 2 * FF :], down_first, down_second, down_rate, WEIGHT_DECAY
    )
    gains_new = adam_step(gains, gains_sum, gains_first, gains_second, 0.5, 0.0)
    return (
        block_out,
        input_grad[None],
        qkv_new[0],
        out_new[0],
        gate_up_new[0],
        down_new[0],
        gains_new[0],
        qkv_new[1],
        out_new[1],
        gate_up_new[1],
        down_new[1],
        gains_new[1],
        qkv_new[2],
        out_new[2],
        gate_up_new[2],
        down_new[2],
        gains_new[2],
    )


GRID = ("z", "x", "y", "c")
RING = ("z", "c")
PLANE = ("x", "y")
LOW = jnp.bfloat16
WIDE = jnp.float32
CONTRACT_LAST = (((1,), (1,)), ((), ()))
CONTRACT_FIRST = (((0,), (0,)), ((), ()))
DMA = pltpu.SemaphoreType.DMA
ANYWHERE = pl.BlockSpec(memory_space=pl.ANY)
IN_VMEM = pl.BlockSpec(memory_space=pltpu.VMEM)


def remote(source, target, send, receive, **place):
    return pltpu.make_async_remote_copy(
        src_ref=source,
        dst_ref=target,
        send_sem=send,
        recv_sem=receive,
        device_id=place,
        device_id_type=pl.DeviceIdType.MESH,
    )


def lanes(start, size):
    return pl.ds(pl.multiple_of(start, 128), size)


class Place:
    def __init__(self):
        self.z, self.x, self.y, self.c = (lax.axis_index(name) for name in GRID)
        self.slot = 2 * self.z + self.c
        self.block_here = self.block(self.slot, self.x, self.y)

    def block(self, slot, x, y):
        return (((slot // 2) * 2 + x) * 2 + y) * 2 + lax.rem(slot, 2)

    def meet(self, plane):
        barrier = pltpu.get_barrier_semaphore()
        others = [
            {"z": slot // 2, "c": lax.rem(slot, 2)}
            for slot in (lax.rem(self.slot + step, 8) for step in range(1, 8))
        ]
        if plane:
            others += [{"x": 1 - self.x}, {"y": 1 - self.y}, {"x": 1 - self.x, "c": 1 - self.c}]
        for other in others:
            pl.semaphore_signal(
                barrier, inc=1, device_id=other, device_id_type=pl.DeviceIdType.MESH
            )
        pl.semaphore_wait(barrier, len(others))


class Swap:
    def __init__(self, place, source, spot_there, spot_here, sems):
        p = self.place = place
        self.away = lambda: remote(
            source, spot_there, sems.at[0], sems.at[1], x=1 - p.x, c=1 - p.c
        )
        self.here = lambda: pltpu.make_async_copy(source, spot_here, sems.at[2])

    def start(self):
        p = self.place
        pl.when(p.x != p.c)(lambda: self.away().start())
        pl.when(p.x == p.c)(lambda: self.here().start())

    def wait(self):
        p = self.place
        pl.when(p.x != p.c)(lambda: self.away().wait_recv())
        pl.when(p.x == p.c)(lambda: self.here().wait())

    def drain(self):
        p = self.place
        pl.when(p.x != p.c)(lambda: self.away().wait_send())


class LineGather:
    SEMS = (4, 8)

    def __init__(self, place, buffer, sems, mine=None, rows=None):
        self.place, self.sems, self.mine = place, sems, mine
        self.spot = (lambda slot: buffer.at[slot]) if rows is None else (lambda slot: buffer.at[slot, rows])

    def copy(self, slot, way, own=False):
        p, block = self.place, self.spot(slot)
        if way == 0:
            where = {"z": jnp.minimum(p.z + 1, 3)}
        elif way == 1:
            where = {"z": jnp.maximum(p.z - 1, 0)}
        else:
            where = {"c": 1 - p.c}
        source = self.mine if own and self.mine is not None else block
        return remote(source, block, self.sems.at[way, slot], self.sems.at[3, slot], **where)

    def _pass_on(self, slot, way, own=False):
        p = self.place
        if way == 0:
            pl.when(p.z < 3)(lambda: self.copy(slot, 0, own).start())
        elif way == 1:
            pl.when(p.z > 0)(lambda: self.copy(slot, 1, own).start())

    def start(self):
        slot = self.place.slot
        self._pass_on(slot, 0, True)
        self._pass_on(slot, 1, True)
        self.copy(slot, 2, True).start()
        if self.mine is not None:
            self.keep().start()

    def start_part(self, inside):
        p = self.place
        in_line = (p.z == 1) | (p.z == 2)
        pl.when(in_line if inside else jnp.logical_not(in_line))(self.start)

    def keep(self):
        slot = self.place.slot
        return pltpu.make_async_copy(self.mine, self.spot(slot), self.sems.at[3, slot])

    def inner(self, distance):
        p = self.place
        side = 1 - 2 * (p.z // 2)
        source = p.z + distance * side

        @pl.when((source >= 0) & (source <= 3))
        def _():
            slot = 2 * source + p.c
            self.copy(slot, 2).wait_recv()
            pl.when(p.z == 1)(lambda: self.copy(slot, 1).start())
            pl.when(p.z == 2)(lambda: self.copy(slot, 0).start())
            self.copy(slot, 2).start()

    def outer(self):
        p = self.place
        for here, way in ((1, 0), (2, 1)):

            @pl.when(p.z == here)
            def _():
                slot = p.slot - 2 + 4 * way
                self.copy(slot, 2).wait_recv()
                self.copy(slot, way).start()
                self.copy(slot, 2).start()

    def steps(self):
        self.inner(1)
        self.outer()
        self.inner(2)
        self.inner(3)

    def finish(self):
        p = self.place
        if self.mine is not None:
            self.keep().wait()
        for z in range(4):
            self.copy(2 * z + 1 - p.c, 2).wait_recv()

    def drain(self):
        p = self.place
        for z in range(4):
            slot = 2 * z + p.c
            self.copy(slot, 2).wait_send()
            pl.when((z <= p.z) & (p.z < 3))(lambda: self.copy(slot, 0).wait_send())
            pl.when((z >= p.z) & (p.z > 0))(lambda: self.copy(slot, 1).wait_send())


def add_blocks(target, sources):
    def some(step, carry):
        rows = pl.ds(pl.multiple_of(step * 16, 16), 16)
        total = sources[0][rows, :].astype(WIDE)
        for source in sources[1:]:
            total = total + source[rows, :].astype(WIDE)
        target[rows, :] = total.astype(target.dtype)
        return carry

    lax.fori_loop(0, target.shape[0] // 16, some, 0)


class LineScatter:
    SEMS = (6, 4)

    @staticmethod
    def buffers(rows, width):
        return [pltpu.VMEM((4, rows, width), LOW), pltpu.VMEM((5, rows, width), LOW)]

    def __init__(self, place, partial, across, passing, sems, rows):
        self.place, self.partial, self.sems, self.rows = place, partial, sems, rows
        self.across, self.passing = across, passing

    def cross(self, z):
        p = self.place
        return remote(
            self.partial.at[2 * z + 1 - p.c, self.rows],
            self.across.at[z, self.rows],
            self.sems.at[0, z],
            self.sems.at[1, z],
            c=1 - p.c,
        )

    def hop(self, z, way, landing):
        p = self.place
        there = jnp.minimum(p.z + 1, 3) if way == 0 else jnp.maximum(p.z - 1, 0)
        return remote(
            self.across.at[z, self.rows],
            self.passing.at[landing, self.rows],
            self.sems.at[2 + 2 * way, z],
            self.sems.at[3 + 2 * way, z],
            z=there,
        )

    def send(self, z, way):
        p = self.place
        if way == 0:
            self.hop(z, 0, z).start()
        else:
            pl.when(p.z - 1 == z)(lambda: self.hop(z, 1, 4).start())
            pl.when(p.z - 1 != z)(lambda: self.hop(z, 1, z).start())

    def start(self):
        for z in range(4):
            self.cross(z).start()

    def head(self):
        p = self.place
        for z in range(4):
            self.cross(z).wait_recv()
        for way, end in ((0, 0), (1, 3)):

            @pl.when(p.z == end)
            def _():
                for index in range(3):
                    z = 3 - index if way == 0 else index
                    spot = self.across.at[z, self.rows]
                    add_blocks(spot, [self.partial.at[2 * z + p.c, self.rows], spot])
                    self.send(z, way)

    def step(self, index):
        p = self.place
        for here, way, z in ((1, index // 2, (3, 2, 0)[index]), (2, 1 - index // 2, (0, 1, 3)[index])):

            @pl.when(p.z == here)
            def _():
                self.hop(z, way, z).wait_recv()
                spot = self.across.at[z, self.rows]
                add_blocks(
                    spot,
                    [
                        self.partial.at[2 * z + p.c, self.rows],
                        spot,
                        self.passing.at[z, self.rows],
                    ],
                )
                self.send(z, way)

    def steps(self):
        for index in range(3):
            self.step(index)

    def arrive(self):
        p = self.place
        pl.when(p.z > 0)(lambda: self.hop(p.z, 0, p.z).wait_recv())
        pl.when(p.z < 3)(lambda: self.hop(p.z, 1, 4).wait_recv())
        for end, landing in ((0, 0), (3, 4)):

            @pl.when(p.z == end)
            def _():
                spot = self.passing.at[landing, self.rows]
                spot[...] = jnp.zeros(spot.shape, LOW)

    def total(self, rows):
        p = self.place
        parts = (
            self.partial[p.slot, rows, :],
            self.across[p.z, rows, :],
            self.passing[p.z, rows, :],
            self.passing[4, rows, :],
        )
        return sum(part.astype(WIDE) for part in parts)

    def drain(self):
        p = self.place
        for z in range(4):
            self.cross(z).wait_send()
            pl.when(p.z < z)(lambda: self.hop(z, 0, z).wait_send())
            pl.when(p.z > z)(lambda: self.hop(z, 1, z).wait_send())


class Relayout:
    SEMS = (8, 8)

    def __init__(self, place, parts, target, sems):
        self.place, self.parts, self.target, self.sems = place, parts, target, sems

    def sem(self, kind, slot):
        return self.sems.at[kind, slot]

    def line(self, step):
        p = self.place
        slot = lax.rem(p.slot + step, 8)
        copies = []
        for source, first, size, there in self.parts:
            same_for_all = source.shape[1] == size
            columns = lanes(first if same_for_all else first + size * slot, size)
            piece = source.at[:, columns]
            spot = self.target.at[p.block_here, :, pl.ds(there, size)]
            if step == 0:
                copies.append(pltpu.make_async_copy(piece, spot, self.sem(1, p.slot)))
            else:
                copies.append(
                    remote(
                        piece,
                        spot,
                        self.sem(0, slot),
                        self.sem(1, p.slot),
                        z=slot // 2,
                        c=lax.rem(slot, 2),
                    )
                )
        return copies

    def whole(self, slot):
        p = self.place
        spot = self.target.at[p.block(slot, p.x, p.y)]
        return remote(spot, spot, self.sem(0, slot), self.sem(1, slot), c=1 - p.c)

    def plane(self, slot, x, y, way, send, receive):
        p = self.place
        spot = self.target.at[p.block(slot, x, y)]
        where = {"x": 1 - p.x} if way == 0 else {"y": 1 - p.y}
        return remote(spot, spot, self.sem(send, slot), self.sem(receive, slot), **where)

    def from_own(self, slot, way):
        p = self.place
        return self.plane(slot, p.x, p.y, way, 2 + 2 * way, 3 + 2 * way)

    def corner(self, slot, way):
        p = self.place
        x, y = (p.x, 1 - p.y) if way == 0 else (1 - p.x, p.y)
        return self.plane(slot, x, y, way, 6, 7)

    def start(self, steps=range(8)):
        for step in steps:
            for copy in self.line(step):
                copy.start()

    def spread(self, step):
        p = self.place
        slot = lax.rem(p.slot + 8 - step, 8)
        if isinstance(step, int) and step == 0:
            spot = self.target.at[p.block_here]
            pltpu.make_async_copy(spot, spot, self.sem(1, p.slot)).wait()
        else:
            self.whole(slot).wait_recv()
        for way in range(2):
            self.from_own(slot, way).start()

    def spread_from(self, slot):
        p = self.place

        @pl.when(p.slot == slot)
        def _():
            spot = self.target.at[p.block_here]
            pltpu.make_async_copy(spot, spot, self.sem(1, p.slot)).wait()

        pl.when(p.slot != slot)(lambda: self.whole(slot).wait_recv())
        for way in range(2):
            self.from_own(slot, way).start()

    def corners(self, z):
        self.from_own(2 * z, 0).wait_recv()
        self.corner(2 * z, 1).start()
        self.from_own(2 * z + 1, 1).wait_recv()
        self.corner(2 * z + 1, 0).start()

    def finish(self):
        for z in range(4):
            self.from_own(2 * z, 1).wait_recv()
            self.from_own(2 * z + 1, 0).wait_recv()
            self.corner(2 * z, 1).wait_recv()
            self.corner(2 * z + 1, 0).wait_recv()

    def drain(self):
        for step in range(1, 8):
            self.whole(lax.rem(self.place.slot + step, 8)).wait_send()
        for z in range(4):
            self.corner(2 * z, 1).wait_send()
            self.corner(2 * z + 1, 0).wait_send()
        for slot in range(8):
            for way in range(2):
                self.from_own(slot, way).wait_send()


class PlaneScatter:
    @staticmethod
    def scratch(units, rows, width):
        shape = (rows, width)
        return [
            pltpu.VMEM((2, 2, units) + shape, LOW),
            pltpu.VMEM((2, units) + shape, LOW),
            DMA((4, 2, 2, units)),
        ]

    def __init__(self, place, part, units, got, last, sems):
        self.place, self.part, self.units = place, part, units
        self.got, self.last, self.sems = got, last, sems

    def pair(self, near):
        p = self.place
        x, y = (p.x, p.y) if near else (1 - p.x, 1 - p.y)
        return ((p.x, y), (x, p.y))

    def own(self, half, near, unit):
        x, y = self.pair(near)[half]
        return self.part(half, unit, x, y)

    def sums(self, half, unit):
        return self.own(half, 1, unit)

    def first(self, half, near, unit):
        p = self.place
        x, y = self.pair(near)[half]
        x, y = (1 - x, y) if half == 0 else (x, 1 - y)
        where = {"x": 1 - p.x} if half == 0 else {"y": 1 - p.y}
        return remote(
            self.part(half, unit, x, y),
            self.got.at[half, near, unit],
            self.sems.at[0, half, near, unit],
            self.sems.at[1, half, near, unit],
            **where,
        )

    def second(self, half, unit):
        p = self.place
        where = {"y": 1 - p.y} if half == 0 else {"x": 1 - p.x}
        return remote(
            self.own(half, 0, unit),
            self.last.at[half, unit],
            self.sems.at[2, half, 0, unit],
            self.sems.at[3, half, 0, unit],
            **where,
        )

    def each(self, call):
        lax.fori_loop(0, self.units, lambda unit, carry: (call(unit), carry)[1], 0)

    def start_unit(self, unit):
        for near in range(2):
            for half in range(2):
                self.first(half, near, unit).start()

    def start(self):
        for near in range(2):

            def begin(unit):
                for half in range(2):
                    self.first(half, near, unit).start()

            self.each(begin)

    def middle(self, unit):
        for half in range(2):
            self.first(half, 0, unit).wait_recv()
            spot = self.own(half, 0, unit)
            add_blocks(spot, [spot, self.got.at[half, 0, unit]])
            self.second(half, unit).start()

    def final(self, unit):
        for half in range(2):
            self.first(half, 1, unit).wait_recv()
            self.second(half, unit).wait_recv()
            spot = self.own(half, 1, unit)
            add_blocks(spot, [spot, self.got.at[half, 1, unit], self.last.at[half, unit]])

    def drain(self):
        def end(unit):
            for half in range(2):
                for near in range(2):
                    self.first(half, near, unit).wait_send()
                self.second(half, unit).wait_send()

        self.each(end)


class LineReturn:
    SEMS = (2, 8)

    def __init__(self, place, sums, parts, target, sems):
        self.place, self.sums, self.parts = place, sums, parts
        self.target, self.sems = target, sems

    def copies(self, z, c, local):
        p = self.place
        made = []
        for here, size, first in self.parts:
            piece = self.sums(c, z).at[:, pl.ds(here, size)]
            spot = self.target.at[:, lanes(first + size * p.slot, size)]
            if local:
                made.append(pltpu.make_async_copy(piece, spot, self.sems.at[1, p.slot]))
            else:
                made.append(
                    remote(
                        piece, spot, self.sems.at[0, 2 * z + c], self.sems.at[1, p.slot], z=z, c=c
                    )
                )
        return made

    def send(self, z):
        p = self.place
        for c in range(2):
            mine = (z == p.z) & (c == p.c)

            @pl.when(mine)
            def _():
                for copy in self.copies(z, c, True):
                    copy.start()

            @pl.when(jnp.logical_not(mine))
            def _():
                for copy in self.copies(z, c, False):
                    copy.start()

    def finish(self):
        p = self.place
        spot = self.sums(0, 0)
        pltpu.make_async_copy(spot, spot, self.sems.at[1, p.slot]).wait()
        for step in range(1, 8):
            slot = lax.rem(p.slot + step, 8)
            whole = remote(
                spot, spot, self.sems.at[0, slot], self.sems.at[1, slot], c=1 - p.c
            )
            whole.wait_recv()
            whole.wait_send()


def kernel_call(kernel, name, number, inputs, in_specs, outputs, out_specs, scratch):
    return pl.pallas_call(
        kernel,
        out_shape=[jax.ShapeDtypeStruct(shape, dtype) for shape, dtype in outputs],
        in_specs=in_specs,
        out_specs=out_specs,
        scratch_shapes=scratch,
        compiler_params=pltpu.CompilerParams(
            collective_id=number, has_side_effects=True, vmem_limit_bytes=60 * 2**20
        ),
        name=name,
    )(*inputs)


CHUNK = 16


def by_rows(count, call):
    def some(step, carry):
        call(pl.ds(pl.multiple_of(step * CHUNK, CHUNK), CHUNK))
        return carry

    lax.fori_loop(0, count // CHUNK, some, 0)


def normed_back(grad_normed, unit, inverse, gain):
    grad_unit = grad_normed * gain
    return inverse * (grad_unit - unit * jnp.mean(grad_unit * unit, axis=-1, keepdims=True))


def turn_tables(length):
    half_dim = HEAD_DIM // 2
    exponent = np.arange(half_dim, dtype=np.float32) * np.float32(2.0 / HEAD_DIM)
    frequency = np.float32(ROPE_BASE) ** (-exponent)
    angles = np.arange(length, dtype=np.float32)[:, None] * frequency[None, :]
    angles = angles.astype(np.float64)
    cosines, sines = np.cos(angles).astype(np.float32), np.sin(angles).astype(np.float32)
    return (
        jnp.asarray(np.tile(cosines, (1, 4))),
        jnp.asarray(np.tile(np.concatenate([-sines, sines], axis=1), (1, 2))),
    )


def turn(values, cosines, sines):
    lane = lax.broadcasted_iota(jnp.int32, values.shape, 1)
    half_dim = HEAD_DIM // 2
    width = values.shape[1]
    partner = jnp.where(
        lax.rem(lane, HEAD_DIM) < half_dim,
        pltpu.roll(values, width - half_dim, 1),
        pltpu.roll(values, half_dim, 1),
    )
    return values * cosines + partner * sines


def head_mask(head):
    lane = lax.broadcasted_iota(jnp.int32, (1, 128), 1)
    return (lane // HEAD_DIM == lax.rem(head, 2)).astype(WIDE).astype(LOW)


def scaled_probs(queries, keys, first_row):
    scores = lax.dot_general(queries, keys, CONTRACT_LAST, preferred_element_type=WIDE)
    scores = scores * HEAD_DIM ** (-0.5)
    row = lax.broadcasted_iota(jnp.int32, scores.shape, 0) + first_row
    column = lax.broadcasted_iota(jnp.int32, scores.shape, 1)
    scores = jnp.where(column <= row, scores, MASKED)
    expo = jnp.exp(scores - jnp.max(scores, axis=1, keepdims=True))
    return expo * (1.0 / jnp.sum(expo, axis=1, keepdims=True))


QUERY_ROWS = 256


def attend_head(head, qkv, total):
    pair = lanes(head // 2 * 128, 128)
    mask = head_mask(head)
    for block in range(qkv.shape[1] // QUERY_ROWS):
        rows = pl.ds(block * QUERY_ROWS, QUERY_ROWS)
        keys = pl.ds(0, (block + 1) * QUERY_ROWS)
        probs = scaled_probs(qkv[0, rows, pair] * mask, qkv[1, keys, pair], block * QUERY_ROWS)
        total[rows, pair] += jnp.dot(
            probs.astype(LOW), qkv[2, keys, pair] * mask, preferred_element_type=WIDE
        )


def forward_kernel(
    tok,
    cot,
    wide_q,
    gain,
    wide_g,
    wide_d,
    wide_o,
    cosines,
    sines,
    all_cot,
    normed_two,
    full_g,
    full_d,
    out_q,
    out_o,
    out_normed,
    out_qkv,
    out_attended,
    out_residual,
    out_gains,
    out_tok,
    all_tok,
    full_q,
    full_o,
    normed_one,
    qkv,
    heads,
    attended,
    residual,
    gain_rows,
    mine,
    partial,
    from_q,
    from_g,
    from_d,
    from_o,
    wq,
    wg,
    wd,
    wo,
    *scratch,
):
    buffers, sems = scratch[:2], scratch[2:]
    tok_swap, cot_swap, out_swap, tok_sems, cot_sems, q_sems, g_sems, d_sems = sems[:8]
    o_sems, sum_a, sum_b, gather_a, gather_b, keep_sems, cast_sems = sems[8:]
    casts = [
        (wide_q, from_q, wq),
        (wide_o, from_o, wo),
        (wide_g, from_g, wg),
        (wide_d, from_d, wd),
    ]
    loads = [
        pltpu.make_async_copy(source, target, cast_sems.at[index])
        for index, (source, target, _) in enumerate(casts)
    ]
    for copy in loads:
        copy.start()

    def cast(index):
        _, source, target = casts[index]
        loads[index].wait()
        parts = source.shape[1] // 2048

        def some(step, carry):
            rows = pl.ds(pl.multiple_of(step // parts * CHUNK, CHUNK), CHUNK)
            columns = lanes(lax.rem(step, parts) * 2048, 2048)
            target[rows, columns] = source[rows, columns].astype(LOW)
            return carry

        lax.fori_loop(0, source.shape[0] // CHUNK * parts, some, 0)

    p = Place()
    p.meet(True)
    rows_own = tok.shape[0]
    seq_len = 8 * rows_own
    step_q, step_g, step_d = wq.shape[1] // 24, wg.shape[1] // 16, wd.shape[1] // 8
    q_parts = [(wq, i * 8 * step_q, step_q, i * step_q) for i in range(3)]
    q_parts.append((gain, 0, gain.shape[1], 3 * step_q))
    move_q = Relayout(p, q_parts, full_q, q_sems)
    move_g = Relayout(
        p, [(wg, i * 8 * step_g, step_g, i * step_g) for i in range(2)], full_g, g_sems
    )
    move_d = Relayout(p, [(wd, 0, step_d, 0)], full_d, d_sems)
    tokens = LineGather(p, all_tok, tok_sems)
    cotangents = LineGather(p, all_cot, cot_sems, rows=pl.ds(0, rows_own // 2))
    away = 2 * p.z + 1 - p.c
    swap_tok = Swap(p, tok, all_tok.at[away], all_tok.at[p.slot], tok_swap)
    swap_cot = Swap(p, cot, all_cot.at[away], all_cot.at[p.slot], cot_swap)
    swap_out = Swap(p, wo, full_o.at[2 * p.y + 1 - p.x], full_o.at[2 * p.y + p.x], out_swap)
    half = wo.shape[0] // 2

    def out_copy(kind):
        own, beside, above = 2 * p.y + p.x, 2 * p.y + 1 - p.x, 2 * (1 - p.y) + p.x
        send, got = o_sems.at[0, kind], o_sems.at[1, kind]
        if kind < 2:
            where = {"x": 1 - p.x} if kind == 0 else {"y": 1 - p.y}
            return remote(full_o.at[own], full_o.at[own], send, got, **where)
        spot = full_o.at[beside if kind == 2 else above, pl.ds((kind - 2) * half, half)]
        where = {"y": 1 - p.y} if kind == 2 else {"x": 1 - p.x}
        return remote(spot, spot, send, got, **where)

    kept = []

    def keep(source, target):
        copy = pltpu.make_async_copy(source, target, keep_sems.at[len(kept)])
        copy.start()
        kept.append(copy)

    swap_tok.start()
    cast(0)
    move_q.start()
    cast(1)
    swap_tok.wait()
    tokens.start()
    swap_out.start()
    swap_cot.start()
    cast(2)
    cast(3)
    for step in range(8):
        move_q.spread(step)
    tokens.inner(1)
    tokens.outer()
    move_g.start(range(3))
    tokens.inner(2)
    swap_out.wait()
    out_copy(0).start()
    out_copy(1).start()
    for z in range(4):
        move_q.corners(z)
    out_copy(0).wait_recv()
    out_copy(2).start()
    out_copy(1).wait_recv()
    out_copy(3).start()
    tokens.inner(3)
    tokens.drain()
    move_g.start(range(3, 8))
    swap_cot.wait()
    cotangents.start_part(True)
    move_q.finish()
    for step in range(3):
        move_g.spread(step)
    columns = full_q.shape[2]
    gain_block = full_q[:, :, pl.ds(3 * step_q, columns - 3 * step_q)].reshape(-1, 128)
    pick = lax.broadcasted_iota(jnp.int32, (8, 128), 0) == lax.broadcasted_iota(
        jnp.int32, (8, 128), 1
    )
    gain_rows[...] = lax.dot_general(
        pick.astype(WIDE).astype(LOW), gain_block, CONTRACT_LAST, preferred_element_type=WIDE
    )
    keep(full_q, out_q)
    keep(gain_rows, out_gains)
    tokens.finish()
    keep(all_tok.at[p.slot], out_tok)

    def norm_slot(slot, carry):
        def some(rows):
            unit, _ = rms_parts(all_tok[slot, rows, :].astype(WIDE))
            there = pl.ds(pl.multiple_of(slot * rows_own + rows.start, CHUNK), CHUNK)
            normed_one[there, :] = (unit * gain_rows[pl.ds(0, 1), :]).astype(LOW)

        by_rows(rows_own, some)
        return carry

    lax.fori_loop(0, 8, norm_slot, 0)
    keep(normed_one, out_normed)

    def project(part, carry):
        rows = pl.ds(pl.multiple_of(part * 512, 512), 512)
        for kind in range(3):
            weight = full_q[:, :, pl.ds(kind * step_q, step_q)].reshape(-1, step_q)
            made = jnp.dot(normed_one[rows, :], weight, preferred_element_type=WIDE)
            if kind < 2:
                made = turn(
                    made,
                    jnp.concatenate([cosines[rows, :]] * 2, axis=1),
                    jnp.concatenate([sines[rows, :]] * 2, axis=1),
                )
            qkv[kind, rows, :] = made.astype(LOW)
        return carry

    lax.fori_loop(0, seq_len // 512, project, 0)
    keep(qkv, out_qkv)
    heads[...] = jnp.zeros_like(heads)

    def one_head(head, carry):
        attend_head(head, qkv, heads)
        return carry

    lax.fori_loop(0, 4, one_head, 0)
    move_g.spread(3)
    attended[...] = heads[...].astype(LOW)
    keep(attended, out_attended)
    out_copy(2).wait_recv()
    out_copy(3).wait_recv()
    keep(full_o, out_o)
    out_weight = lambda: full_o[...].reshape(-1, full_o.shape[2])

    def project_out(part, carry):
        rows = pl.ds(pl.multiple_of(part * 256, 256), 256)
        made = jnp.dot(attended[rows, :], out_weight(), preferred_element_type=WIDE)
        partial[pl.ds(2 * part, 2)] = made.astype(LOW).reshape(2, rows_own, -1)
        return carry

    lax.fori_loop(0, seq_len // 256, project_out, 0)

    part_rows = [pl.ds(0, rows_own // 2), pl.ds(rows_own // 2, rows_own // 2)]
    sums = [
        LineScatter(p, partial, *buffers, sem, rows) for sem, rows in zip((sum_a, sum_b), part_rows)
    ]
    gathers = [
        LineGather(p, normed_two, sem, mine.at[rows], rows)
        for sem, rows in zip((gather_a, gather_b), part_rows)
    ]

    def local(part):
        def some(rows):
            there = pl.ds(pl.multiple_of(part * (rows_own // 2) + rows.start, CHUNK), CHUNK)
            total = all_tok[p.slot, there, :].astype(WIDE) + sums[part].total(there)
            residual[there, :] = total
            unit, _ = rms_parts(total)
            mine[there, :] = (unit * gain_rows[pl.ds(1, 1), :]).astype(LOW)

        by_rows(rows_own // 2, some)

    for part in sums:
        part.start()
    for part in sums:
        part.head()
    move_g.spread(4)
    move_g.spread(5)
    in_line = (p.z == 1) | (p.z == 2)
    pl.when(in_line)(lambda: cotangents.inner(1))
    sums[0].steps()
    move_g.spread(6)
    move_g.spread(7)
    pl.when(jnp.logical_not(in_line))(lambda: cotangents.inner(1))
    pl.when(in_line)(move_d.start)
    sums[0].arrive()
    local(0)
    gathers[0].start()
    move_g.corners(0)
    move_g.corners(1)
    sums[1].steps()
    move_g.corners(2)
    move_g.corners(3)
    gathers[0].inner(1)
    sums[1].arrive()
    local(1)
    gathers[1].start()
    keep(residual, out_residual)
    cotangents.start_part(False)
    pl.when(jnp.logical_not(in_line))(move_d.start)
    for slot in range(2, 6):
        move_d.spread_from(slot)
    gathers[0].outer()
    gathers[1].inner(1)
    gathers[0].inner(2)
    gathers[1].outer()
    gathers[1].inner(2)
    cotangents.outer()
    for slot in (0, 1, 6, 7):
        move_d.spread_from(slot)
    cotangents.inner(2)
    for z in range(4):
        move_d.corners(z)
    gathers[0].inner(3)
    gathers[1].inner(3)
    cotangents.inner(3)
    for kind in range(4):
        out_copy(kind).wait_send()
    for part in (swap_tok, swap_cot, swap_out):
        part.drain()
    for part in gathers + [cotangents, move_g, move_d]:
        part.finish()
    for part in gathers + sums + [cotangents, move_q, move_g, move_d]:
        part.drain()
    for copy in kept:
        copy.wait()


def forward(tokens, cotangent, qkv, gain_columns, gate_up, down, out_rows, cosines, sines):
    rows, width = tokens.shape
    own = qkv.shape[0]
    here = qkv.shape[1] // 24
    q_shape = (32, own, 3 * here + gain_columns.shape[1])
    vmem = lambda shape, dtype=LOW: pltpu.VMEM(shape, dtype)
    outputs = [
        ((8, rows, width), LOW),
        ((8, rows, width), LOW),
        ((32, own, gate_up.shape[1] // 8), LOW),
        ((32, own, down.shape[1] // 8), LOW),
        (q_shape, LOW),
        ((4, own, width), LOW),
        ((8 * rows, width), LOW),
        ((3, 8 * rows, here), LOW),
        ((8 * rows, here), LOW),
        ((rows, width), WIDE),
        ((8, width), WIDE),
        ((rows, width), LOW),
    ]
    return kernel_call(
        forward_kernel,
        "forward",
        1,
        (tokens, cotangent, qkv, gain_columns, gate_up, down, out_rows, cosines, sines),
        [ANYWHERE] * 7 + [IN_VMEM] * 2,
        outputs,
        [ANYWHERE] * len(outputs),
        [
            vmem((8, rows, width)),
            vmem(q_shape),
            vmem((4, own, width)),
            vmem((8 * rows, width)),
            vmem((3, 8 * rows, here)),
            vmem((8 * rows, here), WIDE),
            vmem((8 * rows, here)),
            vmem((rows, width), WIDE),
            vmem((8, width), WIDE),
            vmem((rows, width)),
            vmem((8, rows, width)),
        ]
        + [vmem(array.shape, WIDE) for array in (qkv, gate_up, down, out_rows)]
        + [vmem(array.shape) for array in (qkv, gate_up, down, out_rows)]
        + LineScatter.buffers(rows, width)
        + [DMA((3,))] * 3
        + [DMA(LineGather.SEMS)] * 2
        + [DMA(Relayout.SEMS)] * 3
        + [DMA((2, 4))]
        + [DMA(LineScatter.SEMS)] * 2
        + [DMA(LineGather.SEMS)] * 2
        + [DMA((8,)), DMA((4,))],
    )


def weight_part(place, ref):
    return lambda half, unit, x, y: ref.at[place.block(2 * unit + half, x, y)]


def attend_back(head, qkv, grad_heads, grads):
    pair = lanes(head // 2 * 128, 128)
    mask = head_mask(head)
    for block in range(qkv.shape[1] // QUERY_ROWS):
        rows = pl.ds(block * QUERY_ROWS, QUERY_ROWS)
        keys = pl.ds(0, (block + 1) * QUERY_ROWS)
        queries, grad_rows = qkv[0, rows, pair] * mask, grad_heads[rows, pair] * mask
        key_rows = qkv[1, keys, pair]
        probs = scaled_probs(queries, key_rows, block * QUERY_ROWS)
        grad_probs = lax.dot_general(
            grad_rows, qkv[2, keys, pair], CONTRACT_LAST, preferred_element_type=WIDE
        )
        delta = jnp.sum(probs * grad_probs, axis=1, keepdims=True)
        grad_scores = (probs * (grad_probs - delta) * HEAD_DIM ** (-0.5)).astype(LOW)
        grads[0, rows, pair] += jnp.dot(grad_scores, key_rows * mask, preferred_element_type=WIDE)
        grads[1, keys, pair] += lax.dot_general(
            grad_scores, queries, CONTRACT_FIRST, preferred_element_type=WIDE
        )
        grads[2, keys, pair] += lax.dot_general(
            probs.astype(LOW), grad_rows, CONTRACT_FIRST, preferred_element_type=WIDE
        )


def mlp_kernel(
    normed,
    wg,
    wd,
    cot,
    residual,
    gain_rows,
    branch,
    g_sum,
    d_part,
    block_out,
    out_grad,
    nt,
    full_g,
    full_d,
    ct,
    active,
    grad_wide,
    part_two,
    part_out,
    grad_residual,
    mine,
    *scratch,
):
    p = Place()
    rows_own, width = residual.shape
    seq_len = 8 * rows_own
    own, ff = wd.shape[1], wd.shape[2]
    units = wd.shape[0] // 8
    block_rows = seq_len // 2
    part = ff // 4
    wide = width // 4
    blocks = wide // own
    load_sems, sum_a, sum_b, sum_c, gather_a, gather_b, cot_sems, swap_sems, keep_sems = scratch[7:]
    part_rows = [pl.ds(0, rows_own // 2), pl.ds(rows_own // 2, rows_own // 2)]
    sum_two = [
        LineScatter(p, part_two, *scratch[:2], sem, rows)
        for sem, rows in zip((sum_a, sum_b), part_rows)
    ]
    sum_out = LineScatter(p, part_out, *scratch[2:4], sum_c, pl.ds(0, rows_own))
    plane = PlaneScatter(p, weight_part(p, full_g), units, *scratch[4:7])
    gathers = [
        LineGather(p, branch, sem, mine.at[rows], rows)
        for sem, rows in zip((gather_a, gather_b), part_rows)
    ]

    rest = LineGather(p, ct.at[1], cot_sems)

    def load(index):
        if index == 3:
            return pltpu.make_async_copy(
                cot.at[p.slot, part_rows[1]], ct.at[1, p.slot], load_sems.at[3]
            )
        if index < 4:
            source, target = ((normed, nt), (cot, ct))[index // 2]
            return pltpu.make_async_copy(
                source.at[:, part_rows[index % 2]], target.at[index % 2], load_sems.at[index]
            )
        return pltpu.make_async_copy(wd, full_d, load_sems.at[4])

    def load_wide(index, side):
        columns = lanes(side * ff + index * part, part)
        return pltpu.make_async_copy(
            wg.at[:, :, columns], full_g.at[:, :, columns], load_sems.at[5 + 2 * index + side]
        )

    load(3).start()
    load(0).start()
    for index in range(4):
        for side in range(2):
            load_wide(index, side).start()
        if index == 0:
            for other in (2, 4, 1):
                load(other).start()
    p.meet(True)
    load(3).wait()
    rest.start()
    for index in (0, 2, 4):
        load(index).wait()

    def stage_one(half, first, last):
        rows = pl.ds(half * block_rows, block_rows)

        def some(index, carry):
            if half == 0:
                load_wide(index, 0).wait()
                load_wide(index, 1).wait()
            here, there = lanes(index * part, part), lanes(ff + index * part, part)
            left = nt[half].reshape(block_rows, width)
            gate = jnp.dot(left, full_g[:, :, here].reshape(width, part), preferred_element_type=WIDE)
            up = jnp.dot(left, full_g[:, :, there].reshape(width, part), preferred_element_type=WIDE)
            grad = jnp.dot(
                ct[half].reshape(block_rows, width),
                full_d[:, :, here].reshape(width, part),
                preferred_element_type=WIDE,
            )
            sigmoid_gate = jax.nn.sigmoid(gate)
            active[rows, here] = (gate * sigmoid_gate * up).astype(LOW)
            grad_wide[rows, here] = (
                grad * up * sigmoid_gate * (1.0 + gate * (1.0 - sigmoid_gate))
            ).astype(LOW)
            grad_wide[rows, there] = (grad * gate * sigmoid_gate).astype(LOW)
            return carry

        lax.fori_loop(first, last, some, 0)

    def rows_times(left, weight, target, half, first, last):
        def some(index, carry):
            made = lax.dot_general(
                left[pl.ds(half * block_rows, block_rows), :],
                weight[pl.ds(index * blocks, blocks)].reshape(wide, -1),
                CONTRACT_LAST,
                preferred_element_type=WIDE,
            )
            target[:, part_rows[half], lanes(index * wide, wide)] = made.astype(LOW).reshape(
                8, rows_own // 2, wide
            )
            return carry

        lax.fori_loop(first, last, some, 0)

    def down_grad(index, carry):
        made = lax.dot_general(
            ct[:, :, :, lanes(index * wide, wide)].reshape(seq_len, wide),
            active[...],
            CONTRACT_FIRST,
            preferred_element_type=WIDE,
        )
        full_d[pl.ds(index * blocks, blocks)] = made.astype(LOW).reshape(blocks, own, ff)
        return carry

    def wide_grad(index):
        for side in range(2):
            made = lax.dot_general(
                nt[:, :, :, pl.ds(index * wide, wide)].reshape(seq_len, wide),
                grad_wide[:, pl.ds(side * ff, ff)],
                CONTRACT_FIRST,
                preferred_element_type=WIDE,
            )
            full_g[pl.ds(index * blocks, blocks), :, pl.ds(side * ff, ff)] = made.astype(
                LOW
            ).reshape(blocks, own, ff)
        plane.start_unit(index)

    def local_two(part):
        def some(rows):
            spot = pl.ds(pl.multiple_of(part * (rows_own // 2) + rows.start, CHUNK), CHUNK)
            unit, inverse = rms_parts(residual[spot, :])
            total = ct[part, p.slot, rows, :].astype(WIDE) + normed_back(
                sum_two[part].total(spot), unit, inverse, gain_rows[pl.ds(1, 1), :]
            )
            grad_residual[spot, :] = total
            mine[spot, :] = total.astype(LOW)

        by_rows(rows_own // 2, some)

    stage_one(0, 0, 4)
    rest.inner(1)
    rest.outer()
    rows_times(grad_wide, full_g, part_two, 0, 0, 4)
    sum_two[0].start()
    rest.inner(2)
    rows_times(active, full_d, part_out, 0, 0, 4)
    sum_two[0].head()
    load(1).wait()
    rest.inner(3)
    rest.finish()
    stage_one(1, 0, 2)
    sum_two[0].step(0)
    stage_one(1, 2, 4)
    sum_two[0].step(1)
    rows_times(grad_wide, full_g, part_two, 1, 0, 2)
    sum_two[0].step(2)
    rows_times(grad_wide, full_g, part_two, 1, 2, 4)
    sum_two[1].start()
    wide_grad(0)
    sum_two[1].head()
    sum_two[0].arrive()
    local_two(0)
    gathers[0].start()
    sum_two[1].step(0)
    rows_times(active, full_d, part_out, 1, 0, 4)
    sum_out.start()
    sum_two[1].step(1)
    sum_two[1].step(2)
    wide_grad(1)
    gathers[0].inner(1)
    sum_two[1].arrive()
    local_two(1)
    gathers[1].start()
    sum_out.head()
    keep_grad = pltpu.make_async_copy(grad_residual, out_grad, keep_sems.at[1])
    keep_grad.start()
    wide_grad(2)
    gathers[0].outer()
    gathers[1].inner(1)
    wide_grad(3)
    gathers[0].inner(2)
    gathers[1].outer()
    plane.middle(0)
    lax.fori_loop(0, 2, down_grad, 0)
    gathers[1].inner(2)
    lax.fori_loop(2, 4, down_grad, 0)
    keep_d = pltpu.make_async_copy(full_d, d_part, keep_sems.at[0])
    keep_d.start()
    plane.middle(1)
    sum_out.step(0)
    gathers[0].inner(3)
    gathers[1].inner(3)
    plane.middle(2)
    sum_out.step(1)
    sum_out.step(2)
    plane.middle(3)
    for gather in gathers:
        gather.finish()
    for gather in gathers:
        gather.drain()
    def keep_g(half, unit):
        return pltpu.make_async_copy(
            plane.sums(half, unit), g_sum.at[half, unit], keep_sems.at[2 + 4 * half + unit]
        )

    def finish_unit(unit):
        plane.final(unit)
        for half in range(2):
            keep_g(half, unit).start()

    for unit in range(units - 1):
        finish_unit(unit)
    sum_out.arrive()

    def local_out(rows):
        mine[rows, :] = (residual[rows, :] + sum_out.total(rows)).astype(LOW)

    by_rows(rows_own, local_out)
    keep_block = pltpu.make_async_copy(mine, block_out, swap_sems.at[0])
    keep_block.start()
    finish_unit(units - 1)
    keep_block.wait()
    for part in sum_two + [sum_out, plane, rest]:
        part.drain()
    keep_d.wait()
    keep_grad.wait()
    for unit in range(units):
        for half in range(2):
            keep_g(half, unit).wait()


def mlp(normed, wg, wd, cot, residual, gain_rows):
    _, rows, width = normed.shape
    own, ff = wd.shape[1:]
    units = wd.shape[0] // 8
    vmem = lambda shape, dtype=LOW: pltpu.VMEM(shape, dtype)
    return kernel_call(
        mlp_kernel,
        "mlp",
        2,
        (normed, wg, wd, cot, residual, gain_rows),
        [ANYWHERE] * 4 + [IN_VMEM] * 2,
        [
            (normed.shape, LOW),
            ((2, units, own, 2 * ff), LOW),
            (wd.shape, LOW),
            ((rows, width), LOW),
            ((rows, width), WIDE),
        ],
        [ANYWHERE] * 5,
        [
            vmem((2, 8, rows // 2, width)),
            vmem(wg.shape),
            vmem(wd.shape),
            vmem((2, 8, rows // 2, width)),
            vmem((8 * rows, ff)),
            vmem((8 * rows, 2 * ff)),
            vmem(normed.shape),
            vmem(normed.shape),
            vmem((rows, width), WIDE),
            vmem((rows, width)),
        ]
        + LineScatter.buffers(rows, width) * 2
        + PlaneScatter.scratch(units, own, 2 * ff)
        + [DMA((13,))]
        + [DMA(LineScatter.SEMS)] * 3
        + [DMA(LineGather.SEMS)] * 3
        + [DMA((3,)), DMA((2 + 2 * units,))],
    )


def backward_kernel(
    branch_all,
    grad_in,
    gain_rows,
    own_tok,
    full_q,
    full_o,
    qkv,
    attended,
    normed_one,
    cosines,
    sines,
    g_sum,
    d_part,
    block,
    input_grad,
    block_out,
    q_out,
    g_out,
    d_out,
    o_out,
    work,
    branch,
    grad_residual,
    grad_heads,
    grads,
    grad_projected,
    q_part,
    o_part,
    o_sum,
    d_here,
    *scratch,
):
    buffers, rest = scratch[:2], scratch[2:]
    p = Place()
    rows_own, width = grad_residual.shape
    seq_len = 8 * rows_own
    own = full_o.shape[1]
    units = g_sum.shape[1]
    half = own // 2
    step_q, step_g, step_d = q_part.shape[2] // 3, g_sum.shape[3] // 2, d_part.shape[2]
    plane_d = PlaneScatter(p, weight_part(p, d_here), units, *rest[:3])
    plane_q = PlaneScatter(p, weight_part(p, q_part), units, *rest[3:6])
    plane_o = PlaneScatter(
        p, lambda h, u, x, y: o_part.at[2 * y + x, pl.ds(h * half, half)], 1, *rest[6:9]
    )
    sum_sems, return_sems, swap_sems, load_sems = rest[9:11], rest[11:14], rest[14:18], rest[18]
    part_rows = [pl.ds(0, rows_own // 2), pl.ds(rows_own // 2, rows_own // 2)]
    sum_one = [
        LineScatter(p, branch, *buffers, sem, rows) for sem, rows in zip(sum_sems, part_rows)
    ]
    return_q = LineReturn(
        p, plane_q.sums, [(i * step_q, step_q, i * 8 * step_q) for i in range(3)], q_out, return_sems[0]
    )
    return_g = LineReturn(
        p,
        lambda c, z: g_sum.at[c, z],
        [(i * step_g, step_g, i * 8 * step_g) for i in range(2)],
        g_out,
        return_sems[1],
    )
    return_d = LineReturn(p, plane_d.sums, [(0, step_d, 0)], d_out, return_sems[2])
    swap_in = [
        Swap(p, grad_residual.at[rows], input_grad.at[rows], input_grad.at[rows], sem)
        for sem, rows in zip(swap_sems[:2], part_rows)
    ]
    swap_out = Swap(p, o_sum, o_out, o_out, swap_sems[2])
    swap_block = Swap(p, block, block_out, block_out, swap_sems[3])

    def load(source, target, index):
        return pltpu.make_async_copy(source, target, load_sems.at[index])

    loads = [
        load(branch_all, branch, 0),
        load(d_part, d_here, 1),
        load(normed_one, work, 2),
        load(grad_in, grad_residual, 3),
    ]
    for copy in loads:
        copy.start()
    p.meet(True)
    swap_block.start()
    for z in range(4):
        return_g.send(z)
    loads[0].wait()

    def back_out(part, carry):
        rows = pl.ds(pl.multiple_of(part * 256, 256), 256)
        made = lax.dot_general(
            branch[pl.ds(2 * part, 2)].reshape(256, width),
            full_o[...].reshape(-1, width),
            CONTRACT_LAST,
            preferred_element_type=WIDE,
        )
        grad_heads[rows, :] = made.astype(LOW)
        return carry

    lax.fori_loop(0, seq_len // 256, back_out, 0)
    loads[1].wait()
    plane_d.start()

    def out_grad(part, carry):
        columns = lanes(part * 512, 512)
        made = lax.dot_general(
            attended[...],
            branch[:, :, columns].reshape(seq_len, 512),
            CONTRACT_FIRST,
            preferred_element_type=WIDE,
        )
        o_part[:, :, columns] = made.astype(LOW).reshape(4, own, 512)
        return carry

    lax.fori_loop(0, width // 512, out_grad, 0)
    plane_o.start()
    grads[...] = jnp.zeros_like(grads)

    def one_head(head, carry):
        attend_back(head, qkv, grad_heads, grads)
        plane_d.middle(head)
        return carry

    lax.fori_loop(0, 4, one_head, 0)

    def back_turn(part, carry):
        rows = pl.ds(pl.multiple_of(part * 256, 256), 256)
        for kind in range(3):
            made = grads[kind, rows, :]
            if kind < 2:
                made = turn(
                    made,
                    jnp.concatenate([cosines[rows, :]] * 2, axis=1),
                    jnp.concatenate([-sines[rows, :]] * 2, axis=1),
                )
            grad_projected[rows, pl.ds(kind * step_q, step_q)] = made.astype(LOW)
        return carry

    lax.fori_loop(0, seq_len // 256, back_turn, 0)

    def back_qkv(part, carry):
        weight = full_q[pl.ds(part * 8, 8), :, pl.ds(0, 3 * step_q)].reshape(8 * own, 3 * step_q)
        for block in range(seq_len // 512):
            made = lax.dot_general(
                grad_projected[pl.ds(block * 512, 512), :],
                weight,
                CONTRACT_LAST,
                preferred_element_type=WIDE,
            )
            branch[pl.ds(block * 4, 4), :, lanes(part * 8 * own, 8 * own)] = made.astype(
                LOW
            ).reshape(4, rows_own, 8 * own)
        return carry

    lax.fori_loop(0, 4, back_qkv, 0)
    for part in sum_one:
        part.start()
    loads[2].wait()
    loads[3].wait()
    for part in sum_one:
        part.head()

    def qkv_grad(part, carry):
        made = lax.dot_general(
            work[:, :, lanes(part * 8 * own, 8 * own)].reshape(seq_len, 8 * own),
            grad_projected[...],
            CONTRACT_FIRST,
            preferred_element_type=WIDE,
        )
        q_part[pl.ds(part * 8, 8)] = made.astype(LOW).reshape(8, own, 3 * step_q)
        plane_q.start_unit(part)
        return carry

    lax.fori_loop(0, 4, qkv_grad, 0)

    def local_one(part):
        def some(rows):
            spot = pl.ds(pl.multiple_of(part * (rows_own // 2) + rows.start, CHUNK), CHUNK)
            unit, inverse = rms_parts(own_tok[spot, :].astype(WIDE))
            grad_residual[spot, :] = grad_residual[spot, :] + normed_back(
                sum_one[part].total(spot), unit, inverse, gain_rows[pl.ds(0, 1), :]
            )

        by_rows(rows_own // 2, some)

    for part in sum_one:
        part.steps()
    for unit in range(units):
        plane_d.final(unit)
        return_d.send(unit)
    plane_o.middle(0)
    for unit in range(units):
        plane_q.middle(unit)
    for part in range(2):
        sum_one[part].arrive()
        local_one(part)
        swap_in[part].start()
    plane_o.final(0)
    for h in range(2):
        o_sum[pl.ds(h * half, half), :] = plane_o.sums(h, 0)[...]
    swap_out.start()
    for unit in range(units):
        plane_q.final(unit)
        return_q.send(unit)
    for part in (return_g, return_d, return_q):
        part.finish()
    for part in swap_in + [swap_out, swap_block]:
        part.wait()
        part.drain()
    for part in sum_one + [plane_d, plane_q, plane_o]:
        part.drain()


def backward(
    branch,
    grad_residual,
    gain_rows,
    own_tok,
    full_q,
    full_o,
    qkv,
    attended,
    normed_one,
    cosines,
    sines,
    g_sum,
    d_part,
    block,
):
    _, rows, width = branch.shape
    own, here = full_o.shape[1], attended.shape[1]
    units = g_sum.shape[1]
    vmem = lambda shape, dtype=LOW: pltpu.VMEM(shape, dtype)
    step_g, step_d = g_sum.shape[3], d_part.shape[2]
    return kernel_call(
        backward_kernel,
        "backward",
        3,
        (
            branch,
            grad_residual,
            gain_rows,
            own_tok,
            full_q,
            full_o,
            qkv,
            attended,
            normed_one,
            cosines,
            sines,
            g_sum,
            d_part,
            block,
        ),
        [ANYWHERE] * 2 + [IN_VMEM] * 6 + [ANYWHERE] + [IN_VMEM] * 2 + [ANYWHERE] * 3,
        [
            ((rows, width), WIDE),
            ((rows, width), LOW),
            ((own, 24 * here), LOW),
            ((own, 8 * step_g), LOW),
            ((own, 8 * step_d), LOW),
            ((own, width), LOW),
        ],
        [ANYWHERE] * 6,
        [
            vmem((8, rows, width)),
            vmem((8, rows, width)),
            vmem((rows, width), WIDE),
            vmem((8 * rows, here)),
            vmem((3, 8 * rows, here), WIDE),
            vmem((8 * rows, 3 * here)),
            vmem((32, own, 3 * here)),
            vmem((4, own, width)),
            vmem((own, width)),
            vmem(d_part.shape),
        ]
        + LineScatter.buffers(rows, width)
        + PlaneScatter.scratch(units, own, step_d)
        + PlaneScatter.scratch(units, own, 3 * here)
        + PlaneScatter.scratch(1, own // 2, width)
        + [DMA(LineScatter.SEMS)] * 2
        + [DMA(LineReturn.SEMS)] * 3
        + [DMA((3,))] * 4
        + [DMA((4,))],
    )


ADAM_STEPS = 4
WIDE_RATE = 2.5 * D ** (-0.5)
OUT_RATE = 2.5 * max(D // 512, 1) ** (-0.5)
DOWN_RATE = 2.5 * FF ** (-0.5)


def adam_quick(weight, gradient, first, second, rate, decay):
    new_first = BETA_ONE * first + (1.0 - BETA_ONE) * gradient
    new_second = BETA_TWO * second + (1.0 - BETA_TWO) * gradient * gradient
    root = jnp.sqrt(new_second * (1.0 / (1.0 - BETA_TWO**STEP))) + ADAM_EPS
    moved = new_first * (rate / (1.0 - BETA_ONE**STEP)) / root
    return ((1.0 - rate * decay) * weight - moved, new_first, new_second)


def adam_kernel(*refs):
    inputs, gains, handed = refs[:16], refs[16:19], refs[19:21]
    outputs, gains_new, placed = refs[21:33], refs[33:36], refs[36:38]
    sums = refs[38:]
    step = pl.program_id(0)
    for source, target in zip(handed, placed):
        target[...] = source[...]

    @pl.when(step == 0)
    def _():
        for total in sums:
            total[...] = jnp.zeros_like(total)

    for index, rate in enumerate((WIDE_RATE, OUT_RATE, WIDE_RATE, DOWN_RATE)):
        weight, first, second, low_gradient = (ref[...] for ref in inputs[4 * index : 4 * index + 4])
        gradient = low_gradient.astype(WIDE)
        made = adam_quick(weight, gradient, first, second, rate, WEIGHT_DECAY)
        for target, value in zip(outputs[3 * index : 3 * index + 3], made):
            target[...] = value
        if index % 2 == 0:
            total = jnp.sum(weight.astype(LOW).astype(WIDE) * gradient, axis=1, keepdims=True)
            sums[index // 2][...] += jnp.broadcast_to(total, sums[index // 2].shape)

    @pl.when(step == ADAM_STEPS - 1)
    def _():
        rows = [jnp.transpose(total[...])[:1] for total in sums]
        weight, first, second = (ref[...] for ref in gains)
        gradient = jnp.concatenate(rows, axis=0) / weight.astype(LOW).astype(WIDE)
        for target, value in zip(gains_new, adam_quick(weight, gradient, first, second, 0.5, 0.0)):
            target[...] = value


def adam_all(groups, gains, handed):
    specs, out_specs, out_shape = [], [], []
    rows = groups[0][0].shape[0]
    for group in groups:
        spec = pl.BlockSpec((rows, group[0].shape[1] // ADAM_STEPS), lambda step: (0, step))
        specs += [spec] * 4
        out_specs += [spec] * 3
        out_shape += [jax.ShapeDtypeStruct(group[0].shape, WIDE)] * 3
    whole = [pl.BlockSpec(gains[0].shape, lambda step: (0, 0))] * 3
    whole += [
        pl.BlockSpec((a.shape[0], a.shape[1] // ADAM_STEPS), lambda step: (0, step)) for a in handed
    ]
    arrays = list(gains) + list(handed)
    return pl.pallas_call(
        adam_kernel,
        grid=(ADAM_STEPS,),
        in_specs=specs + whole,
        out_specs=out_specs + whole,
        out_shape=out_shape + [jax.ShapeDtypeStruct(a.shape, a.dtype) for a in arrays],
        scratch_shapes=[pltpu.VMEM((rows, 128), WIDE)] * 2,
        compiler_params=pltpu.CompilerParams(vmem_limit_bytes=56 * 2**20),
        name="adam",
    )(*[array for group in groups for array in group], *arrays)


def grid_shards(
    tokens,
    cotangent,
    qkv_weight,
    out_weight,
    gate_up_weight,
    down_weight,
    gains,
    qkv_first,
    out_first,
    gate_up_first,
    down_first,
    gains_first,
    qkv_second,
    out_second,
    gate_up_second,
    down_second,
    gains_second,
):
    rows, width = tokens.shape[1:]
    seq_len = 8 * rows
    gain_columns = jnp.pad(gains.astype(LOW).T, ((0, 0), (0, 126)))
    cosines, sines = turn_tables(seq_len)
    (
        grad_out,
        normed_two,
        gate_up_full,
        down_full,
        qkv_full,
        out_full,
        normed_one,
        qkv_heads,
        attended,
        residual,
        gain_full,
        own_tokens,
    ) = forward(
        tokens[0],
        cotangent[0],
        qkv_weight,
        gain_columns,
        gate_up_weight,
        down_weight,
        out_weight,
        cosines,
        sines,
    )
    grad_branch, gate_up_half, down_part, block_own, grad_residual = mlp(
        normed_two, gate_up_full, down_full, grad_out, residual, gain_full
    )
    input_grad, block_out, qkv_sum, gate_up_sum, down_sum, out_sum = backward(
        grad_branch,
        grad_residual,
        gain_full,
        own_tokens,
        qkv_full,
        out_full,
        qkv_heads,
        attended,
        normed_one.reshape(8, rows, width),
        cosines,
        sines,
        gate_up_half,
        down_part,
        block_own,
    )
    made = adam_all(
        [
            (qkv_weight, qkv_first, qkv_second, qkv_sum),
            (out_weight, out_first, out_second, out_sum),
            (gate_up_weight, gate_up_first, gate_up_second, gate_up_sum),
            (down_weight, down_first, down_second, down_sum),
        ],
        (gains, gains_first, gains_second),
        (input_grad, block_out),
    )
    qkv_new, out_new, gate_up_new, down_new, gains_new = (
        made[3 * i : 3 * i + 3] for i in range(5)
    )
    input_grad, block_out = made[15:]
    return (
        block_out[None],
        input_grad[None],
        qkv_new[0],
        out_new[0],
        gate_up_new[0],
        down_new[0],
        gains_new[0],
        qkv_new[1],
        out_new[1],
        gate_up_new[1],
        down_new[1],
        gains_new[1],
        qkv_new[2],
        out_new[2],
        gate_up_new[2],
        down_new[2],
        gains_new[2],
    )


def mapped(body, mesh, token_spec, row_spec, gain_spec):
    one_set = (row_spec, row_spec, row_spec, row_spec, gain_spec)
    return jax.shard_map(
        body,
        mesh=mesh,
        in_specs=(token_spec, token_spec) + one_set * 3,
        out_specs=(token_spec, token_spec) + one_set * 3,
        check_vma=False,
    )


def solution(mesh):
    if mesh.shape["seq"] == 8 and mesh.shape["dp"] == 4:
        grid_mesh = Mesh(mesh.devices.reshape(4, 2, 2, 2), GRID)
        return mapped(
            grid_shards,
            grid_mesh,
            P(("y", "c"), ("z", "x"), None),
            P(GRID, None),
            P(None, GRID),
        )
    return mapped(
        shards, mesh, P("dp", "seq", None), P(("seq", "dp"), None), P(None, ("seq", "dp"))
    )
```
